32 devices in a mesh: wide: 2 (over x), narrow: 16 (over z, y, core).
Axes of the slice: x: 2, y: 2, z: 4, core: 2. Of those that a mesh axis runs over, the one named last changes fastest.
Arguments:
- target: bfloat16 [32, 1024, 768], P('narrow', 'wide'), may hold values from -6 to 6
- encoded: bfloat16 [32, 1024, 768], P('narrow', 'wide'), may hold values from -6 to 6
- segments: int32 [32, 1024], P('narrow', 'wide'), may hold values from 0 to 3, as said below
- out_grad: bfloat16 [32, 1024, 768], P('narrow', 'wide'), may hold values from -6 to 6
- self_qkv_w: bfloat16 [768, 2304], replicated, may hold values from -0.3125 to 0.3125
- self_q_b: float32 [768], replicated, may hold values from -2 to 2
- self_v_b: float32 [768], replicated, may hold values from -2 to 2
- self_out_w: bfloat16 [768, 768], replicated, may hold values from -0.625 to 0.625
- self_out_b: float32 [768], replicated, may hold values from -3 to 3
- norm1_gain: float32 [768], replicated, may hold values from 0.5 to 1.5
- norm1_bias: float32 [768], replicated, may hold values from -2 to 2
- cross_q_w: bfloat16 [768, 768], replicated, may hold values from -0.3125 to 0.3125
- cross_q_b: float32 [768], replicated, may hold values from -2 to 2
- cross_kv_w: bfloat16 [768, 1536], replicated, may hold values from -0.3125 to 0.3125
- cross_v_b: float32 [768], replicated, may hold values from -2 to 2
- cross_out_w: bfloat16 [768, 768], replicated, may hold values from -0.625 to 0.625
- cross_out_b: float32 [768], replicated, may hold values from -3 to 3
- norm2_gain: float32 [768], replicated, may hold values from 0.5 to 1.5
- norm2_bias: float32 [768], replicated, may hold values from -2 to 2
- ffn_in_w: bfloat16 [768, 3072], replicated, may hold values from -0.21875 to 0.21875
- ffn_in_b: float32 [3072], replicated, may hold values from -2 to 2
- ffn_out_w: bfloat16 [3072, 768], replicated, may hold values from -0.15625 to 0.15625
- ffn_out_b: float32 [768], replicated, may hold values from -2 to 2
- norm3_gain: float32 [768], replicated, may hold values from 0.5 to 1.5
- norm3_bias: float32 [768], replicated, may hold values from -2 to 2
Outputs:
- layer_out: bfloat16 [32, 1024, 768], P('narrow', 'wide')
- target_grad: float32 [32, 1024, 768], P('narrow', 'wide')
- encoded_grad: float32 [32, 1024, 768], P('narrow', 'wide')
- self_qkv_w_grad: float32 [768, 2304], P('wide')
- self_q_b_grad: float32 [768], P('wide')
- self_v_b_grad: float32 [768], P('wide')
- self_out_w_grad: float32 [768, 768], P('wide')
- self_out_b_grad: float32 [768], P('wide')
- norm1_gain_grad: float32 [768], P('wide')
- norm1_bias_grad: float32 [768], P('wide')
- cross_q_w_grad: float32 [768, 768], P('wide')
- cross_q_b_grad: float32 [768], P('wide')
- cross_kv_w_grad: float32 [768, 1536], P('wide')
- cross_v_b_grad: float32 [768], P('wide')
- cross_out_w_grad: float32 [768, 768], P('wide')
- cross_out_b_grad: float32 [768], P('wide')
- norm2_gain_grad: float32 [768], P('wide')
- norm2_bias_grad: float32 [768], P('wide')
- ffn_in_w_grad: float32 [768, 3072], P('wide')
- ffn_in_b_grad: float32 [3072], P('wide')
- ffn_out_w_grad: float32 [3072, 768], P('wide')
- ffn_out_b_grad: float32 [768], P('wide')
- norm3_gain_grad: float32 [768], P('wide')
- norm3_bias_grad: float32 [768], P('wide')
The draws below stay inside these ranges and needn't reach their ends.
Inputs may be any that keep to these rules, and one draw needn't show every extreme that they name: `segments`: rows come in aligned pairs (rows 2 i and 2 i + 1). In each pair one row, which one drawn from the seed, is a single document (id 0 throughout); the other holds four documents with ids 0, 1, 2, 3 in order, each of 256 tokens give or take 1024 // 8.
All inputs are finite; a program needn't handle non-finite values.
Results may differ from the reference program's by a relative error of at most 0.03.
Values may be sent and summed in bfloat16 or wider, within the bound.
No kernel may reach another device: no remote copies, remote signals or barrier semaphores. Data moves between devices by JAX's collectives and lax.ppermute only.
A program may use at most 256 MiB of HBM per device.

```python
import math
import jax
import jax.numpy as jnp
from jax import lax

D = 768
HD = 64
FF = 3072
LEN = 1024
ROWS = 32


def draw_segments(key, part):
    key = jax.random.fold_in(key, 11)
    flip_key, cut_key = jax.random.split(key, 2)
    pair_flip = jax.random.randint(flip_key, (ROWS // 2, 1), 0, 2)
    whole_row = jnp.concatenate([pair_flip, 1 - pair_flip], 1).reshape(ROWS, 1)
    jitter = LEN // 16
    cuts = jnp.arange(1, 4, dtype=jnp.int32)[None, :] * (LEN // 4) + jax.random.randint(cut_key, (ROWS, 3), -jitter, jitter + 1)
    positions = jnp.arange(LEN, dtype=jnp.int32)[None, :, None]
    packed = jnp.sum((positions >= cuts[:, None, :]).astype(jnp.int32), -1)
    return packed * (1 - whole_row)


def block_levels(key, dims, cuts, smallest, high):
    factor_of, own = 1.0, jax.random.fold_in(key, 6)
    for position, shards_of in cuts:
        steps = jnp.exp(jax.random.uniform(jax.random.fold_in(own, position), (shards_of,), jnp.float32, smallest / len(cuts), high / len(cuts)))
        factor_of = factor_of * jnp.repeat(steps, dims[position] // shards_of).reshape([-1 if axis == position else 1 for axis in range(len(dims))])
    return factor_of


def normal_values(own_key, extent, scale, most, shards=(), kind=jnp.bfloat16):
    drawn = scale * jax.random.normal(own_key, extent, jnp.float32)
    if shards:
        drawn = drawn * block_levels(own_key, extent, shards, -0.22, 0.18)
    return jnp.clip(drawn, -most, most).astype(kind)


def setup_inputs(seed: int = 0) -> dict:
    seeds = jax.random.split(jax.random.key(seed), 26)
    return {
        "target": normal_values(seeds[0], (ROWS, LEN, D), 1.0, 6.0, ((0, 16), (1, 2))),
        "encoded": normal_values(seeds[1], (ROWS, LEN, D), 1.0, 6.0, ((0, 16), (1, 2))),
        "segments": draw_segments(jax.random.fold_in(seeds[25], 71), 0),
        "out_grad": normal_values(seeds[3], (ROWS, LEN, D), 1.0, 6.0, ((0, 16), (1, 2))),
        "self_qkv_w": normal_values(seeds[4], (D, 3 * D), (D // 2) ** -0.5, 0.3125),
        "self_q_b": normal_values(seeds[5], (D,), 0.3, 2.0, (), jnp.float32),
        "self_v_b": normal_values(seeds[6], (D,), 0.3, 2.0, (), jnp.float32),
        "self_out_w": normal_values(seeds[7], (D, D), (max(D // 8, 1)) ** -0.5, 0.625),
        "self_out_b": normal_values(seeds[8], (D,), 0.5, 3.0, (), jnp.float32),
        "norm1_gain": jnp.clip(1.0 + 0.1 * jax.random.normal(seeds[9], (D,), jnp.float32), 0.5, 1.5),
        "norm1_bias": normal_values(seeds[10], (D,), 0.3, 2.0, (), jnp.float32),
        "cross_q_w": normal_values(seeds[11], (D, D), (D // 2) ** -0.5, 0.3125),
        "cross_q_b": normal_values(seeds[12], (D,), 0.3, 2.0, (), jnp.float32),
        "cross_kv_w": normal_values(seeds[13], (D, 2 * D), (D // 2) ** -0.5, 0.3125),
        "cross_v_b": normal_values(seeds[14], (D,), 0.3, 2.0, (), jnp.float32),
        "cross_out_w": normal_values(seeds[15], (D, D), (max(D // 8, 1)) ** -0.5, 0.625),
        "cross_out_b": normal_values(seeds[16], (D,), 0.5, 3.0, (), jnp.float32),
        "norm2_gain": jnp.clip(1.0 + 0.1 * jax.random.normal(seeds[17], (D,), jnp.float32), 0.5, 1.5),
        "norm2_bias": normal_values(seeds[18], (D,), 0.3, 2.0, (), jnp.float32),
        "ffn_in_w": normal_values(seeds[19], (D, FF), D ** -0.5, 0.21875),
        "ffn_in_b": normal_values(seeds[20], (FF,), 0.3, 2.0, (), jnp.float32),
        "ffn_out_w": normal_values(seeds[21], (FF, D), (FF // 2) ** -0.5, 0.15625),
        "ffn_out_b": normal_values(seeds[22], (D,), 0.3, 2.0, (), jnp.float32),
        "norm3_gain": jnp.clip(1.0 + 0.1 * jax.random.normal(seeds[23], (D,), jnp.float32), 0.5, 1.5),
        "norm3_bias": normal_values(seeds[24], (D,), 0.3, 2.0, (), jnp.float32),
    }


@jax.custom_vjp
def low(v):
    return lax.optimization_barrier(v.astype(jnp.bfloat16)).astype(jnp.float32)

@jax.custom_vjp
def low_back(v):
    return v

def low_keep(v):
    return (low(v), None)

def low_pass(kept, grad):
    return (grad,)

def back_keep(v):
    return (v, None)

def back_low(kept, grad):
    return (low(grad),)
low.defvjp(low_keep, low_pass)
low_back.defvjp(back_keep, back_low)
masked_score = -1000000000.0
norm_epsilon = 1e-05
full_precision = lax.Precision.HIGHEST

def layer_norm(resid, gain_vec, bias_vec):
    center = resid - lax.optimization_barrier(jnp.mean(resid, -1, keepdims=True))
    spread = lax.optimization_barrier(jnp.mean(center * center, -1, keepdims=True))
    return center * lax.rsqrt(spread + norm_epsilon) * gain_vec + bias_vec

def product(left_op, right_op):
    return jnp.dot(left_op, right_op, precision=full_precision)

def attend_rows(queries, keys_all, values_all, segment_ids, causal):
    row_count, length, heads, head_size = queries.shape
    block_rows = math.gcd(length, 512)
    blocks_per_row = length // block_rows

    def one_block(block_index):
        row_index = block_index // blocks_per_row
        first_pos = block_index % blocks_per_row * block_rows
        row_queries = lax.dynamic_index_in_dim(queries, row_index, 0, keepdims=False)
        block_queries = lax.dynamic_slice_in_dim(row_queries, first_pos, block_rows, 0)
        row_keys = lax.dynamic_index_in_dim(keys_all, row_index, 0, keepdims=False)
        row_values = lax.dynamic_index_in_dim(values_all, row_index, 0, keepdims=False)
        row_segments = lax.dynamic_index_in_dim(segment_ids, row_index, 0, keepdims=False)
        query_segments = lax.dynamic_slice_in_dim(row_segments, first_pos, block_rows, 0)
        scores = low_back(jnp.einsum('thd,shd->hts', block_queries, row_keys, precision=full_precision))
        allowed = query_segments[None, :, None] == row_segments[None, None, :]
        if causal:
            query_pos = first_pos + jnp.arange(block_rows, dtype=jnp.int32)
            key_pos = jnp.arange(length, dtype=jnp.int32)
            allowed = allowed & (key_pos[None, None, :] <= query_pos[None, :, None])
        scores = jnp.where(allowed, scores, masked_score)
        top_score = lax.optimization_barrier(jnp.max(scores, -1, keepdims=True))
        expo = jnp.exp(scores - top_score)
        weights = low(expo / lax.optimization_barrier(jnp.sum(expo, -1, keepdims=True)))
        return jnp.einsum('hts,shd->thd', weights, row_values, precision=full_precision)
    blocks = lax.map(jax.checkpoint(one_block), jnp.arange(row_count * blocks_per_row, dtype=jnp.int32))
    return blocks.reshape(row_count, length, heads, head_size)

def reference(target, encoded, segments, out_grad, self_qkv_w, self_q_b, self_v_b, self_out_w, self_out_b, norm1_gain, norm1_bias, cross_q_w, cross_q_b, cross_kv_w, cross_v_b, cross_out_w, cross_out_b, norm2_gain, norm2_bias, ffn_in_w, ffn_in_b, ffn_out_w, ffn_out_b, norm3_gain, norm3_bias):
    row_count, length, width = target.shape
    heads = width // HD
    scaling = HD ** (-0.5)

    def split_heads(tensor):
        return tensor.reshape(row_count, length, heads, HD)

    def forward(target_in, encoded_in, weight_set):
        qkv_weight, query_bias, value_bias, attn_weight, attn_bias, gain_first, shift_first, cross_weight, cross_bias, source_weight, source_bias, merge_weight, merge_bias, gain_second, shift_second, expand_weight, expand_bias, reduce_weight, reduce_bias, gain_third, shift_third = weight_set
        flat_in = target_in.reshape(-1, width)
        qkv_all = product(flat_in, qkv_weight)
        queries = low(low_back((qkv_all[:, :width] + query_bias) * scaling))
        keys_self = low(low_back(qkv_all[:, width:2 * width]))
        values_self = low(low_back(qkv_all[:, 2 * width:] + value_bias))
        attended = attend_rows(split_heads(queries), split_heads(keys_self), split_heads(values_self), segments, True)
        attended = low(low_back(attended.reshape(-1, width)))
        branch_a = low_back(product(attended, attn_weight) + attn_bias)
        hidden_one = layer_norm(flat_in + branch_a, gain_first, shift_first)
        cross_queries = low(low_back((product(low(hidden_one), cross_weight) + cross_bias) * scaling))
        source_both = product(encoded_in.reshape(-1, width), source_weight)
        cross_keys = low(low_back(source_both[:, :width]))
        cross_values = low(low_back(source_both[:, width:] + source_bias))
        cross_att = attend_rows(split_heads(cross_queries), split_heads(cross_keys), split_heads(cross_values), segments, False)
        cross_att = low(low_back(cross_att.reshape(-1, width)))
        branch_c = low_back(product(cross_att, merge_weight) + merge_bias)
        hidden_two = layer_norm(hidden_one + branch_c, gain_second, shift_second)
        pre_act = low_back(product(low(hidden_two), expand_weight) + expand_bias)
        activated = low(jax.nn.gelu(pre_act, approximate=False))
        branch_f = low_back(product(activated, reduce_weight) + reduce_bias)
        result = layer_norm(hidden_two + branch_f, gain_third, shift_third)
        return result.reshape(row_count, length, width)
    weight_floats = tuple((member.astype(jnp.float32) for member in (self_qkv_w, self_q_b, self_v_b, self_out_w, self_out_b, norm1_gain, norm1_bias, cross_q_w, cross_q_b, cross_kv_w, cross_v_b, cross_out_w, cross_out_b, norm2_gain, norm2_bias, ffn_in_w, ffn_in_b, ffn_out_w, ffn_out_b, norm3_gain, norm3_bias)))
    layer_result, pullback = jax.vjp(forward, target.astype(jnp.float32), encoded.astype(jnp.float32), weight_floats)
    grads = pullback(out_grad.astype(jnp.float32))
    weight_grads = grads[2]
    return (layer_result.astype(jnp.bfloat16), grads[0], grads[1], weight_grads[0], weight_grads[1], weight_grads[2], weight_grads[3], weight_grads[4], weight_grads[5], weight_grads[6], weight_grads[7], weight_grads[8], weight_grads[9], weight_grads[10], weight_grads[11], weight_grads[12], weight_grads[13], weight_grads[14], weight_grads[15], weight_grads[16], weight_grads[17], weight_grads[18], weight_grads[19], weight_grads[20])
```

```python
import functools

import jax
import jax.numpy as jnp
from jax import lax
from jax.experimental import pallas as pl
from jax.experimental.pallas import tpu as pltpu
from jax.sharding import Mesh, PartitionSpec as P

HD = 64
LANES = 128
norm_epsilon = 1e-05
masked_score = -1e9
BF = jnp.bfloat16
F32 = jnp.float32

NN = (((1,), (0,)), ((), ()))
NT = (((1,), (1,)), ((), ()))
TN = (((0,), (0,)), ((), ()))


def dot(a, b, dims=NN):
    return lax.dot_general(a, b, dims, preferred_element_type=F32)


def segment_terms(seg):
    lane = jnp.arange(LANES) % HD
    same = seg[..., None] == lane
    query_terms = jnp.where((lane < 4) & ~same, masked_score, 0.0).astype(BF)
    key_terms = jnp.where(((lane < 4) & same) | ((lane >= 4) & (lane < 7)), 1.0, 0.0).astype(BF)
    return query_terms, key_terms


def head_lanes(shape, head):
    lane = lax.broadcasted_iota(jnp.int32, shape, 1)
    return (lane < HD) if head == 0 else (lane >= HD)


def causal_scores(scores, causal, first_query, block, query_axis):
    if causal == "block":
        queries = lax.broadcasted_iota(jnp.int32, (block, block), query_axis)
        keys = lax.broadcasted_iota(jnp.int32, (block, block), 1 - query_axis)
        count = scores.shape[1 - query_axis]
        before = lax.slice_in_dim(scores, 0, count - block, axis=1 - query_axis)
        corner = lax.slice_in_dim(scores, count - block, count, axis=1 - query_axis)
        corner = jnp.where(keys <= queries, corner, masked_score)
        if count == block:
            return corner
        return jnp.concatenate([before, corner], 1 - query_axis)
    if causal == "mask":
        queries = first_query + lax.broadcasted_iota(jnp.int32, scores.shape, query_axis)
        keys = lax.broadcasted_iota(jnp.int32, scores.shape, 1 - query_axis)
        return jnp.where(keys <= queries, scores, masked_score)
    return scores


def half_slices(count, shift, swapped):
    if not swapped:
        return [(slice(0, count), slice(0, count))]
    half = count // 2
    return [
        (
            slice(part * half, (part + 1) * half),
            pl.ds(pl.multiple_of(lax.rem(part * half + shift, count), half), half),
        )
        for part in (0, 1)
    ]


def row_block(index, block, count, shift, swapped):
    if not swapped:
        return pl.ds(index * block, block)
    return pl.ds(pl.multiple_of(lax.rem(index * block + shift, count), block), block)


def forward_kernel(
    shift_ref, q_ref, k_ref, v_ref, qt_ref, kt_ref, o_ref, lse_ref, ka, va, qa,
    *, causal, block, swapped,
):
    tq, ts = q_ref.shape[0], k_ref.shape[0]
    pair = pl.program_id(1)
    shift = shift_ref[0]
    for here, there in half_slices(ts, shift, swapped):
        k, v, extra = k_ref[there, :], v_ref[there, :], kt_ref[there, :]
        for head in (0, 1):
            own = head_lanes(k.shape, head)
            ka[head, here, :] = jnp.where(own, k, extra)
            va[head, here, :] = jnp.where(own, v, extra)
    for here, there in half_slices(tq, shift, swapped):
        q, extra = q_ref[there, :], qt_ref[there, :]
        for head in (0, 1):
            qa[head, here, :] = jnp.where(head_lanes(q.shape, head), q, extra)
    lane = lax.broadcasted_iota(jnp.int32, (block, LANES), 1)
    for index in range(tq // block):
        count = (index + 1) * block if causal == "block" else ts
        outs, lses = [], []
        for head in (0, 1):
            scores = dot(qa[head, index * block : (index + 1) * block, :], ka[head, :count, :], NT)
            scores = causal_scores(scores, causal, shift + index * block, block, 0)
            top = jnp.max(scores, 1, keepdims=True)
            weights = jnp.exp(scores - top).astype(BF)
            sums = dot(weights, va[head, :count, :])
            ones_lane = HD + 6 if head == 0 else 6
            total = sums[:, ones_lane : ones_lane + 1]
            outs.append(sums / total)
            lses.append(top + jnp.log(total))
        there = row_block(index, block, tq, shift, swapped)
        o_ref[there, :] = jnp.where(lane < HD, outs[0], outs[1]).astype(BF)
        lse_ref[there, :] = jnp.where(
            lane == 2 * pair, lses[0], jnp.where(lane == 2 * pair + 1, lses[1], lse_ref[there, :])
        )


def three_parts(x):
    parts = []
    for _ in range(3):
        part = x.astype(BF).astype(F32)
        parts.append(part)
        x = x - part
    return parts


def backward_kernel(
    shift_ref, q_ref, k_ref, v_ref, g_ref, o_ref, qt_ref, kt_ref, lse_ref,
    dq_ref, dk_ref, dv_ref, ka, va, qa, ga, k_turned, dk_sum, dv_sum, dq_turned,
    *, causal, block, swapped, scaling,
):
    tq, ts = q_ref.shape[0], k_ref.shape[0]
    pair = pl.program_id(1)
    shift = shift_ref[0]
    for here, there in half_slices(ts, shift, swapped):
        k, v, extra = k_ref[there, :], v_ref[there, :], kt_ref[there, :]
        for head in (0, 1):
            own = head_lanes(k.shape, head)
            ka[head, here, :] = jnp.where(own, k, extra)
            va[head, here, :] = jnp.where(own, v, extra)
        k_turned[:, here] = k.astype(F32).T.astype(BF)
    for here, there in half_slices(tq, shift, swapped):
        q, g, extra = q_ref[there, :], g_ref[there, :], qt_ref[there, :]
        products = g.astype(F32) * o_ref[there, :].astype(F32)
        lse = lse_ref[there, :]
        lane = lax.broadcasted_iota(jnp.int32, q.shape, 1)
        for head in (0, 1):
            own = head_lanes(q.shape, head)
            first = HD + 4 if head == 0 else 4
            delta = three_parts(-jnp.sum(jnp.where(own, products, 0.0), 1, keepdims=True))
            lse_col = three_parts(
                -jnp.sum(jnp.where(lane == 2 * pair + head, lse, 0.0), 1, keepdims=True)
            )
            q_extra, g_extra = extra.astype(F32), jnp.zeros(q.shape, F32)
            for part in range(3):
                q_extra = jnp.where(lane == first + part, lse_col[part], q_extra)
                g_extra = jnp.where(lane == first + part, delta[part], g_extra)
            qa[head, here, :] = jnp.where(own, q, q_extra.astype(BF))
            ga[head, here, :] = jnp.where(own, g, g_extra.astype(BF))
    blocks = tq // block
    for index in reversed(range(blocks)):
        count = (index + 1) * block if causal == "block" else ts
        rows = slice(index * block, (index + 1) * block)
        for head in (0, 1):
            q, g = qa[head, rows, :], ga[head, rows, :]
            scores = dot(ka[head, :count, :], q, NT)
            scores = causal_scores(scores, causal, shift + index * block, block, 1)
            probs = jnp.exp(scores)
            grads = (probs * dot(va[head, :count, :], g, NT)).astype(BF)
            dv, dk = dot(probs.astype(BF), g), dot(grads, q)
            if index == blocks - 1:
                dv_sum[head, :count, :] = dv
                dk_sum[head, :count, :] = dk
            else:
                dv_sum[head, :count, :] += dv
                dk_sum[head, :count, :] += dk
            own_rows = slice(HD * head, HD * (head + 1))
            dq_turned[own_rows, rows] = dot(k_turned[own_rows, :count], grads)
        there = row_block(index, block, tq, shift, swapped)
        dq_ref[there, :] = dq_turned[:, rows].T.astype(BF) * jnp.asarray(scaling, BF)
    for here, there in half_slices(ts, shift, swapped):
        own = head_lanes((ts // (2 if swapped else 1), LANES), 0)
        dk_ref[there, :] = jnp.where(own, dk_sum[0, here, :], dk_sum[1, here, :]).astype(BF)
        dv_ref[there, :] = jnp.where(own, dv_sum[0, here, :], dv_sum[1, here, :]).astype(BF)


def attention_specs(tq, ts, columns):
    none = pl.Squeezed()

    def of(count, start):
        return pl.BlockSpec((none, count, LANES), lambda row, pair, _: (row, 0, start + pair))

    def shared(count):
        return pl.BlockSpec((none, count, LANES), lambda row, pair, _: (row, 0, 0))

    q, k, v = (c // LANES for c in columns)
    return of(tq, q), of(ts, k), of(ts, v), of(tq, 0), of(ts, 0), shared(tq), shared(ts)


def attend(q, k, v, columns, terms, shift, width, causal, block, swapped):
    rows, tq, ts = q.shape[0], q.shape[1], k.shape[1]
    pairs = width // LANES
    sq, sk, sv, so, _, tq_spec, ts_spec = attention_specs(tq, ts, columns)
    elements = rows * pairs * 2 * tq * ts
    return pl.pallas_call(
        functools.partial(forward_kernel, causal=causal, block=block, swapped=swapped),
        grid_spec=pltpu.PrefetchScalarGridSpec(
            num_scalar_prefetch=1,
            grid=(rows, pairs),
            in_specs=[sq, sk, sv, tq_spec, ts_spec],
            out_specs=[so, tq_spec],
            scratch_shapes=[pltpu.VMEM((2, n, LANES), BF) for n in (ts, ts, tq)],
        ),
        out_shape=[
            jax.ShapeDtypeStruct((rows, tq, width), BF),
            jax.ShapeDtypeStruct((rows, tq, LANES), F32),
        ],
        compiler_params=pltpu.CompilerParams(vmem_limit_bytes=48 * 2**20),
        cost_estimate=pl.CostEstimate(
            flops=elements * 1200, bytes_accessed=rows * (tq + ts) * width * 4, transcendentals=elements
        ),
    )(shift, q, k, v, *terms)


def attend_back(q, k, v, columns, g, o, lse, terms, shift, width, causal, block, swapped):
    rows, tq, ts = q.shape[0], q.shape[1], k.shape[1]
    pairs = width // LANES
    sq, sk, sv, so, ss, tq_spec, ts_spec = attention_specs(tq, ts, columns)
    elements = rows * pairs * 2 * tq * ts
    return pl.pallas_call(
        functools.partial(
            backward_kernel, causal=causal, block=block, swapped=swapped, scaling=HD**-0.5
        ),
        grid_spec=pltpu.PrefetchScalarGridSpec(
            num_scalar_prefetch=1,
            grid=(rows, pairs),
            in_specs=[sq, sk, sv, so, so, tq_spec, ts_spec, tq_spec],
            out_specs=[so, ss, ss],
            scratch_shapes=[pltpu.VMEM((2, n, LANES), BF) for n in (ts, ts, tq, tq)]
            + [
                pltpu.VMEM((LANES, ts), BF),
                pltpu.VMEM((2, ts, LANES), F32),
                pltpu.VMEM((2, ts, LANES), F32),
                pltpu.VMEM((LANES, tq), F32),
            ],
        ),
        out_shape=[
            jax.ShapeDtypeStruct((rows, tq, width), BF),
            jax.ShapeDtypeStruct((rows, ts, width), BF),
            jax.ShapeDtypeStruct((rows, ts, width), BF),
        ],
        compiler_params=pltpu.CompilerParams(vmem_limit_bytes=48 * 2**20),
        cost_estimate=pl.CostEstimate(
            flops=elements * 2000, bytes_accessed=rows * (tq + ts) * width * 8, transcendentals=elements
        ),
    )(shift, q, k, v, g, o, *terms, lse)


def norm(resid, gain_vec, bias_vec):
    center = resid - jnp.mean(resid, -1, keepdims=True)
    inverse = lax.rsqrt(jnp.mean(center * center, -1, keepdims=True) + norm_epsilon)
    normed = center * inverse
    return normed * gain_vec + bias_vec, normed, inverse


def norm_back(upstream, normed, inverse, gain_vec):
    w = upstream * gain_vec
    grad = (
        w - jnp.mean(w, -1, keepdims=True) - normed * jnp.mean(w * normed, -1, keepdims=True)
    ) * inverse
    return grad, jnp.sum(upstream * normed, 0), jnp.sum(upstream, 0)


def column_sum(x):
    return jnp.sum(x.astype(F32), 0)


def partner(x, axis, bit=1):
    count = lax.axis_size(axis)
    return lax.ppermute(x, axis, [(i, i ^ bit) for i in range(count)])


def halve(x, axis):
    index = lax.axis_index(axis)
    half = x.shape[0] // 2
    sent = lax.dynamic_slice_in_dim(x, (1 - index) * half, half, 0)
    got = partner(sent, axis)
    return lax.dynamic_slice_in_dim(x, index * half, half, 0) + got


def join(x, axis):
    got = partner(x, axis)
    first = lax.axis_index(axis) == 0
    return jnp.concatenate([jnp.where(first, x, got), jnp.where(first, got, x)], 0)


def reduce_matrix(x):
    wide, rest, side, core = (lax.axis_size(a) for a in ("wide", "rest", "side", "core"))
    if not (wide == side == core == 2):
        x = lax.psum_scatter(x, "wide", scatter_dimension=0, tiled=True)
        return lax.psum(x, ("rest", "side", "core")).astype(F32)
    cols = x.shape[1]
    x = x.reshape(2, 2, -1, cols).transpose(1, 0, 2, 3).reshape(-1, cols)
    x = halve(x, "core")
    x = halve(x, "wide")
    x = halve(x, "side")
    bit = 1
    while bit < rest:
        x = x + partner(x, "rest", bit)
        bit *= 2
    x = join(x, "side")
    x = join(x, "core")
    return x.astype(F32)


def reduce_vectors(vectors):
    wide, rest, side, core = (lax.axis_size(a) for a in ("wide", "rest", "side", "core"))
    sizes = [v.shape[0] // wide for v in vectors]
    x = jnp.concatenate([v.reshape(wide, -1) for v in vectors], 1)
    if wide == side == core == 2:
        for axis in ("core", "side"):
            x = x + partner(x, axis)
        bit = 1
        while bit < rest:
            x = x + partner(x, "rest", bit)
            bit *= 2
        index = lax.axis_index("wide")
        got = partner(lax.dynamic_index_in_dim(x, 1 - index, 0, keepdims=False), "wide")
        x = lax.dynamic_index_in_dim(x, index, 0, keepdims=False) + got
    else:
        x = lax.psum_scatter(x, "wide", scatter_dimension=0, tiled=True)
        x = lax.psum(x, ("rest", "side", "core"))[0]
    outs, start = [], 0
    for size in sizes:
        outs.append(lax.slice_in_dim(x, start, start + size, axis=0))
        start += size
    return outs


def body(
    target, encoded, segments, out_grad,
    self_qkv_w, self_q_b, self_v_b, self_out_w, self_out_b, norm1_gain, norm1_bias,
    cross_q_w, cross_q_b, cross_kv_w, cross_v_b, cross_out_w, cross_out_b, norm2_gain, norm2_bias,
    ffn_in_w, ffn_in_b, ffn_out_w, ffn_out_b, norm3_gain, norm3_bias,
):
    row_count, tok_count, width = target.shape
    wide = lax.axis_size("wide")
    place = lax.axis_index("wide")
    scaling = HD**-0.5
    full_len = tok_count * wide
    swapped = wide == 2 and row_count == 2

    if swapped:
        def bring(x):
            kept = lax.dynamic_index_in_dim(x, place, 0, keepdims=False)
            sent = lax.dynamic_index_in_dim(x, 1 - place, 0, keepdims=False)
            return jnp.concatenate([kept, partner(sent, "wide")], 0)

        def give(x, dtype):
            kept = x[:tok_count]
            got = partner(x[tok_count:].astype(BF), "wide").astype(dtype)
            kept = kept.astype(dtype)
            first = place == 0
            return jnp.stack([jnp.where(first, kept, got), jnp.where(first, got, kept)])

        tokens, causal, block_f, block_b = full_len, "block", 512, 256
        shift = (place * tok_count).astype(jnp.int32).reshape(1)
        seg = bring(segments)[None]
        key_seg = seg
    else:
        def bring(x):
            return x.reshape((-1,) + x.shape[2:])

        def give(x, dtype):
            return x.astype(dtype).reshape(row_count, tok_count, width)

        tokens, causal = tok_count, "mask"
        block_f = block_b = min(tok_count, 256)
        shift = (place * tok_count).astype(jnp.int32).reshape(1)
        seg = segments
        key_seg = lax.all_gather(segments, "wide", axis=1, tiled=True)

    def by_row(x):
        return x.reshape(-1, tokens, x.shape[-1])

    def flat(x):
        return x.reshape(-1, x.shape[-1])

    def keys_of(x):
        return x if swapped else lax.all_gather(x, "wide", axis=1, tiled=True)

    def key_grads(x):
        return x if swapped else lax.psum_scatter(x, "wide", scatter_dimension=1, tiled=True)

    terms = (segment_terms(seg)[0], segment_terms(key_seg)[1])

    def attention(q, kv, columns, is_causal):
        return attend(
            q, kv, kv, columns, terms, shift, width, causal if is_causal else "no", block_f, swapped
        )

    def attention_back(q, kv, columns, g, o, lse, is_causal):
        dq, dk, dv = attend_back(
            q, kv, kv, columns, by_row(g), o, lse, terms, shift, width,
            causal if is_causal else "no", block_b, swapped,
        )
        return flat(dq), flat(key_grads(dk)), flat(key_grads(dv))

    flat_in = bring(target)
    flat_enc = bring(encoded)
    upstream = bring(out_grad)

    zeros = jnp.zeros_like(self_q_b)
    ones = jnp.ones_like(self_q_b)
    qkv_bias = jnp.concatenate([self_q_b, zeros, self_v_b])
    qkv_scale = jnp.concatenate([ones * scaling, ones, ones])
    qkv = by_row(((dot(flat_in, self_qkv_w) + qkv_bias) * qkv_scale).astype(BF))
    if swapped:
        self_kv, self_cols = qkv, (0, width, 2 * width)
    else:
        self_kv, self_cols = keys_of(qkv[..., width:]), (0, 0, width)
    self_o, self_lse = attention(qkv, self_kv, self_cols, True)
    self_ob = flat(self_o)
    h1, n1, i1 = norm(
        flat_in.astype(F32) + (dot(self_ob, self_out_w) + self_out_b), norm1_gain, norm1_bias
    )
    h1b = h1.astype(BF)
    cq = by_row(((dot(h1b, cross_q_w) + cross_q_b) * scaling).astype(BF))
    ckv = by_row((dot(flat_enc, cross_kv_w) + jnp.concatenate([zeros, cross_v_b])).astype(BF))
    ckv = keys_of(ckv)
    cross_cols = (0, 0, width)
    cross_o, cross_lse = attention(cq, ckv, cross_cols, False)
    cross_ob = flat(cross_o)
    h2, n2, i2 = norm(h1 + (dot(cross_ob, cross_out_w) + cross_out_b), norm2_gain, norm2_bias)
    h2b = h2.astype(BF)
    pre = dot(h2b, ffn_in_w) + ffn_in_b
    phi_sum = 0.5 * lax.erfc(-pre * (0.5**0.5))
    act = (pre * phi_sum).astype(BF)
    slope = phi_sum + pre * (jnp.exp(-0.5 * pre * pre) * 0.3989422804014327)
    h3, n3, i3 = norm(h2 + (dot(act, ffn_out_w) + ffn_out_b), norm3_gain, norm3_bias)
    layer_out = give(h3.astype(BF), BF)

    dr3, norm3_gain_grad, norm3_bias_grad = norm_back(upstream.astype(F32), n3, i3, norm3_gain)
    dbf = dr3.astype(BF)
    ffn_out_w_grad = reduce_matrix(dot(act, dbf, TN).astype(BF))
    dpre = (dot(dbf, ffn_out_w, NT) * slope).astype(BF)
    ffn_in_w_grad = reduce_matrix(dot(h2b, dpre, TN).astype(BF))
    dh2 = dr3 + dot(dpre, ffn_in_w, NT)
    dr2, norm2_gain_grad, norm2_bias_grad = norm_back(dh2, n2, i2, norm2_gain)
    dbc = dr2.astype(BF)
    dco = dot(dbc, cross_out_w, NT).astype(BF)
    dcq, dck, dcv = attention_back(cq, ckv, cross_cols, dco, cross_o, cross_lse, False)
    dckv = jnp.concatenate([dck, dcv], 1)
    cross_grads = reduce_matrix(
        jnp.concatenate(
            [
                dot(cross_ob, dbc, TN).astype(BF),
                dot(h1b, dcq, TN).astype(BF),
                dot(flat_enc, dckv, TN).astype(BF),
            ],
            1,
        )
    )
    encoded_grad = give(dot(dckv, cross_kv_w, NT), F32)
    dh1 = dr2 + dot(dcq, cross_q_w, NT)
    dr1, norm1_gain_grad, norm1_bias_grad = norm_back(dh1, n1, i1, norm1_gain)
    dba = dr1.astype(BF)
    dso = dot(dba, self_out_w, NT).astype(BF)
    dsq, dsk, dsv = attention_back(qkv, self_kv, self_cols, dso, self_o, self_lse, True)
    dqkv = jnp.concatenate([dsq, dsk, dsv], 1)
    self_grads = reduce_matrix(
        jnp.concatenate(
            [dot(self_ob, dba, TN).astype(BF), dot(flat_in, dqkv, TN).astype(BF)], 1
        )
    )
    target_grad = give(dr1 + dot(dqkv, self_qkv_w, NT), F32)

    (
        self_q_b_grad, self_v_b_grad, self_out_b_grad, norm1_gain_grad, norm1_bias_grad,
        cross_q_b_grad, cross_v_b_grad, cross_out_b_grad, norm2_gain_grad, norm2_bias_grad,
        ffn_in_b_grad, ffn_out_b_grad, norm3_gain_grad, norm3_bias_grad,
    ) = reduce_vectors(
        [
            column_sum(dsq), column_sum(dsv), column_sum(dba), norm1_gain_grad, norm1_bias_grad,
            column_sum(dcq), column_sum(dcv), column_sum(dbc), norm2_gain_grad, norm2_bias_grad,
            column_sum(dpre), column_sum(dbf), norm3_gain_grad, norm3_bias_grad,
        ]
    )
    return (
        layer_out, target_grad, encoded_grad,
        self_grads[:, width:], self_q_b_grad, self_v_b_grad,
        self_grads[:, :width], self_out_b_grad, norm1_gain_grad, norm1_bias_grad,
        cross_grads[:, width : 2 * width], cross_q_b_grad,
        cross_grads[:, 2 * width :], cross_v_b_grad,
        cross_grads[:, :width], cross_out_b_grad, norm2_gain_grad, norm2_bias_grad,
        ffn_in_w_grad, ffn_in_b_grad, ffn_out_w_grad, ffn_out_b_grad,
        norm3_gain_grad, norm3_bias_grad,
    )


def solution(mesh):
    wide, narrow = mesh.shape["wide"], mesh.shape["narrow"]
    core = 2 if narrow % 2 == 0 else 1
    side = 2 if narrow % (2 * core) == 0 else 1
    devices = mesh.devices.reshape(wide, narrow // (side * core), side, core)
    split = Mesh(devices, ("wide", "rest", "side", "core"))
    rows = ("rest", "side", "core")
    token_spec = P(rows, "wide", None)
    in_specs = (token_spec, token_spec, P(rows, "wide"), token_spec) + (P(),) * 21
    matrix, vector = P("wide", None), P("wide")
    out_specs = (token_spec,) * 3 + (
        matrix, vector, vector, matrix, vector, vector, vector,
        matrix, vector, matrix, vector, matrix, vector, vector, vector,
        matrix, vector, matrix, vector, vector, vector,
    )
    return jax.shard_map(body, mesh=split, in_specs=in_specs, out_specs=out_specs, check_vma=False)
```

```python
import functools

import jax
import jax.numpy as jnp
from jax import lax
from jax.experimental import pallas as pl
from jax.experimental.pallas import tpu as pltpu
from jax.sharding import Mesh, PartitionSpec as P

HD = 64
LANES = 128
norm_epsilon = 1e-05
masked_score = -1e9
BF = jnp.bfloat16
F32 = jnp.float32

NN = (((1,), (0,)), ((), ()))
NT = (((1,), (1,)), ((), ()))
TN = (((0,), (0,)), ((), ()))


def dot(a, b, dims=NN):
    return lax.dot_general(a, b, dims, preferred_element_type=F32)


def segment_terms(seg):
    lane = jnp.arange(LANES) % HD
    same = seg[..., None] == lane
    query_terms = jnp.where((lane < 4) & ~same, masked_score, 0.0).astype(BF)
    key_terms = jnp.where(((lane < 4) & same) | ((lane >= 4) & (lane < 7)), 1.0, 0.0).astype(BF)
    return query_terms, key_terms


def head_lanes(shape, head):
    lane = lax.broadcasted_iota(jnp.int32, shape, 1)
    return (lane < HD) if head == 0 else (lane >= HD)


def causal_scores(scores, causal, first_query, block, query_axis):
    if causal == "block":
        queries = lax.broadcasted_iota(jnp.int32, (block, block), query_axis)
        keys = lax.broadcasted_iota(jnp.int32, (block, block), 1 - query_axis)
        count = scores.shape[1 - query_axis]
        before = lax.slice_in_dim(scores, 0, count - block, axis=1 - query_axis)
        corner = lax.slice_in_dim(scores, count - block, count, axis=1 - query_axis)
        corner = jnp.where(keys <= queries, corner, masked_score)
        if count == block:
            return corner
        return jnp.concatenate([before, corner], 1 - query_axis)
    if causal == "mask":
        queries = first_query + lax.broadcasted_iota(jnp.int32, scores.shape, query_axis)
        keys = lax.broadcasted_iota(jnp.int32, scores.shape, 1 - query_axis)
        return jnp.where(keys <= queries, scores, masked_score)
    return scores


def half_slices(count, shift, swapped):
    if not swapped:
        return [(slice(0, count), slice(0, count))]
    half = count // 2
    return [
        (
            slice(part * half, (part + 1) * half),
            pl.ds(pl.multiple_of(lax.rem(part * half + shift, count), half), half),
        )
        for part in (0, 1)
    ]


def row_block(index, block, count, shift, swapped):
    if not swapped:
        return pl.ds(index * block, block)
    return pl.ds(pl.multiple_of(lax.rem(index * block + shift, count), block), block)


def forward_kernel(
    shift_ref, q_ref, k_ref, v_ref, qt_ref, kt_ref, o_ref, lse_ref, ka, va, qa,
    *, causal, block, swapped,
):
    tq, ts = q_ref.shape[0], k_ref.shape[0]
    pair = pl.program_id(1)
    shift = shift_ref[0]
    for here, there in half_slices(ts, shift, swapped):
        k, v, extra = k_ref[there, :], v_ref[there, :], kt_ref[there, :]
        for head in (0, 1):
            own = head_lanes(k.shape, head)
            ka[head, here, :] = jnp.where(own, k, extra)
            va[head, here, :] = jnp.where(own, v, extra)
    for here, there in half_slices(tq, shift, swapped):
        q, extra = q_ref[there, :], qt_ref[there, :]
        for head in (0, 1):
            qa[head, here, :] = jnp.where(head_lanes(q.shape, head), q, extra)
    lane = lax.broadcasted_iota(jnp.int32, (block, LANES), 1)
    for index in range(tq // block):
        count = (index + 1) * block if causal == "block" else ts
        outs, lses = [], []
        for head in (0, 1):
            scores = dot(qa[head, index * block : (index + 1) * block, :], ka[head, :count, :], NT)
            scores = causal_scores(scores, causal, shift + index * block, block, 0)
            top = jnp.max(scores, 1, keepdims=True)
            weights = jnp.exp(scores - top).astype(BF)
            sums = dot(weights, va[head, :count, :])
            ones_lane = HD + 6 if head == 0 else 6
            total = sums[:, ones_lane : ones_lane + 1]
            outs.append(sums / total)
            lses.append(top + jnp.log(total))
        there = row_block(index, block, tq, shift, swapped)
        o_ref[there, :] = jnp.where(lane < HD, outs[0], outs[1]).astype(BF)
        lse_ref[there, :] = jnp.where(
            lane == 2 * pair, lses[0], jnp.where(lane == 2 * pair + 1, lses[1], lse_ref[there, :])
        )


def three_parts(x):
    parts = []
    for _ in range(3):
        part = x.astype(BF).astype(F32)
        parts.append(part)
        x = x - part
    return parts


def backward_kernel(
    shift_ref, q_ref, k_ref, v_ref, g_ref, o_ref, qt_ref, kt_ref, lse_ref,
    dq_ref, dk_ref, dv_ref, sums_ref, ka, va, qa, ga, k_turned, dk_sum, dv_sum, dq_turned,
    *, causal, block, swapped, scaling, first,
):
    tq, ts = q_ref.shape[0], k_ref.shape[0]
    pair = pl.program_id(1) + first
    shift = shift_ref[0]
    for here, there in half_slices(ts, shift, swapped):
        k, v, extra = k_ref[there, :], v_ref[there, :], kt_ref[there, :]
        for head in (0, 1):
            own = head_lanes(k.shape, head)
            ka[head, here, :] = jnp.where(own, k, extra)
            va[head, here, :] = jnp.where(own, v, extra)
        k_turned[:, here] = k.astype(F32).T.astype(BF)
    for here, there in half_slices(tq, shift, swapped):
        q, g, extra = q_ref[there, :], g_ref[there, :], qt_ref[there, :]
        products = g.astype(F32) * o_ref[there, :].astype(F32)
        lse = lse_ref[there, :]
        lane = lax.broadcasted_iota(jnp.int32, q.shape, 1)
        for head in (0, 1):
            own = head_lanes(q.shape, head)
            first = HD + 4 if head == 0 else 4
            delta = three_parts(-jnp.sum(jnp.where(own, products, 0.0), 1, keepdims=True))
            lse_col = three_parts(
                -jnp.sum(jnp.where(lane == 2 * pair + head, lse, 0.0), 1, keepdims=True)
            )
            q_extra, g_extra = extra.astype(F32), jnp.zeros(q.shape, F32)
            for part in range(3):
                q_extra = jnp.where(lane == first + part, lse_col[part], q_extra)
                g_extra = jnp.where(lane == first + part, delta[part], g_extra)
            qa[head, here, :] = jnp.where(own, q, q_extra.astype(BF))
            ga[head, here, :] = jnp.where(own, g, g_extra.astype(BF))
    blocks = tq // block
    dq_total = jnp.zeros((1, LANES), F32)
    for index in reversed(range(blocks)):
        count = (index + 1) * block if causal == "block" else ts
        rows = slice(index * block, (index + 1) * block)
        for head in (0, 1):
            q, g = qa[head, rows, :], ga[head, rows, :]
            scores = dot(ka[head, :count, :], q, NT)
            scores = causal_scores(scores, causal, shift + index * block, block, 1)
            probs = jnp.exp(scores)
            grads = (probs * dot(va[head, :count, :], g, NT)).astype(BF)
            dv, dk = dot(probs.astype(BF), g), dot(grads, q)
            if index == blocks - 1:
                dv_sum[head, :count, :] = dv
                dk_sum[head, :count, :] = dk
            else:
                dv_sum[head, :count, :] += dv
                dk_sum[head, :count, :] += dk
            own_rows = slice(HD * head, HD * (head + 1))
            dq_turned[own_rows, rows] = dot(k_turned[own_rows, :count], grads)
        there = row_block(index, block, tq, shift, swapped)
        dq = dq_turned[:, rows].T.astype(BF) * jnp.asarray(scaling, BF)
        dq_ref[there, :] = dq
        dq_total += jnp.sum(dq.astype(F32), 0, keepdims=True)
    dv_total = jnp.zeros((1, LANES), F32)
    for here, there in half_slices(ts, shift, swapped):
        own = head_lanes((ts // (2 if swapped else 1), LANES), 0)
        dk_ref[there, :] = jnp.where(own, dk_sum[0, here, :], dk_sum[1, here, :]).astype(BF)
        dv = jnp.where(own, dv_sum[0, here, :], dv_sum[1, here, :]).astype(BF)
        dv_ref[there, :] = dv
        dv_total += jnp.sum(dv.astype(F32), 0, keepdims=True)
    row = lax.broadcasted_iota(jnp.int32, sums_ref.shape, 0)
    sums_ref[...] = jnp.where(row == 0, dq_total, jnp.where(row == 1, dv_total, 0.0))


def attention_specs(tq, ts, columns, first=0):
    none = pl.Squeezed()

    def of(count, start):
        return pl.BlockSpec((none, count, LANES), lambda row, pair, _: (row, 0, start + pair))

    def shared(count):
        return pl.BlockSpec((none, count, LANES), lambda row, pair, _: (row, 0, 0))

    q, k, v = (c // LANES + first for c in columns)
    return of(tq, q), of(ts, k), of(ts, v), of(tq, first), of(tq, 0), of(ts, 0), shared(tq), shared(ts)


def skip_refs(kernel, start, count):
    def run(*refs):
        kernel(*refs[:start], *refs[start + count :])

    return run


def attend(q, k, v, columns, terms, shift, width, causal, block, swapped, after=()):
    rows, tq, ts = q.shape[0], q.shape[1], k.shape[1]
    pairs = width // LANES
    sq, sk, sv, _, so, _, tq_spec, ts_spec = attention_specs(tq, ts, columns)
    elements = rows * pairs * 2 * tq * ts
    kernel = functools.partial(forward_kernel, causal=causal, block=block, swapped=swapped)
    return pl.pallas_call(
        skip_refs(kernel, 6, len(after)),
        grid_spec=pltpu.PrefetchScalarGridSpec(
            num_scalar_prefetch=1,
            grid=(rows, pairs),
            in_specs=[sq, sk, sv, tq_spec, ts_spec]
            + [pl.BlockSpec(memory_space=pl.ANY)] * len(after),
            out_specs=[so, tq_spec],
            scratch_shapes=[pltpu.VMEM((2, n, LANES), BF) for n in (ts, ts, tq)],
        ),
        out_shape=[
            jax.ShapeDtypeStruct((rows, tq, width), BF),
            jax.ShapeDtypeStruct((rows, tq, LANES), F32),
        ],
        compiler_params=pltpu.CompilerParams(vmem_limit_bytes=48 * 2**20),
        cost_estimate=pl.CostEstimate(
            flops=elements * 1600, bytes_accessed=rows * (tq + ts) * width * 4, transcendentals=0
        ),
    )(shift, q, k, v, *terms, *after)


def attend_back(
    q, k, v, columns, g, o, lse, terms, shift, first, pairs, causal, block, swapped, after=()
):
    rows, tq, ts = q.shape[0], q.shape[1], k.shape[1]
    sq, sk, sv, sg, so, ss, tq_spec, ts_spec = attention_specs(tq, ts, columns, first)
    elements = rows * pairs * 2 * tq * ts
    kernel = functools.partial(
        backward_kernel, causal=causal, block=block, swapped=swapped, scaling=HD**-0.5, first=first
    )
    return pl.pallas_call(
        skip_refs(kernel, 9, len(after)),
        grid_spec=pltpu.PrefetchScalarGridSpec(
            num_scalar_prefetch=1,
            grid=(rows, pairs),
            in_specs=[sq, sk, sv, sg, sg, tq_spec, ts_spec, tq_spec]
            + [pl.BlockSpec(memory_space=pl.ANY)] * len(after),
            out_specs=[
                so, ss, ss,
                pl.BlockSpec((pl.Squeezed(), 8, LANES), lambda row, pair, _: (row, 0, pair)),
            ],
            scratch_shapes=[pltpu.VMEM((2, n, LANES), BF) for n in (ts, ts, tq, tq)]
            + [
                pltpu.VMEM((LANES, ts), BF),
                pltpu.VMEM((2, ts, LANES), F32),
                pltpu.VMEM((2, ts, LANES), F32),
                pltpu.VMEM((LANES, tq), F32),
            ],
        ),
        out_shape=[
            jax.ShapeDtypeStruct((rows, tq, pairs * LANES), BF),
            jax.ShapeDtypeStruct((rows, ts, pairs * LANES), BF),
            jax.ShapeDtypeStruct((rows, ts, pairs * LANES), BF),
            jax.ShapeDtypeStruct((rows, 8, pairs * LANES), F32),
        ],
        compiler_params=pltpu.CompilerParams(vmem_limit_bytes=48 * 2**20),
        cost_estimate=pl.CostEstimate(
            flops=elements * 2600, bytes_accessed=rows * (tq + ts) * pairs * 1024, transcendentals=0
        ),
    )(shift, q, k, v, g, o, *terms, lse, *after)


def norm(resid):
    center = resid - jnp.mean(resid, -1, keepdims=True)
    inverse = lax.rsqrt(jnp.mean(center * center, -1, keepdims=True) + norm_epsilon)
    return center * inverse, inverse


def norm_back(upstream, normed, inverse, gain_vec):
    w = upstream * gain_vec
    return (
        w - jnp.mean(w, -1, keepdims=True) - normed * jnp.mean(w * normed, -1, keepdims=True)
    ) * inverse


def gelu_parts(pre):
    bell = jnp.exp(pre * pre * -0.5)
    t = 1.0 / (1.0 + jnp.abs(pre) * (0.3275911 * 0.5**0.5))
    poly = 0.5 * 1.061405429
    for c in (-1.453152027, 1.421413741, -0.284496736, 0.254829592):
        poly = poly * t + 0.5 * c
    tail = poly * t * bell
    phi_sum = jnp.where(pre >= 0, 1.0 - tail, tail)
    return pre * phi_sum, phi_sum + pre * (bell * 0.3989422804014327)


def add_rows(sums_ref, rows):
    for index, value in enumerate(rows):
        total = jnp.sum(value.astype(F32), 0, keepdims=True)
        here = slice(index, index + 1)
        sums_ref[here, :] = jnp.where(pl.program_id(0) == 0, total, sums_ref[here, :] + total)


def after_self_kernel(
    o_ref, x_ref, w_ref, b_ref, gain_ref, bias_ref, qw_ref, qb_ref,
    n1_ref, i1_ref, h1b_ref, cq_ref, *, scaling,
):
    resid = x_ref[...].astype(F32) + (dot(o_ref[...], w_ref[...]) + b_ref[...])
    n1, i1 = norm(resid)
    h1b = (n1 * gain_ref[...] + bias_ref[...]).astype(BF)
    n1_ref[...] = n1
    i1_ref[...] = jnp.broadcast_to(i1, i1_ref.shape)
    h1b_ref[...] = h1b
    cq_ref[...] = ((dot(h1b, qw_ref[...]) + qb_ref[...]) * scaling).astype(BF)


def middle_kernel(
    o_ref, n1_ref, up_ref, g1_ref, s1_ref, ow_ref, ob_ref, g2_ref, s2_ref,
    w1_ref, b1_ref, w2_ref, b2_ref, g3_ref, s3_ref,
    out_ref, act_ref, dbf_ref, h2b_ref, dpre_ref, dr2_ref, dbc_ref, dco_ref, sums_ref, wide_ref,
    slope, *, chunk,
):
    h1 = n1_ref[...] * g1_ref[...] + s1_ref[...]
    n2, i2 = norm(h1 + (dot(o_ref[...], ow_ref[...]) + ob_ref[...]))
    h2 = n2 * g2_ref[...] + s2_ref[...]
    h2b = h2.astype(BF)
    h2b_ref[...] = h2b
    hidden = w1_ref.shape[1]
    cols = [slice(c, c + chunk) for c in range(0, hidden, chunk)]
    branch = b2_ref[...]
    for c in cols:
        pre = dot(h2b, w1_ref[:, c]) + b1_ref[:, c]
        value, slope_c = gelu_parts(pre)
        slope[:, c] = slope_c
        act_c = value.astype(BF)
        act_ref[:, c] = act_c
        branch = branch + dot(act_c, w2_ref[c, :])
    n3, i3 = norm(h2 + branch)
    out_ref[...] = (n3 * g3_ref[...] + s3_ref[...]).astype(BF)
    up = up_ref[...].astype(F32)
    dr3 = norm_back(up, n3, i3, g3_ref[...])
    dbf = dr3.astype(BF)
    dbf_ref[...] = dbf
    dh2 = dr3
    first = pl.program_id(0) == 0
    for c in cols:
        dpre_c = (dot(dbf, w2_ref[c, :], NT) * slope[:, c]).astype(BF)
        dpre_ref[:, c] = dpre_c
        total = jnp.sum(dpre_c.astype(F32), 0, keepdims=True)
        wide_ref[0:1, c] = jnp.where(first, total, wide_ref[0:1, c] + total)
        dh2 = dh2 + dot(dpre_c, w1_ref[:, c], NT)
    dr2 = norm_back(dh2, n2, i2, g2_ref[...])
    dbc = dr2.astype(BF)
    dr2_ref[...] = dr2
    dbc_ref[...] = dbc
    dco_ref[...] = dot(dbc, ow_ref[...], NT).astype(BF)
    add_rows(sums_ref, (up * n3, up, dbf, dh2 * n2, dh2, dbc))


def before_self_kernel(
    *refs, parts,
):
    dcq = jnp.concatenate([ref[...] for ref in refs[:parts]], 1)
    dr2_ref, n1_ref, i1_ref, qw_ref, g1_ref, ow_ref = refs[parts : parts + 6]
    dr1_ref, dba_ref, dso_ref, sums_ref = refs[parts + 6 :]
    n1 = n1_ref[...]
    dh1 = dr2_ref[...] + dot(dcq, qw_ref[...], NT)
    dr1 = norm_back(dh1, n1, i1_ref[:, 0:1], g1_ref[...])
    dba = dr1.astype(BF)
    dr1_ref[...] = dr1
    dba_ref[...] = dba
    dso_ref[...] = dot(dba, ow_ref[...], NT).astype(BF)
    add_rows(sums_ref, (dh1 * n1, dh1, dba))


def token_call(kernel, block, blocked, whole, outs, scratch=(), flops=0, after=()):
    tokens = blocked[0].shape[0]
    whole = [w.reshape(1, -1) if w.ndim == 1 else w for w in whole]
    in_specs = [pl.BlockSpec((block, a.shape[1]), lambda i: (i, 0)) for a in blocked]
    in_specs += [
        pl.BlockSpec(a.shape, lambda i: (0, 0), pipeline_mode=pl.Buffered(1)) for a in whole
    ]
    in_specs += [pl.BlockSpec(memory_space=pl.ANY)] * len(after)
    out_specs, out_shape = [], []
    for out in outs:
        if len(out) == 2:
            shape = (tokens, out[0])
            out_specs.append(pl.BlockSpec((block, out[0]), lambda i: (i, 0)))
        else:
            shape = out[:2]
            out_specs.append(pl.BlockSpec(shape, lambda i: (0, 0)))
        out_shape.append(jax.ShapeDtypeStruct(shape, out[-1]))
    used = len(blocked) + len(whole)

    def run(*refs):
        kernel(*refs[:used], *refs[used + len(after) :])

    moved = sum(a.size * a.dtype.itemsize for a in (*blocked, *whole, *out_shape))
    return pl.pallas_call(
        run,
        grid=(tokens // block,),
        in_specs=in_specs,
        out_specs=out_specs,
        out_shape=out_shape,
        scratch_shapes=list(scratch),
        compiler_params=pltpu.CompilerParams(vmem_limit_bytes=56 * 2**20),
        cost_estimate=pl.CostEstimate(flops=flops, bytes_accessed=moved, transcendentals=0),
    )(*blocked, *whole, *after)


def partner(x, axis, bit=1):
    count = lax.axis_size(axis)
    return lax.ppermute(x, axis, [(i, i ^ bit) for i in range(count)])


def pick(x, axis, index):
    return lax.dynamic_index_in_dim(x, index, axis, keepdims=False)


class Reduction:
    def __init__(self, parts, order):
        self.split = all(lax.axis_size(a) == 2 for a in ("wide", "side", "core"))
        self.parts = parts
        self.rows = parts[0].shape[0] // lax.axis_size("wide")
        self.got = None
        if self.split:
            eighth = parts[0].shape[0] // 8
            self.acc = [x.reshape(2, 2, 2, 2, eighth // 2, x.shape[1]) for x in parts]
            self.left = ["wide", "core", "side", "rest"]
            self.steps = list(order)
            self.joins = []

    def place(self, axis):
        index = lax.axis_index(axis)
        return index % 2 if axis == "rest" else index

    def send(self):
        if not self.split:
            return ()
        step = self.steps[0]
        if step in ("core", "wide", "side", "rest"):
            at = self.left.index(step)
            sent = [pick(x, at, 1 - self.place(step)) for x in self.acc]
            sent = sent[0] if len(sent) == 1 else jnp.concatenate(sent, -1)
            self.got = partner(sent, step)
        elif step == "far":
            sent = self.acc[0]
            bit, total = 2, self.acc[0]
            assert lax.axis_size("rest") in (2, 4)
            self.got = partner(sent, "rest", 2) if lax.axis_size("rest") == 4 else None
        else:
            sent = self.acc[0]
            self.got = partner(sent, step[5:])
        return (sent,)

    def take(self):
        if not self.split:
            return
        step = self.steps.pop(0)
        if step in ("core", "wide", "side", "rest"):
            at = self.left.index(step)
            kept = [pick(x, at, self.place(step)) for x in self.acc]
            kept = kept[0] if len(kept) == 1 else jnp.concatenate(kept, -1)
            self.acc = [kept + self.got]
            self.left.pop(at)
        elif step == "far":
            if self.got is not None:
                self.acc = [self.acc[0] + self.got]
        else:
            axis = step[5:]
            x = self.acc[0]
            first = self.place(axis) == 0
            both = jnp.stack([jnp.where(first, x, self.got), jnp.where(first, self.got, x)])
            self.acc = [both.reshape((-1,) + x.shape[1:]) if axis != "rest" else both.reshape(-1, x.shape[-1])]

    def result(self):
        if self.split:
            assert not self.steps
            return self.acc[0].reshape(self.rows, -1).astype(F32)
        outs = []
        for x in self.parts:
            x = lax.psum_scatter(x, "wide", scatter_dimension=0, tiled=True)
            outs.append(lax.psum(x, ("rest", "side", "core")).astype(F32))
        return jnp.concatenate(outs, 1)


X_FIRST = ("core", "wide", "side", "rest", "far", "join_rest", "join_side", "join_core")
Y_FIRST = ("core", "side", "wide", "rest", "far", "join_rest", "join_side", "join_core")


def reduce_vectors(vectors):
    wide, rest, side, core = (lax.axis_size(a) for a in ("wide", "rest", "side", "core"))
    sizes = [v.shape[0] // wide for v in vectors]
    x = jnp.concatenate([v.reshape(wide, -1) for v in vectors], 1)
    if wide == side == core == 2:
        for axis in ("core", "side"):
            x = x + partner(x, axis)
        bit = 1
        while bit < rest:
            x = x + partner(x, "rest", bit)
            bit *= 2
        index = lax.axis_index("wide")
        got = partner(lax.dynamic_index_in_dim(x, 1 - index, 0, keepdims=False), "wide")
        x = lax.dynamic_index_in_dim(x, index, 0, keepdims=False) + got
    else:
        x = lax.psum_scatter(x, "wide", scatter_dimension=0, tiled=True)
        x = lax.psum(x, ("rest", "side", "core"))[0]
    outs, start = [], 0
    for size in sizes:
        outs.append(lax.slice_in_dim(x, start, start + size, axis=0))
        start += size
    return outs


def body(
    target, encoded, segments, out_grad,
    self_qkv_w, self_q_b, self_v_b, self_out_w, self_out_b, norm1_gain, norm1_bias,
    cross_q_w, cross_q_b, cross_kv_w, cross_v_b, cross_out_w, cross_out_b, norm2_gain, norm2_bias,
    ffn_in_w, ffn_in_b, ffn_out_w, ffn_out_b, norm3_gain, norm3_bias,
):
    row_count, tok_count, width = target.shape
    wide = lax.axis_size("wide")
    place = lax.axis_index("wide")
    scaling = HD**-0.5
    full_len = tok_count * wide
    swapped = wide == 2 and row_count == 2

    if swapped:
        def bring(x):
            kept = lax.dynamic_index_in_dim(x, place, 0, keepdims=False)
            sent = lax.dynamic_index_in_dim(x, 1 - place, 0, keepdims=False)
            return jnp.concatenate([kept, partner(sent, "wide")], 0)

        def send_back(x):
            return (partner(x[tok_count:].astype(BF), "wide"),)

        def give(x, got, dtype):
            kept = x[:tok_count].astype(dtype)
            got = got[0].astype(dtype)
            first = place == 0
            return jnp.stack([jnp.where(first, kept, got), jnp.where(first, got, kept)])

        tokens, causal, block_f, block_b = full_len, "block", 512, 256
        shift = (place * tok_count).astype(jnp.int32).reshape(1)
        seg = bring(segments)[None]
        key_seg = seg
    else:
        def bring(x):
            return x.reshape((-1,) + x.shape[2:])

        def send_back(x):
            return ()

        def give(x, got, dtype):
            return x.astype(dtype).reshape(row_count, tok_count, width)

        tokens, causal = tok_count, "mask"
        block_f = block_b = min(tok_count, 256)
        shift = (place * tok_count).astype(jnp.int32).reshape(1)
        seg = segments
        key_seg = lax.all_gather(segments, "wide", axis=1, tiled=True)

    def by_row(x):
        return x.reshape(-1, tokens, x.shape[-1])

    def flat(x):
        return x.reshape(-1, x.shape[-1])

    def keys_of(x):
        return x if swapped else lax.all_gather(x, "wide", axis=1, tiled=True)

    def key_grads(x):
        return x if swapped else lax.psum_scatter(x, "wide", scatter_dimension=1, tiled=True)

    terms = (segment_terms(seg)[0], segment_terms(key_seg)[1])
    block = min(256, row_count * tok_count)

    def attention(q, kv, columns, is_causal, after=()):
        return attend(
            q, kv, kv, columns, terms, shift, width, causal if is_causal else "no", block_f,
            swapped, after,
        )

    def attention_back(q, kv, columns, g, o, lse, is_causal, first, pairs, after):
        dq, dk, dv, sums = attend_back(
            q, kv, kv, columns, by_row(g), o, lse, terms, shift, first, pairs,
            causal if is_causal else "no", block_b, swapped, after,
        )
        return flat(dq), flat(key_grads(dk)), flat(key_grads(dv)), jnp.sum(sums, 0)

    flat_in = bring(target)
    flat_enc = bring(encoded)
    zeros = jnp.zeros_like(self_q_b)
    ones = jnp.ones_like(self_q_b)
    qkv_bias = jnp.concatenate([self_q_b, zeros, self_v_b])
    qkv_scale = jnp.concatenate([ones * scaling, ones, ones])
    qkv = by_row(((dot(flat_in, self_qkv_w) + qkv_bias) * qkv_scale).astype(BF))
    if swapped:
        self_kv, self_cols = qkv, (0, width, 2 * width)
    else:
        self_kv, self_cols = keys_of(qkv[..., width:]), (0, 0, width)
    self_o, self_lse = attention(qkv, self_kv, self_cols, True)
    self_ob = flat(self_o)
    n1, i1, h1b, cq = token_call(
        functools.partial(after_self_kernel, scaling=scaling), block,
        (self_ob, flat_in),
        (self_out_w, self_out_b, norm1_gain, norm1_bias, cross_q_w, cross_q_b),
        [(width, F32), (LANES, F32), (width, BF), (width, BF)],
        flops=4 * tokens * width * width, after=(flat_enc,),
    )
    upstream = bring(out_grad)
    cq = by_row(cq)
    ckv = by_row((dot(flat_enc, cross_kv_w) + jnp.concatenate([zeros, cross_v_b])).astype(BF))
    ckv = keys_of(ckv)
    cross_cols = (0, 0, width)
    cross_o, cross_lse = attention(cq, ckv, cross_cols, False)
    cross_ob = flat(cross_o)
    hidden = ffn_in_w.shape[1]
    h3b, act, dbf, h2b, dpre, dr2, dbc, dco, mid_sums, hid_sums = token_call(
        functools.partial(middle_kernel, chunk=width), block,
        (cross_ob, n1, upstream),
        (
            norm1_gain, norm1_bias, cross_out_w, cross_out_b, norm2_gain, norm2_bias,
            ffn_in_w, ffn_in_b, ffn_out_w, ffn_out_b, norm3_gain, norm3_bias,
        ),
        [
            (width, BF), (hidden, BF), (width, BF), (width, BF), (hidden, BF), (width, F32),
            (width, BF), (width, BF), (8, width, F32), (8, hidden, F32),
        ],
        scratch=[pltpu.VMEM((block, hidden), F32)],
        flops=2 * tokens * width * (4 * hidden + 2 * width),
    )
    got_out = send_back(h3b)

    ra = Reduction([dot(act, dbf, TN).astype(BF)], X_FIRST)
    sent_a = ra.send()
    rb = Reduction(
        [dot(h2b, dpre, TN).astype(BF), dot(cross_ob, dbc, TN).astype(BF)], Y_FIRST
    )
    sent_b = rb.send()
    ra.take()
    sent_a = ra.send()

    pairs = width // LANES
    cuts = 3 if pairs % 3 == 0 else 1
    per = pairs // cuts

    def cross_part(index, after):
        return attention_back(
            cq, ckv, cross_cols, dco, cross_o, cross_lse, False, index * per, per, after
        )

    def self_part(index, dso, after):
        return attention_back(
            qkv, self_kv, self_cols, dso, self_o, self_lse, True, index * per, per, after
        )

    cross_parts = [cross_part(0, sent_a + sent_b)]
    rb.take()
    sent_b = rb.send()
    for index in range(1, cuts):
        cross_parts.append(cross_part(index, sent_b if index == 1 else got_out))
    dcq, dck, dcv, csums = ([part[i] for part in cross_parts] for i in range(4))
    ra.take()
    sent_a = ra.send()
    rb.take()
    sent_b = rb.send()
    dr1, dba, dso, low_sums = token_call(
        functools.partial(before_self_kernel, parts=cuts), block,
        (*dcq, dr2, n1, i1),
        (cross_q_w, norm1_gain, self_out_w),
        [(width, F32), (width, BF), (width, BF), (8, width, F32)],
        flops=4 * tokens * width * width, after=sent_a + sent_b,
    )
    dckv = jnp.concatenate(dck + dcv, 1)
    enc_grad = dot(dckv, cross_kv_w, NT)
    got_enc = send_back(enc_grad)
    rc = Reduction(
        [dot(h1b, x, TN).astype(BF) for x in dcq]
        + [dot(flat_enc, x, TN).astype(BF) for x in dck + dcv]
        + [dot(self_ob, dba, TN).astype(BF)],
        Y_FIRST,
    )
    sent_c = rc.send()
    ra.take()
    sent_a = ra.send()
    rb.take()
    sent_b = rb.send()
    self_parts = [self_part(0, dso, sent_a + sent_b + sent_c)]
    for r in (ra, rb, rc):
        r.take()
    sent = ra.send() + rb.send() + rc.send()
    self_parts.append(self_part(1, dso, sent)) if cuts > 1 else None
    for index in range(2, cuts):
        self_parts.append(self_part(index, dso, got_enc))
    dsq, dsk, dsv, ssums = ([part[i] for part in self_parts] for i in range(4))
    dqkv = jnp.concatenate(dsq + dsk + dsv, 1)
    rd = Reduction([dot(flat_in, dqkv, TN).astype(BF)], X_FIRST)
    sent_d = rd.send()
    in_grad = dr1 + dot(dqkv, self_qkv_w, NT)
    got_in = send_back(in_grad)
    if swapped:
        for r in (ra, rb, rc, rd):
            r.take()
        left = [ra, rb, rc, rd]
        while left:
            left = [r for r in left if r.steps]
            for r in left:
                r.send()
            for r in left:
                r.take()
    layer_out = give(h3b, got_out, BF)
    encoded_grad = give(enc_grad, got_enc, F32)
    target_grad = give(in_grad, got_in, F32)
    grad_a, grad_b, grad_c, grad_d = (r.result() for r in (ra, rb, rc, rd))

    csums, ssums = (jnp.concatenate(x, 1) for x in (csums, ssums))
    (
        self_q_b_grad, self_v_b_grad, self_out_b_grad, norm1_gain_grad, norm1_bias_grad,
        cross_q_b_grad, cross_v_b_grad, cross_out_b_grad, norm2_gain_grad, norm2_bias_grad,
        ffn_in_b_grad, ffn_out_b_grad, norm3_gain_grad, norm3_bias_grad,
    ) = reduce_vectors(
        [
            ssums[0], ssums[1], low_sums[2], low_sums[0], low_sums[1],
            csums[0], csums[1], mid_sums[5], mid_sums[3], mid_sums[4],
            hid_sums[0], mid_sums[2], mid_sums[0], mid_sums[1],
        ]
    )
    return (
        layer_out, target_grad, encoded_grad,
        grad_d, self_q_b_grad, self_v_b_grad,
        grad_c[:, 3 * width :], self_out_b_grad, norm1_gain_grad, norm1_bias_grad,
        grad_c[:, :width], cross_q_b_grad,
        grad_c[:, width : 3 * width], cross_v_b_grad,
        grad_b[:, hidden:], cross_out_b_grad, norm2_gain_grad, norm2_bias_grad,
        grad_b[:, :hidden], ffn_in_b_grad, grad_a, ffn_out_b_grad,
        norm3_gain_grad, norm3_bias_grad,
    )


def solution(mesh):
    wide, narrow = mesh.shape["wide"], mesh.shape["narrow"]
    core = 2 if narrow % 2 == 0 else 1
    side = 2 if narrow % (2 * core) == 0 else 1
    devices = mesh.devices.reshape(wide, narrow // (side * core), side, core)
    split = Mesh(devices, ("wide", "rest", "side", "core"))
    rows = ("rest", "side", "core")
    token_spec = P(rows, "wide", None)
    in_specs = (token_spec, token_spec, P(rows, "wide"), token_spec) + (P(),) * 21
    matrix, vector = P("wide", None), P("wide")
    out_specs = (token_spec,) * 3 + (
        matrix, vector, vector, matrix, vector, vector, vector,
        matrix, vector, matrix, vector, matrix, vector, vector, vector,
        matrix, vector, matrix, vector, vector, vector,
    )
    return jax.shard_map(body, mesh=split, in_specs=in_specs, out_specs=out_specs, check_vma=False)
```

```python
import functools

import jax
import jax.numpy as jnp
from jax import lax
from jax.experimental import pallas as pl
from jax.experimental.pallas import tpu as pltpu
from jax.sharding import Mesh, PartitionSpec as P

HD = 64
LANES = 128
norm_epsilon = 1e-05
masked_score = -1e9
BF = jnp.bfloat16
F32 = jnp.float32

NN = (((1,), (0,)), ((), ()))
NT = (((1,), (1,)), ((), ()))
TN = (((0,), (0,)), ((), ()))


def dot(a, b, dims=NN):
    return lax.dot_general(a, b, dims, preferred_element_type=F32)


def segment_terms(seg):
    lane = jnp.arange(LANES) % HD
    same = seg[..., None] == lane
    query_terms = jnp.where((lane < 4) & ~same, masked_score, 0.0).astype(BF)
    key_terms = jnp.where(((lane < 4) & same) | ((lane >= 4) & (lane < 7)), 1.0, 0.0).astype(BF)
    return query_terms, key_terms


def head_lanes(shape, head):
    lane = lax.broadcasted_iota(jnp.int32, shape, 1)
    return (lane < HD) if head == 0 else (lane >= HD)


def causal_scores(scores, causal, first_query, block, query_axis):
    if causal == "block":
        queries = lax.broadcasted_iota(jnp.int32, (block, block), query_axis)
        keys = lax.broadcasted_iota(jnp.int32, (block, block), 1 - query_axis)
        count = scores.shape[1 - query_axis]
        before = lax.slice_in_dim(scores, 0, count - block, axis=1 - query_axis)
        corner = lax.slice_in_dim(scores, count - block, count, axis=1 - query_axis)
        corner = jnp.where(keys <= queries, corner, masked_score)
        if count == block:
            return corner
        return jnp.concatenate([before, corner], 1 - query_axis)
    if causal == "mask":
        queries = first_query + lax.broadcasted_iota(jnp.int32, scores.shape, query_axis)
        keys = lax.broadcasted_iota(jnp.int32, scores.shape, 1 - query_axis)
        return jnp.where(keys <= queries, scores, masked_score)
    return scores


def part_places(parts, shift):
    if len(parts) == 1:
        return [slice(0, parts[0].shape[0])]
    half = parts[0].shape[0]
    count = half * len(parts)
    return [
        pl.ds(pl.multiple_of(lax.rem(part * half + shift, count), half), half)
        for part in range(len(parts))
    ]


def array_places(count, shift, swapped):
    if not swapped:
        return [(slice(0, count), slice(0, count))]
    half = count // 2
    return [
        (
            slice(part * half, (part + 1) * half),
            pl.ds(pl.multiple_of(lax.rem(part * half + shift, count), half), half),
        )
        for part in (0, 1)
    ]


def row_block(index, block, count, shift, swapped):
    if not swapped:
        return pl.ds(index * block, block)
    return pl.ds(pl.multiple_of(lax.rem(index * block + shift, count), block), block)


def forward_kernel(*refs, parts, skipped, causal, block, swapped):
    scalars, refs = refs[0], refs[1:]
    q_parts, k_parts, v_parts = refs[:parts], refs[parts : 2 * parts], refs[2 * parts : 3 * parts]
    qt_ref, kt_ref = refs[3 * parts : 3 * parts + 2]
    o_ref, lse_ref, ka, va, qa = refs[3 * parts + 2 + skipped :]
    tq, ts = qa.shape[1], ka.shape[1]
    pair = pl.program_id(1)
    shift = scalars[0]
    extra = kt_ref[...]
    for part, here in enumerate(part_places(k_parts, shift)):
        k, v = k_parts[part][...], v_parts[part][...]
        extra = kt_ref[part * k.shape[0] : (part + 1) * k.shape[0], :]
        for head in (0, 1):
            own = head_lanes(k.shape, head)
            ka[head, here, :] = jnp.where(own, k, extra)
            va[head, here, :] = jnp.where(own, v, extra)
    for part, here in enumerate(part_places(q_parts, shift)):
        q = q_parts[part][...]
        extra = qt_ref[part * q.shape[0] : (part + 1) * q.shape[0], :]
        for head in (0, 1):
            qa[head, here, :] = jnp.where(head_lanes(q.shape, head), q, extra)
    lane = lax.broadcasted_iota(jnp.int32, (block, LANES), 1)
    for index in range(tq // block):
        count = (index + 1) * block if causal == "block" else ts
        outs, lses = [], []
        for head in (0, 1):
            scores = dot(qa[head, index * block : (index + 1) * block, :], ka[head, :count, :], NT)
            scores = causal_scores(scores, causal, shift + index * block, block, 0)
            top = jnp.max(scores, 1, keepdims=True)
            weights = jnp.exp(scores - top).astype(BF)
            sums = dot(weights, va[head, :count, :])
            ones_lane = HD + 6 if head == 0 else 6
            total = sums[:, ones_lane : ones_lane + 1]
            outs.append(sums / total)
            lses.append(top + jnp.log(total))
        there = row_block(index, block, tq, shift, swapped)
        o_ref[there, :] = jnp.where(lane < HD, outs[0], outs[1]).astype(BF)
        lse_ref[there, :] = jnp.where(
            lane == 2 * pair, lses[0], jnp.where(lane == 2 * pair + 1, lses[1], lse_ref[there, :])
        )


def three_parts(x):
    parts = []
    for _ in range(3):
        part = x.astype(BF).astype(F32)
        parts.append(part)
        x = x - part
    return parts


def backward_kernel(*refs, parts, skipped, causal, block, swapped, scaling, first):
    scalars, refs = refs[0], refs[1:]
    q_parts, k_parts, v_parts = refs[:parts], refs[parts : 2 * parts], refs[2 * parts : 3 * parts]
    g_ref, o_ref, qt_ref, kt_ref, lse_ref = refs[3 * parts : 3 * parts + 5]
    (
        dq_ref, dk_ref, dv_ref, ka, va, qa, ga, k_turned, dk_sum, dv_sum, dq_turned,
    ) = refs[3 * parts + 5 + skipped :]
    tq, ts = qa.shape[1], ka.shape[1]
    pair = pl.program_id(1) + first
    shift = scalars[0]
    for part, here in enumerate(part_places(k_parts, shift)):
        k, v = k_parts[part][...], v_parts[part][...]
        extra = kt_ref[part * k.shape[0] : (part + 1) * k.shape[0], :]
        for head in (0, 1):
            own = head_lanes(k.shape, head)
            ka[head, here, :] = jnp.where(own, k, extra)
            va[head, here, :] = jnp.where(own, v, extra)
    for here in [s for s, _ in array_places(ts, shift, swapped)]:
        k = jnp.where(head_lanes((here.stop - here.start, LANES), 0), ka[0, here, :], ka[1, here, :])
        k_turned[:, here] = k.astype(F32).T.astype(BF)
    for part, here in enumerate(part_places(q_parts, shift)):
        q = q_parts[part][...]
        there = slice(part * q.shape[0], (part + 1) * q.shape[0])
        g, extra = g_ref[there, :], qt_ref[there, :]
        products = g.astype(F32) * o_ref[there, :].astype(F32)
        lse = lse_ref[there, :]
        lane = lax.broadcasted_iota(jnp.int32, q.shape, 1)
        for head in (0, 1):
            own = head_lanes(q.shape, head)
            at = HD + 4 if head == 0 else 4
            delta = three_parts(-jnp.sum(jnp.where(own, products, 0.0), 1, keepdims=True))
            lse_col = three_parts(
                -jnp.sum(jnp.where(lane == 2 * pair + head, lse, 0.0), 1, keepdims=True)
            )
            q_extra, g_extra = extra.astype(F32), jnp.zeros(q.shape, F32)
            for i in range(3):
                q_extra = jnp.where(lane == at + i, lse_col[i], q_extra)
                g_extra = jnp.where(lane == at + i, delta[i], g_extra)
            qa[head, here, :] = jnp.where(own, q, q_extra.astype(BF))
            ga[head, here, :] = jnp.where(own, g, g_extra.astype(BF))
    blocks = tq // block
    for index in reversed(range(blocks)):
        count = (index + 1) * block if causal == "block" else ts
        rows = slice(index * block, (index + 1) * block)
        for head in (0, 1):
            q, g = qa[head, rows, :], ga[head, rows, :]
            scores = dot(ka[head, :count, :], q, NT)
            scores = causal_scores(scores, causal, shift + index * block, block, 1)
            probs = jnp.exp(scores)
            grads = (probs * dot(va[head, :count, :], g, NT)).astype(BF)
            dv, dk = dot(probs.astype(BF), g), dot(grads, q)
            if index == blocks - 1:
                dv_sum[head, :count, :] = dv
                dk_sum[head, :count, :] = dk
            else:
                dv_sum[head, :count, :] += dv
                dk_sum[head, :count, :] += dk
            own_rows = slice(HD * head, HD * (head + 1))
            dq_turned[own_rows, rows] = dot(k_turned[own_rows, :count], grads)
        there = row_block(index, block, tq, shift, swapped)
        dq_ref[there, :] = dq_turned[:, rows].T.astype(BF) * jnp.asarray(scaling, BF)
    for here, there in array_places(ts, shift, swapped):
        own = head_lanes((here.stop - here.start, LANES), 0)
        dk_ref[there, :] = jnp.where(own, dk_sum[0, here, :], dk_sum[1, here, :]).astype(BF)
        dv_ref[there, :] = jnp.where(own, dv_sum[0, here, :], dv_sum[1, here, :]).astype(BF)


ANYWHERE = pl.BlockSpec(memory_space=pl.ANY)


def head_spec(count, start):
    return pl.BlockSpec((pl.Squeezed(), count, LANES), lambda row, pair, _: (row, 0, start + pair))


def shared_spec(count):
    return pl.BlockSpec((pl.Squeezed(), count, LANES), lambda row, pair, _: (row, 0, 0))


def part_specs(q, k, v, first):
    specs, arrays = [], []
    for parts, column in (q, k, v):
        for x in parts:
            specs.append(head_spec(x.shape[1], column // LANES + first))
            arrays.append(x)
    return specs, arrays


def attend(q, k, v, terms, shift, width, causal, block, swapped, after=()):
    specs, arrays = part_specs(q, k, v, 0)
    rows = arrays[0].shape[0]
    tq, ts = (sum(x.shape[1] for x in one[0]) for one in (q, k))
    pairs = width // LANES
    elements = rows * pairs * 2 * tq * ts
    return pl.pallas_call(
        functools.partial(
            forward_kernel, parts=len(q[0]), skipped=len(after), causal=causal, block=block,
            swapped=swapped,
        ),
        grid_spec=pltpu.PrefetchScalarGridSpec(
            num_scalar_prefetch=1,
            grid=(rows, pairs),
            in_specs=specs + [shared_spec(tq), shared_spec(ts)] + [ANYWHERE] * len(after),
            out_specs=[head_spec(tq, 0), shared_spec(tq)],
            scratch_shapes=[pltpu.VMEM((2, n, LANES), BF) for n in (ts, ts, tq)],
        ),
        out_shape=[
            jax.ShapeDtypeStruct((rows, tq, width), BF),
            jax.ShapeDtypeStruct((rows, tq, LANES), F32),
        ],
        compiler_params=pltpu.CompilerParams(vmem_limit_bytes=48 * 2**20),
        cost_estimate=pl.CostEstimate(
            flops=elements * 1600, bytes_accessed=rows * (tq + ts) * width * 4, transcendentals=0
        ),
    )(shift, *arrays, *terms, *after)


def attend_back(
    q, k, v, g, o, lse, terms, shift, first, pairs, causal, block, swapped, held=(), after=()
):
    specs, arrays = part_specs(q, k, v, first)
    rows, _, width = o.shape
    tq, ts = (sum(x.shape[1] for x in one[0]) for one in (q, k))
    elements = rows * pairs * 2 * tq * ts
    skipped = len(held) + len(after)
    count = len(arrays) + 5
    return pl.pallas_call(
        functools.partial(
            backward_kernel, parts=len(q[0]), skipped=skipped, causal=causal, block=block,
            swapped=swapped, scaling=HD**-0.5, first=first,
        ),
        grid_spec=pltpu.PrefetchScalarGridSpec(
            num_scalar_prefetch=1,
            grid=(rows, pairs),
            in_specs=specs
            + [head_spec(tq, first)] * 2
            + [shared_spec(tq), shared_spec(ts), shared_spec(tq)]
            + [ANYWHERE] * skipped,
            out_specs=[head_spec(tq, first), head_spec(ts, first), head_spec(ts, first)],
            scratch_shapes=[pltpu.VMEM((2, n, LANES), BF) for n in (ts, ts, tq, tq)]
            + [
                pltpu.VMEM((LANES, ts), BF),
                pltpu.VMEM((2, ts, LANES), F32),
                pltpu.VMEM((2, ts, LANES), F32),
                pltpu.VMEM((LANES, tq), F32),
            ],
        ),
        out_shape=[jax.ShapeDtypeStruct((rows, n, width), BF) for n in (tq, ts, ts)],
        input_output_aliases={1 + count + i: i for i in range(len(held))},
        compiler_params=pltpu.CompilerParams(vmem_limit_bytes=48 * 2**20),
        cost_estimate=pl.CostEstimate(
            flops=elements * 2600, bytes_accessed=rows * (tq + ts) * pairs * 1024, transcendentals=0
        ),
    )(shift, *arrays, g, o, *terms, lse, *held, *after)


def norm(resid):
    center = resid - jnp.mean(resid, -1, keepdims=True)
    inverse = lax.rsqrt(jnp.mean(center * center, -1, keepdims=True) + norm_epsilon)
    return center * inverse, inverse


def norm_back(upstream, normed, inverse, gain_vec):
    w = upstream * gain_vec
    return (
        w - jnp.mean(w, -1, keepdims=True) - normed * jnp.mean(w * normed, -1, keepdims=True)
    ) * inverse


def gelu_parts(pre):
    bell = jnp.exp(pre * pre * -0.5)
    t = 1.0 / (1.0 + jnp.abs(pre) * (0.3275911 * 0.5**0.5))
    poly = 0.5 * 1.061405429
    for c in (-1.453152027, 1.421413741, -0.284496736, 0.254829592):
        poly = poly * t + 0.5 * c
    tail = poly * t * bell
    phi_sum = jnp.where(pre >= 0, 1.0 - tail, tail)
    return pre * phi_sum, phi_sum + pre * (bell * 0.3989422804014327)


def add_rows(sums_ref, first, rows):
    for index, value in enumerate(rows):
        here = slice(first + index, first + index + 1)
        sums_ref[here, :] += jnp.sum(value.astype(F32), 0, keepdims=True)


def finish_rows(sums_ref, out_ref):
    @pl.when(pl.program_id(0) == pl.num_programs(0) - 1)
    def _():
        out_ref[...] = sums_ref[...].T


def clear(ref):
    @pl.when(pl.program_id(0) == 0)
    def _():
        ref[...] = jnp.zeros_like(ref)


def row(ref):
    return ref[...][None, :]


def project_kernel(x_ref, w_ref, b_ref, out_ref, *, scaled):
    width = b_ref.shape[0] // 3
    y = dot(x_ref[...], w_ref[...]) + row(b_ref)
    if scaled:
        out_ref[:, :width] = (y[:, :width] * HD**-0.5).astype(BF)
        out_ref[:, width:] = y[:, width:].astype(BF)
    else:
        out_ref[...] = y.astype(BF)


def after_self_kernel(
    o_ref, x_ref, w_ref, b_ref, gain_ref, bias_ref, qw_ref, qb_ref, n1_ref, i1_ref, h1b_ref, cq_ref,
):
    resid = x_ref[...].astype(F32) + (dot(o_ref[...], w_ref[...]) + row(b_ref))
    n1, i1 = norm(resid)
    h1b = (n1 * row(gain_ref) + row(bias_ref)).astype(BF)
    n1_ref[...] = n1
    i1_ref[...] = jnp.broadcast_to(i1, i1_ref.shape)
    h1b_ref[...] = h1b
    cq_ref[...] = ((dot(h1b, qw_ref[...]) + row(qb_ref)) * HD**-0.5).astype(BF)


def middle_kernel(
    o_ref, n1_ref, up_ref, g1_ref, s1_ref, ow_ref, ob_ref, g2_ref, s2_ref,
    w1_ref, b1_ref, w2_ref, b2_ref, g3_ref, s3_ref,
    *refs, chunk, kept_blocks,
):
    if kept_blocks is None:
        out_ref, *refs = refs
    else:
        out_ref, sent_ref, *refs = refs
    act_ref, dbf_ref, h2b_ref, dpre_ref, dr2_ref, dbc_ref, dco_ref, sums_ref, slope, sums = refs
    clear(sums)
    h1 = n1_ref[...] * row(g1_ref) + row(s1_ref)
    n2, i2 = norm(h1 + (dot(o_ref[...], ow_ref[...]) + row(ob_ref)))
    h2 = n2 * row(g2_ref) + row(s2_ref)
    h2b = h2.astype(BF)
    h2b_ref[...] = h2b
    hidden = w1_ref.shape[1]
    cols = [slice(c, c + chunk) for c in range(0, hidden, chunk)]
    bias1 = row(b1_ref)
    branch = row(b2_ref)
    for c in cols:
        pre = dot(h2b, w1_ref[:, c]) + bias1[:, c]
        value, slope_c = gelu_parts(pre)
        slope[:, c] = slope_c
        act_c = value.astype(BF)
        act_ref[:, c] = act_c
        branch = branch + dot(act_c, w2_ref[c, :])
    n3, i3 = norm(h2 + branch)
    out = (n3 * row(g3_ref) + row(s3_ref)).astype(BF)
    if kept_blocks is None:
        out_ref[...] = out
    else:
        step = pl.program_id(0)

        @pl.when(step < kept_blocks)
        def _():
            out_ref[...] = out

        @pl.when(step >= kept_blocks)
        def _():
            sent_ref[...] = out

    up = up_ref[...].astype(F32)
    dr3 = norm_back(up, n3, i3, row(g3_ref))
    dbf = dr3.astype(BF)
    dbf_ref[...] = dbf
    dh2 = dr3
    for c in cols:
        dpre_c = (dot(dbf, w2_ref[c, :], NT) * slope[:, c]).astype(BF)
        dpre_ref[:, c] = dpre_c
        dh2 = dh2 + dot(dpre_c, w1_ref[:, c], NT)
    dr2 = norm_back(dh2, n2, i2, row(g2_ref))
    dbc = dr2.astype(BF)
    dr2_ref[...] = dr2
    dbc_ref[...] = dbc
    dco_ref[...] = dot(dbc, ow_ref[...], NT).astype(BF)
    add_rows(sums, MID_ROWS, (up * n3, up, dbf, dh2 * n2, dh2))
    finish_rows(sums, sums_ref)


def before_self_kernel(
    dcq_ref, dr2_ref, n1_ref, i1_ref, qw_ref, g1_ref, ow_ref, dr1_ref, dba_ref, dso_ref, sums_ref,
    sums,
):
    clear(sums)
    n1 = n1_ref[...]
    dh1 = dr2_ref[...] + dot(dcq_ref[...], qw_ref[...], NT)
    dr1 = norm_back(dh1, n1, i1_ref[:, 0:1], row(g1_ref))
    dba = dr1.astype(BF)
    dr1_ref[...] = dr1
    dba_ref[...] = dba
    dso_ref[...] = dot(dba, ow_ref[...], NT).astype(BF)
    add_rows(sums, LOW_ROWS, (dh1 * n1, dh1))
    finish_rows(sums, sums_ref)


def input_grad_kernel(*refs, count, start):
    grads, w_ref, out_ref = refs[:count], refs[count + start], refs[count + start + 1]
    total = refs[count][...] if start else None
    width = grads[0].shape[-1]
    for index, ref in enumerate(grads):
        part = dot(ref[...], w_ref[:, index * width : (index + 1) * width], NT)
        total = part if total is None else total + part
    out_ref[...] = total.astype(out_ref.dtype)


class Joined:
    def __init__(self, kept, got, use_kept):
        self.kept, self.got, self.use_kept = kept, got, use_kept

    def __getitem__(self, index):
        return jnp.where(self.use_kept, self.kept[index], self.got[index])


def token_call(kernel, block, blocked, whole, outs, place, scratch=(), flops=0, after=(), span=None):
    def length(x):
        return x.shape[0] if not isinstance(x, tuple) else x[0].shape[1] * (1 if x[1] is None else 2)

    tokens = length(blocked[0])
    half = tokens // block // 2
    first, count = span if span is not None else (0, tokens // block)
    in_specs, arrays, kinds = [], [], []
    for x in blocked:
        if not isinstance(x, tuple):
            in_specs.append(pl.BlockSpec((block, x.shape[1]), lambda i, _: (i + first, 0)))
            arrays.append(x)
            kinds.append(1)
            continue
        stack, got = x
        shape = (pl.Squeezed(), block, stack.shape[2])
        if got is None:
            in_specs.append(pl.BlockSpec(shape, lambda i, p: (p[0], i, 0)))
            arrays.append(stack)
            kinds.append(1)
        else:
            in_specs.append(pl.BlockSpec(shape, lambda i, p: (p[0], jnp.minimum(i, half - 1), 0)))
            in_specs.append(
                pl.BlockSpec(shape[1:], lambda i, p: (jnp.maximum(i - half, 0), 0))
            )
            arrays += [stack, got]
            kinds.append(2)
    for x in whole:
        zeros = (0,) * x.ndim
        in_specs.append(
            pl.BlockSpec(x.shape, lambda i, _, z=zeros: z, pipeline_mode=pl.Buffered(1))
        )
    in_specs += [ANYWHERE] * len(after)
    out_specs, out_shape = [], []
    for out in outs:
        if out[0] == "whole":
            out_specs.append(pl.BlockSpec(out[1:3], lambda i, _: (0, 0)))
            shape = out[1:3]
        elif out[0] == "kept":
            shape = (out[1], tokens // 2, out[2])
            out_specs.append(
                pl.BlockSpec(
                    (pl.Squeezed(), block, out[2]),
                    lambda i, p: (p[0], jnp.minimum(i, half - 1), 0),
                )
            )
        elif out[0] == "sent":
            shape = (tokens // 2, out[1])
            out_specs.append(
                pl.BlockSpec(
                    (block, out[1]), lambda i, _: (jnp.maximum(i + first - half, 0), 0)
                )
            )
        else:
            shape = (count * block, out[0])
            out_specs.append(pl.BlockSpec((block, out[0]), lambda i, _: (i, 0)))
        out_shape.append(jax.ShapeDtypeStruct(shape, out[-1]))

    def run(_, *refs):
        used = []
        for kind in kinds:
            if kind == 1:
                used.append(refs[0])
            else:
                used.append(Joined(refs[0], refs[1], pl.program_id(0) < half))
            refs = refs[kind:]
        kernel(*used, *refs[: len(whole)], *refs[len(whole) + len(after) :])

    moved = sum(a.size * a.dtype.itemsize for a in (*arrays, *whole, *out_shape))
    return pl.pallas_call(
        run,
        grid_spec=pltpu.PrefetchScalarGridSpec(
            num_scalar_prefetch=1,
            grid=(count,),
            in_specs=in_specs,
            out_specs=out_specs,
            scratch_shapes=list(scratch),
        ),
        out_shape=out_shape,
        compiler_params=pltpu.CompilerParams(vmem_limit_bytes=56 * 2**20),
        cost_estimate=pl.CostEstimate(
            flops=flops * count * block // tokens, bytes_accessed=moved, transcendentals=0
        ),
    )(place, *arrays, *whole, *after)


def store_kernel(_, got_ref, __, out_ref):
    out_ref[...] = got_ref[...].astype(out_ref.dtype)


def store_other(held, got, place):
    n, c = got.shape
    return pl.pallas_call(
        store_kernel,
        grid_spec=pltpu.PrefetchScalarGridSpec(
            num_scalar_prefetch=1,
            grid=(2,),
            in_specs=[pl.BlockSpec((n // 2, c), lambda i, _: (i, 0)), ANYWHERE],
            out_specs=pl.BlockSpec((pl.Squeezed(), n // 2, c), lambda i, p: (1 - p[0], i, 0)),
        ),
        out_shape=jax.ShapeDtypeStruct(held.shape, held.dtype),
        input_output_aliases={2: 0},
        cost_estimate=pl.CostEstimate(flops=0, bytes_accessed=n * c * 6, transcendentals=0),
    )(place, got, held)


MID_ROWS, LOW_ROWS = 8, 16


def weight_grads(items, extras, place, wide, order, after=()):
    width = items[0][0].shape[-1] if not isinstance(items[0][0], tuple) else items[0][0][0].shape[-1]
    specs, arrays, lefts, steps = [], [], [], []
    known = {}
    for left, right, sum_row in items:
        if id(left) not in known:
            where = len(arrays)
            if isinstance(left, tuple):
                stack, got = left
                specs.append(
                    pl.BlockSpec(
                        (pl.Squeezed(),) + stack.shape[1:], lambda j, p: (p[0], 0, 0),
                        pipeline_mode=pl.Buffered(1),
                    )
                )
                specs.append(
                    pl.BlockSpec(got.shape, lambda j, p: (0, 0), pipeline_mode=pl.Buffered(1))
                )
                arrays += [stack, got]
            else:
                specs.append(
                    pl.BlockSpec(left.shape, lambda j, p: (0, 0), pipeline_mode=pl.Buffered(1))
                )
                arrays.append(left)
            known[id(left)] = (where, isinstance(left, tuple))
        begin, blocks = len(steps), right.shape[1] // width
        where = len(arrays)
        specs.append(
            pl.BlockSpec(
                (right.shape[0], width),
                lambda j, p, b=begin, n=blocks: (0, jnp.clip(j - b, 0, n - 1)),
            )
        )
        arrays.append(right)
        for index in range(blocks):
            steps.append((known[id(left)], where, sum_row, index, blocks))
    for extra in extras:
        specs.append(
            pl.BlockSpec(extra.shape, lambda j, p: (0, 0), pipeline_mode=pl.Buffered(1))
        )
    slab = width // len(order)
    size = width // wide

    def kernel(_, *refs):
        ins, rest = refs[: len(arrays)], refs[len(arrays) :]
        extra_refs, (out_ref, sums) = rest[: len(extras)], rest[len(extras) + len(after) :]
        clear(sums)
        step = pl.program_id(0)

        def store(value):
            for to, source in enumerate(order):
                out_ref[to * slab : (to + 1) * slab, :] = value[
                    source * slab : (source + 1) * slab
                ].astype(BF)

        for index, ((left, split), right, sum_row, part, parts) in enumerate(steps):

            @pl.when(step == index)
            def _():
                grad = ins[right][...]
                if split:
                    half = ins[left].shape[0]
                    value = dot(ins[left][...], grad[:half], TN)
                    value = value + dot(ins[left + 1][...], grad[half:], TN)
                else:
                    value = dot(ins[left][...], grad, TN)
                store(value)
                if sum_row is not None:
                    total = jnp.sum(grad.astype(F32), 0, keepdims=True)
                    if parts == 1:
                        sums[sum_row : sum_row + 1, :] = total
                    else:
                        for piece in range(wide):
                            w, k = divmod(wide * part + piece, parts)
                            sums[sum_row + k : sum_row + k + 1, w * size : (w + 1) * size] = total[
                                :, piece * size : (piece + 1) * size
                            ]

        @pl.when(step == len(steps))
        def _():
            value = sums[...].T
            for ref in extra_refs:
                value = value + ref[...]
            store(jnp.concatenate([value, jnp.zeros((width, width - LANES), F32)], 1))

    columns = width * len(steps) + LANES
    tokens = items[0][1].shape[0]
    return pl.pallas_call(
        kernel,
        grid_spec=pltpu.PrefetchScalarGridSpec(
            num_scalar_prefetch=1,
            grid=(len(steps) + 1,),
            in_specs=specs + [ANYWHERE] * len(after),
            out_specs=pl.BlockSpec((width, width), lambda j, _: (0, j)),
            scratch_shapes=[pltpu.VMEM((LANES, width), F32)],
        ),
        out_shape=jax.ShapeDtypeStruct((width, columns), BF),
        compiler_params=pltpu.CompilerParams(vmem_limit_bytes=48 * 2**20),
        cost_estimate=pl.CostEstimate(
            flops=2 * tokens * width * columns,
            bytes_accessed=sum(a.size * 2 for a in arrays) + width * columns * 2,
            transcendentals=0,
        ),
    )(place, *arrays, *extras, *after)


def tall_grad(left, right, place, order, after=()):
    tokens, rows = left.shape
    width = right.shape[1]
    slabs = len(order)
    size = rows // slabs

    def out_row(j):
        to = 0
        for at, source in enumerate(order):
            to = jnp.where(j == source, at, to)
        return to

    def kernel(_, left_ref, right_ref, *refs):
        refs[-1][...] = dot(left_ref[...], right_ref[...], TN).astype(BF)

    return pl.pallas_call(
        kernel,
        grid_spec=pltpu.PrefetchScalarGridSpec(
            num_scalar_prefetch=1,
            grid=(slabs,),
            in_specs=[
                pl.BlockSpec((tokens, size), lambda j, _: (0, j)),
                pl.BlockSpec(right.shape, lambda j, _: (0, 0), pipeline_mode=pl.Buffered(1)),
            ]
            + [ANYWHERE] * len(after),
            out_specs=pl.BlockSpec((size, width), lambda j, _: (out_row(j), 0)),
        ),
        out_shape=jax.ShapeDtypeStruct((rows, width), BF),
        compiler_params=pltpu.CompilerParams(vmem_limit_bytes=48 * 2**20),
        cost_estimate=pl.CostEstimate(
            flops=2 * tokens * rows * width,
            bytes_accessed=2 * (left.size + right.size + rows * width),
            transcendentals=0,
        ),
    )(place, left, right, *after)


def vectors_kernel(x_ref, *outs, columns):
    turned = x_ref[...].astype(F32).T
    for (start, count), out in zip(columns, outs):
        rows = [turned[start + i] for i in range(count)]
        out[...] = rows[0] if count == 1 else jnp.concatenate(rows)


def vectors_of(x, columns):
    return pl.pallas_call(
        functools.partial(vectors_kernel, columns=columns),
        out_shape=[jax.ShapeDtypeStruct((count * x.shape[0],), F32) for _, count in columns],
    )(x)


def partner(x, axis, bit=1):
    count = lax.axis_size(axis)
    return lax.ppermute(x, axis, [(i, i ^ bit) for i in range(count)])


ROWS = ("far", "near", "side", "core")


def pick(x, index):
    half = x.shape[0] // 2
    return lax.dynamic_slice_in_dim(x, index * half, half, 0)


class Reduction:
    def __init__(self, x, order):
        self.split = all(lax.axis_size(a) == 2 for a in ("wide", "side", "near", "core"))
        self.x = x
        self.steps = list(order) if self.split else []
        self.terms = [x]
        self.got = None

    def total(self, terms):
        value = sum(t.astype(F32) for t in terms)
        return value.astype(BF)

    def send(self):
        if not self.steps:
            return ()
        step = self.steps[0]
        if step == "core_sum":
            self.got = lax.psum_scatter(self.x, "core", scatter_dimension=0, tiled=True)
            return ()
        if step == "gather":
            self.got = lax.all_gather(self.total(self.terms), ("core", "side", "near"), axis=0, tiled=True)
            return ()
        if step in ("core", "wide", "side", "near"):
            sent = self.total([pick(t, 1 - lax.axis_index(step)) for t in self.terms])
            axis = step
        elif step == "far":
            sent = self.total(self.terms)
            axis = step
        else:
            sent = self.total(self.terms)
            self.terms = [sent]
            axis = step[5:]
        if step == "far":
            self.got = []
            count, bit = lax.axis_size("far"), 1
            assert count <= 2
            while bit < count:
                self.got.append(partner(sent, "far", bit))
                bit *= 2
        else:
            self.got = [partner(sent, axis)]
        return (sent,)

    def take(self):
        if not self.steps:
            return
        step = self.steps.pop(0)
        if step in ("core_sum", "gather"):
            self.terms = [self.got]
        elif step in ("core", "wide", "side", "near"):
            self.terms = [pick(t, lax.axis_index(step)) for t in self.terms] + self.got
        elif step == "far":
            self.terms = self.terms + self.got
        else:
            x, got = self.terms[0], self.got[0]
            first = lax.axis_index(step[5:]) == 0
            self.terms = [
                jnp.concatenate([jnp.where(first, x, got), jnp.where(first, got, x)], 0)
            ]

    def result(self):
        assert not self.steps
        if self.split:
            return self.terms[0]
        x = lax.psum_scatter(self.x, "wide", scatter_dimension=0, tiled=True)
        return lax.psum(x, ROWS)


CORE_WIDE = (0, 2, 1, 3)
CORE_SIDE = (0, 4, 1, 5, 2, 6, 3, 7)
JOINS = ("join_near", "join_side", "join_core")
X_FIRST = ("core", "wide", "side", "near", "far") + JOINS
Y_FIRST = ("core", "side", "wide", "near", "far") + JOINS


def body(
    target, encoded, segments, out_grad,
    self_qkv_w, self_q_b, self_v_b, self_out_w, self_out_b, norm1_gain, norm1_bias,
    cross_q_w, cross_q_b, cross_kv_w, cross_v_b, cross_out_w, cross_out_b, norm2_gain, norm2_bias,
    ffn_in_w, ffn_in_b, ffn_out_w, ffn_out_b, norm3_gain, norm3_bias,
):
    row_count, tok_count, width = target.shape
    hidden = ffn_in_w.shape[1]
    wide = lax.axis_size("wide")
    index = lax.axis_index("wide").astype(jnp.int32)
    place = index.reshape(1)
    shift = (index * tok_count).reshape(1)
    swapped = wide == 2 and row_count == 2
    split = all(lax.axis_size(a) == 2 for a in ("wide", "side", "near", "core"))
    core_wide = CORE_WIDE if split else (0, 1, 2, 3)
    core_side = CORE_SIDE if split else (0,)
    tokens = row_count * tok_count
    block = min(256, tok_count)

    if swapped:
        def bring(x):
            sent = lax.dynamic_index_in_dim(x, 1 - index, 0, keepdims=False)
            return x, partner(sent, "wide")

        causal, block_f, block_b = "block", 2 * block, block
        seg_kept, seg_got = bring(segments)
        seg = jnp.concatenate(
            [lax.dynamic_index_in_dim(seg_kept, index, 0, keepdims=False), seg_got]
        )[None]
        key_seg = seg
        row_tokens = tokens
    else:
        def bring(x):
            return x.reshape(tokens, -1)

        causal, block_f, block_b = "mask", block, block
        seg = segments
        key_seg = lax.all_gather(segments, "wide", axis=1, tiled=True)
        row_tokens = tok_count
    terms = (segment_terms(seg)[0], segment_terms(key_seg)[1])

    def by_row(x):
        return x.reshape(-1, row_tokens, x.shape[-1])

    def flat(x):
        return x.reshape(-1, x.shape[-1])

    def keys_of(x):
        return lax.all_gather(x, "wide", axis=1, tiled=True)

    def key_grads(x):
        return x if swapped else lax.psum_scatter(x, "wide", scatter_dimension=1, tiled=True)

    def project(x, w, bias, scaled, after=()):
        if not swapped:
            parts = [(x, None)]
        else:
            parts = [((x[0], None), None), (x[1], after)]
        outs = []
        for part, deps in parts:
            (out,) = token_call(
                functools.partial(project_kernel, scaled=scaled), block, (part,), (w, bias),
                [(w.shape[1], BF)], place, flops=2 * tokens * width * w.shape[1],
                after=deps or (),
            )
            outs.append(out[None] if swapped else by_row(out))
        return outs

    def attention(q, k, v, is_causal, after=()):
        return attend(
            q, k, v, terms, shift, width, causal if is_causal else "no", block_f, swapped, after
        )

    def attention_back(q, k, v, g, o, lse, is_causal, cuts, after):
        held = ()
        pairs = width // LANES
        per = pairs // cuts
        for cut in range(cuts):
            held = attend_back(
                q, k, v, by_row(g), o, lse, terms, shift, cut * per, per,
                causal if is_causal else "no", block_b, swapped, held, after[cut](),
            )
        dq, dk, dv = held
        return flat(dq), flat(key_grads(dk)), flat(key_grads(dv))

    def input_grad(grads, w, start=None, after=()):
        blocked = list(grads) + ([] if start is None else [start])
        kernel = functools.partial(
            input_grad_kernel, count=len(grads), start=0 if start is None else 1
        )
        flops = 2 * tokens * width * w.shape[1]
        if not swapped:
            return token_call(kernel, block, blocked, (w,), [(width, F32)], place, flops=flops)[0], None
        half = tokens // block // 2
        (sent,) = token_call(
            kernel, block, blocked, (w,), [("sent", width, BF)], place, flops=flops,
            span=(half, half), after=after,
        )
        (kept,) = token_call(
            kernel, block, blocked, (w,), [("kept", 2, width, F32)], place, flops=flops,
            span=(0, half), after=(sent,),
        )
        return kept, sent

    def give(out, got):
        if not swapped:
            return out.reshape(row_count, tok_count, width)
        return store_other(out, got, place)

    def send_back(x):
        return partner(x, "wide") if swapped else None

    zeros = jnp.zeros_like(self_q_b)
    x_in = bring(target)
    x_enc = bring(encoded)
    qkv = project(x_in, self_qkv_w, jnp.concatenate([self_q_b, zeros, self_v_b]), True)
    if swapped:
        self_q, self_k, self_v = (qkv, 0), (qkv, width), (qkv, 2 * width)
    else:
        both = [keys_of(qkv[0][..., width:])]
        self_q, self_k, self_v = (qkv, 0), (both, 0), (both, width)
    self_o, self_lse = attention(self_q, self_k, self_v, True)
    self_ob = flat(self_o)
    n1, i1, h1b, cq = token_call(
        after_self_kernel, block, (self_ob, x_in),
        (self_out_w, self_out_b, norm1_gain, norm1_bias, cross_q_w, cross_q_b),
        [(width, F32), (LANES, F32), (width, BF), (width, BF)], place,
        flops=4 * tokens * width * width,
    )
    ckv = project(
        x_enc, cross_kv_w, jnp.concatenate([zeros, cross_v_b]), False, (h1b,)
    )
    upstream = bring(out_grad)
    cross_q = ([by_row(cq)], 0)
    if swapped:
        half = row_tokens // 2
        cross_q = ([by_row(cq)[:, :half], by_row(cq)[:, half:]], 0)
        cross_k, cross_v = (ckv, 0), (ckv, width)
    else:
        both = [keys_of(ckv[0])]
        cross_k, cross_v = (both, 0), (both, width)
    cross_o, cross_lse = attention(cross_q, cross_k, cross_v, False)
    cross_ob = flat(cross_o)
    outs = [("kept", 2, width, BF), ("sent", width, BF)] if swapped else [(width, BF)]
    *h3, act, dbf, h2b, dpre, dr2, dbc, dco, mid_sums = token_call(
        functools.partial(
            middle_kernel, chunk=width, kept_blocks=tok_count // block if swapped else None
        ),
        block, (cross_ob, n1, upstream),
        (
            norm1_gain, norm1_bias, cross_out_w, cross_out_b, norm2_gain, norm2_bias,
            ffn_in_w, ffn_in_b, ffn_out_w, ffn_out_b, norm3_gain, norm3_bias,
        ),
        outs
        + [
            (hidden, BF), (width, BF), (width, BF), (hidden, BF), (width, F32),
            (width, BF), (width, BF), ("whole", width, LANES, F32),
        ],
        place,
        scratch=[pltpu.VMEM((block, hidden), F32), pltpu.VMEM((LANES, width), F32)],
        flops=2 * tokens * width * (4 * hidden + 2 * width),
    )
    got_out = send_back(h3[-1])

    ra = Reduction(tall_grad(act, dbf, place, core_wide), X_FIRST)
    sent_a = ra.send()
    rb = Reduction(
        weight_grads(
            [(h2b, dpre, 0), (cross_ob, dbc, 4)], [mid_sums], place, wide, core_side, sent_a
        ),
        Y_FIRST,
    )
    sent_b = rb.send()
    ra.take()
    sent_a = ra.send()

    def step(*reductions):
        for r in reductions:
            r.take()
        return sum((r.send() for r in reductions), ())

    dcq, dck, dcv = attention_back(
        cross_q, cross_k, cross_v, dco, cross_o, cross_lse, False, 2,
        [lambda: sent_a + sent_b, lambda: step(rb)],
    )
    sent = step(ra, rb)
    dr1, dba, dso, low_sums = token_call(
        before_self_kernel, block, (dcq, dr2, n1, i1), (cross_q_w, norm1_gain, self_out_w),
        [(width, F32), (width, BF), (width, BF), ("whole", width, LANES, F32)], place,
        scratch=[pltpu.VMEM((LANES, width), F32)],
        flops=4 * tokens * width * width, after=sent,
    )
    rc = Reduction(
        weight_grads(
            [(h1b, dcq, 0), (x_enc, dck, None), (x_enc, dcv, 1), (self_ob, dba, 2)],
            [low_sums], place, wide, core_side,
        ),
        Y_FIRST,
    )
    sent_c = rc.send()
    enc_kept, enc_sent = input_grad([dck, dcv], cross_kv_w)
    got_enc = send_back(enc_sent)
    out_first = (got_out,) if swapped else ()
    dsq, dsk, dsv = attention_back(
        self_q, self_k, self_v, dso, self_o, self_lse, True, 2,
        [lambda: step(ra, rb) + sent_c + out_first, lambda: step(ra, rb, rc)],
    )
    sent = step(ra, rb, rc)
    rd = Reduction(
        weight_grads(
            [(x_in, dsq, 0), (x_in, dsk, None), (x_in, dsv, 1)], [], place, wide, core_wide, sent
        ),
        X_FIRST,
    )
    sent = rd.send()
    in_kept, in_sent = input_grad([dsq, dsk, dsv], self_qkv_w, dr1, sent)
    got_in = send_back(in_sent)
    while any(r.steps for r in (ra, rb, rc, rd)):
        step(ra, rb, rc, rd)
    layer_out = give(h3[0], got_out)
    encoded_grad = give(enc_kept, got_enc)
    target_grad = give(in_kept, got_in)
    grad_a, grad_b, grad_c, grad_d = (r.result() for r in (ra, rb, rc, rd))

    def matrix(x, first, count):
        return x[:, first * width : (first + count) * width].astype(F32)

    parts = hidden // width
    (
        ffn_in_b_grad, cross_out_b_grad, norm3_gain_grad, norm3_bias_grad, ffn_out_b_grad,
        norm2_gain_grad, norm2_bias_grad,
    ) = vectors_of(
        grad_b[:, -LANES:], [(0, parts), (parts, 1)] + [(MID_ROWS + i, 1) for i in range(5)]
    )
    cross_q_b_grad, cross_v_b_grad, self_out_b_grad, norm1_gain_grad, norm1_bias_grad = vectors_of(
        grad_c[:, -LANES:], [(0, 1), (1, 1), (2, 1), (LOW_ROWS, 1), (LOW_ROWS + 1, 1)]
    )
    self_q_b_grad, self_v_b_grad = vectors_of(grad_d[:, -LANES:], [(0, 1), (1, 1)])
    return (
        layer_out, target_grad, encoded_grad,
        matrix(grad_d, 0, 3), self_q_b_grad, self_v_b_grad,
        matrix(grad_c, 3, 1), self_out_b_grad, norm1_gain_grad, norm1_bias_grad,
        matrix(grad_c, 0, 1), cross_q_b_grad,
        matrix(grad_c, 1, 2), cross_v_b_grad,
        matrix(grad_b, parts, 1), cross_out_b_grad, norm2_gain_grad, norm2_bias_grad,
        matrix(grad_b, 0, parts), ffn_in_b_grad, grad_a.astype(F32), ffn_out_b_grad,
        norm3_gain_grad, norm3_bias_grad,
    )


def solution(mesh):
    wide, narrow = mesh.shape["wide"], mesh.shape["narrow"]
    core = 2 if narrow % 2 == 0 else 1
    side = 2 if narrow % (2 * core) == 0 else 1
    near = 2 if narrow % (2 * core * side) == 0 else 1
    devices = mesh.devices.reshape(wide, narrow // (near * side * core), near, side, core)
    split = Mesh(devices, ("wide",) + ROWS)
    token_spec = P(ROWS, "wide", None)
    in_specs = (token_spec, token_spec, P(ROWS, "wide"), token_spec) + (P(),) * 21
    matrix, vector = P("wide", None), P("wide")
    out_specs = (token_spec,) * 3 + (
        matrix, vector, vector, matrix, vector, vector, vector,
        matrix, vector, matrix, vector, matrix, vector, vector, vector,
        matrix, vector, matrix, vector, vector, vector,
    )
    return jax.shard_map(body, mesh=split, in_specs=in_specs, out_specs=out_specs, check_vma=False)
```

```python
import functools

import jax
import jax.numpy as jnp
from jax import lax
from jax.experimental import pallas as pl
from jax.experimental.pallas import tpu as pltpu
from jax.sharding import Mesh, PartitionSpec as P

HD = 64
LANES = 128
VMEM = 56 * 2**20
norm_epsilon = 1e-05
masked_score = -1e9
BF = jnp.bfloat16
F32 = jnp.float32

NN = (((1,), (0,)), ((), ()))
NT = (((1,), (1,)), ((), ()))
TN = (((0,), (0,)), ((), ()))


def dot(a, b, dims=NN):
    return lax.dot_general(a, b, dims, preferred_element_type=F32)


def segment_terms(seg):
    lane = jnp.arange(LANES) % HD
    same = seg[..., None] == lane
    query_terms = jnp.where((lane < 4) & ~same, masked_score, 0.0).astype(BF)
    key_terms = jnp.where(((lane < 4) & same) | ((lane >= 4) & (lane < 7)), 1.0, 0.0).astype(BF)
    return query_terms, key_terms


def head_lanes(shape, head):
    lane = lax.broadcasted_iota(jnp.int32, shape, 1)
    return (lane < HD) if head == 0 else (lane >= HD)


def causal_scores(scores, causal, first_query, block, query_axis):
    if causal == "block":
        queries = lax.broadcasted_iota(jnp.int32, (block, block), query_axis)
        keys = lax.broadcasted_iota(jnp.int32, (block, block), 1 - query_axis)
        count = scores.shape[1 - query_axis]
        before = lax.slice_in_dim(scores, 0, count - block, axis=1 - query_axis)
        corner = lax.slice_in_dim(scores, count - block, count, axis=1 - query_axis)
        corner = jnp.where(keys <= queries, corner, masked_score)
        if count == block:
            return corner
        return jnp.concatenate([before, corner], 1 - query_axis)
    if causal == "mask":
        queries = first_query + lax.broadcasted_iota(jnp.int32, scores.shape, query_axis)
        keys = lax.broadcasted_iota(jnp.int32, scores.shape, 1 - query_axis)
        return jnp.where(keys <= queries, scores, masked_score)
    return scores


def in_order(parts, shift, half_index):
    if len(parts) == 1:
        return parts[0]
    return jnp.where(shift == 0, parts[half_index], parts[1 - half_index])


def array_places(count, shift, swapped):
    if not swapped:
        return [(slice(0, count), slice(0, count))]
    half = count // 2
    return [
        (
            slice(part * half, (part + 1) * half),
            pl.ds(pl.multiple_of(lax.rem(part * half + shift, count), half), half),
        )
        for part in (0, 1)
    ]


def row_block(index, block, count, shift, swapped):
    if not swapped:
        return pl.ds(index * block, block)
    return pl.ds(pl.multiple_of(lax.rem(index * block + shift, count), block), block)


def forward_kernel(*refs, parts, skipped, causal, block, swapped):
    scalars, refs = refs[0], refs[1:]
    q_parts, k_parts, v_parts = refs[:parts], refs[parts : 2 * parts], refs[2 * parts : 3 * parts]
    qt_ref, kt_ref = refs[3 * parts : 3 * parts + 2]
    o_ref, qx_ref, ka, va, qa = refs[3 * parts + 2 + skipped :]
    tq, ts = qa.shape[1], ka.shape[1]
    shift = scalars[0]
    for part, (here, there) in enumerate(array_places(ts, shift, swapped)):
        k = in_order([ref[...] for ref in k_parts], shift, part)
        v = in_order([ref[...] for ref in v_parts], shift, part)
        extra = kt_ref[there, :]
        for head in (0, 1):
            own = head_lanes(k.shape, head)
            ka[head, here, :] = jnp.where(own, k, extra)
            va[head, here, :] = jnp.where(own, v, extra)
    for part, (here, there) in enumerate(array_places(tq, shift, swapped)):
        q = in_order([ref[...] for ref in q_parts], shift, part)
        extra = qt_ref[there, :]
        for head in (0, 1):
            qa[head, here, :] = jnp.where(head_lanes(q.shape, head), q, extra)
    lane = lax.broadcasted_iota(jnp.int32, (block, LANES), 1)
    for index in range(tq // block):
        count = (index + 1) * block if causal == "block" else ts
        there = row_block(index, block, tq, shift, swapped)
        outs, extra = [], qt_ref[there, :].astype(F32)
        for head in (0, 1):
            scores = dot(qa[head, index * block : (index + 1) * block, :], ka[head, :count, :], NT)
            scores = causal_scores(scores, causal, shift + index * block, block, 0)
            top = jnp.max(scores, 1, keepdims=True)
            weights = jnp.exp(scores - top).astype(BF)
            sums = dot(weights, va[head, :count, :])
            at = HD + 4 if head == 0 else 4
            total = sums[:, at + 2 : at + 3]
            outs.append(sums / total)
            for i, piece in enumerate(three_parts(-(top + jnp.log(total)))):
                extra = jnp.where(lane == at + i, piece, extra)
        o_ref[there, :] = jnp.where(lane < HD, outs[0], outs[1]).astype(BF)
        qx_ref[there, :] = extra.astype(BF)


def three_parts(x):
    parts = []
    for _ in range(3):
        part = x.astype(BF).astype(F32)
        parts.append(part)
        x = x - part
    return parts


def backward_kernel(*refs, parts, skipped, causal, block, swapped, scaling):
    scalars, refs = refs[0], refs[1:]
    q_parts, k_parts, v_parts = refs[:parts], refs[parts : 2 * parts], refs[2 * parts : 3 * parts]
    g_ref, o_ref, qx_ref, kt_ref = refs[3 * parts : 3 * parts + 4]
    (
        dq_ref, dk_ref, dv_ref, ka, va, qa, ga, k_turned, dk_sum, dv_sum, dq_turned,
    ) = refs[3 * parts + 4 + skipped :]
    tq, ts = qa.shape[1], ka.shape[1]
    shift = scalars[0]
    for part, (here, there) in enumerate(array_places(ts, shift, swapped)):
        k = in_order([ref[...] for ref in k_parts], shift, part)
        v = in_order([ref[...] for ref in v_parts], shift, part)
        extra = kt_ref[there, :]
        for head in (0, 1):
            own = head_lanes(k.shape, head)
            ka[head, here, :] = jnp.where(own, k, extra)
            va[head, here, :] = jnp.where(own, v, extra)
        k_turned[:, here] = k.astype(F32).T.astype(BF)
    source = lax.broadcasted_iota(jnp.int32, (LANES, LANES), 0)
    target = lax.broadcasted_iota(jnp.int32, (LANES, LANES), 1)
    rides = (target % HD >= 4) & (target % HD < 7) & ((source < HD) == (target >= HD))
    spread = jnp.where(rides, -1.0, 0.0).astype(BF)
    for part, (here, there) in enumerate(array_places(tq, shift, swapped)):
        q = in_order([ref[...] for ref in q_parts], shift, part)
        g, extra = g_ref[there, :], qx_ref[there, :]
        products = g.astype(F32) * o_ref[there, :].astype(F32)
        rough = products.astype(BF)
        delta = dot(rough, spread) + dot((products - rough.astype(F32)).astype(BF), spread)
        lane = lax.broadcasted_iota(jnp.int32, q.shape, 1) % HD
        pieces = three_parts(delta)
        g_extra = jnp.where(lane == 4, pieces[0], jnp.where(lane == 5, pieces[1], pieces[2]))
        g_extra = g_extra.astype(BF)
        for head in (0, 1):
            own = head_lanes(q.shape, head)
            qa[head, here, :] = jnp.where(own, q, extra)
            ga[head, here, :] = jnp.where(own, g, g_extra)
    blocks = tq // block
    for index in reversed(range(blocks)):
        count = (index + 1) * block if causal == "block" else ts
        rows = slice(index * block, (index + 1) * block)
        for head in (0, 1):
            q, g = qa[head, rows, :], ga[head, rows, :]
            scores = dot(ka[head, :count, :], q, NT)
            scores = causal_scores(scores, causal, shift + index * block, block, 1)
            probs = jnp.exp(scores)
            grads = (probs * dot(va[head, :count, :], g, NT)).astype(BF)
            dv, dk = dot(probs.astype(BF), g), dot(grads, q)
            if index == blocks - 1:
                dv_sum[head, :count, :] = dv
                dk_sum[head, :count, :] = dk
            else:
                dv_sum[head, :count, :] += dv
                dk_sum[head, :count, :] += dk
            own_rows = slice(HD * head, HD * (head + 1))
            dq_turned[own_rows, rows] = dot(k_turned[own_rows, :count], grads)
        there = row_block(index, block, tq, shift, swapped)
        dq_ref[there, :] = dq_turned[:, rows].T.astype(BF) * jnp.asarray(scaling, BF)
    for here, there in array_places(ts, shift, swapped):
        own = head_lanes((here.stop - here.start, LANES), 0)
        dk_ref[there, :] = jnp.where(own, dk_sum[0, here, :], dk_sum[1, here, :]).astype(BF)
        dv_ref[there, :] = jnp.where(own, dv_sum[0, here, :], dv_sum[1, here, :]).astype(BF)


ANYWHERE = pl.BlockSpec(memory_space=pl.ANY)


def head_spec(count, start):
    return pl.BlockSpec((pl.Squeezed(), count, LANES), lambda row, pair, _: (row, 0, start + pair))


def shared_spec(count):
    return pl.BlockSpec((pl.Squeezed(), count, LANES), lambda row, pair, _: (row, 0, 0))


def part_specs(q, k, v, first):
    specs, arrays = [], []
    for parts, column in (q, k, v):
        for x in parts:
            specs.append(head_spec(x.shape[1], column // LANES + first))
            arrays.append(x)
    return specs, arrays


def attend(q, k, v, terms, shift, width, causal, block, swapped, after=()):
    specs, arrays = part_specs(q, k, v, 0)
    rows = arrays[0].shape[0]
    tq, ts = (sum(x.shape[1] for x in one[0]) for one in (q, k))
    pairs = width // LANES
    elements = rows * pairs * 2 * tq * ts
    return pl.pallas_call(
        functools.partial(
            forward_kernel, parts=len(q[0]), skipped=len(after), causal=causal, block=block,
            swapped=swapped,
        ),
        grid_spec=pltpu.PrefetchScalarGridSpec(
            num_scalar_prefetch=1,
            grid=(rows, pairs),
            in_specs=specs + [shared_spec(tq), shared_spec(ts)] + [ANYWHERE] * len(after),
            out_specs=[head_spec(tq, 0), head_spec(tq, 0)],
            scratch_shapes=[pltpu.VMEM((2, n, LANES), BF) for n in (ts, ts, tq)],
        ),
        out_shape=[jax.ShapeDtypeStruct((rows, tq, width), BF)] * 2,
        compiler_params=pltpu.CompilerParams(vmem_limit_bytes=VMEM),
        cost_estimate=pl.CostEstimate(
            flops=elements * 1600, bytes_accessed=rows * (tq + ts) * width * 4, transcendentals=0
        ),
    )(shift, *arrays, *terms, *after)


def attend_back(
    q, k, v, g, o, extra, terms, shift, first, pairs, causal, block, swapped, held=(), after=()
):
    specs, arrays = part_specs(q, k, v, first)
    rows, _, width = o.shape
    tq, ts = (sum(x.shape[1] for x in one[0]) for one in (q, k))
    elements = rows * pairs * 2 * tq * ts
    skipped = len(held) + len(after)
    count = len(arrays) + 4
    return pl.pallas_call(
        functools.partial(
            backward_kernel, parts=len(q[0]), skipped=skipped, causal=causal, block=block,
            swapped=swapped, scaling=HD**-0.5,
        ),
        grid_spec=pltpu.PrefetchScalarGridSpec(
            num_scalar_prefetch=1,
            grid=(rows, pairs),
            in_specs=specs
            + [head_spec(tq, first)] * 3
            + [shared_spec(ts)]
            + [ANYWHERE] * skipped,
            out_specs=[head_spec(tq, first), head_spec(ts, first), head_spec(ts, first)],
            scratch_shapes=[pltpu.VMEM((2, n, LANES), BF) for n in (ts, ts, tq, tq)]
            + [
                pltpu.VMEM((LANES, ts), BF),
                pltpu.VMEM((2, ts, LANES), F32),
                pltpu.VMEM((2, ts, LANES), F32),
                pltpu.VMEM((LANES, tq), F32),
            ],
        ),
        out_shape=[jax.ShapeDtypeStruct((rows, n, width), BF) for n in (tq, ts, ts)],
        input_output_aliases={1 + count + i: i for i in range(len(held))},
        compiler_params=pltpu.CompilerParams(vmem_limit_bytes=VMEM),
        cost_estimate=pl.CostEstimate(
            flops=elements * 2600, bytes_accessed=rows * (tq + ts) * pairs * 1024, transcendentals=0
        ),
    )(shift, *arrays, g, o, extra, terms[1], *held, *after)


def norm(resid):
    center = resid - jnp.mean(resid, -1, keepdims=True)
    inverse = lax.rsqrt(jnp.mean(center * center, -1, keepdims=True) + norm_epsilon)
    return center * inverse, inverse


def norm_back(upstream, normed, inverse, gain_vec):
    w = upstream * gain_vec
    return (
        w - jnp.mean(w, -1, keepdims=True) - normed * jnp.mean(w * normed, -1, keepdims=True)
    ) * inverse


def gelu_parts(pre):
    bell = jnp.exp(pre * pre * -0.5)
    t = 1.0 / (1.0 + jnp.abs(pre) * (0.3275911 * 0.5**0.5))
    poly = 0.5 * 1.061405429
    for c in (-1.453152027, 1.421413741, -0.284496736, 0.254829592):
        poly = poly * t + 0.5 * c
    tail = poly * t * bell
    phi_sum = jnp.where(pre >= 0, 1.0 - tail, tail)
    return pre * phi_sum, phi_sum + pre * (bell * 0.3989422804014327)


def add_rows(sums_ref, first, rows):
    for index, value in enumerate(rows):
        here = slice(first + index, first + index + 1)
        sums_ref[here, :] += jnp.sum(value.astype(F32), 0, keepdims=True)


def finish_rows(sums_ref, out_ref):
    @pl.when(pl.program_id(0) == pl.num_programs(0) - 1)
    def _():
        out_ref[...] = sums_ref[...].T


def clear(ref):
    @pl.when(pl.program_id(0) == 0)
    def _():
        ref[...] = jnp.zeros_like(ref)


def row(ref):
    return ref[...][None, :]


def project_kernel(x_ref, w_ref, b_ref, out_ref, *, scaled):
    width = b_ref.shape[0] // 3
    y = dot(x_ref[...], w_ref[...]) + row(b_ref)
    if scaled:
        out_ref[:, :width] = (y[:, :width] * HD**-0.5).astype(BF)
        out_ref[:, width:] = y[:, width:].astype(BF)
    else:
        out_ref[...] = y.astype(BF)


def after_self_kernel(
    o_ref, x_ref, w_ref, b_ref, gain_ref, bias_ref, qw_ref, qb_ref, n1_ref, i1_ref, h1b_ref, cq_ref,
):
    resid = x_ref[...].astype(F32) + (dot(o_ref[...], w_ref[...]) + row(b_ref))
    n1, i1 = norm(resid)
    h1b = (n1 * row(gain_ref) + row(bias_ref)).astype(BF)
    n1_ref[...] = n1
    i1_ref[...] = jnp.broadcast_to(i1, i1_ref.shape)
    h1b_ref[...] = h1b
    cq_ref[...] = ((dot(h1b, qw_ref[...]) + row(qb_ref)) * HD**-0.5).astype(BF)


def middle_kernel(
    o_ref, n1_ref, up_ref, g1_ref, s1_ref, ow_ref, ob_ref, g2_ref, s2_ref,
    w1_ref, b1_ref, w2_ref, b2_ref, g3_ref, s3_ref,
    *refs, chunk, kept_blocks,
):
    *outs, act_ref, dbf_ref, h2b_ref, dpre_ref, dr2_ref, dbc_ref, dco_ref, sums_ref, slope, sums = refs
    clear(sums)
    h1 = n1_ref[...] * row(g1_ref) + row(s1_ref)
    n2, i2 = norm(h1 + (dot(o_ref[...], ow_ref[...]) + row(ob_ref)))
    h2 = n2 * row(g2_ref) + row(s2_ref)
    h2b = h2.astype(BF)
    h2b_ref[...] = h2b
    hidden = w1_ref.shape[1]
    cols = [slice(c, c + chunk) for c in range(0, hidden, chunk)]
    bias1 = row(b1_ref)
    branch = row(b2_ref)
    for c in cols:
        pre = dot(h2b, w1_ref[:, c]) + bias1[:, c]
        value, slope_c = gelu_parts(pre)
        slope[:, c] = slope_c
        act_c = value.astype(BF)
        act_ref[:, c] = act_c
        branch = branch + dot(act_c, w2_ref[c, :])
    n3, i3 = norm(h2 + branch)
    out = (n3 * row(g3_ref) + row(s3_ref)).astype(BF)
    store_halves(outs, out, kept_blocks)
    up = up_ref[...].astype(F32)
    dr3 = norm_back(up, n3, i3, row(g3_ref))
    dbf = dr3.astype(BF)
    dbf_ref[...] = dbf
    dh2 = dr3
    for c in cols:
        dpre_c = (dot(dbf, w2_ref[c, :], NT) * slope[:, c]).astype(BF)
        dpre_ref[:, c] = dpre_c
        dh2 = dh2 + dot(dpre_c, w1_ref[:, c], NT)
    dr2 = norm_back(dh2, n2, i2, row(g2_ref))
    dbc = dr2.astype(BF)
    dr2_ref[...] = dr2
    dbc_ref[...] = dbc
    dco_ref[...] = dot(dbc, ow_ref[...], NT).astype(BF)
    add_rows(sums, MID_ROWS, (up * n3, up, dbf, dh2 * n2, dh2))
    finish_rows(sums, sums_ref)


def before_self_kernel(
    dcq_ref, dr2_ref, n1_ref, i1_ref, qw_ref, g1_ref, ow_ref, dr1_ref, dba_ref, dso_ref, sums_ref,
    sums,
):
    clear(sums)
    n1 = n1_ref[...]
    dh1 = dr2_ref[...] + dot(dcq_ref[...], qw_ref[...], NT)
    dr1 = norm_back(dh1, n1, i1_ref[:, 0:1], row(g1_ref))
    dba = dr1.astype(BF)
    dr1_ref[...] = dr1
    dba_ref[...] = dba
    dso_ref[...] = dot(dba, ow_ref[...], NT).astype(BF)
    add_rows(sums, LOW_ROWS, (dh1 * n1, dh1))
    finish_rows(sums, sums_ref)


def input_grad_kernel(*refs, count, start, kept_blocks):
    grads, w_ref, outs = refs[:count], refs[count + start], refs[count + start + 1 :]
    total = refs[count][...] if start else None
    width = grads[0].shape[-1]
    for index, ref in enumerate(grads):
        part = dot(ref[...], w_ref[:, index * width : (index + 1) * width], NT)
        total = part if total is None else total + part
    store_halves(outs, total, kept_blocks)


def store_halves(outs, value, kept_blocks):
    if kept_blocks is None:
        outs[0][...] = value.astype(outs[0].dtype)
        return
    step = pl.program_id(0)

    @pl.when(step < kept_blocks)
    def _():
        outs[0][...] = value.astype(outs[0].dtype)

    @pl.when(step >= kept_blocks)
    def _():
        outs[1][...] = value.astype(outs[1].dtype)


class Joined:
    def __init__(self, kept, got, use_kept):
        self.kept, self.got, self.use_kept = kept, got, use_kept

    def __getitem__(self, index):
        return jnp.where(self.use_kept, self.kept[index], self.got[index])


def token_call(kernel, block, blocked, whole, outs, place, scratch=(), flops=0, after=(), span=None):
    def length(x):
        return x.shape[0] if not isinstance(x, tuple) else x[0].shape[1] * (1 if x[1] is None else 2)

    tokens = length(blocked[0])
    half = tokens // block // 2
    first, count = span if span is not None else (0, tokens // block)
    in_specs, arrays, kinds = [], [], []
    for x in blocked:
        if not isinstance(x, tuple):
            in_specs.append(pl.BlockSpec((block, x.shape[1]), lambda i, _: (i + first, 0)))
            arrays.append(x)
            kinds.append(1)
            continue
        stack, got = x
        shape = (pl.Squeezed(), block, stack.shape[2])
        if got is None:
            in_specs.append(pl.BlockSpec(shape, lambda i, p: (p[0], i, 0)))
            arrays.append(stack)
            kinds.append(1)
        else:
            in_specs.append(pl.BlockSpec(shape, lambda i, p: (p[0], jnp.minimum(i, half - 1), 0)))
            in_specs.append(
                pl.BlockSpec(shape[1:], lambda i, p: (jnp.maximum(i - half, 0), 0))
            )
            arrays += [stack, got]
            kinds.append(2)
    for x in whole:
        zeros = (0,) * x.ndim
        in_specs.append(
            pl.BlockSpec(x.shape, lambda i, _, z=zeros: z, pipeline_mode=pl.Buffered(1))
        )
    in_specs += [ANYWHERE] * len(after)
    out_specs, out_shape = [], []
    for out in outs:
        if out[0] == "whole":
            out_specs.append(pl.BlockSpec(out[1:3], lambda i, _: (0, 0)))
            shape = out[1:3]
        elif out[0] == "kept":
            shape = (out[1], tokens // 2, out[2])
            out_specs.append(
                pl.BlockSpec(
                    (pl.Squeezed(), block, out[2]),
                    lambda i, p: (p[0], jnp.minimum(i, half - 1), 0),
                )
            )
        elif out[0] == "sent":
            shape = (tokens // 2, out[1])
            out_specs.append(
                pl.BlockSpec((block, out[1]), lambda i, _: (jnp.maximum(i - half, 0), 0))
            )
        else:
            shape = (count * block, out[0])
            out_specs.append(pl.BlockSpec((block, out[0]), lambda i, _: (i, 0)))
        out_shape.append(jax.ShapeDtypeStruct(shape, out[-1]))

    def run(_, *refs):
        used = []
        for kind in kinds:
            if kind == 1:
                used.append(refs[0])
            else:
                used.append(Joined(refs[0], refs[1], pl.program_id(0) < half))
            refs = refs[kind:]
        kernel(*used, *refs[: len(whole)], *refs[len(whole) + len(after) :])

    moved = sum(a.size * a.dtype.itemsize for a in (*arrays, *whole, *out_shape))
    return pl.pallas_call(
        run,
        grid_spec=pltpu.PrefetchScalarGridSpec(
            num_scalar_prefetch=1,
            grid=(count,),
            in_specs=in_specs,
            out_specs=out_specs,
            scratch_shapes=list(scratch),
        ),
        out_shape=out_shape,
        compiler_params=pltpu.CompilerParams(vmem_limit_bytes=VMEM),
        cost_estimate=pl.CostEstimate(
            flops=flops * count * block // tokens, bytes_accessed=moved, transcendentals=0
        ),
    )(place, *arrays, *whole, *after)


def store_kernel(_, got_ref, __, out_ref):
    out_ref[...] = got_ref[...].astype(out_ref.dtype)


def store_other(held, got, place):
    n, c = got.shape
    return pl.pallas_call(
        store_kernel,
        grid_spec=pltpu.PrefetchScalarGridSpec(
            num_scalar_prefetch=1,
            grid=(2,),
            in_specs=[pl.BlockSpec((n // 2, c), lambda i, _: (i, 0)), ANYWHERE],
            out_specs=pl.BlockSpec((pl.Squeezed(), n // 2, c), lambda i, p: (1 - p[0], i, 0)),
        ),
        out_shape=jax.ShapeDtypeStruct(held.shape, held.dtype),
        input_output_aliases={2: 0},
        cost_estimate=pl.CostEstimate(flops=0, bytes_accessed=n * c * 6, transcendentals=0),
    )(place, got, held)


MID_ROWS, LOW_ROWS = 8, 16


def weight_grads(items, extras, scalars, wide, order, after=()):
    first_left = items[0][0]
    m = (first_left[0] if isinstance(first_left, tuple) else first_left).shape[-1]
    block = min(item[3] for item in items)
    block = min(block, m)
    specs, arrays, steps = [], [], []
    known = {}
    for left, right, start, columns, sum_row in items:
        key = id(left)
        if key not in known:
            known[key] = (len(arrays), isinstance(left, tuple))
            if isinstance(left, tuple):
                stack, got = left
                specs.append(
                    pl.BlockSpec(
                        (pl.Squeezed(),) + stack.shape[1:], lambda j, p: (p[0], 0, 0),
                        pipeline_mode=pl.Buffered(1),
                    )
                )
                arrays.append(stack)
                left = got
            specs.append(
                pl.BlockSpec(left.shape, lambda j, p: (0, 0), pipeline_mode=pl.Buffered(1))
            )
            arrays.append(left)
        begin, blocks = len(steps), columns // block
        where = len(arrays)
        specs.append(
            pl.BlockSpec(
                (right.shape[0], block),
                lambda j, p, b=begin, n=blocks, f=start // block: (0, f + jnp.clip(j - b, 0, n - 1)),
            )
        )
        arrays.append(right)
        for index in range(blocks):
            steps.append((known[key], where, sum_row, start + index * block, right.shape[1]))
    for extra in extras:
        specs.append(
            pl.BlockSpec(extra.shape, lambda j, p: (0, 0), pipeline_mode=pl.Buffered(1))
        )
    slab = m // len(order)
    size = m // wide
    apart = len(order) > 1
    slabs = len(order) // 2

    def kernel(scalar_ref, *refs):
        ins, rest = refs[: len(arrays)], refs[len(arrays) :]
        extra_refs, (*outs, sums) = rest[: len(extras)], rest[len(extras) + len(after) :]
        clear(sums)
        step = pl.program_id(0)

        def store(value):
            if not apart:
                outs[0][...] = value.astype(BF)
                return
            core = scalar_ref[1]
            for to in range(slabs):
                halves = [
                    value[order[at] * slab : (order[at] + 1) * slab].astype(BF)
                    for at in (to, slabs + to)
                ]
                here = slice(to * slab, (to + 1) * slab)
                outs[0][here, :] = jnp.where(core == 0, halves[1], halves[0])
                outs[1][here, :] = jnp.where(core == 0, halves[0], halves[1])

        for index, ((left, split), right, sum_row, column, columns) in enumerate(steps):

            @pl.when(step == index)
            def _():
                grad = ins[right][...]
                if split:
                    half = ins[left].shape[0]
                    value = dot(ins[left][...], grad[:half], TN)
                    value = value + dot(ins[left + 1][...], grad[half:], TN)
                else:
                    value = dot(ins[left][...], grad, TN)
                store(value)
                if sum_row is None:
                    return
                total = jnp.sum(grad.astype(F32), 0, keepdims=True)
                if columns == m:
                    sums[sum_row : sum_row + 1, column : column + block] = total
                    return
                for piece in range(block // size):
                    w, k = divmod(column // size + piece, columns // m)
                    sums[sum_row + k : sum_row + k + 1, w * size : (w + 1) * size] = total[
                        :, piece * size : (piece + 1) * size
                    ]

        @pl.when(step == len(steps))
        def _():
            value = sums[...].T
            for ref in extra_refs:
                value = value + ref[...]
            store(jnp.concatenate([value, jnp.zeros((m, block - LANES), F32)], 1))

    n = block * len(steps) + LANES
    tokens = items[0][1].shape[0]
    rows = m // 2 if apart else m
    return pl.pallas_call(
        kernel,
        grid_spec=pltpu.PrefetchScalarGridSpec(
            num_scalar_prefetch=1,
            grid=(len(steps) + 1,),
            in_specs=specs + [ANYWHERE] * len(after),
            out_specs=[pl.BlockSpec((rows, block), lambda j, _: (0, j))] * (m // rows),
            scratch_shapes=[pltpu.VMEM((LANES, m), F32)],
        ),
        out_shape=[jax.ShapeDtypeStruct((rows, n), BF)] * (m // rows),
        compiler_params=pltpu.CompilerParams(vmem_limit_bytes=VMEM),
        cost_estimate=pl.CostEstimate(
            flops=2 * tokens * m * n,
            bytes_accessed=sum(a.size * 2 for a in arrays) + m * n * 2,
            transcendentals=0,
        ),
    )(scalars, *arrays, *extras, *after)


def tall_grad(left, right, scalars, order, after=()):
    tokens, rows = left.shape
    width = right.shape[1]
    apart = len(order) > 1
    blocks = len(order) if apart else 4
    size = rows // blocks
    half = blocks // 2

    def source(j, s):
        if not apart:
            return j
        to = jnp.where(s[1] == 0, (j + half) % blocks, j)
        block = 0
        for at, slab in enumerate(order):
            block = jnp.where(to == at, slab, block)
        return block

    def kernel(_, left_ref, right_ref, *refs):
        value = dot(left_ref[...], right_ref[...], TN).astype(BF)
        if not apart:
            refs[-1][...] = value
            return
        other, own = refs[-2:]

        @pl.when(pl.program_id(0) < half)
        def _():
            other[...] = value

        @pl.when(pl.program_id(0) >= half)
        def _():
            own[...] = value

    if apart:
        out_specs = [
            pl.BlockSpec((size, width), lambda j, _: (jnp.minimum(j, half - 1), 0)),
            pl.BlockSpec((size, width), lambda j, _: (jnp.maximum(j - half, 0), 0)),
        ]
        out_shape = [jax.ShapeDtypeStruct((rows // 2, width), BF)] * 2
    else:
        out_specs = [pl.BlockSpec((size, width), lambda j, _: (j, 0))]
        out_shape = [jax.ShapeDtypeStruct((rows, width), BF)]
    return pl.pallas_call(
        kernel,
        grid_spec=pltpu.PrefetchScalarGridSpec(
            num_scalar_prefetch=1,
            grid=(blocks,),
            in_specs=[
                pl.BlockSpec((tokens, size), lambda j, s: (0, source(j, s))),
                pl.BlockSpec(right.shape, lambda j, _: (0, 0), pipeline_mode=pl.Buffered(1)),
            ]
            + [ANYWHERE] * len(after),
            out_specs=out_specs,
        ),
        out_shape=out_shape,
        compiler_params=pltpu.CompilerParams(vmem_limit_bytes=VMEM),
        cost_estimate=pl.CostEstimate(
            flops=2 * tokens * rows * width,
            bytes_accessed=2 * (left.size + right.size + rows * width),
            transcendentals=0,
        ),
    )(scalars, left, right, *after)


def vector_rows(x, columns, outs):
    turned = x.astype(F32).T
    for (start, count), out in zip(columns, outs):
        rows = [turned[start + i] for i in range(count)]
        out[...] = rows[0] if count == 1 else jnp.concatenate(rows)


def vectors_kernel(x_ref, *outs, columns):
    vector_rows(x_ref[...], columns, outs)


def vectors_of(x, columns):
    return pl.pallas_call(
        functools.partial(vectors_kernel, columns=columns),
        out_shape=[jax.ShapeDtypeStruct((count * x.shape[0],), F32) for _, count in columns],
    )(x)


def widen_kernel(*refs, count, pieces, columns):
    ins, outs = refs[:count], refs[count:]
    vectors = outs[len(pieces) :]
    for out, parts in zip(outs, pieces):
        at = 0
        for which, start, size in parts:
            out[:, at : at + size] = ins[which][:, start : start + size].astype(F32)
            at += size
    extra = sum(ref[:, ref.shape[1] - LANES :].astype(F32) for ref in ins)
    vector_rows(extra, columns, vectors)


def widen(arrays, pieces, columns):
    rows = arrays[0].shape[0]
    return pl.pallas_call(
        functools.partial(widen_kernel, count=len(arrays), pieces=pieces, columns=columns),
        out_shape=[jax.ShapeDtypeStruct((rows, sum(p[2] for p in parts)), F32) for parts in pieces]
        + [jax.ShapeDtypeStruct((count * rows,), F32) for _, count in columns],
        compiler_params=pltpu.CompilerParams(vmem_limit_bytes=VMEM),
    )(*arrays)


def partner(x, axis, bit=1):
    count = lax.axis_size(axis)
    return lax.ppermute(x, axis, [(i, i ^ bit) for i in range(count)])


ROWS = ("far", "near", "side", "core")


def pick(x, index):
    half = x.shape[0] // 2
    return lax.dynamic_slice_in_dim(x, index * half, half, 0)


class Reduction:
    def __init__(self, arrays, order):
        self.split = len(arrays) == 2
        self.arrays = arrays
        self.steps = list(order) if self.split else []
        self.terms = []
        self.got = None

    def total(self, terms):
        return sum(t.astype(F32) for t in terms).astype(BF)

    def send(self):
        if not self.steps:
            return ()
        step = self.steps[0]
        if step == "gather":
            sent = self.total(self.terms)
            self.got = lax.all_gather(sent, ("core", "side", "near"), axis=0, tiled=True)
            return (sent,)
        if step == "core":
            sent = self.arrays[0]
        elif step == "far":
            sent = self.total(self.terms)
            assert lax.axis_size("far") <= 2
            if lax.axis_size("far") == 1:
                return ()
        else:
            sent = self.total([pick(t, 1 - lax.axis_index(step)) for t in self.terms])
        self.got = partner(sent, step)
        return (sent,)

    def take(self):
        if not self.steps:
            return
        step = self.steps.pop(0)
        if step == "gather":
            self.terms = [self.got]
        elif step == "core":
            self.terms = [self.arrays[1], self.got]
        elif step == "far":
            if lax.axis_size("far") == 2:
                self.terms.append(self.got)
        else:
            self.terms = [pick(t, lax.axis_index(step)) for t in self.terms] + [self.got]

    def result(self):
        assert not self.steps
        if self.split:
            return self.terms[0]
        x = lax.psum_scatter(self.arrays[0], "wide", scatter_dimension=0, tiled=True)
        return lax.psum(x, ROWS)


CORE_WIDE = (0, 2, 1, 3)
CORE_SIDE = (0, 4, 1, 5, 2, 6, 3, 7)
X_FIRST = ("core", "wide", "side", "near", "far", "gather")
Y_FIRST = ("core", "side", "wide", "near", "far", "gather")


def body(
    target, encoded, segments, out_grad,
    self_qkv_w, self_q_b, self_v_b, self_out_w, self_out_b, norm1_gain, norm1_bias,
    cross_q_w, cross_q_b, cross_kv_w, cross_v_b, cross_out_w, cross_out_b, norm2_gain, norm2_bias,
    ffn_in_w, ffn_in_b, ffn_out_w, ffn_out_b, norm3_gain, norm3_bias,
):
    row_count, tok_count, width = target.shape
    hidden = ffn_in_w.shape[1]
    parts = hidden // width
    wide = lax.axis_size("wide")
    index = lax.axis_index("wide").astype(jnp.int32)
    place = jnp.stack([index, lax.axis_index("core").astype(jnp.int32)])
    shift = (index * tok_count).reshape(1)
    swapped = wide == 2 and row_count == 2
    split = all(lax.axis_size(a) == 2 for a in ("wide", "side", "near", "core"))
    core_wide = CORE_WIDE if split else (0,)
    core_side = CORE_SIDE if split else (0,)
    tokens = row_count * tok_count
    block = min(256, tok_count)

    if swapped:
        def bring(x):
            sent = lax.dynamic_index_in_dim(x, 1 - index, 0, keepdims=False)
            return x, partner(sent, "wide")

        causal, block_f, block_b = "block", 2 * block, block
        seg_kept, seg_got = bring(segments)
        seg = jnp.concatenate(
            [lax.dynamic_index_in_dim(seg_kept, index, 0, keepdims=False), seg_got]
        )[None]
        key_seg = seg
        row_tokens = tokens
    else:
        def bring(x):
            return x.reshape(tokens, -1)

        causal, block_f, block_b = "mask", block, block
        seg = segments
        key_seg = lax.all_gather(segments, "wide", axis=1, tiled=True)
        row_tokens = tok_count
    kept_blocks = tok_count // block if swapped else None
    terms = (segment_terms(seg)[0], segment_terms(key_seg)[1])

    def by_row(x):
        return x.reshape(-1, row_tokens, x.shape[-1])

    def flat(x):
        return x.reshape(-1, x.shape[-1])

    def keys_of(x):
        return lax.all_gather(x, "wide", axis=1, tiled=True)

    def by_keys(x):
        return x.reshape(row_count, -1, width)

    def key_grads(x):
        return x if swapped else lax.psum_scatter(x, "wide", scatter_dimension=1, tiled=True)

    def project(x, w, bias, scaled, after=()):
        if not swapped:
            parts = [(x, None)]
        else:
            parts = [((x[0], None), None), (x[1], after)]
        outs = []
        for part, deps in parts:
            (out,) = token_call(
                functools.partial(project_kernel, scaled=scaled), block, (part,), (w, bias),
                [(w.shape[1], BF)], place, flops=2 * tokens * width * w.shape[1],
                after=deps or (),
            )
            outs.append(out[None] if swapped else by_row(out))
        return outs

    def attention(q, k, v, is_causal, after=()):
        return attend(
            q, k, v, terms, shift, width, causal if is_causal else "no", block_f, swapped, after
        )

    def attention_back(q, k, v, g, o, extra, is_causal, first, pairs, held, after):
        return attend_back(
            q, k, v, by_row(g), o, extra, terms, shift, first, pairs,
            causal if is_causal else "no", block_b, swapped, held, after,
        )

    def input_grad(grads, w, start=None, after=()):
        blocked = list(grads) + ([] if start is None else [start])
        outs = [("kept", 2, width, F32), ("sent", width, BF)] if swapped else [(width, F32)]
        kernel = functools.partial(
            input_grad_kernel, count=len(grads), start=0 if start is None else 1,
            kept_blocks=kept_blocks,
        )
        out = token_call(
            kernel, block, blocked, (w,), outs, place, flops=2 * tokens * width * w.shape[1],
            after=after,
        )
        return out[0], out[-1]

    def give(out, got):
        if not swapped:
            return out.reshape(row_count, tok_count, width)
        return store_other(out, got, place)

    def send_back(x):
        return partner(x, "wide") if swapped else None

    zeros = jnp.zeros_like(self_q_b)
    x_in = bring(target)
    x_enc = bring(encoded)
    qkv = project(x_in, self_qkv_w, jnp.concatenate([self_q_b, zeros, self_v_b]), True)
    if swapped:
        self_q, self_k, self_v = (qkv, 0), (qkv, width), (qkv, 2 * width)
    else:
        both = [keys_of(qkv[0][..., width:])]
        self_q, self_k, self_v = (qkv, 0), (both, 0), (both, width)
    self_o, self_x = attention(self_q, self_k, self_v, True)
    self_ob = flat(self_o)
    n1, i1, h1b, cq = token_call(
        after_self_kernel, block, (self_ob, x_in),
        (self_out_w, self_out_b, norm1_gain, norm1_bias, cross_q_w, cross_q_b),
        [(width, F32), (LANES, F32), (width, BF), (width, BF)], place,
        flops=4 * tokens * width * width,
    )
    ckv = project(
        x_enc, cross_kv_w, jnp.concatenate([zeros, cross_v_b]), False, (h1b,)
    )
    upstream = bring(out_grad)
    cross_q = ([by_row(cq)], 0)
    if swapped:
        half = row_tokens // 2
        cross_q = ([by_row(cq)[:, :half], by_row(cq)[:, half:]], 0)
        cross_k, cross_v = (ckv, 0), (ckv, width)
    else:
        both = [keys_of(ckv[0])]
        cross_k, cross_v = (both, 0), (both, width)
    cross_o, cross_x = attention(cross_q, cross_k, cross_v, False)
    cross_ob = flat(cross_o)
    outs = [("kept", 2, width, BF), ("sent", width, BF)] if swapped else [(width, BF)]
    *h3, act, dbf, h2b, dpre, dr2, dbc, dco, mid_sums = token_call(
        functools.partial(
            middle_kernel, chunk=width, kept_blocks=kept_blocks
        ),
        block, (cross_ob, n1, upstream),
        (
            norm1_gain, norm1_bias, cross_out_w, cross_out_b, norm2_gain, norm2_bias,
            ffn_in_w, ffn_in_b, ffn_out_w, ffn_out_b, norm3_gain, norm3_bias,
        ),
        outs
        + [
            (hidden, BF), (width, BF), (width, BF), (hidden, BF), (width, F32),
            (width, BF), (width, BF), ("whole", width, LANES, F32),
        ],
        place,
        scratch=[pltpu.VMEM((block, hidden), F32), pltpu.VMEM((LANES, width), F32)],
        flops=2 * tokens * width * (4 * hidden + 2 * width),
    )
    got_out = send_back(h3[-1])

    def step(*reductions):
        for r in reductions:
            r.take()
        return sum((r.send() for r in reductions), ())

    ra = Reduction(tall_grad(act, dbf, place, core_wide), X_FIRST)
    sent_a = ra.send()
    rb = Reduction(
        weight_grads(
            [(h2b, dpre, 0, hidden, 0), (cross_ob, dbc, 0, width, parts)], [mid_sums], place, wide,
            core_side, sent_a,
        ),
        Y_FIRST,
    )
    sent_b = rb.send()
    sent_a = step(ra)
    layer_out = give(h3[0], got_out)
    sent_b = step(rb)
    pairs = width // LANES
    dcq, dck, dcv = attention_back(
        cross_q, cross_k, cross_v, dco, cross_o, cross_x, False, 0, pairs, (),
        sent_a + sent_b + (layer_out,),
    )
    dcq, dck, dcv = flat(dcq), flat(key_grads(dck)), flat(key_grads(dcv))
    sent = step(ra, rb)
    rc = Reduction(
        weight_grads(
            [(h1b, dcq, 0, width, 0), (x_enc, dck, 0, width, None), (x_enc, dcv, 0, width, 1)],
            [], place, wide, core_side, sent,
        ),
        Y_FIRST,
    )
    sent_c = rc.send()
    dr1, dba, dso, low_sums = token_call(
        before_self_kernel, block, (dcq, dr2, n1, i1), (cross_q_w, norm1_gain, self_out_w),
        [(width, F32), (width, BF), (width, BF), ("whole", width, LANES, F32)], place,
        scratch=[pltpu.VMEM((LANES, width), F32)],
        flops=4 * tokens * width * width, after=sent_c,
    )
    sent = step(ra, rb, rc)
    enc_kept, enc_sent = input_grad([dck, dcv], cross_kv_w, None, sent)
    got_enc = send_back(enc_sent)
    sent = step(ra, rb)
    cut = pairs // 2
    first = attention_back(
        self_q, self_k, self_v, dso, self_o, self_x, True, 0, cut, (), sent,
    )
    sent = step(ra, rb, rc)
    if swapped:
        dsq, dsk, dsv = (flat(x) for x in first)
        rd = Reduction(
            weight_grads(
                [
                    (self_ob, dba, 0, width, 2),
                    (x_in, dsq, 0, cut * LANES, 0),
                    (x_in, dsk, 0, cut * LANES, None),
                    (x_in, dsv, 0, cut * LANES, 1),
                ],
                [low_sums], place, wide, core_wide, sent,
            ),
            X_FIRST,
        )
        sent = rd.send()
    encoded_grad = give(enc_kept, got_enc)
    second = attention_back(
        self_q, self_k, self_v, dso, self_o, self_x, True, cut, pairs - cut, first,
        sent + (encoded_grad,),
    )
    dsq, dsk, dsv = (flat(x) for x in second)
    if swapped:
        re = Reduction(
            weight_grads(
                [
                    (x_in, dsq, cut * LANES, width - cut * LANES, 0),
                    (x_in, dsk, cut * LANES, width - cut * LANES, None),
                    (x_in, dsv, cut * LANES, width - cut * LANES, 1),
                ],
                [], place, wide, core_wide, sent,
            ),
            X_FIRST,
        )
    else:
        dsk, dsv = (flat(key_grads(by_keys(x))) for x in (dsk, dsv))
        rd = Reduction(
            weight_grads([(self_ob, dba, 0, width, 2)], [low_sums], place, wide, core_wide), X_FIRST
        )
        re = Reduction(
            weight_grads(
                [(x_in, dsq, 0, width, 0), (x_in, dsk, 0, width, None), (x_in, dsv, 0, width, 1)],
                [], place, wide, core_wide,
            ),
            X_FIRST,
        )
    sent = re.send()
    sent += step(rd)
    sent += step(re)
    in_kept, in_sent = input_grad([dsq, dsk, dsv], self_qkv_w, dr1, sent)
    got_in = send_back(in_sent)
    everything = (ra, rb, rc, rd, re)
    while any(r.steps for r in everything):
        step(*everything)
    target_grad = give(in_kept, got_in)
    grad_a, grad_b, grad_c, grad_d, grad_e = (r.result() for r in everything)

    def matrix(x, first, count):
        return x[:, first * width : (first + count) * width].astype(F32)

    (
        ffn_in_b_grad, cross_out_b_grad, norm3_gain_grad, norm3_bias_grad, ffn_out_b_grad,
        norm2_gain_grad, norm2_bias_grad,
    ) = vectors_of(
        grad_b[:, -LANES:], [(0, parts), (parts, 1)] + [(MID_ROWS + i, 1) for i in range(5)]
    )
    cross_q_b_grad, cross_v_b_grad = vectors_of(grad_c[:, -LANES:], [(0, 1), (1, 1)])
    if swapped:
        one, two = cut * LANES, width - cut * LANES
        pieces = []
        for i in range(3):
            pieces += [(0, width + i * one, one), (1, i * two, two)]
    else:
        pieces = [(1, 0, 3 * width)]
    (
        self_out_w_grad, self_qkv_w_grad, self_q_b_grad, self_v_b_grad, self_out_b_grad,
        norm1_gain_grad, norm1_bias_grad,
    ) = widen(
        (grad_d, grad_e), ([(0, 0, width)], pieces),
        [(0, 1), (1, 1), (2, 1), (LOW_ROWS, 1), (LOW_ROWS + 1, 1)],
    )
    return (
        layer_out, target_grad, encoded_grad,
        self_qkv_w_grad, self_q_b_grad, self_v_b_grad,
        self_out_w_grad, self_out_b_grad, norm1_gain_grad, norm1_bias_grad,
        matrix(grad_c, 0, 1), cross_q_b_grad,
        matrix(grad_c, 1, 2), cross_v_b_grad,
        matrix(grad_b, parts, 1), cross_out_b_grad, norm2_gain_grad, norm2_bias_grad,
        matrix(grad_b, 0, parts), ffn_in_b_grad, grad_a.astype(F32), ffn_out_b_grad,
        norm3_gain_grad, norm3_bias_grad,
    )


def solution(mesh):
    wide, narrow = mesh.shape["wide"], mesh.shape["narrow"]
    core = 2 if narrow % 2 == 0 else 1
    side = 2 if narrow % (2 * core) == 0 else 1
    near = 2 if narrow % (2 * core * side) == 0 else 1
    devices = mesh.devices.reshape(wide, narrow // (near * side * core), near, side, core)
    split = Mesh(devices, ("wide",) + ROWS)
    token_spec = P(ROWS, "wide", None)
    in_specs = (token_spec, token_spec, P(ROWS, "wide"), token_spec) + (P(),) * 21
    matrix, vector = P("wide", None), P("wide")
    out_specs = (token_spec,) * 3 + (
        matrix, vector, vector, matrix, vector, vector, vector,
        matrix, vector, matrix, vector, matrix, vector, vector, vector,
        matrix, vector, matrix, vector, vector, vector,
    )
    return jax.shard_map(body, mesh=split, in_specs=in_specs, out_specs=out_specs, check_vma=False)
```

```python
import functools

import jax
import jax.numpy as jnp
from jax import lax
from jax.experimental import pallas as pl
from jax.experimental.pallas import tpu as pltpu
from jax.sharding import Mesh, PartitionSpec as P

HD = 64
LANES = 128
WIDE, CORE, SIDE, NEAR, SHIFT = range(5)
MB = 2**20
norm_epsilon = 1e-05
masked_score = -1e9
BF = jnp.bfloat16
F32 = jnp.float32

NN = (((1,), (0,)), ((), ()))
NT = (((1,), (1,)), ((), ()))
TN = (((0,), (0,)), ((), ()))


def dot(a, b, dims=NN):
    return lax.dot_general(a, b, dims, preferred_element_type=F32)


def segment_terms(seg):
    lane = jnp.arange(LANES) % HD
    same = seg[..., None] == lane
    query_terms = jnp.where((lane < 4) & ~same, masked_score, 0.0).astype(BF)
    key_terms = jnp.where(((lane < 4) & same) | ((lane >= 4) & (lane < 7)), 1.0, 0.0).astype(BF)
    return query_terms, key_terms


def head_lanes(shape, head):
    lane = lax.broadcasted_iota(jnp.int32, shape, 1)
    return (lane < HD) if head == 0 else (lane >= HD)


def causal_scores(scores, causal, first_query, block, query_axis):
    if causal == "block":
        queries = lax.broadcasted_iota(jnp.int32, (block, block), query_axis)
        keys = lax.broadcasted_iota(jnp.int32, (block, block), 1 - query_axis)
        count = scores.shape[1 - query_axis]
        before = lax.slice_in_dim(scores, 0, count - block, axis=1 - query_axis)
        corner = lax.slice_in_dim(scores, count - block, count, axis=1 - query_axis)
        corner = jnp.where(keys <= queries, corner, masked_score)
        if count == block:
            return corner
        return jnp.concatenate([before, corner], 1 - query_axis)
    if causal == "mask":
        queries = first_query + lax.broadcasted_iota(jnp.int32, scores.shape, query_axis)
        keys = lax.broadcasted_iota(jnp.int32, scores.shape, 1 - query_axis)
        return jnp.where(keys <= queries, scores, masked_score)
    return scores


def in_order(parts, shift, half, there):
    if len(parts) == 1:
        return parts[0][there, :]
    return jnp.where(shift == 0, parts[half][...], parts[1 - half][...])


def array_places(count, shift, swapped):
    if not swapped:
        return [(slice(0, count), slice(0, count))]
    half = count // 2
    return [
        (
            slice(part * half, (part + 1) * half),
            pl.ds(pl.multiple_of(lax.rem(part * half + shift, count), half), half),
        )
        for part in (0, 1)
    ]


def row_block(index, block, count, shift, swapped):
    if not swapped:
        return pl.ds(index * block, block)
    return pl.ds(pl.multiple_of(lax.rem(index * block + shift, count), block), block)


def split_parts(refs, counts):
    groups = []
    for count in counts:
        groups.append(refs[:count])
        refs = refs[count:]
    return groups, refs


def forward_kernel(*refs, counts, skipped, causal, block, swapped):
    scalars, refs = refs[0], refs[1:]
    (q_parts, k_parts, v_parts), refs = split_parts(refs, counts)
    qt_ref, kt_ref = refs[:2]
    o_ref, qx_ref, ka, va, qa = refs[2 + skipped :]
    tq, ts = qa.shape[1], ka.shape[1]
    shift = scalars[SHIFT]
    for part, (here, there) in enumerate(array_places(ts, shift, swapped)):
        k = in_order(k_parts, shift, part, there)
        v = in_order(v_parts, shift, part, there)
        extra = kt_ref[there, :]
        for head in (0, 1):
            own = head_lanes(k.shape, head)
            ka[head, here, :] = jnp.where(own, k, extra)
            va[head, here, :] = jnp.where(own, v, extra)
    for part, (here, there) in enumerate(array_places(tq, shift, swapped)):
        q = in_order(q_parts, shift, part, there)
        extra = qt_ref[there, :]
        for head in (0, 1):
            qa[head, here, :] = jnp.where(head_lanes(q.shape, head), q, extra)
    lane = lax.broadcasted_iota(jnp.int32, (block, LANES), 1)
    for index in range(tq // block):
        count = (index + 1) * block if causal == "block" else ts
        there = row_block(index, block, tq, shift, swapped)
        outs, extra = [], qt_ref[there, :].astype(F32)
        for head in (0, 1):
            scores = dot(qa[head, index * block : (index + 1) * block, :], ka[head, :count, :], NT)
            scores = causal_scores(scores, causal, shift + index * block, block, 0)
            top = jnp.max(scores, 1, keepdims=True)
            weights = jnp.exp(scores - top).astype(BF)
            sums = dot(weights, va[head, :count, :])
            at = HD + 4 if head == 0 else 4
            total = sums[:, at + 2 : at + 3]
            outs.append(sums / total)
            for i, piece in enumerate(three_parts(-(top + jnp.log(total)))):
                extra = jnp.where(lane == at + i, piece, extra)
        o_ref[there, :] = jnp.where(lane < HD, outs[0], outs[1]).astype(BF)
        qx_ref[there, :] = extra.astype(BF)


def three_parts(x):
    parts = []
    for _ in range(3):
        part = x.astype(BF).astype(F32)
        parts.append(part)
        x = x - part
    return parts


def backward_kernel(*refs, counts, skipped, causal, block, swapped, scaling):
    scalars, refs = refs[0], refs[1:]
    (q_parts, k_parts, v_parts), refs = split_parts(refs, counts)
    g_ref, o_ref, qx_ref, kt_ref = refs[:4]
    (
        dq_ref, dk_ref, dv_ref, ka, va, qa, ga, k_turned, dk_sum, dv_sum, dq_turned,
    ) = refs[4 + skipped :]
    tq, ts = qa.shape[1], ka.shape[1]
    shift = scalars[SHIFT]
    for part, (here, there) in enumerate(array_places(ts, shift, swapped)):
        k = in_order(k_parts, shift, part, there)
        v = in_order(v_parts, shift, part, there)
        extra = kt_ref[there, :]
        for head in (0, 1):
            own = head_lanes(k.shape, head)
            ka[head, here, :] = jnp.where(own, k, extra)
            va[head, here, :] = jnp.where(own, v, extra)
        k_turned[:, here] = k.astype(F32).T.astype(BF)
    source = lax.broadcasted_iota(jnp.int32, (LANES, LANES), 0)
    target = lax.broadcasted_iota(jnp.int32, (LANES, LANES), 1)
    rides = (target % HD >= 4) & (target % HD < 7) & ((source < HD) == (target >= HD))
    spread = jnp.where(rides, -1.0, 0.0).astype(BF)
    for part, (here, there) in enumerate(array_places(tq, shift, swapped)):
        q = in_order(q_parts, shift, part, there)
        g, extra = g_ref[there, :], qx_ref[there, :]
        products = g.astype(F32) * o_ref[there, :].astype(F32)
        rough = products.astype(BF)
        delta = dot(rough, spread) + dot((products - rough.astype(F32)).astype(BF), spread)
        lane = lax.broadcasted_iota(jnp.int32, q.shape, 1) % HD
        pieces = three_parts(delta)
        g_extra = jnp.where(lane == 4, pieces[0], jnp.where(lane == 5, pieces[1], pieces[2]))
        g_extra = g_extra.astype(BF)
        for head in (0, 1):
            own = head_lanes(q.shape, head)
            qa[head, here, :] = jnp.where(own, q, extra)
            ga[head, here, :] = jnp.where(own, g, g_extra)
    blocks = tq // block
    for index in reversed(range(blocks)):
        count = (index + 1) * block if causal == "block" else ts
        rows = slice(index * block, (index + 1) * block)
        for head in (0, 1):
            q, g = qa[head, rows, :], ga[head, rows, :]
            scores = dot(ka[head, :count, :], q, NT)
            scores = causal_scores(scores, causal, shift + index * block, block, 1)
            probs = jnp.exp(scores)
            grads = (probs * dot(va[head, :count, :], g, NT)).astype(BF)
            dv, dk = dot(probs.astype(BF), g), dot(grads, q)
            if index == blocks - 1:
                dv_sum[head, :count, :] = dv
                dk_sum[head, :count, :] = dk
            else:
                dv_sum[head, :count, :] += dv
                dk_sum[head, :count, :] += dk
            own_rows = slice(HD * head, HD * (head + 1))
            dq_turned[own_rows, rows] = dot(k_turned[own_rows, :count], grads)
        there = row_block(index, block, tq, shift, swapped)
        dq_ref[there, :] = dq_turned[:, rows].T.astype(BF) * jnp.asarray(scaling, BF)
    for here, there in array_places(ts, shift, swapped):
        own = head_lanes((here.stop - here.start, LANES), 0)
        dk_ref[there, :] = jnp.where(own, dk_sum[0, here, :], dk_sum[1, here, :]).astype(BF)
        dv_ref[there, :] = jnp.where(own, dv_sum[0, here, :], dv_sum[1, here, :]).astype(BF)


ANYWHERE = pl.BlockSpec(memory_space=pl.ANY)


def head_spec(count, start):
    return pl.BlockSpec((pl.Squeezed(), count, LANES), lambda row, pair, _: (row, 0, start + pair))


def shared_spec(count):
    return pl.BlockSpec((pl.Squeezed(), count, LANES), lambda row, pair, _: (row, 0, 0))


def part_specs(q, k, v, first):
    specs, arrays = [], []
    for parts, column in (q, k, v):
        for x in parts:
            specs.append(head_spec(x.shape[1], column // LANES + first))
            arrays.append(x)
    return specs, arrays


def attend(q, k, v, terms, scalars, width, causal, block, swapped, after=()):
    specs, arrays = part_specs(q, k, v, 0)
    rows = arrays[0].shape[0]
    tq, ts = (sum(x.shape[1] for x in one[0]) for one in (q, k))
    pairs = width // LANES
    elements = rows * pairs * 2 * tq * ts
    return pl.pallas_call(
        functools.partial(
            forward_kernel, counts=[len(x[0]) for x in (q, k, v)], skipped=len(after), causal=causal, block=block,
            swapped=swapped,
        ),
        grid_spec=pltpu.PrefetchScalarGridSpec(
            num_scalar_prefetch=1,
            grid=(rows, pairs),
            in_specs=specs + [shared_spec(tq), shared_spec(ts)] + [ANYWHERE] * len(after),
            out_specs=[head_spec(tq, 0), head_spec(tq, 0)],
            scratch_shapes=[pltpu.VMEM((2, n, LANES), BF) for n in (ts, ts, tq)],
        ),
        out_shape=[jax.ShapeDtypeStruct((rows, tq, width), BF)] * 2,
        compiler_params=pltpu.CompilerParams(vmem_limit_bytes=12 * MB),
        cost_estimate=pl.CostEstimate(
            flops=elements * 1600, bytes_accessed=rows * (tq + ts) * width * 4, transcendentals=0
        ),
    )(scalars, *arrays, *terms, *after)


def attend_back(
    q, k, v, g, o, extra, terms, scalars, first, pairs, causal, block, swapped, held=(), after=()
):
    specs, arrays = part_specs(q, k, v, first)
    rows, _, width = o.shape
    tq, ts = (sum(x.shape[1] for x in one[0]) for one in (q, k))
    elements = rows * pairs * 2 * tq * ts
    skipped = len(held) + len(after)
    count = len(arrays) + 4
    return pl.pallas_call(
        functools.partial(
            backward_kernel, counts=[len(x[0]) for x in (q, k, v)], skipped=skipped, causal=causal, block=block,
            swapped=swapped, scaling=HD**-0.5,
        ),
        grid_spec=pltpu.PrefetchScalarGridSpec(
            num_scalar_prefetch=1,
            grid=(rows, pairs),
            in_specs=specs
            + [head_spec(tq, first)] * 3
            + [shared_spec(ts)]
            + [ANYWHERE] * skipped,
            out_specs=[head_spec(tq, first), head_spec(ts, first), head_spec(ts, first)],
            scratch_shapes=[pltpu.VMEM((2, n, LANES), BF) for n in (ts, ts, tq, tq)]
            + [
                pltpu.VMEM((LANES, ts), BF),
                pltpu.VMEM((2, ts, LANES), F32),
                pltpu.VMEM((2, ts, LANES), F32),
                pltpu.VMEM((LANES, tq), F32),
            ],
        ),
        out_shape=[jax.ShapeDtypeStruct((rows, n, width), BF) for n in (tq, ts, ts)],
        input_output_aliases={1 + count + i: i for i in range(len(held))},
        compiler_params=pltpu.CompilerParams(vmem_limit_bytes=16 * MB),
        cost_estimate=pl.CostEstimate(
            flops=elements * 2600, bytes_accessed=rows * (tq + ts) * pairs * 1024, transcendentals=0
        ),
    )(scalars, *arrays, g, o, extra, terms[1], *held, *after)


def norm(resid):
    center = resid - jnp.mean(resid, -1, keepdims=True)
    inverse = lax.rsqrt(jnp.mean(center * center, -1, keepdims=True) + norm_epsilon)
    return center * inverse, inverse


def norm_back(upstream, normed, inverse, gain_vec):
    w = upstream * gain_vec
    return (
        w - jnp.mean(w, -1, keepdims=True) - normed * jnp.mean(w * normed, -1, keepdims=True)
    ) * inverse


def gelu_parts(pre):
    bell = jnp.exp(pre * pre * -0.5)
    t = 1.0 / (1.0 + jnp.abs(pre) * (0.3275911 * 0.5**0.5))
    poly = 0.5 * 1.061405429
    for c in (-1.453152027, 1.421413741, -0.284496736, 0.254829592):
        poly = poly * t + 0.5 * c
    tail = poly * t * bell
    phi_sum = jnp.where(pre >= 0, 1.0 - tail, tail)
    return pre * phi_sum, phi_sum + pre * (bell * 0.3989422804014327)


def add_rows(sums_ref, first, rows):
    for index, value in enumerate(rows):
        here = slice(first + index, first + index + 1)
        sums_ref[here, :] += jnp.sum(value.astype(F32), 0, keepdims=True)


def finish_rows(sums_ref, out_ref):
    @pl.when(pl.program_id(0) == pl.num_programs(0) - 1)
    def _():
        out_ref[...] = sums_ref[...].T


def clear(ref):
    @pl.when(pl.program_id(0) == 0)
    def _():
        ref[...] = jnp.zeros_like(ref)


def row(ref):
    return ref[...][None, :]


def project_kernel(x_ref, w_ref, b_ref, out_ref, *, scaled):
    width = b_ref.shape[0] // 3
    y = dot(x_ref[...], w_ref[...]) + row(b_ref)
    if scaled:
        out_ref[:, :width] = (y[:, :width] * HD**-0.5).astype(BF)
        out_ref[:, width:] = y[:, width:].astype(BF)
    else:
        out_ref[...] = y.astype(BF)


def after_self_kernel(
    o_ref, x_ref, w_ref, b_ref, gain_ref, bias_ref, qw_ref, qb_ref, n1_ref, i1_ref, h1b_ref, cq_ref,
):
    resid = x_ref[...].astype(F32) + (dot(o_ref[...], w_ref[...]) + row(b_ref))
    n1, i1 = norm(resid)
    h1b = (n1 * row(gain_ref) + row(bias_ref)).astype(BF)
    n1_ref[...] = n1
    i1_ref[...] = jnp.broadcast_to(i1, i1_ref.shape)
    h1b_ref[...] = h1b
    cq_ref[...] = ((dot(h1b, qw_ref[...]) + row(qb_ref)) * HD**-0.5).astype(BF)


def middle_kernel(
    o_ref, n1_ref, up_ref, g1_ref, s1_ref, ow_ref, ob_ref, g2_ref, s2_ref,
    w1_ref, b1_ref, w2_ref, b2_ref, g3_ref, s3_ref,
    *refs, chunk, kept_blocks,
):
    *outs, act_ref, dbf_ref, h2b_ref, dpre_ref, dr2_ref, dbc_ref, dco_ref, sums_ref, slope, sums = refs
    clear(sums)
    h1 = n1_ref[...] * row(g1_ref) + row(s1_ref)
    n2, i2 = norm(h1 + (dot(o_ref[...], ow_ref[...]) + row(ob_ref)))
    h2 = n2 * row(g2_ref) + row(s2_ref)
    h2b = h2.astype(BF)
    h2b_ref[...] = h2b
    hidden = w1_ref.shape[1]
    cols = [slice(c, c + chunk) for c in range(0, hidden, chunk)]
    bias1 = row(b1_ref)
    branch = row(b2_ref)
    for c in cols:
        pre = dot(h2b, w1_ref[:, c]) + bias1[:, c]
        value, slope_c = gelu_parts(pre)
        slope[:, c] = slope_c
        act_c = value.astype(BF)
        act_ref[:, c] = act_c
        branch = branch + dot(act_c, w2_ref[c, :])
    n3, i3 = norm(h2 + branch)
    out = (n3 * row(g3_ref) + row(s3_ref)).astype(BF)
    store_halves(outs, out, kept_blocks)
    up = up_ref[...].astype(F32)
    dr3 = norm_back(up, n3, i3, row(g3_ref))
    dbf = dr3.astype(BF)
    dbf_ref[...] = dbf
    dh2 = dr3
    for c in cols:
        dpre_c = (dot(dbf, w2_ref[c, :], NT) * slope[:, c]).astype(BF)
        dpre_ref[:, c] = dpre_c
        dh2 = dh2 + dot(dpre_c, w1_ref[:, c], NT)
    dr2 = norm_back(dh2, n2, i2, row(g2_ref))
    dbc = dr2.astype(BF)
    dr2_ref[...] = dr2
    dbc_ref[...] = dbc
    dco_ref[...] = dot(dbc, ow_ref[...], NT).astype(BF)
    add_rows(sums, MID_ROWS, (up * n3, up, dbf, dh2 * n2, dh2))
    finish_rows(sums, sums_ref)


def before_self_kernel(
    dcq_ref, dr2_ref, n1_ref, i1_ref, qw_ref, g1_ref, ow_ref, dr1_ref, dba_ref, dso_ref, sums_ref,
    sums,
):
    clear(sums)
    n1 = n1_ref[...]
    dh1 = dr2_ref[...] + dot(dcq_ref[...], qw_ref[...], NT)
    dr1 = norm_back(dh1, n1, i1_ref[:, 0:1], row(g1_ref))
    dba = dr1.astype(BF)
    dr1_ref[...] = dr1
    dba_ref[...] = dba
    dso_ref[...] = dot(dba, ow_ref[...], NT).astype(BF)
    add_rows(sums, LOW_ROWS, (dh1 * n1, dh1))
    finish_rows(sums, sums_ref)


def input_grad_kernel(*refs, count, start, kept_blocks):
    grads, w_ref, outs = refs[:count], refs[count + start], refs[count + start + 1 :]
    total = refs[count][...] if start else None
    width = grads[0].shape[-1]
    for index, ref in enumerate(grads):
        part = dot(ref[...], w_ref[:, index * width : (index + 1) * width], NT)
        total = part if total is None else total + part
    store_halves(outs, total, kept_blocks)


def store_halves(outs, value, kept_blocks):
    if kept_blocks is None:
        outs[0][...] = value.astype(outs[0].dtype)
        return
    step = pl.program_id(0)

    @pl.when(step < kept_blocks)
    def _():
        outs[0][...] = value.astype(outs[0].dtype)

    @pl.when(step >= kept_blocks)
    def _():
        outs[1][...] = value.astype(outs[1].dtype)


class Joined:
    def __init__(self, kept, got, use_kept):
        self.kept, self.got, self.use_kept = kept, got, use_kept

    def __getitem__(self, index):
        return jnp.where(self.use_kept, self.kept[index], self.got[index])


def token_call(kernel, block, blocked, whole, outs, scalars, scratch=(), flops=0, after=(),
    vmem=16,
):
    def length(x):
        return x.shape[0] if not isinstance(x, tuple) else x[0].shape[1] * (1 if x[1] is None else 2)

    tokens = length(blocked[0])
    half = tokens // block // 2
    count = tokens // block
    in_specs, arrays, kinds = [], [], []
    for x in blocked:
        if not isinstance(x, tuple):
            in_specs.append(pl.BlockSpec((block, x.shape[1]), lambda i, _: (i, 0)))
            arrays.append(x)
            kinds.append(1)
            continue
        stack, got = x
        shape = (pl.Squeezed(), block, stack.shape[2])
        if got is None:
            in_specs.append(pl.BlockSpec(shape, lambda i, p: (p[0], i, 0)))
            arrays.append(stack)
            kinds.append(1)
        else:
            in_specs.append(pl.BlockSpec(shape, lambda i, p: (p[0], jnp.minimum(i, half - 1), 0)))
            in_specs.append(
                pl.BlockSpec(shape[1:], lambda i, p: (jnp.maximum(i - half, 0), 0))
            )
            arrays += [stack, got]
            kinds.append(2)
    for x in whole:
        zeros = (0,) * x.ndim
        in_specs.append(
            pl.BlockSpec(x.shape, lambda i, _, z=zeros: z, pipeline_mode=pl.Buffered(1))
        )
    in_specs += [ANYWHERE] * len(after)
    out_specs, out_shape = [], []
    for out in outs:
        if out[0] == "whole":
            out_specs.append(pl.BlockSpec(out[1:3], lambda i, _: (0, 0)))
            shape = out[1:3]
        elif out[0] == "kept":
            shape = (out[1], tokens // 2, out[2])
            out_specs.append(
                pl.BlockSpec(
                    (pl.Squeezed(), block, out[2]),
                    lambda i, p: (p[0], jnp.minimum(i, half - 1), 0),
                )
            )
        elif out[0] == "sent":
            shape = (tokens // 2, out[1])
            out_specs.append(
                pl.BlockSpec((block, out[1]), lambda i, _: (jnp.maximum(i - half, 0), 0))
            )
        else:
            shape = (count * block, out[0])
            out_specs.append(pl.BlockSpec((block, out[0]), lambda i, _: (i, 0)))
        out_shape.append(jax.ShapeDtypeStruct(shape, out[-1]))

    def run(_, *refs):
        used = []
        for kind in kinds:
            if kind == 1:
                used.append(refs[0])
            else:
                used.append(Joined(refs[0], refs[1], pl.program_id(0) < half))
            refs = refs[kind:]
        kernel(*used, *refs[: len(whole)], *refs[len(whole) + len(after) :])

    moved = sum(a.size * a.dtype.itemsize for a in (*arrays, *whole, *out_shape))
    return pl.pallas_call(
        run,
        grid_spec=pltpu.PrefetchScalarGridSpec(
            num_scalar_prefetch=1,
            grid=(count,),
            in_specs=in_specs,
            out_specs=out_specs,
            scratch_shapes=list(scratch),
        ),
        out_shape=out_shape,
        compiler_params=pltpu.CompilerParams(vmem_limit_bytes=vmem * MB),
        cost_estimate=pl.CostEstimate(
            flops=flops, bytes_accessed=moved, transcendentals=0
        ),
    )(scalars, *arrays, *whole, *after)


def store_kernel(_, got_ref, *refs):
    refs[-1][...] = got_ref[...].astype(refs[-1].dtype)


def store_other(held, got, scalars, after=()):
    n, c = got.shape
    return pl.pallas_call(
        store_kernel,
        grid_spec=pltpu.PrefetchScalarGridSpec(
            num_scalar_prefetch=1,
            grid=(2,),
            in_specs=[pl.BlockSpec((n // 2, c), lambda i, _: (i, 0))] + [ANYWHERE] * (1 + len(after)),
            out_specs=pl.BlockSpec((pl.Squeezed(), n // 2, c), lambda i, p: (1 - p[0], i, 0)),
        ),
        out_shape=jax.ShapeDtypeStruct(held.shape, held.dtype),
        input_output_aliases={2: 0},
        cost_estimate=pl.CostEstimate(flops=0, bytes_accessed=n * c * 6, transcendentals=0),
    )(scalars, got, held, *after)


MID_ROWS, LOW_ROWS = 8, 16


def weight_grads(items, extras, scalars, wide, order, after=()):
    first_left = items[0][0]
    m = (first_left[0] if isinstance(first_left, tuple) else first_left).shape[-1]
    block = min(item[3] for item in items)
    block = min(block, m)
    specs, arrays, steps = [], [], []
    known = {}
    for left, right, start, columns, sum_row in items:
        key = id(left)
        if key not in known:
            known[key] = (len(arrays), isinstance(left, tuple))
            if isinstance(left, tuple):
                stack, got = left
                specs.append(
                    pl.BlockSpec(
                        (pl.Squeezed(),) + stack.shape[1:], lambda j, p: (p[0], 0, 0),
                        pipeline_mode=pl.Buffered(1),
                    )
                )
                arrays.append(stack)
                left = got
            specs.append(
                pl.BlockSpec(left.shape, lambda j, p: (0, 0), pipeline_mode=pl.Buffered(1))
            )
            arrays.append(left)
        begin, blocks = len(steps), columns // block
        where = len(arrays)
        specs.append(
            pl.BlockSpec(
                (right.shape[0], block),
                lambda j, p, b=begin, n=blocks, f=start // block: (0, f + jnp.clip(j - b, 0, n - 1)),
            )
        )
        arrays.append(right)
        for index in range(blocks):
            steps.append((known[key], where, sum_row, start + index * block, right.shape[1]))
    for extra in extras:
        specs.append(
            pl.BlockSpec(extra.shape, lambda j, p: (0, 0), pipeline_mode=pl.Buffered(1))
        )
    slab = m // len(order)
    size = m // wide
    apart = len(order) > 1
    slabs = len(order) // 2

    def kernel(scalar_ref, *refs):
        ins, rest = refs[: len(arrays)], refs[len(arrays) :]
        extra_refs, (*outs, sums) = rest[: len(extras)], rest[len(extras) + len(after) :]
        clear(sums)
        step = pl.program_id(0)

        def store(value):
            if not apart:
                outs[0][...] = value.astype(BF)
                return
            core = scalar_ref[CORE]
            for to in range(slabs):
                halves = [
                    value[order[at] * slab : (order[at] + 1) * slab].astype(BF)
                    for at in (to, slabs + to)
                ]
                here = slice(to * slab, (to + 1) * slab)
                outs[0][here, :] = jnp.where(core == 0, halves[1], halves[0])
                outs[1][here, :] = jnp.where(core == 0, halves[0], halves[1])

        for index, ((left, split), right, sum_row, column, columns) in enumerate(steps):

            @pl.when(step == index)
            def _():
                grad = ins[right][...]
                if split:
                    half = ins[left].shape[0]
                    value = dot(ins[left][...], grad[:half], TN)
                    value = value + dot(ins[left + 1][...], grad[half:], TN)
                else:
                    value = dot(ins[left][...], grad, TN)
                store(value)
                if sum_row is None:
                    return
                total = jnp.sum(grad.astype(F32), 0, keepdims=True)
                if columns == m:
                    sums[sum_row : sum_row + 1, column : column + block] = total
                    return
                for piece in range(block // size):
                    w, k = divmod(column // size + piece, columns // m)
                    sums[sum_row + k : sum_row + k + 1, w * size : (w + 1) * size] = total[
                        :, piece * size : (piece + 1) * size
                    ]

        @pl.when(step == len(steps))
        def _():
            value = sums[...].T
            for ref in extra_refs:
                value = value + ref[...]
            store(jnp.concatenate([value, jnp.zeros((m, block - LANES), F32)], 1))

    n = block * len(steps) + LANES
    tokens = items[0][1].shape[0]
    rows = m // 2 if apart else m
    return pl.pallas_call(
        kernel,
        grid_spec=pltpu.PrefetchScalarGridSpec(
            num_scalar_prefetch=1,
            grid=(len(steps) + 1,),
            in_specs=specs + [ANYWHERE] * len(after),
            out_specs=[pl.BlockSpec((rows, block), lambda j, _: (0, j))] * (m // rows),
            scratch_shapes=[pltpu.VMEM((LANES, m), F32)],
        ),
        out_shape=[jax.ShapeDtypeStruct((rows, n), BF)] * (m // rows),
        compiler_params=pltpu.CompilerParams(vmem_limit_bytes=16 * MB),
        cost_estimate=pl.CostEstimate(
            flops=2 * tokens * m * n,
            bytes_accessed=sum(a.size * 2 for a in arrays) + m * n * 2,
            transcendentals=0,
        ),
    )(scalars, *arrays, *extras, *after)


def tall_grad(left, right, scalars, order, after=()):
    tokens, rows = left.shape
    width = right.shape[1]
    apart = len(order) > 1
    blocks = len(order) if apart else 4
    size = rows // blocks
    half = blocks // 2

    def source(j, s):
        if not apart:
            return j
        to = jnp.where(s[CORE] == 0, (j + half) % blocks, j)
        block = 0
        for at, slab in enumerate(order):
            block = jnp.where(to == at, slab, block)
        return block

    def kernel(_, left_ref, right_ref, *refs):
        value = dot(left_ref[...], right_ref[...], TN).astype(BF)
        if not apart:
            refs[-1][...] = value
            return
        other, own = refs[-2:]

        @pl.when(pl.program_id(0) < half)
        def _():
            other[...] = value

        @pl.when(pl.program_id(0) >= half)
        def _():
            own[...] = value

    if apart:
        out_specs = [
            pl.BlockSpec((size, width), lambda j, _: (jnp.minimum(j, half - 1), 0)),
            pl.BlockSpec((size, width), lambda j, _: (jnp.maximum(j - half, 0), 0)),
        ]
        out_shape = [jax.ShapeDtypeStruct((rows // 2, width), BF)] * 2
    else:
        out_specs = [pl.BlockSpec((size, width), lambda j, _: (j, 0))]
        out_shape = [jax.ShapeDtypeStruct((rows, width), BF)]
    return pl.pallas_call(
        kernel,
        grid_spec=pltpu.PrefetchScalarGridSpec(
            num_scalar_prefetch=1,
            grid=(blocks,),
            in_specs=[
                pl.BlockSpec((tokens, size), lambda j, s: (0, source(j, s))),
                pl.BlockSpec(right.shape, lambda j, _: (0, 0), pipeline_mode=pl.Buffered(1)),
            ]
            + [ANYWHERE] * len(after),
            out_specs=out_specs,
        ),
        out_shape=out_shape,
        compiler_params=pltpu.CompilerParams(vmem_limit_bytes=12 * MB),
        cost_estimate=pl.CostEstimate(
            flops=2 * tokens * rows * width,
            bytes_accessed=2 * (left.size + right.size + rows * width),
            transcendentals=0,
        ),
    )(scalars, left, right, *after)


def vector_rows(x, columns, outs):
    turned = x.astype(F32).T
    for (start, count), out in zip(columns, outs):
        rows = [turned[start + i] for i in range(count)]
        out[...] = rows[0] if count == 1 else jnp.concatenate(rows)


def widen(pairs, pieces, columns, scalars, after=()):
    half = pairs[0][0].shape[0]
    flat_pairs = [x for pair in pairs for x in pair]

    def kernel(scalar_ref, *refs):
        ins = refs[: len(flat_pairs)]
        outs = refs[len(flat_pairs) + len(after) :]
        matrices, vectors = outs[: len(pieces)], outs[len(pieces) :]
        core = scalar_ref[CORE]
        step = pl.program_id(0)

        def rows(which, here, start, size):
            mine, other = ins[2 * which], ins[2 * which + 1]
            cols = slice(start, start + size)
            return jnp.where(core == here, mine[:, cols], other[:, cols])

        for out, parts in zip(matrices, pieces):
            at = 0
            for which, start, size in parts:
                out[:, at : at + size] = rows(which, step, start, size).astype(F32)
                at += size
        if columns:

            @pl.when(step == 1)
            def _():
                halves = [
                    sum(
                        rows(which, here, x.shape[1] - LANES, LANES).astype(F32)
                        for which, (x, _) in enumerate(pairs)
                    )
                    for here in (0, 1)
                ]
                vector_rows(jnp.concatenate(halves, 0), columns, vectors)

    widths = [sum(p[2] for p in parts) for parts in pieces]
    lengths = [count * 2 * half for _, count in columns]
    return pl.pallas_call(
        kernel,
        grid_spec=pltpu.PrefetchScalarGridSpec(
            num_scalar_prefetch=1,
            grid=(2,),
            in_specs=[
                pl.BlockSpec(x.shape, lambda i, _: (0, 0), pipeline_mode=pl.Buffered(1))
                for x in flat_pairs
            ]
            + [ANYWHERE] * len(after),
            out_specs=[pl.BlockSpec((half, w), lambda i, _: (i, 0)) for w in widths]
            + [pl.BlockSpec((n,), lambda i, _: (0,)) for n in lengths],
        ),
        out_shape=[jax.ShapeDtypeStruct((2 * half, w), F32) for w in widths]
        + [jax.ShapeDtypeStruct((n,), F32) for n in lengths],
        compiler_params=pltpu.CompilerParams(vmem_limit_bytes=24 * MB),
        cost_estimate=pl.CostEstimate(
            flops=0, bytes_accessed=half * sum(widths) * 12, transcendentals=0
        ),
    )(scalars, *flat_pairs, *after)


def vectors_kernel(x_ref, *outs, columns):
    vector_rows(x_ref[...], columns, outs)


def vectors_of(x, columns):
    return pl.pallas_call(
        functools.partial(vectors_kernel, columns=columns),
        out_shape=[jax.ShapeDtypeStruct((count * x.shape[0],), F32) for _, count in columns],
    )(x)


def partner(x, axis, bit=1):
    count = lax.axis_size(axis)
    return lax.ppermute(x, axis, [(i, i ^ bit) for i in range(count)])


def partner_both(x):
    return lax.ppermute(x, ("near", "side"), [(i, 3 - i) for i in range(4)])


ROWS = ("far", "near", "side", "core")


def merge(jobs, scalars, after):
    sizes = [terms[0][0].shape[0] >> len(terms[0][1]) for terms in jobs]
    steps = next(g for g in (4, 3, 2, 1) if all(n % (16 * g) == 0 for n in sizes))
    specs, arrays = [], []
    for terms, n in zip(jobs, sizes):
        for x, path in terms:
            assert x.shape[0] == n << len(path)

            def place(i, s, path=path):
                index = 0
                for scalar, flipped in path:
                    index = 2 * index + (1 - s[scalar] if flipped else s[scalar])
                return (index * steps + i, 0)

            specs.append(pl.BlockSpec((n // steps, x.shape[1]), place))
            arrays.append(x)

    def kernel(_, *refs):
        outs = refs[len(arrays) + len(after) :]
        at = 0
        for terms, out in zip(jobs, outs):
            total = refs[at][...].astype(F32)
            for ref in refs[at + 1 : at + len(terms)]:
                total = total + ref[...].astype(F32)
            at += len(terms)
            out[...] = total.astype(BF)

    shapes = [(n, terms[0][0].shape[1]) for terms, n in zip(jobs, sizes)]
    return pl.pallas_call(
        kernel,
        grid_spec=pltpu.PrefetchScalarGridSpec(
            num_scalar_prefetch=1,
            grid=(steps,),
            in_specs=specs + [ANYWHERE] * len(after),
            out_specs=[pl.BlockSpec((n // steps, c), lambda i, _: (i, 0)) for n, c in shapes],
        ),
        out_shape=[jax.ShapeDtypeStruct(shape, BF) for shape in shapes],
        compiler_params=pltpu.CompilerParams(vmem_limit_bytes=16 * MB),
        cost_estimate=pl.CostEstimate(
            flops=0,
            bytes_accessed=sum(2 * n * c * (1 + len(t)) for (n, c), t in zip(shapes, jobs)),
            transcendentals=0,
        ),
    )(scalars, *arrays, *after)


def line_up(jobs, scalars, after):
    arrays = [x for pieces in jobs for x in pieces]

    def kernel(s, *refs):
        outs = refs[len(arrays) + len(after) :]
        step = pl.program_id(0)
        side, near = step // 2, step % 2
        which = 2 * (side != s[SIDE]).astype(jnp.int32) + (near != s[NEAR]).astype(jnp.int32)
        for index in range(4):

            @pl.when(which == index)
            def _():
                for job, out in enumerate(outs):
                    out[...] = refs[4 * job + index][...]

    return pl.pallas_call(
        kernel,
        grid_spec=pltpu.PrefetchScalarGridSpec(
            num_scalar_prefetch=1,
            grid=(4,),
            in_specs=[
                pl.BlockSpec(x.shape, lambda i, _: (0, 0), pipeline_mode=pl.Buffered(1))
                for x in arrays
            ]
            + [ANYWHERE] * len(after),
            out_specs=[pl.BlockSpec(p[0].shape, lambda i, _: (i, 0)) for p in jobs],
        ),
        out_shape=[
            jax.ShapeDtypeStruct((4 * p[0].shape[0], p[0].shape[1]), BF) for p in jobs
        ],
        compiler_params=pltpu.CompilerParams(vmem_limit_bytes=16 * MB),
        cost_estimate=pl.CostEstimate(
            flops=0, bytes_accessed=sum(x.size * 4 for x in arrays), transcendentals=0
        ),
    )(scalars, *arrays, *after)


AXES = {"wide": WIDE, "side": SIDE, "near": NEAR}


class Reduction:
    def __init__(self, arrays, order):
        self.split = len(arrays) == 2
        self.arrays = arrays
        self.steps = list(order) if self.split else []
        self.terms = []
        if self.split:
            self.got = partner(arrays[0], "core")
            self.terms = [(arrays[1], ()), (self.got, ())]
            self.waits = ()

    def result(self):
        x = lax.psum_scatter(self.arrays[0], "wide", scatter_dimension=0, tiled=True)
        return lax.psum(x, ROWS)


def advance(reductions, scalars, after):
    sums, joins = [], []
    for r in reductions:
        step = r.steps[0]
        if step == "join":
            joins.append(r)
        else:
            path = ((AXES[step], True),) if step in AXES else ()
            sums.append((r, [(x, p + path) for x, p in r.terms]))
    last = after
    if sums:
        outs = merge([terms for _, terms in sums], scalars, last)
        last = (outs[0],)
        for (r, _), sent in zip(sums, outs):
            step = r.steps.pop(0)
            if step == "spread":
                near = partner(sent, "near")
                side = partner(sent, "side")
                both = partner_both(sent)
                r.pieces = [sent, near, side, both]
                continue
            if step in AXES:
                r.terms = [(x, p + ((AXES[step], False),)) for x, p in r.terms]
            if step != "far" or lax.axis_size("far") == 2:
                r.terms.append((partner(sent, step), ()))
    if joins:
        outs = line_up([r.pieces for r in joins], scalars, last)
        last = (outs[0],)
        for r, mine in zip(joins, outs):
            r.steps.pop(0)
            r.pair = (mine, partner(mine, "core"))
    return last


CORE_WIDE = (0, 2, 1, 3)
CORE_SIDE = (0, 4, 1, 5, 2, 6, 3, 7)
X_FIRST = ("wide", "side", "near", "far", "spread", "join")
Y_FIRST = ("side", "wide", "near", "far", "spread", "join")


def body(
    target, encoded, segments, out_grad,
    self_qkv_w, self_q_b, self_v_b, self_out_w, self_out_b, norm1_gain, norm1_bias,
    cross_q_w, cross_q_b, cross_kv_w, cross_v_b, cross_out_w, cross_out_b, norm2_gain, norm2_bias,
    ffn_in_w, ffn_in_b, ffn_out_w, ffn_out_b, norm3_gain, norm3_bias,
):
    row_count, tok_count, width = target.shape
    hidden = ffn_in_w.shape[1]
    parts = hidden // width
    pairs = width // LANES
    wide = lax.axis_size("wide")
    index = lax.axis_index("wide").astype(jnp.int32)
    scalars = jnp.stack(
        [index]
        + [lax.axis_index(a).astype(jnp.int32) for a in ("core", "side", "near")]
        + [index * tok_count]
    )
    swapped = wide == 2 and row_count == 2
    split = swapped and all(lax.axis_size(a) == 2 for a in ("side", "near", "core"))
    core_wide = CORE_WIDE if split else (0,)
    core_side = CORE_SIDE if split else (0,)
    tokens = row_count * tok_count
    block = min(256, tok_count)
    kept_blocks = tok_count // block if swapped else None

    last = ()

    def run(call, *args, **kwargs):
        nonlocal last
        out = call(*args, after=last, **kwargs)
        last = (out[0] if isinstance(out, (tuple, list)) else out,)
        return out

    if swapped:
        def bring(x):
            sent = lax.dynamic_index_in_dim(x, 1 - index, 0, keepdims=False)
            return x, partner(sent, "wide")

        causal, block_f, block_b = "block", 2 * block, block
        seg_kept, seg_got = bring(segments)
        seg = jnp.concatenate(
            [lax.dynamic_index_in_dim(seg_kept, index, 0, keepdims=False), seg_got]
        )[None]
        key_seg = seg
        row_tokens = tokens
    else:
        def bring(x):
            return x.reshape(tokens, -1)

        causal, block_f, block_b = "mask", block, block
        seg = segments
        key_seg = lax.all_gather(segments, "wide", axis=1, tiled=True)
        row_tokens = tok_count
    terms = (segment_terms(seg)[0], segment_terms(key_seg)[1])

    def by_row(x):
        return x.reshape(-1, row_tokens, x.shape[-1])

    def flat(x):
        return x.reshape(-1, x.shape[-1])

    def keys_of(x):
        return lax.all_gather(x, "wide", axis=1, tiled=True)

    def key_grads(x):
        return x if swapped else lax.psum_scatter(x, "wide", scatter_dimension=1, tiled=True)

    def project(x, w, bias, scaled):
        (out,) = run(
            token_call, functools.partial(project_kernel, scaled=scaled), block, (x,), (w, bias),
            [(w.shape[1], BF)], scalars, flops=2 * tokens * width * w.shape[1],
        )
        return out[None] if swapped else by_row(out)

    def attention(q, k, v, is_causal):
        return run(
            attend, q, k, v, terms, scalars, width, causal if is_causal else "no", block_f, swapped
        )

    def attention_back(q, k, v, g, o, extra, is_causal, first, count, held=()):
        return run(
            attend_back, q, k, v, by_row(g), o, extra, terms, scalars, first, count,
            causal if is_causal else "no", block_b, swapped, held,
        )

    def input_grad(grads, w, start=None):
        blocked = list(grads) + ([] if start is None else [start])
        outs = [("kept", 2, width, F32), ("sent", width, BF)] if swapped else [(width, F32)]
        kernel = functools.partial(
            input_grad_kernel, count=len(grads), start=0 if start is None else 1,
            kept_blocks=kept_blocks,
        )
        out = run(
            token_call, kernel, block, blocked, (w,), outs, scalars,
            flops=2 * tokens * width * w.shape[1],
        )
        return out[0], out[-1]

    def send_back(x):
        return partner(x, "wide") if swapped else None

    def give(out, got):
        if not swapped:
            return out.reshape(row_count, tok_count, width)
        return run(store_other, out, got, scalars)

    def exchange(*reductions):
        nonlocal last
        if split:
            last = advance(reductions, scalars, last)

    zeros = jnp.zeros_like(self_q_b)
    qkv_bias = jnp.concatenate([self_q_b, zeros, self_v_b])
    ckv_bias = jnp.concatenate([zeros, cross_v_b])
    x_in = bring(target)
    x_enc = bring(encoded)
    upstream = bring(out_grad)
    if swapped:
        ckv = [project((x_enc[0], None), cross_kv_w, ckv_bias, False)]
        qkv = [project((x_in[0], None), self_qkv_w, qkv_bias, True)]
        qkv.append(project(x_in[1], self_qkv_w, qkv_bias, True))
        self_q, self_k, self_v = (qkv, 0), (qkv, width), (qkv, 2 * width)
    else:
        ckv = [keys_of(project(x_enc, cross_kv_w, ckv_bias, False))]
        qkv = [project(x_in, self_qkv_w, qkv_bias, True)]
        both = [keys_of(qkv[0][..., width:])]
        self_q, self_k, self_v = (qkv, 0), (both, 0), (both, width)
    self_o, self_x = attention(self_q, self_k, self_v, True)
    self_ob = flat(self_o)
    n1, i1, h1b, cq = run(
        token_call, after_self_kernel, block, (self_ob, x_in),
        (self_out_w, self_out_b, norm1_gain, norm1_bias, cross_q_w, cross_q_b),
        [(width, F32), (LANES, F32), (width, BF), (width, BF)], scalars,
        flops=4 * tokens * width * width,
    )
    if swapped:
        ckv.append(project(x_enc[1], cross_kv_w, ckv_bias, False))
    cross_q, cross_k, cross_v = ([by_row(cq)], 0), (ckv, 0), (ckv, width)
    cross_o, cross_x = attention(cross_q, cross_k, cross_v, False)
    cross_ob = flat(cross_o)
    outs = [("kept", 2, width, BF), ("sent", width, BF)] if swapped else [(width, BF)]
    *h3, act, dbf, h2b, dpre, dr2, dbc, dco, mid_sums = run(
        token_call, functools.partial(middle_kernel, chunk=width, kept_blocks=kept_blocks),
        block, (cross_ob, n1, upstream),
        (
            norm1_gain, norm1_bias, cross_out_w, cross_out_b, norm2_gain, norm2_bias,
            ffn_in_w, ffn_in_b, ffn_out_w, ffn_out_b, norm3_gain, norm3_bias,
        ),
        outs
        + [
            (hidden, BF), (width, BF), (width, BF), (hidden, BF), (width, F32),
            (width, BF), (width, BF), ("whole", width, LANES, F32),
        ],
        scalars,
        scratch=[pltpu.VMEM((block, hidden), F32), pltpu.VMEM((LANES, width), F32)],
        flops=2 * tokens * width * (4 * hidden + 2 * width),
        vmem=40,
    )
    got_out = send_back(h3[-1])

    ra = Reduction(run(tall_grad, act, dbf, scalars, core_wide), X_FIRST)
    rb = Reduction(
        run(
            weight_grads, [(h2b, dpre, 0, hidden, 0), (cross_ob, dbc, 0, width, parts)],
            [mid_sums], scalars, wide, core_side,
        ),
        Y_FIRST,
    )
    layer_out = give(h3[0], got_out)
    exchange(ra, rb)
    dcq, dck, dcv = attention_back(
        cross_q, cross_k, cross_v, dco, cross_o, cross_x, False, 0, pairs
    )
    dcq, dck, dcv = flat(dcq), flat(key_grads(dck)), flat(key_grads(dcv))
    exchange(ra, rb)
    rc = Reduction(
        run(
            weight_grads,
            [(h1b, dcq, 0, width, 0), (x_enc, dck, 0, width, None), (x_enc, dcv, 0, width, 1)],
            [], scalars, wide, core_side,
        ),
        Y_FIRST,
    )
    dr1, dba, dso, low_sums = run(
        token_call, before_self_kernel, block, (dcq, dr2, n1, i1),
        (cross_q_w, norm1_gain, self_out_w),
        [(width, F32), (width, BF), (width, BF), ("whole", width, LANES, F32)], scalars,
        scratch=[pltpu.VMEM((LANES, width), F32)],
        flops=4 * tokens * width * width,
    )
    exchange(ra, rb, rc)
    enc_kept, enc_sent = input_grad([dck, dcv], cross_kv_w)
    got_enc = send_back(enc_sent)
    exchange(ra, rb)
    cut = pairs // 2
    first = attention_back(
        self_q, self_k, self_v, dso, self_o, self_x, True, 0, cut if swapped else pairs
    )
    dsq, dsk, dsv = (flat(x) for x in first)
    exchange(ra, rb, rc)
    if swapped:
        one, two = cut * LANES, width - cut * LANES
        rd = Reduction(
            run(
                weight_grads,
                [
                    (self_ob, dba, 0, width, 2),
                    (x_in, dsq, 0, one, 0), (x_in, dsk, 0, one, None), (x_in, dsv, 0, one, 1),
                ],
                [low_sums], scalars, wide, core_wide,
            ),
            X_FIRST,
        )
        encoded_grad = give(enc_kept, got_enc)
        exchange(rd, rc)
        second = attention_back(
            self_q, self_k, self_v, dso, self_o, self_x, True, cut, pairs - cut, first
        )
        dsq, dsk, dsv = (flat(x) for x in second)
        exchange(ra, rb, rc, rd)
        re = Reduction(
            run(
                weight_grads,
                [(x_in, dsq, one, two, 0), (x_in, dsk, one, two, None), (x_in, dsv, one, two, 1)],
                [], scalars, wide, core_wide,
            ),
            X_FIRST,
        )
        exchange(rd, re)
    else:
        encoded_grad = give(enc_kept, got_enc)
        dsk, dsv = (
            flat(key_grads(x.reshape(row_count, -1, width))) for x in (dsk, dsv)
        )
        rd = Reduction(
            run(
                weight_grads, [(self_ob, dba, 0, width, 2)], [low_sums], scalars, wide, core_wide
            ),
            X_FIRST,
        )
        re = Reduction(
            run(
                weight_grads,
                [(x_in, dsq, 0, width, 0), (x_in, dsk, 0, width, None), (x_in, dsv, 0, width, 1)],
                [], scalars, wide, core_wide,
            ),
            X_FIRST,
        )
    in_kept, in_sent = input_grad([dsq, dsk, dsv], self_qkv_w, dr1)
    got_in = send_back(in_sent)

    vectors_b = [(0, parts), (parts, 1)] + [(MID_ROWS + i, 1) for i in range(5)]
    vectors_c = [(0, 1), (1, 1)]
    vectors_d = [(0, 1), (1, 1), (2, 1), (LOW_ROWS, 1), (LOW_ROWS + 1, 1)]
    pieces_b = [[(0, 0, hidden)], [(0, hidden, width)]]
    pieces_c = [[(0, 0, width)], [(0, width, 2 * width)]]
    if split:
        exchange(re, rd, rc)
        (ffn_out_w_grad,) = run(widen, [ra.pair], [[(0, 0, width)]], [], scalars)
        out_b = run(widen, [rb.pair], pieces_b, vectors_b, scalars)
        exchange(re, rd, rc)
        target_grad = give(in_kept, got_in)
        exchange(re, rd)
        out_c = run(widen, [rc.pair], pieces_c, vectors_c, scalars)
        exchange(re)
        exchange(re)
        pieces_d = [[(0, 0, width)], []]
        for i in range(3):
            pieces_d[1] += [(0, width + i * one, one), (1, i * two, two)]
        out_d = run(widen, [rd.pair, re.pair], pieces_d, vectors_d, scalars)
    else:
        target_grad = give(in_kept, got_in)

        def columns_of(x, pieces, vectors):
            return [
                jnp.concatenate([x[:, start : start + size] for _, start, size in p], 1).astype(F32)
                for p in pieces
            ] + list(vectors_of(x[:, -LANES:], vectors))

        ffn_out_w_grad = ra.result().astype(F32)
        out_b = columns_of(rb.result(), pieces_b, vectors_b)
        out_c = columns_of(rc.result(), pieces_c, vectors_c)
        low = rd.result()
        high = re.result()
        both = jnp.concatenate(
            [low[:, :width], high[:, : 3 * width], low[:, -LANES:] + high[:, -LANES:]], 1
        )
        out_d = columns_of(both, [[(0, 0, width)], [(0, width, 3 * width)]], vectors_d)
    (
        ffn_in_w_grad, cross_out_w_grad, ffn_in_b_grad, cross_out_b_grad, norm3_gain_grad,
        norm3_bias_grad, ffn_out_b_grad, norm2_gain_grad, norm2_bias_grad,
    ) = out_b
    cross_q_w_grad, cross_kv_w_grad, cross_q_b_grad, cross_v_b_grad = out_c
    (
        self_out_w_grad, self_qkv_w_grad, self_q_b_grad, self_v_b_grad, self_out_b_grad,
        norm1_gain_grad, norm1_bias_grad,
    ) = out_d
    return (
        layer_out, target_grad, encoded_grad,
        self_qkv_w_grad, self_q_b_grad, self_v_b_grad,
        self_out_w_grad, self_out_b_grad, norm1_gain_grad, norm1_bias_grad,
        cross_q_w_grad, cross_q_b_grad, cross_kv_w_grad, cross_v_b_grad,
        cross_out_w_grad, cross_out_b_grad, norm2_gain_grad, norm2_bias_grad,
        ffn_in_w_grad, ffn_in_b_grad, ffn_out_w_grad, ffn_out_b_grad,
        norm3_gain_grad, norm3_bias_grad,
    )


def solution(mesh):
    wide, narrow = mesh.shape["wide"], mesh.shape["narrow"]
    core = 2 if narrow % 2 == 0 else 1
    side = 2 if narrow % (2 * core) == 0 else 1
    near = 2 if narrow % (2 * core * side) == 0 else 1
    devices = mesh.devices.reshape(wide, narrow // (near * side * core), near, side, core)
    split = Mesh(devices, ("wide",) + ROWS)
    token_spec = P(ROWS, "wide", None)
    in_specs = (token_spec, token_spec, P(ROWS, "wide"), token_spec) + (P(),) * 21
    matrix, vector = P("wide", None), P("wide")
    out_specs = (token_spec,) * 3 + (
        matrix, vector, vector, matrix, vector, vector, vector,
        matrix, vector, matrix, vector, matrix, vector, vector, vector,
        matrix, vector, matrix, vector, vector, vector,
    )
    return jax.shard_map(body, mesh=split, in_specs=in_specs, out_specs=out_specs, check_vma=False)
```

```python
import functools

import jax
import jax.numpy as jnp
from jax import lax
from jax.experimental import pallas as pl
from jax.experimental.pallas import tpu as pltpu
from jax.sharding import Mesh, PartitionSpec as P

HD = 64
LANES = 128
WIDE, CORE, SIDE, NEAR, SHIFT = range(5)
MB = 2**20
norm_epsilon = 1e-05
masked_score = -1e9
BF = jnp.bfloat16
F32 = jnp.float32

NN = (((1,), (0,)), ((), ()))
NT = (((1,), (1,)), ((), ()))
TN = (((0,), (0,)), ((), ()))


def dot(a, b, dims=NN):
    return lax.dot_general(a, b, dims, preferred_element_type=F32)


def segment_terms(seg):
    lane = jnp.arange(LANES) % HD
    same = seg[..., None] == lane
    query_terms = jnp.where((lane < 4) & ~same, masked_score, 0.0).astype(BF)
    key_terms = jnp.where(((lane < 4) & same) | ((lane >= 4) & (lane < 7)), 1.0, 0.0).astype(BF)
    return query_terms, key_terms


def head_lanes(shape, head):
    lane = lax.broadcasted_iota(jnp.int32, shape, 1)
    return (lane < HD) if head == 0 else (lane >= HD)


def causal_scores(scores, causal, first_query, block, query_axis):
    if causal == "block":
        queries = lax.broadcasted_iota(jnp.int32, (block, block), query_axis)
        keys = lax.broadcasted_iota(jnp.int32, (block, block), 1 - query_axis)
        count = scores.shape[1 - query_axis]
        before = lax.slice_in_dim(scores, 0, count - block, axis=1 - query_axis)
        corner = lax.slice_in_dim(scores, count - block, count, axis=1 - query_axis)
        corner = jnp.where(keys <= queries, corner, masked_score)
        if count == block:
            return corner
        return jnp.concatenate([before, corner], 1 - query_axis)
    if causal == "mask":
        queries = first_query + lax.broadcasted_iota(jnp.int32, scores.shape, query_axis)
        keys = lax.broadcasted_iota(jnp.int32, scores.shape, 1 - query_axis)
        return jnp.where(keys <= queries, scores, masked_score)
    return scores


def in_order(parts, shift, half, there):
    if len(parts) == 1:
        return parts[0][there, :]
    return jnp.where(shift == 0, parts[half][...], parts[1 - half][...])


def array_places(count, shift, swapped):
    if not swapped:
        return [(slice(0, count), slice(0, count))]
    half = count // 2
    return [
        (
            slice(part * half, (part + 1) * half),
            pl.ds(pl.multiple_of(lax.rem(part * half + shift, count), half), half),
        )
        for part in (0, 1)
    ]


def row_block(index, block, count, shift, swapped):
    if not swapped:
        return pl.ds(index * block, block)
    return pl.ds(pl.multiple_of(lax.rem(index * block + shift, count), block), block)


def split_parts(refs, counts):
    groups = []
    for count in counts:
        groups.append(refs[:count])
        refs = refs[count:]
    return groups, refs


def forward_kernel(*refs, counts, skipped, causal, block, swapped):
    scalars, refs = refs[0], refs[1:]
    (q_parts, k_parts, v_parts), refs = split_parts(refs, counts)
    qt_ref, kt_ref = refs[:2]
    o_ref, qx_ref, ka, va, qa = refs[2 + skipped :]
    tq, ts = qa.shape[1], ka.shape[1]
    shift = scalars[SHIFT]
    for part, (here, there) in enumerate(array_places(ts, shift, swapped)):
        k = in_order(k_parts, shift, part, there)
        v = in_order(v_parts, shift, part, there)
        extra = kt_ref[there, :]
        for head in (0, 1):
            own = head_lanes(k.shape, head)
            ka[head, here, :] = jnp.where(own, k, extra)
            va[head, here, :] = jnp.where(own, v, extra)
    for part, (here, there) in enumerate(array_places(tq, shift, swapped)):
        q = in_order(q_parts, shift, part, there)
        extra = qt_ref[there, :]
        for head in (0, 1):
            qa[head, here, :] = jnp.where(head_lanes(q.shape, head), q, extra)
    lane = lax.broadcasted_iota(jnp.int32, (block, LANES), 1)
    for index in range(tq // block):
        count = (index + 1) * block if causal == "block" else ts
        there = row_block(index, block, tq, shift, swapped)
        outs, extra = [], qt_ref[there, :].astype(F32)
        for head in (0, 1):
            scores = dot(qa[head, index * block : (index + 1) * block, :], ka[head, :count, :], NT)
            scores = causal_scores(scores, causal, shift + index * block, block, 0)
            top = jnp.max(scores, 1, keepdims=True)
            weights = jnp.exp(scores - top).astype(BF)
            sums = dot(weights, va[head, :count, :])
            at = HD + 4 if head == 0 else 4
            total = sums[:, at + 2 : at + 3]
            outs.append(sums / total)
            for i, piece in enumerate(three_parts(-(top + jnp.log(total)))):
                extra = jnp.where(lane == at + i, piece, extra)
        o_ref[there, :] = jnp.where(lane < HD, outs[0], outs[1]).astype(BF)
        qx_ref[there, :] = extra.astype(BF)


def three_parts(x):
    parts = []
    for _ in range(3):
        part = x.astype(BF).astype(F32)
        parts.append(part)
        x = x - part
    return parts


def backward_kernel(*refs, counts, skipped, causal, block, swapped, scaling):
    scalars, refs = refs[0], refs[1:]
    (q_parts, k_parts, v_parts), refs = split_parts(refs, counts)
    g_ref, o_ref, qx_ref, kt_ref = refs[:4]
    (
        dq_ref, dk_ref, dv_ref, ka, va, qa, ga, k_turned, dk_sum, dv_sum, dq_turned,
    ) = refs[4 + skipped :]
    tq, ts = qa.shape[1], ka.shape[1]
    shift = scalars[SHIFT]
    for part, (here, there) in enumerate(array_places(ts, shift, swapped)):
        k = in_order(k_parts, shift, part, there)
        v = in_order(v_parts, shift, part, there)
        extra = kt_ref[there, :]
        for head in (0, 1):
            own = head_lanes(k.shape, head)
            ka[head, here, :] = jnp.where(own, k, extra)
            va[head, here, :] = jnp.where(own, v, extra)
        k_turned[:, here] = k.astype(F32).T.astype(BF)
    source = lax.broadcasted_iota(jnp.int32, (LANES, LANES), 0)
    target = lax.broadcasted_iota(jnp.int32, (LANES, LANES), 1)
    rides = (target % HD >= 4) & (target % HD < 7) & ((source < HD) == (target >= HD))
    spread = jnp.where(rides, -1.0, 0.0).astype(BF)
    for part, (here, there) in enumerate(array_places(tq, shift, swapped)):
        q = in_order(q_parts, shift, part, there)
        g, extra = g_ref[there, :], qx_ref[there, :]
        products = g.astype(F32) * o_ref[there, :].astype(F32)
        rough = products.astype(BF)
        delta = dot(rough, spread) + dot((products - rough.astype(F32)).astype(BF), spread)
        lane = lax.broadcasted_iota(jnp.int32, q.shape, 1) % HD
        pieces = three_parts(delta)
        g_extra = jnp.where(lane == 4, pieces[0], jnp.where(lane == 5, pieces[1], pieces[2]))
        g_extra = g_extra.astype(BF)
        for head in (0, 1):
            own = head_lanes(q.shape, head)
            qa[head, here, :] = jnp.where(own, q, extra)
            ga[head, here, :] = jnp.where(own, g, g_extra)
    blocks = tq // block
    for index in reversed(range(blocks)):
        count = (index + 1) * block if causal == "block" else ts
        rows = slice(index * block, (index + 1) * block)
        for head in (0, 1):
            q, g = qa[head, rows, :], ga[head, rows, :]
            scores = dot(ka[head, :count, :], q, NT)
            scores = causal_scores(scores, causal, shift + index * block, block, 1)
            probs = jnp.exp(scores)
            grads = (probs * dot(va[head, :count, :], g, NT)).astype(BF)
            dv, dk = dot(probs.astype(BF), g), dot(grads, q)
            if index == blocks - 1:
                dv_sum[head, :count, :] = dv
                dk_sum[head, :count, :] = dk
            else:
                dv_sum[head, :count, :] += dv
                dk_sum[head, :count, :] += dk
            own_rows = slice(HD * head, HD * (head + 1))
            dq_turned[own_rows, rows] = dot(k_turned[own_rows, :count], grads)
        there = row_block(index, block, tq, shift, swapped)
        dq_ref[there, :] = dq_turned[:, rows].T.astype(BF) * jnp.asarray(scaling, BF)
    for here, there in array_places(ts, shift, swapped):
        own = head_lanes((here.stop - here.start, LANES), 0)
        dk_ref[there, :] = jnp.where(own, dk_sum[0, here, :], dk_sum[1, here, :]).astype(BF)
        dv_ref[there, :] = jnp.where(own, dv_sum[0, here, :], dv_sum[1, here, :]).astype(BF)


BRIEF = pl.CostEstimate(flops=1, bytes_accessed=1, transcendentals=0)
ANYWHERE = pl.BlockSpec(memory_space=pl.ANY)


def head_spec(count, start):
    return pl.BlockSpec((pl.Squeezed(), count, LANES), lambda row, pair, _: (row, 0, start + pair))


def shared_spec(count):
    return pl.BlockSpec((pl.Squeezed(), count, LANES), lambda row, pair, _: (row, 0, 0))


def part_specs(q, k, v, first):
    specs, arrays = [], []
    for parts, column in (q, k, v):
        for x in parts:
            specs.append(head_spec(x.shape[1], column // LANES + first))
            arrays.append(x)
    return specs, arrays


def attend(q, k, v, terms, scalars, width, causal, block, swapped, after=()):
    specs, arrays = part_specs(q, k, v, 0)
    rows = arrays[0].shape[0]
    tq, ts = (sum(x.shape[1] for x in one[0]) for one in (q, k))
    pairs = width // LANES
    return pl.pallas_call(
        functools.partial(
            forward_kernel, counts=[len(x[0]) for x in (q, k, v)], skipped=len(after), causal=causal, block=block,
            swapped=swapped,
        ),
        grid_spec=pltpu.PrefetchScalarGridSpec(
            num_scalar_prefetch=1,
            grid=(rows, pairs),
            in_specs=specs + [shared_spec(tq), shared_spec(ts)] + [ANYWHERE] * len(after),
            out_specs=[head_spec(tq, 0), head_spec(tq, 0)],
            scratch_shapes=[pltpu.VMEM((2, n, LANES), BF) for n in (ts, ts, tq)],
        ),
        out_shape=[jax.ShapeDtypeStruct((rows, tq, width), BF)] * 2,
        compiler_params=pltpu.CompilerParams(vmem_limit_bytes=12 * MB),
        cost_estimate=BRIEF,
    )(scalars, *arrays, *terms, *after)


def attend_back(
    q, k, v, g, o, extra, terms, scalars, first, pairs, causal, block, swapped, held=(), after=()
):
    specs, arrays = part_specs(q, k, v, first)
    rows, _, width = o.shape
    tq, ts = (sum(x.shape[1] for x in one[0]) for one in (q, k))
    skipped = len(held) + len(after)
    count = len(arrays) + 4
    return pl.pallas_call(
        functools.partial(
            backward_kernel, counts=[len(x[0]) for x in (q, k, v)], skipped=skipped, causal=causal, block=block,
            swapped=swapped, scaling=HD**-0.5,
        ),
        grid_spec=pltpu.PrefetchScalarGridSpec(
            num_scalar_prefetch=1,
            grid=(rows, pairs),
            in_specs=specs
            + [head_spec(tq, first)] * 3
            + [shared_spec(ts)]
            + [ANYWHERE] * skipped,
            out_specs=[head_spec(tq, first), head_spec(ts, first), head_spec(ts, first)],
            scratch_shapes=[pltpu.VMEM((2, n, LANES), BF) for n in (ts, ts, tq, tq)]
            + [
                pltpu.VMEM((LANES, ts), BF),
                pltpu.VMEM((2, ts, LANES), F32),
                pltpu.VMEM((2, ts, LANES), F32),
                pltpu.VMEM((LANES, tq), F32),
            ],
        ),
        out_shape=[jax.ShapeDtypeStruct((rows, n, width), BF) for n in (tq, ts, ts)],
        input_output_aliases={1 + count + i: i for i in range(len(held))},
        compiler_params=pltpu.CompilerParams(vmem_limit_bytes=16 * MB),
        cost_estimate=BRIEF,
    )(scalars, *arrays, g, o, extra, terms[1], *held, *after)


def norm(resid):
    center = resid - jnp.mean(resid, -1, keepdims=True)
    inverse = lax.rsqrt(jnp.mean(center * center, -1, keepdims=True) + norm_epsilon)
    return center * inverse, inverse


def norm_back(upstream, normed, inverse, gain_vec):
    w = upstream * gain_vec
    return (
        w - jnp.mean(w, -1, keepdims=True) - normed * jnp.mean(w * normed, -1, keepdims=True)
    ) * inverse


def gelu_parts(pre):
    bell = jnp.exp(pre * pre * -0.5)
    t = 1.0 / (1.0 + jnp.abs(pre) * (0.3275911 * 0.5**0.5))
    poly = 0.5 * 1.061405429
    for c in (-1.453152027, 1.421413741, -0.284496736, 0.254829592):
        poly = poly * t + 0.5 * c
    tail = poly * t * bell
    phi_sum = jnp.where(pre >= 0, 1.0 - tail, tail)
    return pre * phi_sum, phi_sum + pre * (bell * 0.3989422804014327)


def add_rows(sums_ref, first, rows):
    for index, value in enumerate(rows):
        here = slice(first + index, first + index + 1)
        sums_ref[here, :] += jnp.sum(value.astype(F32), 0, keepdims=True)


def finish_rows(sums_ref, out_ref):
    @pl.when(pl.program_id(0) == pl.num_programs(0) - 1)
    def _():
        out_ref[...] = sums_ref[...].T


def clear(ref):
    @pl.when(pl.program_id(0) == 0)
    def _():
        ref[...] = jnp.zeros_like(ref)


def row(ref):
    return ref[...][None, :]


def project_kernel(x_ref, w_ref, b_ref, out_ref, *, scaled):
    width = b_ref.shape[0] // 3
    y = dot(x_ref[...], w_ref[...]) + row(b_ref)
    if scaled:
        out_ref[:, :width] = (y[:, :width] * HD**-0.5).astype(BF)
        out_ref[:, width:] = y[:, width:].astype(BF)
    else:
        out_ref[...] = y.astype(BF)


def after_self_kernel(
    o_ref, x_ref, w_ref, b_ref, gain_ref, bias_ref, qw_ref, qb_ref, n1_ref, i1_ref, h1b_ref, cq_ref,
):
    resid = x_ref[...].astype(F32) + (dot(o_ref[...], w_ref[...]) + row(b_ref))
    n1, i1 = norm(resid)
    h1b = (n1 * row(gain_ref) + row(bias_ref)).astype(BF)
    n1_ref[...] = n1
    i1_ref[...] = jnp.broadcast_to(i1, i1_ref.shape)
    h1b_ref[...] = h1b
    cq_ref[...] = ((dot(h1b, qw_ref[...]) + row(qb_ref)) * HD**-0.5).astype(BF)


def middle_kernel(
    o_ref, n1_ref, up_ref, g1_ref, s1_ref, ow_ref, ob_ref, g2_ref, s2_ref,
    w1_ref, b1_ref, w2_ref, b2_ref, g3_ref, s3_ref,
    *refs, chunk, kept_blocks,
):
    *outs, act_ref, dbf_ref, h2b_ref, dpre_ref, dr2_ref, dbc_ref, dco_ref, sums_ref, slope, sums = refs
    clear(sums)
    h1 = n1_ref[...] * row(g1_ref) + row(s1_ref)
    n2, i2 = norm(h1 + (dot(o_ref[...], ow_ref[...]) + row(ob_ref)))
    h2 = n2 * row(g2_ref) + row(s2_ref)
    h2b = h2.astype(BF)
    h2b_ref[...] = h2b
    hidden = w1_ref.shape[1]
    cols = [slice(c, c + chunk) for c in range(0, hidden, chunk)]
    bias1 = row(b1_ref)
    branch = row(b2_ref)
    for c in cols:
        pre = dot(h2b, w1_ref[:, c]) + bias1[:, c]
        value, slope_c = gelu_parts(pre)
        slope[:, c] = slope_c
        act_c = value.astype(BF)
        act_ref[:, c] = act_c
        branch = branch + dot(act_c, w2_ref[c, :])
    n3, i3 = norm(h2 + branch)
    out = (n3 * row(g3_ref) + row(s3_ref)).astype(BF)
    store_halves(outs, out, kept_blocks)
    up = up_ref[...].astype(F32)
    dr3 = norm_back(up, n3, i3, row(g3_ref))
    dbf = dr3.astype(BF)
    dbf_ref[...] = dbf
    dh2 = dr3
    for c in cols:
        dpre_c = (dot(dbf, w2_ref[c, :], NT) * slope[:, c]).astype(BF)
        dpre_ref[:, c] = dpre_c
        dh2 = dh2 + dot(dpre_c, w1_ref[:, c], NT)
    dr2 = norm_back(dh2, n2, i2, row(g2_ref))
    dbc = dr2.astype(BF)
    dr2_ref[...] = dr2
    dbc_ref[...] = dbc
    dco_ref[...] = dot(dbc, ow_ref[...], NT).astype(BF)
    add_rows(sums, MID_ROWS, (up * n3, up, dbf, dh2 * n2, dh2))
    finish_rows(sums, sums_ref)


def before_self_kernel(
    dcq_ref, dr2_ref, n1_ref, i1_ref, qw_ref, g1_ref, ow_ref, dr1_ref, dba_ref, dso_ref, sums_ref,
    sums,
):
    clear(sums)
    n1 = n1_ref[...]
    dh1 = dr2_ref[...] + dot(dcq_ref[...], qw_ref[...], NT)
    dr1 = norm_back(dh1, n1, i1_ref[:, 0:1], row(g1_ref))
    dba = dr1.astype(BF)
    dr1_ref[...] = dr1
    dba_ref[...] = dba
    dso_ref[...] = dot(dba, ow_ref[...], NT).astype(BF)
    add_rows(sums, LOW_ROWS, (dh1 * n1, dh1))
    finish_rows(sums, sums_ref)


def input_grad_kernel(*refs, count, start, kept_blocks):
    grads, w_ref, outs = refs[:count], refs[count + start], refs[count + start + 1 :]
    total = refs[count][...] if start else None
    width = grads[0].shape[-1]
    for index, ref in enumerate(grads):
        part = dot(ref[...], w_ref[:, index * width : (index + 1) * width], NT)
        total = part if total is None else total + part
    store_halves(outs, total, kept_blocks)


def store_halves(outs, value, kept_blocks):
    if kept_blocks is None:
        outs[0][...] = value.astype(outs[0].dtype)
        return
    step = pl.program_id(0)

    @pl.when(step < kept_blocks)
    def _():
        outs[0][...] = value.astype(outs[0].dtype)

    @pl.when(step >= kept_blocks)
    def _():
        outs[1][...] = value.astype(outs[1].dtype)


class Joined:
    def __init__(self, kept, got, use_kept):
        self.kept, self.got, self.use_kept = kept, got, use_kept

    def __getitem__(self, index):
        return jnp.where(self.use_kept, self.kept[index], self.got[index])


def token_call(kernel, block, blocked, whole, outs, scalars, scratch=(), after=(), vmem=16
):
    def length(x):
        return x.shape[0] if not isinstance(x, tuple) else x[0].shape[1] * (1 if x[1] is None else 2)

    tokens = length(blocked[0])
    half = tokens // block // 2
    count = tokens // block
    in_specs, arrays, kinds = [], [], []
    for x in blocked:
        if not isinstance(x, tuple):
            in_specs.append(pl.BlockSpec((block, x.shape[1]), lambda i, _: (i, 0)))
            arrays.append(x)
            kinds.append(1)
            continue
        stack, got = x
        shape = (pl.Squeezed(), block, stack.shape[2])
        if got is None:
            in_specs.append(pl.BlockSpec(shape, lambda i, p: (p[0], i, 0)))
            arrays.append(stack)
            kinds.append(1)
        else:
            in_specs.append(pl.BlockSpec(shape, lambda i, p: (p[0], jnp.minimum(i, half - 1), 0)))
            in_specs.append(
                pl.BlockSpec(shape[1:], lambda i, p: (jnp.maximum(i - half, 0), 0))
            )
            arrays += [stack, got]
            kinds.append(2)
    for x in whole:
        zeros = (0,) * x.ndim
        in_specs.append(
            pl.BlockSpec(x.shape, lambda i, _, z=zeros: z, pipeline_mode=pl.Buffered(1))
        )
    in_specs += [ANYWHERE] * len(after)
    out_specs, out_shape = [], []
    for out in outs:
        if out[0] == "whole":
            out_specs.append(pl.BlockSpec(out[1:3], lambda i, _: (0, 0)))
            shape = out[1:3]
        elif out[0] == "kept":
            shape = (out[1], tokens // 2, out[2])
            out_specs.append(
                pl.BlockSpec(
                    (pl.Squeezed(), block, out[2]),
                    lambda i, p: (p[0], jnp.minimum(i, half - 1), 0),
                )
            )
        elif out[0] == "sent":
            shape = (tokens // 2, out[1])
            out_specs.append(
                pl.BlockSpec((block, out[1]), lambda i, _: (jnp.maximum(i - half, 0), 0))
            )
        else:
            shape = (count * block, out[0])
            out_specs.append(pl.BlockSpec((block, out[0]), lambda i, _: (i, 0)))
        out_shape.append(jax.ShapeDtypeStruct(shape, out[-1]))

    def run(_, *refs):
        used = []
        for kind in kinds:
            if kind == 1:
                used.append(refs[0])
            else:
                used.append(Joined(refs[0], refs[1], pl.program_id(0) < half))
            refs = refs[kind:]
        kernel(*used, *refs[: len(whole)], *refs[len(whole) + len(after) :])

    return pl.pallas_call(
        run,
        grid_spec=pltpu.PrefetchScalarGridSpec(
            num_scalar_prefetch=1,
            grid=(count,),
            in_specs=in_specs,
            out_specs=out_specs,
            scratch_shapes=list(scratch),
        ),
        out_shape=out_shape,
        compiler_params=pltpu.CompilerParams(vmem_limit_bytes=vmem * MB),
        cost_estimate=BRIEF,
    )(scalars, *arrays, *whole, *after)


def store_kernel(_, got_ref, *refs):
    out_ref, mark_ref = refs[-2:]
    out_ref[...] = got_ref[...].astype(out_ref.dtype)
    mark_ref[...] = jnp.zeros_like(mark_ref)


def store_other(held, got, scalars, after=()):
    n, c = got.shape
    return pl.pallas_call(
        store_kernel,
        grid_spec=pltpu.PrefetchScalarGridSpec(
            num_scalar_prefetch=1,
            grid=(2,),
            in_specs=[pl.BlockSpec((n // 2, c), lambda i, _: (i, 0))] + [ANYWHERE] * (1 + len(after)),
            out_specs=[
                pl.BlockSpec((pl.Squeezed(), n // 2, c), lambda i, p: (1 - p[0], i, 0)),
                pl.BlockSpec((8, LANES), lambda i, _: (0, 0)),
            ],
        ),
        out_shape=[
            jax.ShapeDtypeStruct(held.shape, held.dtype),
            jax.ShapeDtypeStruct((8, LANES), F32),
        ],
        input_output_aliases={2: 0},
        cost_estimate=BRIEF,
    )(scalars, got, held, *after)


MID_ROWS, LOW_ROWS = 8, 16


def weight_grads(items, extras, scalars, wide, order, after=()):
    first_left = items[0][0]
    m = (first_left[0] if isinstance(first_left, tuple) else first_left).shape[-1]
    block = min(item[3] for item in items)
    block = min(block, m)
    specs, arrays, steps = [], [], []
    known = {}
    for left, right, start, columns, sum_row in items:
        key = id(left)
        if key not in known:
            known[key] = (len(arrays), isinstance(left, tuple))
            if isinstance(left, tuple):
                stack, got = left
                specs.append(
                    pl.BlockSpec(
                        (pl.Squeezed(),) + stack.shape[1:], lambda j, p: (p[0], 0, 0),
                        pipeline_mode=pl.Buffered(1),
                    )
                )
                arrays.append(stack)
                left = got
            specs.append(
                pl.BlockSpec(left.shape, lambda j, p: (0, 0), pipeline_mode=pl.Buffered(1))
            )
            arrays.append(left)
        begin, blocks = len(steps), columns // block
        where = len(arrays)
        specs.append(
            pl.BlockSpec(
                (right.shape[0], block),
                lambda j, p, b=begin, n=blocks, f=start // block: (0, f + jnp.clip(j - b, 0, n - 1)),
            )
        )
        arrays.append(right)
        for index in range(blocks):
            steps.append((known[key], where, sum_row, start + index * block, right.shape[1]))
    for extra in extras:
        specs.append(
            pl.BlockSpec(extra.shape, lambda j, p: (0, 0), pipeline_mode=pl.Buffered(1))
        )
    slab = m // len(order)
    size = m // wide
    apart = len(order) > 1
    slabs = len(order) // 2

    def kernel(scalar_ref, *refs):
        ins, rest = refs[: len(arrays)], refs[len(arrays) :]
        extra_refs, (*outs, sums) = rest[: len(extras)], rest[len(extras) + len(after) :]
        clear(sums)
        step = pl.program_id(0)

        def store(value):
            if not apart:
                outs[0][...] = value.astype(BF)
                return
            core = scalar_ref[CORE]
            for to in range(slabs):
                halves = [
                    value[order[at] * slab : (order[at] + 1) * slab].astype(BF)
                    for at in (to, slabs + to)
                ]
                here = slice(to * slab, (to + 1) * slab)
                outs[0][here, :] = jnp.where(core == 0, halves[1], halves[0])
                outs[1][here, :] = jnp.where(core == 0, halves[0], halves[1])

        for index, ((left, split), right, sum_row, column, columns) in enumerate(steps):

            @pl.when(step == index)
            def _():
                grad = ins[right][...]
                if split:
                    half = ins[left].shape[0]
                    value = dot(ins[left][...], grad[:half], TN)
                    value = value + dot(ins[left + 1][...], grad[half:], TN)
                else:
                    value = dot(ins[left][...], grad, TN)
                store(value)
                if sum_row is None:
                    return
                total = jnp.sum(grad.astype(F32), 0, keepdims=True)
                if columns == m:
                    sums[sum_row : sum_row + 1, column : column + block] = total
                    return
                for piece in range(block // size):
                    w, k = divmod(column // size + piece, columns // m)
                    sums[sum_row + k : sum_row + k + 1, w * size : (w + 1) * size] = total[
                        :, piece * size : (piece + 1) * size
                    ]

        @pl.when(step == len(steps))
        def _():
            value = sums[...].T
            for ref in extra_refs:
                value = value + ref[...]
            store(jnp.concatenate([value, jnp.zeros((m, block - LANES), F32)], 1))

    n = block * len(steps) + LANES
    rows = m // 2 if apart else m
    return pl.pallas_call(
        kernel,
        grid_spec=pltpu.PrefetchScalarGridSpec(
            num_scalar_prefetch=1,
            grid=(len(steps) + 1,),
            in_specs=specs + [ANYWHERE] * len(after),
            out_specs=[pl.BlockSpec((rows, block), lambda j, _: (0, j))] * (m // rows),
            scratch_shapes=[pltpu.VMEM((LANES, m), F32)],
        ),
        out_shape=[jax.ShapeDtypeStruct((rows, n), BF)] * (m // rows),
        compiler_params=pltpu.CompilerParams(vmem_limit_bytes=16 * MB),
        cost_estimate=BRIEF,
    )(scalars, *arrays, *extras, *after)


def tall_grad(left, right, scalars, order, after=()):
    tokens, rows = left.shape
    width = right.shape[1]
    apart = len(order) > 1
    blocks = len(order) if apart else 4
    size = rows // blocks
    half = blocks // 2

    def source(j, s):
        if not apart:
            return j
        to = jnp.where(s[CORE] == 0, (j + half) % blocks, j)
        block = 0
        for at, slab in enumerate(order):
            block = jnp.where(to == at, slab, block)
        return block

    def kernel(_, left_ref, right_ref, *refs):
        value = dot(left_ref[...], right_ref[...], TN).astype(BF)
        if not apart:
            refs[-1][...] = value
            return
        other, own = refs[-2:]

        @pl.when(pl.program_id(0) < half)
        def _():
            other[...] = value

        @pl.when(pl.program_id(0) >= half)
        def _():
            own[...] = value

    if apart:
        out_specs = [
            pl.BlockSpec((size, width), lambda j, _: (jnp.minimum(j, half - 1), 0)),
            pl.BlockSpec((size, width), lambda j, _: (jnp.maximum(j - half, 0), 0)),
        ]
        out_shape = [jax.ShapeDtypeStruct((rows // 2, width), BF)] * 2
    else:
        out_specs = [pl.BlockSpec((size, width), lambda j, _: (j, 0))]
        out_shape = [jax.ShapeDtypeStruct((rows, width), BF)]
    return pl.pallas_call(
        kernel,
        grid_spec=pltpu.PrefetchScalarGridSpec(
            num_scalar_prefetch=1,
            grid=(blocks,),
            in_specs=[
                pl.BlockSpec((tokens, size), lambda j, s: (0, source(j, s))),
                pl.BlockSpec(right.shape, lambda j, _: (0, 0), pipeline_mode=pl.Buffered(1)),
            ]
            + [ANYWHERE] * len(after),
            out_specs=out_specs,
        ),
        out_shape=out_shape,
        compiler_params=pltpu.CompilerParams(vmem_limit_bytes=12 * MB),
        cost_estimate=BRIEF,
    )(scalars, left, right, *after)


def vector_rows(x, columns, outs):
    turned = x.astype(F32).T
    for (start, count), out in zip(columns, outs):
        rows = [turned[start + i] for i in range(count)]
        out[...] = rows[0] if count == 1 else jnp.concatenate(rows)


def widen(pairs, pieces, columns, scalars, after=()):
    half = pairs[0][0].shape[0]
    flat_pairs = [x for pair in pairs for x in pair]

    def kernel(scalar_ref, *refs):
        ins = refs[: len(flat_pairs)]
        outs = refs[len(flat_pairs) + len(after) :]
        matrices, vectors = outs[: len(pieces)], outs[len(pieces) :]
        core = scalar_ref[CORE]
        step = pl.program_id(0)

        def rows(which, here, start, size):
            mine, other = ins[2 * which], ins[2 * which + 1]
            cols = slice(start, start + size)
            return jnp.where(core == here, mine[:, cols], other[:, cols])

        for out, parts in zip(matrices, pieces):
            at = 0
            for which, start, size in parts:
                out[:, at : at + size] = rows(which, step, start, size).astype(F32)
                at += size
        if columns:

            @pl.when(step == 1)
            def _():
                halves = [
                    sum(
                        rows(which, here, x.shape[1] - LANES, LANES).astype(F32)
                        for which, (x, _) in enumerate(pairs)
                    )
                    for here in (0, 1)
                ]
                vector_rows(jnp.concatenate(halves, 0), columns, vectors)

    widths = [sum(p[2] for p in parts) for parts in pieces]
    lengths = [count * 2 * half for _, count in columns]
    return pl.pallas_call(
        kernel,
        grid_spec=pltpu.PrefetchScalarGridSpec(
            num_scalar_prefetch=1,
            grid=(2,),
            in_specs=[
                pl.BlockSpec(x.shape, lambda i, _: (0, 0), pipeline_mode=pl.Buffered(1))
                for x in flat_pairs
            ]
            + [ANYWHERE] * len(after),
            out_specs=[pl.BlockSpec((half, w), lambda i, _: (i, 0)) for w in widths]
            + [pl.BlockSpec((n,), lambda i, _: (0,)) for n in lengths],
        ),
        out_shape=[jax.ShapeDtypeStruct((2 * half, w), F32) for w in widths]
        + [jax.ShapeDtypeStruct((n,), F32) for n in lengths],
        compiler_params=pltpu.CompilerParams(vmem_limit_bytes=24 * MB),
        cost_estimate=BRIEF,
    )(scalars, *flat_pairs, *after)


def vectors_kernel(x_ref, *outs, columns):
    vector_rows(x_ref[...], columns, outs)


def vectors_of(x, columns):
    return pl.pallas_call(
        functools.partial(vectors_kernel, columns=columns),
        out_shape=[jax.ShapeDtypeStruct((count * x.shape[0],), F32) for _, count in columns],
    )(x)


def partner(x, axis, bit=1):
    count = lax.axis_size(axis)
    return lax.ppermute(x, axis, [(i, i ^ bit) for i in range(count)])


def partner_both(x):
    return lax.ppermute(x, ("near", "side"), [(i, 3 - i) for i in range(4)])


ROWS = ("far", "near", "side", "core")


def merge(jobs, scalars, after):
    sizes = [terms[0][0].shape[0] >> len(terms[0][1]) for terms in jobs]
    steps = next(g for g in (4, 3, 2, 1) if all(n % (16 * g) == 0 for n in sizes))
    specs, arrays = [], []
    for terms, n in zip(jobs, sizes):
        for x, path in terms:
            assert x.shape[0] == n << len(path)

            def place(i, s, path=path):
                index = 0
                for scalar, flipped in path:
                    index = 2 * index + (1 - s[scalar] if flipped else s[scalar])
                return (index * steps + i, 0)

            specs.append(pl.BlockSpec((n // steps, x.shape[1]), place))
            arrays.append(x)

    def kernel(_, *refs):
        outs = refs[len(arrays) + len(after) :]
        at = 0
        for terms, out in zip(jobs, outs):
            total = refs[at][...].astype(F32)
            for ref in refs[at + 1 : at + len(terms)]:
                total = total + ref[...].astype(F32)
            at += len(terms)
            out[...] = total.astype(BF)

    shapes = [(n, terms[0][0].shape[1]) for terms, n in zip(jobs, sizes)]
    return pl.pallas_call(
        kernel,
        grid_spec=pltpu.PrefetchScalarGridSpec(
            num_scalar_prefetch=1,
            grid=(steps,),
            in_specs=specs + [ANYWHERE] * len(after),
            out_specs=[pl.BlockSpec((n // steps, c), lambda i, _: (i, 0)) for n, c in shapes],
        ),
        out_shape=[jax.ShapeDtypeStruct(shape, BF) for shape in shapes],
        compiler_params=pltpu.CompilerParams(vmem_limit_bytes=16 * MB),
        cost_estimate=BRIEF,
    )(scalars, *arrays, *after)


def line_up(jobs, scalars, after):
    arrays = [x for pieces in jobs for x in pieces]

    def kernel(s, *refs):
        outs = refs[len(arrays) + len(after) :]
        step = pl.program_id(0)
        side, near = step // 2, step % 2
        which = 2 * (side != s[SIDE]).astype(jnp.int32) + (near != s[NEAR]).astype(jnp.int32)
        for index in range(4):

            @pl.when(which == index)
            def _():
                for job, out in enumerate(outs):
                    out[...] = refs[4 * job + index][...]

    return pl.pallas_call(
        kernel,
        grid_spec=pltpu.PrefetchScalarGridSpec(
            num_scalar_prefetch=1,
            grid=(4,),
            in_specs=[
                pl.BlockSpec(x.shape, lambda i, _: (0, 0), pipeline_mode=pl.Buffered(1))
                for x in arrays
            ]
            + [ANYWHERE] * len(after),
            out_specs=[pl.BlockSpec(p[0].shape, lambda i, _: (i, 0)) for p in jobs],
        ),
        out_shape=[
            jax.ShapeDtypeStruct((4 * p[0].shape[0], p[0].shape[1]), BF) for p in jobs
        ],
        compiler_params=pltpu.CompilerParams(vmem_limit_bytes=16 * MB),
        cost_estimate=BRIEF,
    )(scalars, *arrays, *after)


AXES = {"wide": WIDE, "side": SIDE, "near": NEAR}


class Reduction:
    def __init__(self, arrays, order):
        self.split = len(arrays) == 2
        self.arrays = arrays
        self.steps = list(order) if self.split else []
        self.terms = []
        if self.split:
            self.got = partner(arrays[0], "core")
            self.terms = [(arrays[1], ()), (self.got, ())]
            self.waits = ()

    def result(self):
        x = lax.psum_scatter(self.arrays[0], "wide", scatter_dimension=0, tiled=True)
        return lax.psum(x, ROWS)


def advance(reductions, scalars, after):
    sums, joins = [], []
    for r in reductions:
        step = r.steps[0]
        if step == "join":
            joins.append(r)
        else:
            path = ((AXES[step], True),) if step in AXES else ()
            sums.append((r, [(x, p + path) for x, p in r.terms]))
    last = after
    if sums:
        outs = merge([terms for _, terms in sums], scalars, last)
        last = (outs[0],)
        for (r, _), sent in zip(sums, outs):
            step = r.steps.pop(0)
            if step == "spread":
                near = partner(sent, "near")
                side = partner(sent, "side")
                both = partner_both(sent)
                r.pieces = [sent, near, side, both]
                continue
            if step in AXES:
                r.terms = [(x, p + ((AXES[step], False),)) for x, p in r.terms]
            if step != "far" or lax.axis_size("far") == 2:
                r.terms.append((partner(sent, step), ()))
    if joins:
        outs = line_up([r.pieces for r in joins], scalars, last)
        last = (outs[0],)
        for r, mine in zip(joins, outs):
            r.steps.pop(0)
            r.pair = (mine, partner(mine, "core"))
    return last


CORE_WIDE = (0, 2, 1, 3)
CORE_SIDE = (0, 4, 1, 5, 2, 6, 3, 7)
X_FIRST = ("wide", "side", "near", "far", "spread", "join")
Y_FIRST = ("side", "wide", "near", "far", "spread", "join")


def body(
    target, encoded, segments, out_grad,
    self_qkv_w, self_q_b, self_v_b, self_out_w, self_out_b, norm1_gain, norm1_bias,
    cross_q_w, cross_q_b, cross_kv_w, cross_v_b, cross_out_w, cross_out_b, norm2_gain, norm2_bias,
    ffn_in_w, ffn_in_b, ffn_out_w, ffn_out_b, norm3_gain, norm3_bias,
):
    row_count, tok_count, width = target.shape
    hidden = ffn_in_w.shape[1]
    parts = hidden // width
    pairs = width // LANES
    wide = lax.axis_size("wide")
    index = lax.axis_index("wide").astype(jnp.int32)
    scalars = jnp.stack(
        [index]
        + [lax.axis_index(a).astype(jnp.int32) for a in ("core", "side", "near")]
        + [index * tok_count]
    )
    swapped = wide == 2 and row_count == 2
    split = swapped and all(lax.axis_size(a) == 2 for a in ("side", "near", "core"))
    core_wide = CORE_WIDE if split else (0,)
    core_side = CORE_SIDE if split else (0,)
    tokens = row_count * tok_count
    block = min(256, tok_count)
    kept_blocks = tok_count // block if swapped else None

    last = ()

    def run(call, *args, **kwargs):
        nonlocal last
        out = call(*args, after=last, **kwargs)
        last = (min(out, key=lambda x: x.size * x.dtype.itemsize),)
        return out

    if swapped:
        def bring(x):
            sent = lax.dynamic_index_in_dim(x, 1 - index, 0, keepdims=False)
            return x, partner(sent, "wide")

        causal, block_f, block_b = "block", 2 * block, block
        seg_kept, seg_got = bring(segments)
        seg = jnp.concatenate(
            [lax.dynamic_index_in_dim(seg_kept, index, 0, keepdims=False), seg_got]
        )[None]
        key_seg = seg
        row_tokens = tokens
    else:
        def bring(x):
            return x.reshape(tokens, -1)

        causal, block_f, block_b = "mask", block, block
        seg = segments
        key_seg = lax.all_gather(segments, "wide", axis=1, tiled=True)
        row_tokens = tok_count
    terms = (segment_terms(seg)[0], segment_terms(key_seg)[1])

    def by_row(x):
        return x.reshape(-1, row_tokens, x.shape[-1])

    def flat(x):
        return x.reshape(-1, x.shape[-1])

    def keys_of(x):
        return lax.all_gather(x, "wide", axis=1, tiled=True)

    def key_grads(x):
        return x if swapped else lax.psum_scatter(x, "wide", scatter_dimension=1, tiled=True)

    def project(x, w, bias, scaled):
        (out,) = run(
            token_call, functools.partial(project_kernel, scaled=scaled), block, (x,), (w, bias),
            [(w.shape[1], BF)], scalars
        )
        return out[None] if swapped else by_row(out)

    def attention(q, k, v, is_causal):
        return run(
            attend, q, k, v, terms, scalars, width, causal if is_causal else "no", block_f, swapped
        )

    def attention_back(q, k, v, g, o, extra, is_causal, first, count, held=()):
        return run(
            attend_back, q, k, v, by_row(g), o, extra, terms, scalars, first, count,
            causal if is_causal else "no", block_b, swapped, held,
        )

    def input_grad(grads, w, start=None):
        blocked = list(grads) + ([] if start is None else [start])
        outs = [("kept", 2, width, F32), ("sent", width, BF)] if swapped else [(width, F32)]
        kernel = functools.partial(
            input_grad_kernel, count=len(grads), start=0 if start is None else 1,
            kept_blocks=kept_blocks,
        )
        out = run(
            token_call, kernel, block, blocked, (w,), outs, scalars
        )
        return out[0], out[-1]

    def send_back(x):
        return partner(x, "wide") if swapped else None

    def give(out, got):
        if not swapped:
            return out.reshape(row_count, tok_count, width)
        return run(store_other, out, got, scalars)[0]

    def exchange(*reductions):
        nonlocal last
        if split:
            last = advance(reductions, scalars, last)

    zeros = jnp.zeros_like(self_q_b)
    qkv_bias = jnp.concatenate([self_q_b, zeros, self_v_b])
    ckv_bias = jnp.concatenate([zeros, cross_v_b])
    x_in = bring(target)
    x_enc = bring(encoded)
    upstream = bring(out_grad)
    if swapped:
        ckv = [project((x_enc[0], None), cross_kv_w, ckv_bias, False)]
        qkv = [project((x_in[0], None), self_qkv_w, qkv_bias, True)]
        qkv.append(project(x_in[1], self_qkv_w, qkv_bias, True))
        self_q, self_k, self_v = (qkv, 0), (qkv, width), (qkv, 2 * width)
    else:
        ckv = [keys_of(project(x_enc, cross_kv_w, ckv_bias, False))]
        qkv = [project(x_in, self_qkv_w, qkv_bias, True)]
        both = [keys_of(qkv[0][..., width:])]
        self_q, self_k, self_v = (qkv, 0), (both, 0), (both, width)
    self_o, self_x = attention(self_q, self_k, self_v, True)
    self_ob = flat(self_o)
    n1, i1, h1b, cq = run(
        token_call, after_self_kernel, block, (self_ob, x_in),
        (self_out_w, self_out_b, norm1_gain, norm1_bias, cross_q_w, cross_q_b),
        [(width, F32), (LANES, F32), (width, BF), (width, BF)], scalars,
    )
    if swapped:
        ckv.append(project(x_enc[1], cross_kv_w, ckv_bias, False))
    cross_q, cross_k, cross_v = ([by_row(cq)], 0), (ckv, 0), (ckv, width)
    cross_o, cross_x = attention(cross_q, cross_k, cross_v, False)
    cross_ob = flat(cross_o)
    outs = [("kept", 2, width, BF), ("sent", width, BF)] if swapped else [(width, BF)]
    *h3, act, dbf, h2b, dpre, dr2, dbc, dco, mid_sums = run(
        token_call, functools.partial(middle_kernel, chunk=width, kept_blocks=kept_blocks),
        block, (cross_ob, n1, upstream),
        (
            norm1_gain, norm1_bias, cross_out_w, cross_out_b, norm2_gain, norm2_bias,
            ffn_in_w, ffn_in_b, ffn_out_w, ffn_out_b, norm3_gain, norm3_bias,
        ),
        outs
        + [
            (hidden, BF), (width, BF), (width, BF), (hidden, BF), (width, F32),
            (width, BF), (width, BF), ("whole", width, LANES, F32),
        ],
        scalars,
        scratch=[pltpu.VMEM((block, hidden), F32), pltpu.VMEM((LANES, width), F32)],
        vmem=56,
    )
    got_out = send_back(h3[-1])

    ra = Reduction(run(tall_grad, act, dbf, scalars, core_wide), X_FIRST)
    rb = Reduction(
        run(
            weight_grads, [(h2b, dpre, 0, hidden, 0), (cross_ob, dbc, 0, width, parts)],
            [mid_sums], scalars, wide, core_side,
        ),
        Y_FIRST,
    )
    layer_out = give(h3[0], got_out)
    exchange(ra, rb)
    dcq, dck, dcv = attention_back(
        cross_q, cross_k, cross_v, dco, cross_o, cross_x, False, 0, pairs
    )
    dcq, dck, dcv = flat(dcq), flat(key_grads(dck)), flat(key_grads(dcv))
    exchange(ra, rb)
    rc = Reduction(
        run(
            weight_grads,
            [(h1b, dcq, 0, width, 0), (x_enc, dck, 0, width, None), (x_enc, dcv, 0, width, 1)],
            [], scalars, wide, core_side,
        ),
        Y_FIRST,
    )
    dr1, dba, dso, low_sums = run(
        token_call, before_self_kernel, block, (dcq, dr2, n1, i1),
        (cross_q_w, norm1_gain, self_out_w),
        [(width, F32), (width, BF), (width, BF), ("whole", width, LANES, F32)], scalars,
        scratch=[pltpu.VMEM((LANES, width), F32)],
    )
    exchange(ra, rb, rc)
    enc_kept, enc_sent = input_grad([dck, dcv], cross_kv_w)
    got_enc = send_back(enc_sent)
    exchange(ra, rb)
    cut = pairs // 2
    first = attention_back(
        self_q, self_k, self_v, dso, self_o, self_x, True, 0, cut if swapped else pairs
    )
    dsq, dsk, dsv = (flat(x) for x in first)
    exchange(ra, rb, rc)
    if swapped:
        one, two = cut * LANES, width - cut * LANES
        rd = Reduction(
            run(
                weight_grads,
                [
                    (self_ob, dba, 0, width, 2),
                    (x_in, dsq, 0, one, 0), (x_in, dsk, 0, one, None), (x_in, dsv, 0, one, 1),
                ],
                [low_sums], scalars, wide, core_wide,
            ),
            X_FIRST,
        )
        encoded_grad = give(enc_kept, got_enc)
        exchange(rd, rc)
        second = attention_back(
            self_q, self_k, self_v, dso, self_o, self_x, True, cut, pairs - cut, first
        )
        dsq, dsk, dsv = (flat(x) for x in second)
        exchange(ra, rb, rc, rd)
        re = Reduction(
            run(
                weight_grads,
                [(x_in, dsq, one, two, 0), (x_in, dsk, one, two, None), (x_in, dsv, one, two, 1)],
                [], scalars, wide, core_wide,
            ),
            X_FIRST,
        )
        exchange(rd, re)
    else:
        encoded_grad = give(enc_kept, got_enc)
        dsk, dsv = (
            flat(key_grads(x.reshape(row_count, -1, width))) for x in (dsk, dsv)
        )
        rd = Reduction(
            run(
                weight_grads, [(self_ob, dba, 0, width, 2)], [low_sums], scalars, wide, core_wide
            ),
            X_FIRST,
        )
        re = Reduction(
            run(
                weight_grads,
                [(x_in, dsq, 0, width, 0), (x_in, dsk, 0, width, None), (x_in, dsv, 0, width, 1)],
                [], scalars, wide, core_wide,
            ),
            X_FIRST,
        )
    in_kept, in_sent = input_grad([dsq, dsk, dsv], self_qkv_w, dr1)
    got_in = send_back(in_sent)

    vectors_b = [(0, parts), (parts, 1)] + [(MID_ROWS + i, 1) for i in range(5)]
    vectors_c = [(0, 1), (1, 1)]
    vectors_d = [(0, 1), (1, 1), (2, 1), (LOW_ROWS, 1), (LOW_ROWS + 1, 1)]
    pieces_b = [[(0, 0, hidden)], [(0, hidden, width)]]
    pieces_c = [[(0, 0, width)], [(0, width, 2 * width)]]
    if split:
        exchange(re, rd, rc)
        (ffn_out_w_grad,) = run(widen, [ra.pair], [[(0, 0, width)]], [], scalars)
        out_b = run(widen, [rb.pair], pieces_b, vectors_b, scalars)
        exchange(re, rd, rc)
        target_grad = give(in_kept, got_in)
        exchange(re, rd)
        out_c = run(widen, [rc.pair], pieces_c, vectors_c, scalars)
        exchange(re)
        exchange(re)
        pieces_d = [[(0, 0, width)], []]
        for i in range(3):
            pieces_d[1] += [(0, width + i * one, one), (1, i * two, two)]
        out_d = run(widen, [rd.pair, re.pair], pieces_d, vectors_d, scalars)
    else:
        target_grad = give(in_kept, got_in)

        def columns_of(x, pieces, vectors):
            return [
                jnp.concatenate([x[:, start : start + size] for _, start, size in p], 1).astype(F32)
                for p in pieces
            ] + list(vectors_of(x[:, -LANES:], vectors))

        ffn_out_w_grad = ra.result().astype(F32)
        out_b = columns_of(rb.result(), pieces_b, vectors_b)
        out_c = columns_of(rc.result(), pieces_c, vectors_c)
        low = rd.result()
        high = re.result()
        both = jnp.concatenate(
            [low[:, :width], high[:, : 3 * width], low[:, -LANES:] + high[:, -LANES:]], 1
        )
        out_d = columns_of(both, [[(0, 0, width)], [(0, width, 3 * width)]], vectors_d)
    (
        ffn_in_w_grad, cross_out_w_grad, ffn_in_b_grad, cross_out_b_grad, norm3_gain_grad,
        norm3_bias_grad, ffn_out_b_grad, norm2_gain_grad, norm2_bias_grad,
    ) = out_b
    cross_q_w_grad, cross_kv_w_grad, cross_q_b_grad, cross_v_b_grad = out_c
    (
        self_out_w_grad, self_qkv_w_grad, self_q_b_grad, self_v_b_grad, self_out_b_grad,
        norm1_gain_grad, norm1_bias_grad,
    ) = out_d
    return (
        layer_out, target_grad, encoded_grad,
        self_qkv_w_grad, self_q_b_grad, self_v_b_grad,
        self_out_w_grad, self_out_b_grad, norm1_gain_grad, norm1_bias_grad,
        cross_q_w_grad, cross_q_b_grad, cross_kv_w_grad, cross_v_b_grad,
        cross_out_w_grad, cross_out_b_grad, norm2_gain_grad, norm2_bias_grad,
        ffn_in_w_grad, ffn_in_b_grad, ffn_out_w_grad, ffn_out_b_grad,
        norm3_gain_grad, norm3_bias_grad,
    )


def solution(mesh):
    wide, narrow = mesh.shape["wide"], mesh.shape["narrow"]
    core = 2 if narrow % 2 == 0 else 1
    side = 2 if narrow % (2 * core) == 0 else 1
    near = 2 if narrow % (2 * core * side) == 0 else 1
    devices = mesh.devices.reshape(wide, narrow // (near * side * core), near, side, core)
    split = Mesh(devices, ("wide",) + ROWS)
    token_spec = P(ROWS, "wide", None)
    in_specs = (token_spec, token_spec, P(ROWS, "wide"), token_spec) + (P(),) * 21
    matrix, vector = P("wide", None), P("wide")
    out_specs = (token_spec,) * 3 + (
        matrix, vector, vector, matrix, vector, vector, vector,
        matrix, vector, matrix, vector, matrix, vector, vector, vector,
        matrix, vector, matrix, vector, vector, vector,
    )
    return jax.shard_map(body, mesh=split, in_specs=in_specs, out_specs=out_specs, check_vma=False)
```

```python
import functools

import jax
import jax.numpy as jnp
from jax import lax
from jax.experimental import pallas as pl
from jax.experimental.pallas import tpu as pltpu
from jax.sharding import Mesh, PartitionSpec as P

HD = 64
LANES = 128
WIDE, CORE, SIDE, NEAR, SHIFT = range(5)
MB = 2**20
norm_epsilon = 1e-05
masked_score = -1e9
BF = jnp.bfloat16
F32 = jnp.float32

NN = (((1,), (0,)), ((), ()))
NT = (((1,), (1,)), ((), ()))
TN = (((0,), (0,)), ((), ()))


def dot(a, b, dims=NN):
    return lax.dot_general(a, b, dims, preferred_element_type=F32)


def segment_terms(seg):
    lane = jnp.arange(LANES) % HD
    same = seg[..., None] == lane
    query_terms = jnp.where((lane < 4) & ~same, masked_score, 0.0).astype(BF)
    key_terms = jnp.where(((lane < 4) & same) | ((lane >= 4) & (lane < 7)), 1.0, 0.0).astype(BF)
    return query_terms, key_terms


def head_lanes(shape, head):
    lane = lax.broadcasted_iota(jnp.int32, shape, 1)
    return (lane < HD) if head == 0 else (lane >= HD)


def causal_scores(scores, causal, first_query, block, query_axis):
    if causal == "block":
        queries = lax.broadcasted_iota(jnp.int32, (block, block), query_axis)
        keys = lax.broadcasted_iota(jnp.int32, (block, block), 1 - query_axis)
        count = scores.shape[1 - query_axis]
        before = lax.slice_in_dim(scores, 0, count - block, axis=1 - query_axis)
        corner = lax.slice_in_dim(scores, count - block, count, axis=1 - query_axis)
        corner = jnp.where(keys <= queries, corner, masked_score)
        if count == block:
            return corner
        return jnp.concatenate([before, corner], 1 - query_axis)
    if causal == "mask":
        queries = first_query + lax.broadcasted_iota(jnp.int32, scores.shape, query_axis)
        keys = lax.broadcasted_iota(jnp.int32, scores.shape, 1 - query_axis)
        return jnp.where(keys <= queries, scores, masked_score)
    return scores


def in_order(parts, shift, half, there):
    if len(parts) == 1:
        return parts[0][there, :]
    return jnp.where(shift == 0, parts[half][...], parts[1 - half][...])


def array_places(count, shift, swapped):
    if not swapped:
        return [(slice(0, count), slice(0, count))]
    half = count // 2
    return [
        (
            slice(part * half, (part + 1) * half),
            pl.ds(pl.multiple_of(lax.rem(part * half + shift, count), half), half),
        )
        for part in (0, 1)
    ]


def row_block(index, block, count, shift, swapped):
    if not swapped:
        return pl.ds(index * block, block)
    return pl.ds(pl.multiple_of(lax.rem(index * block + shift, count), block), block)


def split_parts(refs, counts):
    groups = []
    for count in counts:
        groups.append(refs[:count])
        refs = refs[count:]
    return groups, refs


def forward_kernel(*refs, counts, skipped, causal, block, swapped):
    scalars, refs = refs[0], refs[1:]
    (q_parts, k_parts, v_parts), refs = split_parts(refs, counts)
    qt_ref, kt_ref = refs[:2]
    o_ref, qx_ref, ka, va, qa = refs[2 + skipped :]
    tq, ts = qa.shape[1], ka.shape[1]
    shift = scalars[SHIFT]
    for part, (here, there) in enumerate(array_places(ts, shift, swapped)):
        k = in_order(k_parts, shift, part, there)
        v = in_order(v_parts, shift, part, there)
        extra = kt_ref[there, :]
        for head in (0, 1):
            own = head_lanes(k.shape, head)
            ka[head, here, :] = jnp.where(own, k, extra)
            va[head, here, :] = jnp.where(own, v, extra)
    for part, (here, there) in enumerate(array_places(tq, shift, swapped)):
        q = in_order(q_parts, shift, part, there)
        extra = qt_ref[there, :]
        for head in (0, 1):
            qa[head, here, :] = jnp.where(head_lanes(q.shape, head), q, extra)
    lane = lax.broadcasted_iota(jnp.int32, (block, LANES), 1)
    for index in range(tq // block):
        count = (index + 1) * block if causal == "block" else ts
        there = row_block(index, block, tq, shift, swapped)
        outs, extra = [], qt_ref[there, :].astype(F32)
        for head in (0, 1):
            scores = dot(qa[head, index * block : (index + 1) * block, :], ka[head, :count, :], NT)
            scores = causal_scores(scores, causal, shift + index * block, block, 0)
            top = jnp.max(scores, 1, keepdims=True)
            weights = jnp.exp(scores - top).astype(BF)
            sums = dot(weights, va[head, :count, :])
            at = HD + 4 if head == 0 else 4
            total = sums[:, at + 2 : at + 3]
            outs.append(sums / total)
            for i, piece in enumerate(three_parts(-(top + jnp.log(total)))):
                extra = jnp.where(lane == at + i, piece, extra)
        o_ref[there, :] = jnp.where(lane < HD, outs[0], outs[1]).astype(BF)
        qx_ref[there, :] = extra.astype(BF)


def three_parts(x):
    parts = []
    for _ in range(3):
        part = x.astype(BF).astype(F32)
        parts.append(part)
        x = x - part
    return parts


def backward_kernel(*refs, counts, skipped, causal, block, swapped, scaling):
    scalars, refs = refs[0], refs[1:]
    (q_parts, k_parts, v_parts), refs = split_parts(refs, counts)
    g_ref, o_ref, qx_ref, kt_ref = refs[:4]
    (
        dq_ref, dk_ref, dv_ref, ka, va, qa, ga, k_turned, dk_sum, dv_sum, dq_turned,
    ) = refs[4 + skipped :]
    tq, ts = qa.shape[1], ka.shape[1]
    shift = scalars[SHIFT]
    for part, (here, there) in enumerate(array_places(ts, shift, swapped)):
        k = in_order(k_parts, shift, part, there)
        v = in_order(v_parts, shift, part, there)
        extra = kt_ref[there, :]
        for head in (0, 1):
            own = head_lanes(k.shape, head)
            ka[head, here, :] = jnp.where(own, k, extra)
            va[head, here, :] = jnp.where(own, v, extra)
        k_turned[:, here] = k.astype(F32).T.astype(BF)
    source = lax.broadcasted_iota(jnp.int32, (LANES, LANES), 0)
    target = lax.broadcasted_iota(jnp.int32, (LANES, LANES), 1)
    rides = (target % HD >= 4) & (target % HD < 7) & ((source < HD) == (target >= HD))
    spread = jnp.where(rides, -1.0, 0.0).astype(BF)
    for part, (here, there) in enumerate(array_places(tq, shift, swapped)):
        q = in_order(q_parts, shift, part, there)
        g, extra = g_ref[there, :], qx_ref[there, :]
        products = g.astype(F32) * o_ref[there, :].astype(F32)
        rough = products.astype(BF)
        delta = dot(rough, spread) + dot((products - rough.astype(F32)).astype(BF), spread)
        lane = lax.broadcasted_iota(jnp.int32, q.shape, 1) % HD
        pieces = three_parts(delta)
        g_extra = jnp.where(lane == 4, pieces[0], jnp.where(lane == 5, pieces[1], pieces[2]))
        g_extra = g_extra.astype(BF)
        for head in (0, 1):
            own = head_lanes(q.shape, head)
            qa[head, here, :] = jnp.where(own, q, extra)
            ga[head, here, :] = jnp.where(own, g, g_extra)
    blocks = tq // block
    for index in reversed(range(blocks)):
        count = (index + 1) * block if causal == "block" else ts
        rows = slice(index * block, (index + 1) * block)
        for head in (0, 1):
            q, g = qa[head, rows, :], ga[head, rows, :]
            scores = dot(ka[head, :count, :], q, NT)
            scores = causal_scores(scores, causal, shift + index * block, block, 1)
            probs = jnp.exp(scores)
            grads = (probs * dot(va[head, :count, :], g, NT)).astype(BF)
            dv, dk = dot(probs.astype(BF), g), dot(grads, q)
            if index == blocks - 1:
                dv_sum[head, :count, :] = dv
                dk_sum[head, :count, :] = dk
            else:
                dv_sum[head, :count, :] += dv
                dk_sum[head, :count, :] += dk
            own_rows = slice(HD * head, HD * (head + 1))
            dq_turned[own_rows, rows] = dot(k_turned[own_rows, :count], grads)
        there = row_block(index, block, tq, shift, swapped)
        dq_ref[there, :] = dq_turned[:, rows].T.astype(BF) * jnp.asarray(scaling, BF)
    for here, there in array_places(ts, shift, swapped):
        own = head_lanes((here.stop - here.start, LANES), 0)
        dk_ref[there, :] = jnp.where(own, dk_sum[0, here, :], dk_sum[1, here, :]).astype(BF)
        dv_ref[there, :] = jnp.where(own, dv_sum[0, here, :], dv_sum[1, here, :]).astype(BF)


BRIEF = pl.CostEstimate(flops=1, bytes_accessed=1, transcendentals=0)
ANYWHERE = pl.BlockSpec(memory_space=pl.ANY)


def head_spec(count, start):
    return pl.BlockSpec((pl.Squeezed(), count, LANES), lambda row, pair, _: (row, 0, start + pair))


def shared_spec(count):
    return pl.BlockSpec((pl.Squeezed(), count, LANES), lambda row, pair, _: (row, 0, 0))


def part_specs(q, k, v, first):
    specs, arrays = [], []
    for parts, column in (q, k, v):
        for x in parts:
            specs.append(head_spec(x.shape[1], column // LANES + first))
            arrays.append(x)
    return specs, arrays


def attend(q, k, v, terms, scalars, width, causal, block, swapped, after=()):
    specs, arrays = part_specs(q, k, v, 0)
    rows = arrays[0].shape[0]
    tq, ts = (sum(x.shape[1] for x in one[0]) for one in (q, k))
    pairs = width // LANES
    return pl.pallas_call(
        functools.partial(
            forward_kernel, counts=[len(x[0]) for x in (q, k, v)], skipped=len(after), causal=causal, block=block,
            swapped=swapped,
        ),
        grid_spec=pltpu.PrefetchScalarGridSpec(
            num_scalar_prefetch=1,
            grid=(rows, pairs),
            in_specs=specs + [shared_spec(tq), shared_spec(ts)] + [ANYWHERE] * len(after),
            out_specs=[head_spec(tq, 0), head_spec(tq, 0)],
            scratch_shapes=[pltpu.VMEM((2, n, LANES), BF) for n in (ts, ts, tq)],
        ),
        out_shape=[pltpu.HBM((rows, tq, width), BF)] * 2,
        compiler_params=pltpu.CompilerParams(vmem_limit_bytes=12 * MB),
        cost_estimate=BRIEF,
    )(scalars, *arrays, *terms, *after)


def attend_back(
    q, k, v, g, o, extra, terms, scalars, first, pairs, causal, block, swapped, held=(), after=()
):
    specs, arrays = part_specs(q, k, v, first)
    rows, _, width = o.shape
    tq, ts = (sum(x.shape[1] for x in one[0]) for one in (q, k))
    skipped = len(held) + len(after)
    count = len(arrays) + 4
    return pl.pallas_call(
        functools.partial(
            backward_kernel, counts=[len(x[0]) for x in (q, k, v)], skipped=skipped, causal=causal, block=block,
            swapped=swapped, scaling=HD**-0.5,
        ),
        grid_spec=pltpu.PrefetchScalarGridSpec(
            num_scalar_prefetch=1,
            grid=(rows, pairs),
            in_specs=specs
            + [head_spec(tq, first)] * 3
            + [shared_spec(ts)]
            + [ANYWHERE] * skipped,
            out_specs=[head_spec(tq, first), head_spec(ts, first), head_spec(ts, first)],
            scratch_shapes=[pltpu.VMEM((2, n, LANES), BF) for n in (ts, ts, tq, tq)]
            + [
                pltpu.VMEM((LANES, ts), BF),
                pltpu.VMEM((2, ts, LANES), F32),
                pltpu.VMEM((2, ts, LANES), F32),
                pltpu.VMEM((LANES, tq), F32),
            ],
        ),
        out_shape=[pltpu.HBM((rows, n, width), BF) for n in (tq, ts, ts)],
        input_output_aliases={1 + count + i: i for i in range(len(held))},
        compiler_params=pltpu.CompilerParams(vmem_limit_bytes=16 * MB),
        cost_estimate=BRIEF,
    )(scalars, *arrays, g, o, extra, terms[1], *held, *after)


def norm(resid):
    center = resid - jnp.mean(resid, -1, keepdims=True)
    inverse = lax.rsqrt(jnp.mean(center * center, -1, keepdims=True) + norm_epsilon)
    return center * inverse, inverse


def norm_back(upstream, normed, inverse, gain_vec):
    w = upstream * gain_vec
    return (
        w - jnp.mean(w, -1, keepdims=True) - normed * jnp.mean(w * normed, -1, keepdims=True)
    ) * inverse


def gelu_parts(pre):
    bell = jnp.exp(pre * pre * -0.5)
    t = 1.0 / (1.0 + jnp.abs(pre) * (0.3275911 * 0.5**0.5))
    poly = 0.5 * 1.061405429
    for c in (-1.453152027, 1.421413741, -0.284496736, 0.254829592):
        poly = poly * t + 0.5 * c
    tail = poly * t * bell
    phi_sum = jnp.where(pre >= 0, 1.0 - tail, tail)
    return pre * phi_sum, phi_sum + pre * (bell * 0.3989422804014327)


def add_rows(sums_ref, first, rows):
    for index, value in enumerate(rows):
        here = slice(first + index, first + index + 1)
        sums_ref[here, :] += jnp.sum(value.astype(F32), 0, keepdims=True)


def finish_rows(sums_ref, out_ref):
    @pl.when(pl.program_id(0) == pl.num_programs(0) - 1)
    def _():
        out_ref[...] = sums_ref[...].T


def clear(ref):
    @pl.when(pl.program_id(0) == 0)
    def _():
        ref[...] = jnp.zeros_like(ref)


def row(ref):
    return ref[...][None, :]


def project_kernel(x_ref, *refs, scaled, carried):
    if carried:
        refs[-1][...] = refs[0][...]
        refs = refs[1:-1]
    w_ref, b_ref, out_ref = refs
    width = b_ref.shape[0] // 3
    y = dot(x_ref[...], w_ref[...]) + row(b_ref)
    if scaled:
        out_ref[:, :width] = (y[:, :width] * HD**-0.5).astype(BF)
        out_ref[:, width:] = y[:, width:].astype(BF)
    else:
        out_ref[...] = y.astype(BF)


def after_self_kernel(
    o_ref, x_ref, w_ref, b_ref, gain_ref, bias_ref, qw_ref, qb_ref, n1_ref, i1_ref, h1b_ref, cq_ref,
):
    resid = x_ref[...].astype(F32) + (dot(o_ref[...], w_ref[...]) + row(b_ref))
    n1, i1 = norm(resid)
    h1b = (n1 * row(gain_ref) + row(bias_ref)).astype(BF)
    n1_ref[...] = n1
    i1_ref[...] = jnp.broadcast_to(i1, i1_ref.shape)
    h1b_ref[...] = h1b
    cq_ref[...] = ((dot(h1b, qw_ref[...]) + row(qb_ref)) * HD**-0.5).astype(BF)


def middle_kernel(
    o_ref, n1_ref, up_ref, g1_ref, s1_ref, ow_ref, ob_ref, g2_ref, s2_ref,
    w1_ref, b1_ref, w2_ref, b2_ref, g3_ref, s3_ref,
    *refs, chunk, kept_blocks,
):
    *outs, act_ref, dbf_ref, h2b_ref, dpre_ref, dr2_ref, dbc_ref, dco_ref, sums_ref, slope, sums = refs
    clear(sums)
    h1 = n1_ref[...] * row(g1_ref) + row(s1_ref)
    n2, i2 = norm(h1 + (dot(o_ref[...], ow_ref[...]) + row(ob_ref)))
    h2 = n2 * row(g2_ref) + row(s2_ref)
    h2b = h2.astype(BF)
    h2b_ref[...] = h2b
    hidden = w1_ref.shape[1]
    cols = [slice(c, c + chunk) for c in range(0, hidden, chunk)]
    bias1 = row(b1_ref)
    branch = row(b2_ref)
    for c in cols:
        pre = dot(h2b, w1_ref[:, c]) + bias1[:, c]
        value, slope_c = gelu_parts(pre)
        slope[:, c] = slope_c
        act_c = value.astype(BF)
        act_ref[:, c] = act_c
        branch = branch + dot(act_c, w2_ref[c, :])
    n3, i3 = norm(h2 + branch)
    out = (n3 * row(g3_ref) + row(s3_ref)).astype(BF)
    store_halves(outs, out, kept_blocks)
    up = up_ref[...].astype(F32)
    dr3 = norm_back(up, n3, i3, row(g3_ref))
    dbf = dr3.astype(BF)
    dbf_ref[...] = dbf
    dh2 = dr3
    for c in cols:
        dpre_c = (dot(dbf, w2_ref[c, :], NT) * slope[:, c]).astype(BF)
        dpre_ref[:, c] = dpre_c
        dh2 = dh2 + dot(dpre_c, w1_ref[:, c], NT)
    dr2 = norm_back(dh2, n2, i2, row(g2_ref))
    dbc = dr2.astype(BF)
    dr2_ref[...] = dr2
    dbc_ref[...] = dbc
    dco_ref[...] = dot(dbc, ow_ref[...], NT).astype(BF)
    add_rows(sums, MID_ROWS, (up * n3, up, dbf, dh2 * n2, dh2))
    finish_rows(sums, sums_ref)


def before_self_kernel(
    dcq_ref, dr2_ref, n1_ref, i1_ref, qw_ref, g1_ref, ow_ref, dr1_ref, dba_ref, dso_ref, sums_ref,
    sums,
):
    clear(sums)
    n1 = n1_ref[...]
    dh1 = dr2_ref[...] + dot(dcq_ref[...], qw_ref[...], NT)
    dr1 = norm_back(dh1, n1, i1_ref[:, 0:1], row(g1_ref))
    dba = dr1.astype(BF)
    dr1_ref[...] = dr1
    dba_ref[...] = dba
    dso_ref[...] = dot(dba, ow_ref[...], NT).astype(BF)
    add_rows(sums, LOW_ROWS, (dh1 * n1, dh1))
    finish_rows(sums, sums_ref)


def input_grad_kernel(*refs, count, start, kept_blocks):
    grads, w_ref, outs = refs[:count], refs[count + start], refs[count + start + 1 :]
    total = refs[count][...] if start else None
    width = grads[0].shape[-1]
    for index, ref in enumerate(grads):
        part = dot(ref[...], w_ref[:, index * width : (index + 1) * width], NT)
        total = part if total is None else total + part
    store_halves(outs, total, kept_blocks)


def store_halves(outs, value, kept_blocks):
    if kept_blocks is None:
        outs[0][...] = value.astype(outs[0].dtype)
        return
    step = pl.program_id(0)

    @pl.when(step < kept_blocks)
    def _():
        outs[0][...] = value.astype(outs[0].dtype)

    @pl.when(step >= kept_blocks)
    def _():
        outs[1][...] = value.astype(outs[1].dtype)


class Joined:
    def __init__(self, kept, got, use_kept):
        self.kept, self.got, self.use_kept = kept, got, use_kept

    def __getitem__(self, index):
        return jnp.where(self.use_kept, self.kept[index], self.got[index])


def token_call(kernel, block, blocked, whole, outs, scalars, scratch=(), after=(), vmem=16
):
    def length(x):
        if not isinstance(x, tuple):
            return x.shape[0]
        return x[0].shape[1] * (1 if x[1] is None or isinstance(x[1], str) else 2)

    tokens = length(blocked[0])
    half = tokens // block // 2
    count = tokens // block
    in_specs, arrays, kinds = [], [], []
    for x in blocked:
        if not isinstance(x, tuple):
            in_specs.append(pl.BlockSpec((block, x.shape[1]), lambda i, _: (i, 0)))
            arrays.append(x)
            kinds.append(1)
            continue
        stack, got = x
        shape = (pl.Squeezed(), block, stack.shape[2])
        if got is None or isinstance(got, str):
            row = (lambda p: 1 - p[0]) if got else (lambda p: p[0])
            in_specs.append(pl.BlockSpec(shape, lambda i, p, row=row: (row(p), i, 0)))
            arrays.append(stack)
            kinds.append(1)
        else:
            in_specs.append(pl.BlockSpec(shape, lambda i, p: (p[0], jnp.minimum(i, half - 1), 0)))
            in_specs.append(
                pl.BlockSpec(shape[1:], lambda i, p: (jnp.maximum(i - half, 0), 0))
            )
            arrays += [stack, got]
            kinds.append(2)
    for x in whole:
        zeros = (0,) * x.ndim
        in_specs.append(
            pl.BlockSpec(x.shape, lambda i, _, z=zeros: z, pipeline_mode=pl.Buffered(1))
        )
    in_specs += [ANYWHERE] * len(after)
    out_specs, out_shape = [], []
    for out in outs:
        if out[0] == "whole":
            out_specs.append(pl.BlockSpec(out[1:3], lambda i, _: (0, 0)))
            shape = out[1:3]
        elif out[0] == "kept":
            shape = (out[1], tokens // 2, out[2])
            out_specs.append(
                pl.BlockSpec(
                    (pl.Squeezed(), block, out[2]),
                    lambda i, p: (p[0], jnp.minimum(i, half - 1), 0),
                )
            )
        elif out[0] == "sent":
            shape = (tokens // 2, out[1])
            out_specs.append(
                pl.BlockSpec((block, out[1]), lambda i, _: (jnp.maximum(i - half, 0), 0))
            )
        else:
            shape = (count * block, out[0])
            out_specs.append(pl.BlockSpec((block, out[0]), lambda i, _: (i, 0)))
        out_shape.append(pltpu.HBM(shape, out[-1]))

    def run(_, *refs):
        used = []
        for kind in kinds:
            if kind == 1:
                used.append(refs[0])
            else:
                used.append(Joined(refs[0], refs[1], pl.program_id(0) < half))
            refs = refs[kind:]
        kernel(*used, *refs[: len(whole)], *refs[len(whole) + len(after) :])

    return pl.pallas_call(
        run,
        grid_spec=pltpu.PrefetchScalarGridSpec(
            num_scalar_prefetch=1,
            grid=(count,),
            in_specs=in_specs,
            out_specs=out_specs,
            scratch_shapes=list(scratch),
        ),
        out_shape=out_shape,
        compiler_params=pltpu.CompilerParams(vmem_limit_bytes=vmem * MB),
        cost_estimate=BRIEF,
    )(scalars, *arrays, *whole, *after)


def store_kernel(_, got_ref, *refs):
    out_ref, mark_ref = refs[-2:]
    out_ref[...] = got_ref[...].astype(out_ref.dtype)
    mark_ref[...] = jnp.zeros_like(mark_ref)


def store_other(held, got, scalars, after=()):
    n, c = got.shape
    return pl.pallas_call(
        store_kernel,
        grid_spec=pltpu.PrefetchScalarGridSpec(
            num_scalar_prefetch=1,
            grid=(2,),
            in_specs=[pl.BlockSpec((n // 2, c), lambda i, _: (i, 0))] + [ANYWHERE] * (1 + len(after)),
            out_specs=[
                pl.BlockSpec((pl.Squeezed(), n // 2, c), lambda i, p: (1 - p[0], i, 0)),
                pl.BlockSpec((8, LANES), lambda i, _: (0, 0)),
            ],
        ),
        out_shape=[
            pltpu.HBM(held.shape, held.dtype),
            pltpu.HBM((8, LANES), F32),
        ],
        input_output_aliases={2: 0},
        cost_estimate=BRIEF,
    )(scalars, got, held, *after)


MID_ROWS, LOW_ROWS = 8, 16


def weight_grads(items, extras, scalars, wide, order, after=()):
    first_left = items[0][0]
    m = (first_left[0] if isinstance(first_left, tuple) else first_left).shape[-1]
    block = min(item[3] for item in items)
    block = min(block, m)
    specs, arrays, steps = [], [], []
    known = {}
    for left, right, start, columns, sum_row in items:
        key = id(left)
        if key not in known:
            known[key] = (len(arrays), isinstance(left, tuple))
            if isinstance(left, tuple):
                stack, got = left
                specs.append(
                    pl.BlockSpec(
                        (pl.Squeezed(),) + stack.shape[1:], lambda j, p: (p[0], 0, 0),
                        pipeline_mode=pl.Buffered(1),
                    )
                )
                arrays.append(stack)
                left = got
            specs.append(
                pl.BlockSpec(left.shape, lambda j, p: (0, 0), pipeline_mode=pl.Buffered(1))
            )
            arrays.append(left)
        begin, blocks = len(steps), columns // block
        where = len(arrays)
        specs.append(
            pl.BlockSpec(
                (right.shape[0], block),
                lambda j, p, b=begin, n=blocks, f=start // block: (0, f + jnp.clip(j - b, 0, n - 1)),
            )
        )
        arrays.append(right)
        for index in range(blocks):
            steps.append((known[key], where, sum_row, start + index * block, right.shape[1]))
    for extra in extras:
        specs.append(
            pl.BlockSpec(extra.shape, lambda j, p: (0, 0), pipeline_mode=pl.Buffered(1))
        )
    slab = m // len(order)
    size = m // wide
    apart = len(order) > 1
    slabs = len(order) // 2

    def kernel(scalar_ref, *refs):
        ins, rest = refs[: len(arrays)], refs[len(arrays) :]
        extra_refs, (*outs, sums) = rest[: len(extras)], rest[len(extras) + len(after) :]
        clear(sums)
        step = pl.program_id(0)

        def store(value):
            if not apart:
                outs[0][...] = value.astype(BF)
                return
            core = scalar_ref[CORE]
            for to in range(slabs):
                halves = [
                    value[order[at] * slab : (order[at] + 1) * slab].astype(BF)
                    for at in (to, slabs + to)
                ]
                here = slice(to * slab, (to + 1) * slab)
                outs[0][here, :] = jnp.where(core == 0, halves[1], halves[0])
                outs[1][here, :] = jnp.where(core == 0, halves[0], halves[1])

        for index, ((left, split), right, sum_row, column, columns) in enumerate(steps):

            @pl.when(step == index)
            def _():
                grad = ins[right][...]
                if split:
                    half = ins[left].shape[0]
                    value = dot(ins[left][...], grad[:half], TN)
                    value = value + dot(ins[left + 1][...], grad[half:], TN)
                else:
                    value = dot(ins[left][...], grad, TN)
                store(value)
                if sum_row is None:
                    return
                total = jnp.sum(grad.astype(F32), 0, keepdims=True)
                if columns == m:
                    sums[sum_row : sum_row + 1, column : column + block] = total
                    return
                for piece in range(block // size):
                    w, k = divmod(column // size + piece, columns // m)
                    sums[sum_row + k : sum_row + k + 1, w * size : (w + 1) * size] = total[
                        :, piece * size : (piece + 1) * size
                    ]

        @pl.when(step == len(steps))
        def _():
            value = sums[...].T
            for ref in extra_refs:
                value = value + ref[...]
            store(jnp.concatenate([value, jnp.zeros((m, block - LANES), F32)], 1))

    n = block * len(steps) + LANES
    rows = m // 2 if apart else m
    return pl.pallas_call(
        kernel,
        grid_spec=pltpu.PrefetchScalarGridSpec(
            num_scalar_prefetch=1,
            grid=(len(steps) + 1,),
            in_specs=specs + [ANYWHERE] * len(after),
            out_specs=[pl.BlockSpec((rows, block), lambda j, _: (0, j))] * (m // rows),
            scratch_shapes=[pltpu.VMEM((LANES, m), F32)],
        ),
        out_shape=[pltpu.HBM((rows, n), BF)] * (m // rows),
        compiler_params=pltpu.CompilerParams(vmem_limit_bytes=16 * MB),
        cost_estimate=BRIEF,
    )(scalars, *arrays, *extras, *after)


def tall_grad(left, right, scalars, order, inner, after=()):
    tokens, rows = left.shape
    width = right.shape[1]
    apart = len(order) > 1
    blocks = len(order) if apart else 4
    size = rows // blocks
    half = blocks // 2

    def source(j, s):
        if not apart:
            return j
        to = jnp.where(s[CORE] == 0, (j + half) % blocks, j)
        block = 0
        for at, slab in enumerate(order):
            block = jnp.where(to == at, slab, block)
        return block

    def kernel(_, left_ref, right_ref, *refs):
        value = dot(left_ref[...], right_ref[...], TN).astype(BF)
        if not apart:
            refs[-1][...] = value
            return
        other, own = refs[-2:]
        part = size // len(inner)
        value = jnp.concatenate([value[at * part : (at + 1) * part] for at in inner], 0)

        @pl.when(pl.program_id(0) < half)
        def _():
            other[...] = value

        @pl.when(pl.program_id(0) >= half)
        def _():
            own[...] = value

    if apart:
        out_specs = [
            pl.BlockSpec((size, width), lambda j, _: (jnp.minimum(j, half - 1), 0)),
            pl.BlockSpec((size, width), lambda j, _: (jnp.maximum(j - half, 0), 0)),
        ]
        out_shape = [pltpu.HBM((rows // 2, width), BF)] * 2
    else:
        out_specs = [pl.BlockSpec((size, width), lambda j, _: (j, 0))]
        out_shape = [pltpu.HBM((rows, width), BF)]
    return pl.pallas_call(
        kernel,
        grid_spec=pltpu.PrefetchScalarGridSpec(
            num_scalar_prefetch=1,
            grid=(blocks,),
            in_specs=[
                pl.BlockSpec((tokens, size), lambda j, s: (0, source(j, s))),
                pl.BlockSpec(right.shape, lambda j, _: (0, 0), pipeline_mode=pl.Buffered(1)),
            ]
            + [ANYWHERE] * len(after),
            out_specs=out_specs,
        ),
        out_shape=out_shape,
        compiler_params=pltpu.CompilerParams(vmem_limit_bytes=12 * MB),
        cost_estimate=BRIEF,
    )(scalars, left, right, *after)


def vector_rows(x, columns, outs):
    turned = x.astype(F32).T
    for (start, count), out in zip(columns, outs):
        rows = [turned[start + i] for i in range(count)]
        out[...] = rows[0] if count == 1 else jnp.concatenate(rows)


def widen(pairs, pieces, columns, scalars, after=()):
    half = pairs[0][0].shape[0]
    flat_pairs = [x for pair in pairs for x in pair]

    def kernel(scalar_ref, *refs):
        ins = refs[: len(flat_pairs)]
        outs = refs[len(flat_pairs) + len(after) :]
        matrices, vectors = outs[: len(pieces)], outs[len(pieces) :]
        core = scalar_ref[CORE]
        step = pl.program_id(0)

        def rows(which, here, start, size):
            mine, other = ins[2 * which], ins[2 * which + 1]
            cols = slice(start, start + size)
            return jnp.where(core == here, mine[:, cols], other[:, cols])

        for out, parts in zip(matrices, pieces):
            at = 0
            for which, start, size in parts:
                out[:, at : at + size] = rows(which, step, start, size).astype(F32)
                at += size
        if columns:

            @pl.when(step == 1)
            def _():
                halves = [
                    sum(
                        rows(which, here, x.shape[1] - LANES, LANES).astype(F32)
                        for which, (x, _) in enumerate(pairs)
                    )
                    for here in (0, 1)
                ]
                vector_rows(jnp.concatenate(halves, 0), columns, vectors)

    widths = [sum(p[2] for p in parts) for parts in pieces]
    lengths = [count * 2 * half for _, count in columns]
    return pl.pallas_call(
        kernel,
        grid_spec=pltpu.PrefetchScalarGridSpec(
            num_scalar_prefetch=1,
            grid=(2,),
            in_specs=[
                pl.BlockSpec(x.shape, lambda i, _: (0, 0), pipeline_mode=pl.Buffered(1))
                for x in flat_pairs
            ]
            + [ANYWHERE] * len(after),
            out_specs=[pl.BlockSpec((half, w), lambda i, _: (i, 0)) for w in widths]
            + [pl.BlockSpec((n,), lambda i, _: (0,)) for n in lengths],
        ),
        out_shape=[pltpu.HBM((2 * half, w), F32) for w in widths]
        + [pltpu.HBM((n,), F32) for n in lengths],
        compiler_params=pltpu.CompilerParams(vmem_limit_bytes=24 * MB),
        cost_estimate=BRIEF,
    )(scalars, *flat_pairs, *after)


def vectors_kernel(x_ref, *outs, columns):
    vector_rows(x_ref[...], columns, outs)


def vectors_of(x, columns):
    return pl.pallas_call(
        functools.partial(vectors_kernel, columns=columns),
        out_shape=[pltpu.HBM((count * x.shape[0],), F32) for _, count in columns],
    )(x)


def partner(x, axis, bit=1):
    count = lax.axis_size(axis)
    return lax.ppermute(x, axis, [(i, i ^ bit) for i in range(count)])


def partner_both(x):
    return lax.ppermute(x, ("near", "side"), [(i, 3 - i) for i in range(4)])


ROWS = ("far", "near", "side", "core")


def merge(jobs, scalars, after):
    sizes = [terms[0][0].shape[0] >> len(terms[0][1]) for terms in jobs]
    steps = next(g for g in (4, 3, 2, 1) if all(n % (16 * g) == 0 for n in sizes))
    specs, arrays = [], []
    for terms, n in zip(jobs, sizes):
        for x, path in terms:
            assert x.shape[0] == n << len(path)

            def place(i, s, path=path):
                index = 0
                for scalar, flipped in path:
                    index = 2 * index + (1 - s[scalar] if flipped else s[scalar])
                return (index * steps + i, 0)

            specs.append(pl.BlockSpec((n // steps, x.shape[1]), place))
            arrays.append(x)

    def kernel(_, *refs):
        outs = refs[len(arrays) + len(after) :]
        at = 0
        for terms, out in zip(jobs, outs):
            total = refs[at][...].astype(F32)
            for ref in refs[at + 1 : at + len(terms)]:
                total = total + ref[...].astype(F32)
            at += len(terms)
            out[...] = total.astype(BF)

    shapes = [(n, terms[0][0].shape[1]) for terms, n in zip(jobs, sizes)]
    return pl.pallas_call(
        kernel,
        grid_spec=pltpu.PrefetchScalarGridSpec(
            num_scalar_prefetch=1,
            grid=(steps,),
            in_specs=specs + [ANYWHERE] * len(after),
            out_specs=[pl.BlockSpec((n // steps, c), lambda i, _: (i, 0)) for n, c in shapes],
        ),
        out_shape=[pltpu.HBM(shape, BF) for shape in shapes],
        compiler_params=pltpu.CompilerParams(vmem_limit_bytes=16 * MB),
        cost_estimate=BRIEF,
    )(scalars, *arrays, *after)


def line_up(jobs, scalars, after):
    arrays = [x for pieces in jobs for x in pieces]

    def kernel(s, *refs):
        outs = refs[len(arrays) + len(after) :]
        step = pl.program_id(0)
        side, near = step // 2, step % 2
        which = 2 * (side != s[SIDE]).astype(jnp.int32) + (near != s[NEAR]).astype(jnp.int32)
        for index in range(4):

            @pl.when(which == index)
            def _():
                for job, out in enumerate(outs):
                    out[...] = refs[4 * job + index][...]

    return pl.pallas_call(
        kernel,
        grid_spec=pltpu.PrefetchScalarGridSpec(
            num_scalar_prefetch=1,
            grid=(4,),
            in_specs=[
                pl.BlockSpec(x.shape, lambda i, _: (0, 0), pipeline_mode=pl.Buffered(1))
                for x in arrays
            ]
            + [ANYWHERE] * len(after),
            out_specs=[pl.BlockSpec(p[0].shape, lambda i, _: (i, 0)) for p in jobs],
        ),
        out_shape=[
            pltpu.HBM((4 * p[0].shape[0], p[0].shape[1]), BF) for p in jobs
        ],
        compiler_params=pltpu.CompilerParams(vmem_limit_bytes=16 * MB),
        cost_estimate=BRIEF,
    )(scalars, *arrays, *after)


AXES = {"wide": WIDE, "side": SIDE, "near": NEAR}


class Reduction:
    def __init__(self, arrays, order):
        self.split = len(arrays) == 2
        self.arrays = arrays
        self.steps = list(order) if self.split else []
        self.terms = []
        if self.split:
            self.got = partner(arrays[0], "core")
            self.terms = [(arrays[1], ()), (self.got, ())]
            self.waits = ()

    def result(self):
        x = lax.psum_scatter(self.arrays[0], "wide", scatter_dimension=0, tiled=True)
        return lax.psum(x, ROWS)


def advance(reductions, scalars, after):
    sums, joins = [], []
    for r in reductions:
        step = r.steps[0]
        if step == "join":
            joins.append(r)
        else:
            path = ((AXES[step], True),) if step in AXES else ()
            sums.append((r, [(x, p + path) for x, p in r.terms]))
    last = after
    if sums:
        outs = merge([terms for _, terms in sums], scalars, last)
        last = (outs[0],)
        for (r, _), sent in zip(sums, outs):
            step = r.steps.pop(0)
            if step == "spread":
                near = partner(sent, "near")
                side = partner(sent, "side")
                both = partner_both(sent)
                r.pieces = [sent, near, side, both]
                continue
            if step in AXES:
                r.terms = [(x, p + ((AXES[step], False),)) for x, p in r.terms]
            if step != "far" or lax.axis_size("far") == 2:
                r.terms.append((partner(sent, step), ()))
    if joins:
        outs = line_up([r.pieces for r in joins], scalars, last)
        last = (outs[0],)
        for r, mine in zip(joins, outs):
            r.steps.pop(0)
            r.pair = (mine, partner(mine, "core"))
    return last


CORE_WIDE = (0, 2, 1, 3)
CORE_SIDE = (0, 4, 1, 5, 2, 6, 3, 7)
X_FIRST = ("wide", "side", "near", "far", "spread", "join")
Y_FIRST = ("side", "wide", "near", "far", "spread", "join")
X_THEN_Z = ("wide", "near", "side", "far", "spread", "join")
NEAR_SIDE = (0, 2, 1, 3)


def body(
    target, encoded, segments, out_grad,
    self_qkv_w, self_q_b, self_v_b, self_out_w, self_out_b, norm1_gain, norm1_bias,
    cross_q_w, cross_q_b, cross_kv_w, cross_v_b, cross_out_w, cross_out_b, norm2_gain, norm2_bias,
    ffn_in_w, ffn_in_b, ffn_out_w, ffn_out_b, norm3_gain, norm3_bias,
):
    row_count, tok_count, width = target.shape
    hidden = ffn_in_w.shape[1]
    parts = hidden // width
    pairs = width // LANES
    wide = lax.axis_size("wide")
    index = lax.axis_index("wide").astype(jnp.int32)
    scalars = jnp.stack(
        [index]
        + [lax.axis_index(a).astype(jnp.int32) for a in ("core", "side", "near")]
        + [index * tok_count]
    )
    swapped = wide == 2 and row_count == 2
    split = swapped and all(lax.axis_size(a) == 2 for a in ("side", "near", "core"))
    core_wide = CORE_WIDE if split else (0,)
    core_side = CORE_SIDE if split else (0,)
    tokens = row_count * tok_count
    block = min(256, tok_count)
    kept_blocks = tok_count // block if swapped else None

    last = ()

    def run(call, *args, **kwargs):
        nonlocal last
        out = call(*args, after=last, **kwargs)
        last = (min(out, key=lambda x: x.size * x.dtype.itemsize),)
        return out

    if swapped:
        def bring(x):
            return x, partner(lax.dynamic_index_in_dim(x, 1 - index, 0, keepdims=False), "wide")

        causal, block_f, block_b = "block", 2 * block, block
        seg_kept, seg_got = bring(segments)
        seg = jnp.concatenate(
            [lax.dynamic_index_in_dim(seg_kept, index, 0, keepdims=False), seg_got]
        )[None]
        key_seg = seg
        row_tokens = tokens
    else:
        def bring(x):
            return x.reshape(tokens, -1)

        causal, block_f, block_b = "mask", block, block
        seg = segments
        key_seg = lax.all_gather(segments, "wide", axis=1, tiled=True)
        row_tokens = tok_count
    terms = (segment_terms(seg)[0], segment_terms(key_seg)[1])

    def by_row(x):
        return x.reshape(-1, row_tokens, x.shape[-1])

    def flat(x):
        return x.reshape(-1, x.shape[-1])

    def keys_of(x):
        return lax.all_gather(x, "wide", axis=1, tiled=True)

    def key_grads(x):
        return x if swapped else lax.psum_scatter(x, "wide", scatter_dimension=1, tiled=True)

    def project(x, w, bias, scaled, carried=None):
        outs = [(w.shape[1], BF)]
        if carried is not None:
            outs.append((carried.shape[-1], BF))
        out = run(
            token_call, functools.partial(project_kernel, scaled=scaled, carried=len(outs) == 2),
            block, (x,) if carried is None else (x, (carried, "other")), (w, bias), outs, scalars,
        )
        y = out[0][None] if swapped else by_row(out[0])
        return y if carried is None else (y, (carried, partner(out[1], "wide")))

    def attention(q, k, v, is_causal):
        return run(
            attend, q, k, v, terms, scalars, width, causal if is_causal else "no", block_f, swapped
        )

    def attention_back(q, k, v, g, o, extra, is_causal, first, count, held=()):
        return run(
            attend_back, q, k, v, by_row(g), o, extra, terms, scalars, first, count,
            causal if is_causal else "no", block_b, swapped, held,
        )

    def input_grad(grads, w, start=None):
        blocked = list(grads) + ([] if start is None else [start])
        outs = [("kept", 2, width, F32), ("sent", width, BF)] if swapped else [(width, F32)]
        kernel = functools.partial(
            input_grad_kernel, count=len(grads), start=0 if start is None else 1,
            kept_blocks=kept_blocks,
        )
        out = run(
            token_call, kernel, block, blocked, (w,), outs, scalars
        )
        return out[0], out[-1]

    def send_back(x):
        return partner(x, "wide") if swapped else None

    def give(out, got):
        if not swapped:
            return out.reshape(row_count, tok_count, width)
        return run(store_other, out, got, scalars)[0]

    def exchange(*reductions):
        nonlocal last
        if split:
            last = advance(reductions, scalars, last)

    zeros = jnp.zeros_like(self_q_b)
    qkv_bias = jnp.concatenate([self_q_b, zeros, self_v_b])
    ckv_bias = jnp.concatenate([zeros, cross_v_b])
    x_in = bring(target)
    if swapped:
        ckv = [project((encoded, None), cross_kv_w, ckv_bias, False)]
        qkv = [project((target, None), self_qkv_w, qkv_bias, True)]
        got, x_enc = project(x_in[1], self_qkv_w, qkv_bias, True, encoded)
        qkv.append(got)
        self_q, self_k, self_v = (qkv, 0), (qkv, width), (qkv, 2 * width)
    else:
        x_enc, upstream = bring(encoded), bring(out_grad)
        ckv = [keys_of(project(x_enc, cross_kv_w, ckv_bias, False))]
        qkv = [project(x_in, self_qkv_w, qkv_bias, True)]
        both = [keys_of(qkv[0][..., width:])]
        self_q, self_k, self_v = (qkv, 0), (both, 0), (both, width)
    self_o, self_x = attention(self_q, self_k, self_v, True)
    self_ob = flat(self_o)
    n1, i1, h1b, cq = run(
        token_call, after_self_kernel, block, (self_ob, x_in),
        (self_out_w, self_out_b, norm1_gain, norm1_bias, cross_q_w, cross_q_b),
        [(width, F32), (LANES, F32), (width, BF), (width, BF)], scalars,
    )
    if swapped:
        got, upstream = project(x_enc[1], cross_kv_w, ckv_bias, False, out_grad)
        ckv.append(got)
    cross_q, cross_k, cross_v = ([by_row(cq)], 0), (ckv, 0), (ckv, width)
    cross_o, cross_x = attention(cross_q, cross_k, cross_v, False)
    cross_ob = flat(cross_o)
    outs = [("kept", 2, width, BF), ("sent", width, BF)] if swapped else [(width, BF)]
    *h3, act, dbf, h2b, dpre, dr2, dbc, dco, mid_sums = run(
        token_call, functools.partial(middle_kernel, chunk=width, kept_blocks=kept_blocks),
        block, (cross_ob, n1, upstream),
        (
            norm1_gain, norm1_bias, cross_out_w, cross_out_b, norm2_gain, norm2_bias,
            ffn_in_w, ffn_in_b, ffn_out_w, ffn_out_b, norm3_gain, norm3_bias,
        ),
        outs
        + [
            (hidden, BF), (width, BF), (width, BF), (hidden, BF), (width, F32),
            (width, BF), (width, BF), ("whole", width, LANES, F32),
        ],
        scalars,
        scratch=[pltpu.VMEM((block, hidden), F32), pltpu.VMEM((LANES, width), F32)],
        vmem=56,
    )
    got_out = send_back(h3[-1])

    ra = Reduction(
        run(tall_grad, act, dbf, scalars, core_wide, NEAR_SIDE if split else (0,)), X_THEN_Z
    )
    rb = Reduction(
        run(
            weight_grads, [(h2b, dpre, 0, hidden, 0), (cross_ob, dbc, 0, width, parts)],
            [mid_sums], scalars, wide, core_side,
        ),
        Y_FIRST,
    )
    exchange(ra)
    exchange(rb)
    cross_args = (cross_q, cross_k, cross_v, dco, cross_o, cross_x, False)
    cut = pairs // 2
    first = attention_back(*cross_args, 0, cut)
    exchange(ra)
    dcq, dck, dcv = attention_back(*cross_args, cut, pairs - cut, first)
    dcq, dck, dcv = flat(dcq), flat(key_grads(dck)), flat(key_grads(dcv))
    exchange(ra, rb)
    layer_out = give(h3[0], got_out)
    rc = Reduction(
        run(
            weight_grads,
            [(h1b, dcq, 0, width, 0), (x_enc, dck, 0, width, None), (x_enc, dcv, 0, width, 1)],
            [], scalars, wide, core_side,
        ),
        Y_FIRST,
    )
    exchange(ra)
    dr1, dba, dso, low_sums = run(
        token_call, before_self_kernel, block, (dcq, dr2, n1, i1),
        (cross_q_w, norm1_gain, self_out_w),
        [(width, F32), (width, BF), (width, BF), ("whole", width, LANES, F32)], scalars,
        scratch=[pltpu.VMEM((LANES, width), F32)],
    )
    exchange(rc)
    exchange(rb)
    enc_kept, enc_sent = input_grad([dck, dcv], cross_kv_w)
    got_enc = send_back(enc_sent)
    exchange(ra)
    self_args = (self_q, self_k, self_v, dso, self_o, self_x, True)
    first = attention_back(*self_args, 0, cut if swapped else pairs)
    dsq, dsk, dsv = (flat(x) for x in first)
    exchange(rc)
    exchange(ra, rb)
    if swapped:
        one, two = cut * LANES, width - cut * LANES
        rd = Reduction(
            run(
                weight_grads,
                [
                    (self_ob, dba, 0, width, 2),
                    (x_in, dsq, 0, one, 0), (x_in, dsk, 0, one, None), (x_in, dsv, 0, one, 1),
                ],
                [low_sums], scalars, wide, core_wide,
            ),
            X_FIRST,
        )
        encoded_grad = give(enc_kept, got_enc)
        exchange(rd)
        exchange(rc)
        second = attention_back(*self_args, cut, pairs - cut, first)
        dsq, dsk, dsv = (flat(x) for x in second)
        exchange(rd)
        re = Reduction(
            run(
                weight_grads,
                [(x_in, dsq, one, two, 0), (x_in, dsk, one, two, None), (x_in, dsv, one, two, 1)],
                [], scalars, wide, core_wide,
            ),
            X_FIRST,
        )
        exchange(rc, rb)
        exchange(re)
    else:
        encoded_grad = give(enc_kept, got_enc)
        dsk, dsv = (
            flat(key_grads(x.reshape(row_count, -1, width))) for x in (dsk, dsv)
        )
        rd = Reduction(
            run(
                weight_grads, [(self_ob, dba, 0, width, 2)], [low_sums], scalars, wide, core_wide
            ),
            X_FIRST,
        )
        re = Reduction(
            run(
                weight_grads,
                [(x_in, dsq, 0, width, 0), (x_in, dsk, 0, width, None), (x_in, dsv, 0, width, 1)],
                [], scalars, wide, core_wide,
            ),
            X_FIRST,
        )
    in_kept, in_sent = input_grad([dsq, dsk, dsv], self_qkv_w, dr1)
    got_in = send_back(in_sent)

    vectors_b = [(0, parts), (parts, 1)] + [(MID_ROWS + i, 1) for i in range(5)]
    vectors_c = [(0, 1), (1, 1)]
    vectors_d = [(0, 1), (1, 1), (2, 1), (LOW_ROWS, 1), (LOW_ROWS + 1, 1)]
    pieces_b = [[(0, 0, hidden)], [(0, hidden, width)]]
    pieces_c = [[(0, 0, width)], [(0, width, 2 * width)]]
    if split:
        exchange(rd)
        exchange(re)
        (ffn_out_w_grad,) = run(widen, [ra.pair], [[(0, 0, width)]], [], scalars)
        exchange(rd)
        exchange(re)
        exchange(rc, rb)
        out_b = run(widen, [rb.pair], pieces_b, vectors_b, scalars)
        exchange(re)
        exchange(rd)
        exchange(rc)
        out_c = run(widen, [rc.pair], pieces_c, vectors_c, scalars)
        exchange(re)
        exchange(rd)
        target_grad = give(in_kept, got_in)
        exchange(re)
        pieces_d = [[(0, 0, width)], []]
        for i in range(3):
            pieces_d[1] += [(0, width + i * one, one), (1, i * two, two)]
        out_d = run(widen, [rd.pair, re.pair], pieces_d, vectors_d, scalars)
    else:
        target_grad = give(in_kept, got_in)

        def columns_of(x, pieces, vectors):
            return [
                jnp.concatenate([x[:, start : start + size] for _, start, size in p], 1).astype(F32)
                for p in pieces
            ] + list(vectors_of(x[:, -LANES:], vectors))

        ffn_out_w_grad = ra.result().astype(F32)
        out_b = columns_of(rb.result(), pieces_b, vectors_b)
        out_c = columns_of(rc.result(), pieces_c, vectors_c)
        low = rd.result()
        high = re.result()
        both = jnp.concatenate(
            [low[:, :width], high[:, : 3 * width], low[:, -LANES:] + high[:, -LANES:]], 1
        )
        out_d = columns_of(both, [[(0, 0, width)], [(0, width, 3 * width)]], vectors_d)
    (
        ffn_in_w_grad, cross_out_w_grad, ffn_in_b_grad, cross_out_b_grad, norm3_gain_grad,
        norm3_bias_grad, ffn_out_b_grad, norm2_gain_grad, norm2_bias_grad,
    ) = out_b
    cross_q_w_grad, cross_kv_w_grad, cross_q_b_grad, cross_v_b_grad = out_c
    (
        self_out_w_grad, self_qkv_w_grad, self_q_b_grad, self_v_b_grad, self_out_b_grad,
        norm1_gain_grad, norm1_bias_grad,
    ) = out_d
    return (
        layer_out, target_grad, encoded_grad,
        self_qkv_w_grad, self_q_b_grad, self_v_b_grad,
        self_out_w_grad, self_out_b_grad, norm1_gain_grad, norm1_bias_grad,
        cross_q_w_grad, cross_q_b_grad, cross_kv_w_grad, cross_v_b_grad,
        cross_out_w_grad, cross_out_b_grad, norm2_gain_grad, norm2_bias_grad,
        ffn_in_w_grad, ffn_in_b_grad, ffn_out_w_grad, ffn_out_b_grad,
        norm3_gain_grad, norm3_bias_grad,
    )


def solution(mesh):
    wide, narrow = mesh.shape["wide"], mesh.shape["narrow"]
    core = 2 if narrow % 2 == 0 else 1
    side = 2 if narrow % (2 * core) == 0 else 1
    near = 2 if narrow % (2 * core * side) == 0 else 1
    devices = mesh.devices.reshape(wide, narrow // (near * side * core), near, side, core)
    split = Mesh(devices, ("wide",) + ROWS)
    token_spec = P(ROWS, "wide", None)
    in_specs = (token_spec, token_spec, P(ROWS, "wide"), token_spec) + (P(),) * 21
    matrix, vector = P("wide", None), P("wide")
    out_specs = (token_spec,) * 3 + (
        matrix, vector, vector, matrix, vector, vector, vector,
        matrix, vector, matrix, vector, matrix, vector, vector, vector,
        matrix, vector, matrix, vector, vector, vector,
    )
    return jax.shard_map(body, mesh=split, in_specs=in_specs, out_specs=out_specs, check_vma=False)
```

```python
import functools

import jax
import jax.numpy as jnp
from jax import lax
from jax.experimental import pallas as pl
from jax.experimental.pallas import tpu as pltpu
from jax.sharding import Mesh, PartitionSpec as P

HD = 64
LANES = 128
WIDE, CORE, SIDE, NEAR, SHIFT = range(5)
MB = 2**20
norm_epsilon = 1e-05
masked_score = -1e9
BF = jnp.bfloat16
F32 = jnp.float32

NN = (((1,), (0,)), ((), ()))
NT = (((1,), (1,)), ((), ()))
TN = (((0,), (0,)), ((), ()))


def dot(a, b, dims=NN):
    return lax.dot_general(a, b, dims, preferred_element_type=F32)


def segment_terms(seg):
    lane = jnp.arange(LANES) % HD
    same = seg[..., None] == lane
    query_terms = jnp.where((lane < 4) & ~same, masked_score, 0.0).astype(BF)
    key_terms = jnp.where(((lane < 4) & same) | ((lane >= 4) & (lane < 7)), 1.0, 0.0).astype(BF)
    return query_terms, key_terms


def head_lanes(shape, head):
    lane = lax.broadcasted_iota(jnp.int32, shape, 1)
    return (lane < HD) if head == 0 else (lane >= HD)


def causal_scores(scores, causal, first_query, block, query_axis):
    if causal == "block":
        queries = lax.broadcasted_iota(jnp.int32, (block, block), query_axis)
        keys = lax.broadcasted_iota(jnp.int32, (block, block), 1 - query_axis)
        count = scores.shape[1 - query_axis]
        before = lax.slice_in_dim(scores, 0, count - block, axis=1 - query_axis)
        corner = lax.slice_in_dim(scores, count - block, count, axis=1 - query_axis)
        corner = jnp.where(keys <= queries, corner, masked_score)
        if count == block:
            return corner
        return jnp.concatenate([before, corner], 1 - query_axis)
    if causal == "mask":
        queries = first_query + lax.broadcasted_iota(jnp.int32, scores.shape, query_axis)
        keys = lax.broadcasted_iota(jnp.int32, scores.shape, 1 - query_axis)
        return jnp.where(keys <= queries, scores, masked_score)
    return scores


def in_order(parts, shift, half, there):
    if len(parts) == 1:
        return parts[0][there, :]
    return jnp.where(shift == 0, parts[half][...], parts[1 - half][...])


def array_places(count, shift, swapped):
    if not swapped:
        return [(slice(0, count), slice(0, count))]
    half = count // 2
    return [
        (
            slice(part * half, (part + 1) * half),
            pl.ds(pl.multiple_of(lax.rem(part * half + shift, count), half), half),
        )
        for part in (0, 1)
    ]


def row_block(index, block, count, shift, swapped):
    if not swapped:
        return pl.ds(index * block, block)
    return pl.ds(pl.multiple_of(lax.rem(index * block + shift, count), block), block)


def split_parts(refs, counts):
    groups = []
    for count in counts:
        groups.append(refs[:count])
        refs = refs[count:]
    return groups, refs


def forward_kernel(*refs, counts, causal, block, swapped):
    scalars, refs = refs[0], refs[1:]
    (q_parts, k_parts, v_parts), refs = split_parts(refs, counts)
    qt_ref, kt_ref = refs[:2]
    o_ref, qx_ref, ka, va, qa = refs[2:]
    tq, ts = qa.shape[1], ka.shape[1]
    shift = scalars[SHIFT]
    for part, (here, there) in enumerate(array_places(ts, shift, swapped)):
        k = in_order(k_parts, shift, part, there)
        v = in_order(v_parts, shift, part, there)
        extra = kt_ref[there, :]
        for head in (0, 1):
            own = head_lanes(k.shape, head)
            ka[head, here, :] = jnp.where(own, k, extra)
            va[head, here, :] = jnp.where(own, v, extra)
    for part, (here, there) in enumerate(array_places(tq, shift, swapped)):
        q = in_order(q_parts, shift, part, there)
        extra = qt_ref[there, :]
        for head in (0, 1):
            qa[head, here, :] = jnp.where(head_lanes(q.shape, head), q, extra)
    lane = lax.broadcasted_iota(jnp.int32, (block, LANES), 1)
    for index in range(tq // block):
        count = (index + 1) * block if causal == "block" else ts
        there = row_block(index, block, tq, shift, swapped)
        outs, extra = [], qt_ref[there, :].astype(F32)
        for head in (0, 1):
            scores = dot(qa[head, index * block : (index + 1) * block, :], ka[head, :count, :], NT)
            scores = causal_scores(scores, causal, shift + index * block, block, 0)
            top = jnp.max(scores, 1, keepdims=True)
            weights = jnp.exp(scores - top).astype(BF)
            sums = dot(weights, va[head, :count, :])
            at = HD + 4 if head == 0 else 4
            total = sums[:, at + 2 : at + 3]
            outs.append(sums / total)
            for i, piece in enumerate(three_parts(-(top + jnp.log(total)))):
                extra = jnp.where(lane == at + i, piece, extra)
        o_ref[there, :] = jnp.where(lane < HD, outs[0], outs[1]).astype(BF)
        qx_ref[there, :] = extra.astype(BF)


def three_parts(x):
    parts = []
    for _ in range(3):
        part = x.astype(BF).astype(F32)
        parts.append(part)
        x = x - part
    return parts


def backward_kernel(*refs, counts, causal, block, swapped, scaling):
    scalars, refs = refs[0], refs[1:]
    (q_parts, k_parts, v_parts), refs = split_parts(refs, counts)
    g_ref, o_ref, qx_ref, kt_ref = refs[:4]
    (
        dq_ref, dk_ref, dv_ref, ka, va, qa, ga, k_turned, dk_sum, dv_sum, dq_turned,
    ) = refs[4:]
    tq, ts = qa.shape[1], ka.shape[1]
    shift = scalars[SHIFT]
    for part, (here, there) in enumerate(array_places(ts, shift, swapped)):
        k = in_order(k_parts, shift, part, there)
        v = in_order(v_parts, shift, part, there)
        extra = kt_ref[there, :]
        for head in (0, 1):
            own = head_lanes(k.shape, head)
            ka[head, here, :] = jnp.where(own, k, extra)
            va[head, here, :] = jnp.where(own, v, extra)
        k_turned[:, here] = k.astype(F32).T.astype(BF)
    source = lax.broadcasted_iota(jnp.int32, (LANES, LANES), 0)
    target = lax.broadcasted_iota(jnp.int32, (LANES, LANES), 1)
    rides = (target % HD >= 4) & (target % HD < 7) & ((source < HD) == (target >= HD))
    spread = jnp.where(rides, -1.0, 0.0).astype(BF)
    for part, (here, there) in enumerate(array_places(tq, shift, swapped)):
        q = in_order(q_parts, shift, part, there)
        g, extra = g_ref[there, :], qx_ref[there, :]
        products = g.astype(F32) * o_ref[there, :].astype(F32)
        rough = products.astype(BF)
        delta = dot(rough, spread) + dot((products - rough.astype(F32)).astype(BF), spread)
        lane = lax.broadcasted_iota(jnp.int32, q.shape, 1) % HD
        pieces = three_parts(delta)
        g_extra = jnp.where(lane == 4, pieces[0], jnp.where(lane == 5, pieces[1], pieces[2]))
        g_extra = g_extra.astype(BF)
        for head in (0, 1):
            own = head_lanes(q.shape, head)
            qa[head, here, :] = jnp.where(own, q, extra)
            ga[head, here, :] = jnp.where(own, g, g_extra)
    blocks = tq // block
    for index in reversed(range(blocks)):
        count = (index + 1) * block if causal == "block" else ts
        rows = slice(index * block, (index + 1) * block)
        for head in (0, 1):
            q, g = qa[head, rows, :], ga[head, rows, :]
            scores = dot(ka[head, :count, :], q, NT)
            scores = causal_scores(scores, causal, shift + index * block, block, 1)
            probs = jnp.exp(scores)
            grads = (probs * dot(va[head, :count, :], g, NT)).astype(BF)
            dv, dk = dot(probs.astype(BF), g), dot(grads, q)
            if index == blocks - 1:
                dv_sum[head, :count, :] = dv
                dk_sum[head, :count, :] = dk
            else:
                dv_sum[head, :count, :] += dv
                dk_sum[head, :count, :] += dk
            own_rows = slice(HD * head, HD * (head + 1))
            dq_turned[own_rows, rows] = dot(k_turned[own_rows, :count], grads)
        there = row_block(index, block, tq, shift, swapped)
        dq_ref[there, :] = dq_turned[:, rows].T.astype(BF) * jnp.asarray(scaling, BF)
    for here, there in array_places(ts, shift, swapped):
        own = head_lanes((here.stop - here.start, LANES), 0)
        dk_ref[there, :] = jnp.where(own, dk_sum[0, here, :], dk_sum[1, here, :]).astype(BF)
        dv_ref[there, :] = jnp.where(own, dv_sum[0, here, :], dv_sum[1, here, :]).astype(BF)


ANYWHERE = pl.BlockSpec(memory_space=pl.ANY)


def stay(*arrays):
    return [pltpu.with_memory_space_constraint(x, pltpu.HBM) for x in arrays]


def head_spec(count, start):
    return pl.BlockSpec((pl.Squeezed(), count, LANES), lambda row, pair, _: (row, 0, start + pair))


def shared_spec(count):
    return pl.BlockSpec((pl.Squeezed(), count, LANES), lambda row, pair, _: (row, 0, 0))


def part_specs(q, k, v, first):
    specs, arrays = [], []
    for parts, column in (q, k, v):
        for x in parts:
            specs.append(head_spec(x.shape[1], column // LANES + first))
            arrays.append(x)
    return specs, arrays


class Chain:
    def __init__(self):
        self.last, self.pending, self.active = (), (), []

    def launch(
        self, kernel, scalars, grid, in_specs, arrays, out_specs, out_shape, scratch=(), vmem=48,
        us=5, held=(), free=0,
    ):
        active = [r for r in self.active if r.steps]
        carried = [r.terms[0][0] for r in active]
        ins, outs = len(arrays), len(out_shape)
        arrays = [*stay(*arrays[: ins - free]), *arrays[ins - free :]]
        extra = [*stay(*held, *self.last), *self.pending, *stay(*carried)]

        def run(scalar_ref, *refs):
            rest = refs[ins + len(extra) :]
            kernel(scalar_ref, *refs[:ins], *rest[:outs], *rest[outs + len(carried) :])

        at = 1 + ins
        aliases = {at + i: i for i in range(len(held))}
        at += len(extra) - len(carried)
        aliases.update({at + i: outs + i for i in range(len(carried))})
        results = pl.pallas_call(
            run,
            grid_spec=pltpu.PrefetchScalarGridSpec(
                num_scalar_prefetch=1,
                grid=grid,
                in_specs=list(in_specs) + [ANYWHERE] * len(extra),
                out_specs=list(out_specs) + [ANYWHERE] * len(carried),
                scratch_shapes=list(scratch),
            ),
            out_shape=[pltpu.HBM(x.shape, x.dtype) for x in (*out_shape, *carried)],
            input_output_aliases=aliases,
            compiler_params=pltpu.CompilerParams(vmem_limit_bytes=vmem * MB),
            cost_estimate=pl.CostEstimate(
                flops=0, bytes_accessed=us * 3600000, transcendentals=0
            ),
        )(scalars, *arrays, *extra)
        for r, x in zip(active, results[outs:]):
            r.terms[0] = (x, r.terms[0][1])
        results = results[:outs]
        self.last = (min(results, key=lambda x: x.size * x.dtype.itemsize),)
        self.pending = ()
        return results


def attend(chain, q, k, v, terms, scalars, width, causal, block, swapped):
    specs, arrays = part_specs(q, k, v, 0)
    rows = arrays[0].shape[0]
    tq, ts = (sum(x.shape[1] for x in one[0]) for one in (q, k))
    return chain.launch(
        functools.partial(
            forward_kernel, counts=[len(x[0]) for x in (q, k, v)], causal=causal, block=block,
            swapped=swapped,
        ),
        scalars,
        (rows, width // LANES),
        specs + [shared_spec(tq), shared_spec(ts)],
        [*arrays, *terms],
        [head_spec(tq, 0), head_spec(tq, 0)],
        [jax.ShapeDtypeStruct((rows, tq, width), BF)] * 2,
        scratch=[pltpu.VMEM((2, n, LANES), BF) for n in (ts, ts, tq)],
        us=21,
    )


def attend_back(
    chain, q, k, v, g, o, extra, terms, scalars, first, pairs, causal, block, swapped, held=()
):
    specs, arrays = part_specs(q, k, v, first)
    rows, _, width = o.shape
    tq, ts = (sum(x.shape[1] for x in one[0]) for one in (q, k))
    return chain.launch(
        functools.partial(
            backward_kernel, counts=[len(x[0]) for x in (q, k, v)], causal=causal, block=block,
            swapped=swapped, scaling=HD**-0.5,
        ),
        scalars,
        (rows, pairs),
        specs + [head_spec(tq, first)] * 3 + [shared_spec(ts)],
        [*arrays, g, o, extra, terms[1]],
        [head_spec(tq, first), head_spec(ts, first), head_spec(ts, first)],
        [jax.ShapeDtypeStruct((rows, n, width), BF) for n in (tq, ts, ts)],
        scratch=[pltpu.VMEM((2, n, LANES), BF) for n in (ts, ts, tq, tq)]
        + [
            pltpu.VMEM((LANES, ts), BF),
            pltpu.VMEM((2, ts, LANES), F32),
            pltpu.VMEM((2, ts, LANES), F32),
            pltpu.VMEM((LANES, tq), F32),
        ],
        us=6 * pairs,
        held=held,
    )


def norm(resid):
    center = resid - jnp.mean(resid, -1, keepdims=True)
    inverse = lax.rsqrt(jnp.mean(center * center, -1, keepdims=True) + norm_epsilon)
    return center * inverse, inverse


def norm_back(upstream, normed, inverse, gain_vec):
    w = upstream * gain_vec
    return (
        w - jnp.mean(w, -1, keepdims=True) - normed * jnp.mean(w * normed, -1, keepdims=True)
    ) * inverse


def gelu_parts(pre):
    bell = jnp.exp(pre * pre * -0.5)
    t = 1.0 / (1.0 + jnp.abs(pre) * (0.3275911 * 0.5**0.5))
    poly = 0.5 * 1.061405429
    for c in (-1.453152027, 1.421413741, -0.284496736, 0.254829592):
        poly = poly * t + 0.5 * c
    tail = poly * t * bell
    phi_sum = jnp.where(pre >= 0, 1.0 - tail, tail)
    return pre * phi_sum, phi_sum + pre * (bell * 0.3989422804014327)


def add_rows(sums_ref, first, rows):
    for index, value in enumerate(rows):
        here = slice(first + index, first + index + 1)
        sums_ref[here, :] += jnp.sum(value.astype(F32), 0, keepdims=True)


def finish_rows(sums_ref, out_ref):
    @pl.when(pl.program_id(0) == pl.num_programs(0) - 1)
    def _():
        out_ref[...] = sums_ref[...].T


def clear(ref):
    @pl.when(pl.program_id(0) == 0)
    def _():
        ref[...] = jnp.zeros_like(ref)


def row(ref):
    return ref[...][None, :]


def project_kernel(x_ref, *refs, scaled, carried):
    if carried:
        refs[-1][...] = refs[0][...]
        refs = refs[1:-1]
    w_ref, b_ref, out_ref = refs
    width = b_ref.shape[0] // 3
    y = dot(x_ref[...], w_ref[...]) + row(b_ref)
    if scaled:
        out_ref[:, :width] = (y[:, :width] * HD**-0.5).astype(BF)
        out_ref[:, width:] = y[:, width:].astype(BF)
    else:
        out_ref[...] = y.astype(BF)


def after_self_kernel(
    o_ref, x_ref, w_ref, b_ref, gain_ref, bias_ref, qw_ref, qb_ref, n1_ref, i1_ref, h1b_ref, cq_ref,
):
    resid = x_ref[...].astype(F32) + (dot(o_ref[...], w_ref[...]) + row(b_ref))
    n1, i1 = norm(resid)
    h1b = (n1 * row(gain_ref) + row(bias_ref)).astype(BF)
    n1_ref[...] = n1
    i1_ref[...] = jnp.broadcast_to(i1, i1_ref.shape)
    h1b_ref[...] = h1b
    cq_ref[...] = ((dot(h1b, qw_ref[...]) + row(qb_ref)) * HD**-0.5).astype(BF)


def middle_kernel(
    o_ref, n1_ref, up_ref, g1_ref, s1_ref, ow_ref, ob_ref, g2_ref, s2_ref,
    w1_ref, b1_ref, w2_ref, b2_ref, g3_ref, s3_ref,
    *refs, chunk, kept_blocks,
):
    *outs, act_ref, dbf_ref, h2b_ref, dpre_ref, dr2_ref, dbc_ref, dco_ref, sums_ref, slope, sums = refs
    clear(sums)
    h1 = n1_ref[...] * row(g1_ref) + row(s1_ref)
    n2, i2 = norm(h1 + (dot(o_ref[...], ow_ref[...]) + row(ob_ref)))
    h2 = n2 * row(g2_ref) + row(s2_ref)
    h2b = h2.astype(BF)
    h2b_ref[...] = h2b
    hidden = w1_ref.shape[1]
    cols = [slice(c, c + chunk) for c in range(0, hidden, chunk)]
    bias1 = row(b1_ref)
    branch = row(b2_ref)
    for c in cols:
        pre = dot(h2b, w1_ref[:, c]) + bias1[:, c]
        value, slope_c = gelu_parts(pre)
        slope[:, c] = slope_c
        act_c = value.astype(BF)
        act_ref[:, c] = act_c
        branch = branch + dot(act_c, w2_ref[c, :])
    n3, i3 = norm(h2 + branch)
    out = (n3 * row(g3_ref) + row(s3_ref)).astype(BF)
    store_halves(outs, out, kept_blocks)
    up = up_ref[...].astype(F32)
    dr3 = norm_back(up, n3, i3, row(g3_ref))
    dbf = dr3.astype(BF)
    dbf_ref[...] = dbf
    dh2 = dr3
    for c in cols:
        dpre_c = (dot(dbf, w2_ref[c, :], NT) * slope[:, c]).astype(BF)
        dpre_ref[:, c] = dpre_c
        dh2 = dh2 + dot(dpre_c, w1_ref[:, c], NT)
    dr2 = norm_back(dh2, n2, i2, row(g2_ref))
    dbc = dr2.astype(BF)
    dr2_ref[...] = dr2
    dbc_ref[...] = dbc
    dco_ref[...] = dot(dbc, ow_ref[...], NT).astype(BF)
    add_rows(sums, MID_ROWS, (up * n3, up, dbf, dh2 * n2, dh2))
    finish_rows(sums, sums_ref)


def before_self_kernel(
    dcq_ref, dr2_ref, n1_ref, i1_ref, qw_ref, g1_ref, ow_ref, dr1_ref, dba_ref, dso_ref, sums_ref,
    sums,
):
    clear(sums)
    n1 = n1_ref[...]
    dh1 = dr2_ref[...] + dot(dcq_ref[...], qw_ref[...], NT)
    dr1 = norm_back(dh1, n1, i1_ref[:, 0:1], row(g1_ref))
    dba = dr1.astype(BF)
    dr1_ref[...] = dr1
    dba_ref[...] = dba
    dso_ref[...] = dot(dba, ow_ref[...], NT).astype(BF)
    add_rows(sums, LOW_ROWS, (dh1 * n1, dh1))
    finish_rows(sums, sums_ref)


def input_grad_kernel(*refs, count, start, kept_blocks):
    grads, w_ref, outs = refs[:count], refs[count + start], refs[count + start + 1 :]
    total = refs[count][...] if start else None
    width = grads[0].shape[-1]
    for index, ref in enumerate(grads):
        part = dot(ref[...], w_ref[:, index * width : (index + 1) * width], NT)
        total = part if total is None else total + part
    store_halves(outs, total, kept_blocks)


def store_halves(outs, value, kept_blocks):
    if kept_blocks is None:
        outs[0][...] = value.astype(outs[0].dtype)
        return
    step = pl.program_id(0)

    @pl.when(step < kept_blocks)
    def _():
        outs[0][...] = value.astype(outs[0].dtype)

    @pl.when(step >= kept_blocks)
    def _():
        outs[1][...] = value.astype(outs[1].dtype)


class Joined:
    def __init__(self, kept, got, use_kept):
        self.kept, self.got, self.use_kept = kept, got, use_kept

    def __getitem__(self, index):
        return jnp.where(self.use_kept, self.kept[index], self.got[index])


def token_call(chain, kernel, block, blocked, whole, outs, scalars, scratch=(), vmem=24, us=5):
    def length(x):
        if not isinstance(x, tuple):
            return x.shape[0]
        return x[0].shape[1] * (1 if x[1] is None or isinstance(x[1], str) else 2)

    tokens = length(blocked[0])
    half = tokens // block // 2
    count = tokens // block
    in_specs, arrays, kinds = [], [], []
    for x in blocked:
        if not isinstance(x, tuple):
            in_specs.append(pl.BlockSpec((block, x.shape[1]), lambda i, _: (i, 0)))
            arrays.append(x)
            kinds.append(1)
            continue
        stack, got = x
        shape = (pl.Squeezed(), block, stack.shape[2])
        if got is None or isinstance(got, str):
            row = (lambda p: 1 - p[0]) if got else (lambda p: p[0])
            in_specs.append(pl.BlockSpec(shape, lambda i, p, row=row: (row(p), i, 0)))
            arrays.append(stack)
            kinds.append(1)
        else:
            in_specs.append(pl.BlockSpec(shape, lambda i, p: (p[0], jnp.minimum(i, half - 1), 0)))
            in_specs.append(
                pl.BlockSpec(shape[1:], lambda i, p: (jnp.maximum(i - half, 0), 0))
            )
            arrays += [stack, got]
            kinds.append(2)
    for x in whole:
        zeros = (0,) * x.ndim
        in_specs.append(
            pl.BlockSpec(x.shape, lambda i, _, z=zeros: z, pipeline_mode=pl.Buffered(1))
        )
    out_specs, out_shape = [], []
    for out in outs:
        if out[0] == "whole":
            out_specs.append(pl.BlockSpec(out[1:3], lambda i, _: (0, 0)))
            shape = out[1:3]
        elif out[0] == "kept":
            shape = (out[1], tokens // 2, out[2])
            out_specs.append(
                pl.BlockSpec(
                    (pl.Squeezed(), block, out[2]),
                    lambda i, p: (p[0], jnp.minimum(i, half - 1), 0),
                )
            )
        elif out[0] == "sent":
            shape = (tokens // 2, out[1])
            out_specs.append(
                pl.BlockSpec((block, out[1]), lambda i, _: (jnp.maximum(i - half, 0), 0))
            )
        else:
            shape = (count * block, out[0])
            out_specs.append(pl.BlockSpec((block, out[0]), lambda i, _: (i, 0)))
        out_shape.append(jax.ShapeDtypeStruct(shape, out[-1]))

    def run(_, *refs):
        used = []
        for kind in kinds:
            if kind == 1:
                used.append(refs[0])
            else:
                used.append(Joined(refs[0], refs[1], pl.program_id(0) < half))
            refs = refs[kind:]
        kernel(*used, *refs)

    return chain.launch(
        run, scalars, (count,), in_specs, [*arrays, *whole], out_specs, out_shape, scratch, vmem, us,
        free=len(whole),
    )


def store_kernel(_, got_ref, out_ref, mark_ref):
    out_ref[...] = got_ref[...].astype(out_ref.dtype)
    mark_ref[...] = jnp.zeros_like(mark_ref)


def store_other(chain, held, got, scalars):
    n, c = got.shape
    return chain.launch(
        store_kernel,
        scalars,
        (2,),
        [pl.BlockSpec((n // 2, c), lambda i, _: (i, 0))],
        [got],
        [
            pl.BlockSpec((pl.Squeezed(), n // 2, c), lambda i, p: (1 - p[0], i, 0)),
            pl.BlockSpec((8, LANES), lambda i, _: (0, 0)),
        ],
        [jax.ShapeDtypeStruct(held.shape, held.dtype), jax.ShapeDtypeStruct((8, LANES), F32)],
        vmem=16,
        us=3,
        held=(held,),
    )


MID_ROWS, LOW_ROWS = 8, 16


def weight_grads(chain, items, extras, scalars, wide, order):
    first_left = items[0][0]
    m = (first_left[0] if isinstance(first_left, tuple) else first_left).shape[-1]
    block = min(item[3] for item in items)
    block = min(block, m)
    specs, arrays, steps = [], [], []
    known = {}
    for left, right, start, columns, sum_row in items:
        key = id(left)
        if key not in known:
            known[key] = (len(arrays), isinstance(left, tuple))
            if isinstance(left, tuple):
                stack, got = left
                specs.append(
                    pl.BlockSpec(
                        (pl.Squeezed(),) + stack.shape[1:], lambda j, p: (p[0], 0, 0),
                        pipeline_mode=pl.Buffered(1),
                    )
                )
                arrays.append(stack)
                left = got
            specs.append(
                pl.BlockSpec(left.shape, lambda j, p: (0, 0), pipeline_mode=pl.Buffered(1))
            )
            arrays.append(left)
        begin, blocks = len(steps), columns // block
        where = len(arrays)
        specs.append(
            pl.BlockSpec(
                (right.shape[0], block),
                lambda j, p, b=begin, n=blocks, f=start // block: (0, f + jnp.clip(j - b, 0, n - 1)),
            )
        )
        arrays.append(right)
        for index in range(blocks):
            steps.append((known[key], where, sum_row, start + index * block, right.shape[1]))
    for extra in extras:
        specs.append(
            pl.BlockSpec(extra.shape, lambda j, p: (0, 0), pipeline_mode=pl.Buffered(1))
        )
    slab = m // len(order)
    size = m // wide
    apart = len(order) > 1
    slabs = len(order) // 2

    def kernel(scalar_ref, *refs):
        ins, rest = refs[: len(arrays)], refs[len(arrays) :]
        extra_refs, (*outs, sums) = rest[: len(extras)], rest[len(extras) :]
        clear(sums)
        step = pl.program_id(0)

        def store(value):
            if not apart:
                outs[0][...] = value.astype(BF)
                return
            core = scalar_ref[CORE]
            for to in range(slabs):
                halves = [
                    value[order[at] * slab : (order[at] + 1) * slab].astype(BF)
                    for at in (to, slabs + to)
                ]
                here = slice(to * slab, (to + 1) * slab)
                outs[0][here, :] = jnp.where(core == 0, halves[1], halves[0])
                outs[1][here, :] = jnp.where(core == 0, halves[0], halves[1])

        for index, ((left, split), right, sum_row, column, columns) in enumerate(steps):

            @pl.when(step == index)
            def _():
                grad = ins[right][...]
                if split:
                    half = ins[left].shape[0]
                    value = dot(ins[left][...], grad[:half], TN)
                    value = value + dot(ins[left + 1][...], grad[half:], TN)
                else:
                    value = dot(ins[left][...], grad, TN)
                store(value)
                if sum_row is None:
                    return
                total = jnp.sum(grad.astype(F32), 0, keepdims=True)
                if columns == m:
                    sums[sum_row : sum_row + 1, column : column + block] = total
                    return
                for piece in range(block // size):
                    w, k = divmod(column // size + piece, columns // m)
                    sums[sum_row + k : sum_row + k + 1, w * size : (w + 1) * size] = total[
                        :, piece * size : (piece + 1) * size
                    ]

        @pl.when(step == len(steps))
        def _():
            value = sums[...].T
            for ref in extra_refs:
                value = value + ref[...]
            store(jnp.concatenate([value, jnp.zeros((m, block - LANES), F32)], 1))

    n = block * len(steps) + LANES
    rows = m // 2 if apart else m
    return chain.launch(
        kernel,
        scalars,
        (len(steps) + 1,),
        specs,
        [*arrays, *extras],
        [pl.BlockSpec((rows, block), lambda j, _: (0, j))] * (m // rows),
        [jax.ShapeDtypeStruct((rows, n), BF)] * (m // rows),
        scratch=[pltpu.VMEM((LANES, m), F32)],
        us=max(4, n // 400),
    )


def tall_grad(chain, left, right, scalars, order):
    tokens, rows = left.shape
    width = right.shape[1]
    apart = len(order) > 1
    blocks = len(order) if apart else 4
    size = rows // blocks
    half = blocks // 2

    def source(j, s):
        if not apart:
            return j
        to = jnp.where(s[CORE] == 0, (j + half) % blocks, j)
        block = 0
        for at, slab in enumerate(order):
            block = jnp.where(to == at, slab, block)
        return block

    def kernel(_, left_ref, right_ref, *refs):
        value = dot(left_ref[...], right_ref[...], TN).astype(BF)
        if not apart:
            refs[-1][...] = value
            return
        other, own = refs[-2:]

        @pl.when(pl.program_id(0) < half)
        def _():
            other[...] = value

        @pl.when(pl.program_id(0) >= half)
        def _():
            own[...] = value

    if apart:
        out_specs = [
            pl.BlockSpec((size, width), lambda j, _: (jnp.minimum(j, half - 1), 0)),
            pl.BlockSpec((size, width), lambda j, _: (jnp.maximum(j - half, 0), 0)),
        ]
        out_shape = [jax.ShapeDtypeStruct((rows // 2, width), BF)] * 2
    else:
        out_specs = [pl.BlockSpec((size, width), lambda j, _: (j, 0))]
        out_shape = [jax.ShapeDtypeStruct((rows, width), BF)]
    return chain.launch(
        kernel,
        scalars,
        (blocks,),
        [
            pl.BlockSpec((tokens, size), lambda j, s: (0, source(j, s))),
            pl.BlockSpec(right.shape, lambda j, _: (0, 0), pipeline_mode=pl.Buffered(1)),
        ],
        [left, right],
        out_specs,
        out_shape,
        us=9,
    )


def vector_rows(x, columns, outs):
    turned = x.astype(F32).T
    for (start, count), out in zip(columns, outs):
        rows = [turned[start + i] for i in range(count)]
        out[...] = rows[0] if count == 1 else jnp.concatenate(rows)


def widen(chain, groups, pieces, columns, scalars):
    arrays = [x for group in groups for x in group]
    size = groups[0][0].shape[0]

    def kernel(s, *refs):
        ins, outs = refs[: len(arrays)], refs[len(arrays) :]
        matrices, vectors = outs[: len(pieces)], outs[len(pieces) :]
        step = pl.program_id(0)
        which = (
            4 * (step // 4 != s[CORE]).astype(jnp.int32)
            + 2 * (step // 2 % 2 != s[SIDE]).astype(jnp.int32)
            + (step % 2 != s[NEAR]).astype(jnp.int32)
        )
        for index in range(8):

            @pl.when(which == index)
            def _():
                for out, parts in zip(matrices, pieces):
                    at = 0
                    for group, start, count in parts:
                        piece = ins[8 * group + index][:, start : start + count]
                        out[:, at : at + count] = piece.astype(F32)
                        at += count

        if columns:

            @pl.when(step == 7)
            def _():
                def place(position):
                    bits = (position // 4, position // 2 % 2, position % 2)
                    total = None
                    for index in range(8):
                        same = None
                        for bit, flip, axis in zip(bits, (index // 4, index // 2 % 2, index % 2), (CORE, SIDE, NEAR)):
                            equal = s[axis] == (bit ^ flip)
                            same = equal if same is None else same & equal
                        value = sum(
                            ins[8 * group + index][:, x[0].shape[1] - LANES :].astype(F32)
                            for group, x in enumerate(groups)
                        )
                        value = jnp.where(same, value, 0.0)
                        total = value if total is None else total + value
                    return total

                vector_rows(jnp.concatenate([place(p) for p in range(8)], 0), columns, vectors)

    widths = [sum(p[2] for p in parts) for parts in pieces]
    lengths = [count * 8 * size for _, count in columns]
    return chain.launch(
        kernel,
        scalars,
        (8,),
        [
            pl.BlockSpec(x.shape, lambda i, _: (0, 0), pipeline_mode=pl.Buffered(1))
            for x in arrays
        ],
        arrays,
        [pl.BlockSpec((size, w), lambda i, _: (i, 0)) for w in widths]
        + [pl.BlockSpec((n,), lambda i, _: (0,)) for n in lengths],
        [jax.ShapeDtypeStruct((8 * size, w), F32) for w in widths]
        + [jax.ShapeDtypeStruct((n,), F32) for n in lengths],
        vmem=24,
        us=4,
        free=len(arrays),
    )


def vectors_kernel(x_ref, *outs, columns):
    vector_rows(x_ref[...], columns, outs)


def vectors_of(x, columns):
    return pl.pallas_call(
        functools.partial(vectors_kernel, columns=columns),
        out_shape=[jax.ShapeDtypeStruct((count * x.shape[0],), F32) for _, count in columns],
    )(x)


def partner(x, axis, bit=1):
    count = lax.axis_size(axis)
    return lax.ppermute(x, axis, [(i, i ^ bit) for i in range(count)])


def partner_both(x):
    return lax.ppermute(x, ("near", "side"), [(i, 3 - i) for i in range(4)])


ROWS = ("far", "near", "side", "core")


class Reduction:
    def __init__(self, chain, arrays, order):
        self.arrays = arrays
        self.steps = []
        if len(arrays) == 2:
            self.steps = list(order)
            self.terms = [(arrays[1], ()), (partner(arrays[0], "core"), ())]
            chain.active.append(self)

    def total(self, turned=None):
        value = 0.0
        for x, path in self.terms:
            index, parts = 0, 1
            for axis in path:
                index, parts = 2 * index + lax.axis_index(axis), 2 * parts
            if turned:
                index, parts = 2 * index + 1 - lax.axis_index(turned), 2 * parts
            rows = x.shape[0] // parts
            value = value + lax.dynamic_slice_in_dim(x, index * rows, rows, 0).astype(F32)
        return value.astype(BF)

    def exchange(self):
        step = self.steps.pop(0)
        if step == "spread":
            sent = self.total()
            near, side, both = partner(sent, "near"), partner(sent, "side"), partner_both(sent)
            self.pieces = [sent, near, side, both]
        elif step == "join":
            self.pieces += [partner(x, "core") for x in self.pieces]
            sent = self.pieces[1]
        elif step == "far":
            sent = self.total()
            if lax.axis_size("far") == 2:
                self.terms.append((partner(sent, "far"), ()))
        else:
            sent = self.total(step)
            self.terms = [(x, path + (step,)) for x, path in self.terms]
            self.terms.append((partner(sent, step), ()))
        return sent

    def result(self):
        x = lax.psum_scatter(self.arrays[0], "wide", scatter_dimension=0, tiled=True)
        return lax.psum(x, ROWS)


CORE_WIDE = (0, 2, 1, 3)
CORE_SIDE = (0, 4, 1, 5, 2, 6, 3, 7)
X_FIRST = ("wide", "side", "near", "far", "spread", "join")
Y_FIRST = ("side", "wide", "near", "far", "spread", "join")


def body(
    target, encoded, segments, out_grad,
    self_qkv_w, self_q_b, self_v_b, self_out_w, self_out_b, norm1_gain, norm1_bias,
    cross_q_w, cross_q_b, cross_kv_w, cross_v_b, cross_out_w, cross_out_b, norm2_gain, norm2_bias,
    ffn_in_w, ffn_in_b, ffn_out_w, ffn_out_b, norm3_gain, norm3_bias,
):
    row_count, tok_count, width = target.shape
    hidden = ffn_in_w.shape[1]
    parts = hidden // width
    pairs = width // LANES
    wide = lax.axis_size("wide")
    index = lax.axis_index("wide").astype(jnp.int32)
    scalars = jnp.stack(
        [index]
        + [lax.axis_index(a).astype(jnp.int32) for a in ("core", "side", "near")]
        + [index * tok_count]
    )
    swapped = wide == 2 and row_count == 2
    split = swapped and all(lax.axis_size(a) == 2 for a in ("side", "near", "core"))
    core_wide = CORE_WIDE if split else (0,)
    core_side = CORE_SIDE if split else (0,)
    tokens = row_count * tok_count
    block = min(256, tok_count)
    kept_blocks = tok_count // block if swapped else None

    chain = Chain()

    def run(call, *args, **kwargs):
        return call(chain, *args, **kwargs)

    if swapped:
        def bring(x):
            return x, partner(lax.dynamic_index_in_dim(x, 1 - index, 0, keepdims=False), "wide")

        causal, block_f, block_b = "block", 2 * block, block
        seg_kept, seg_got = bring(segments)
        seg = jnp.concatenate(
            [lax.dynamic_index_in_dim(seg_kept, index, 0, keepdims=False), seg_got]
        )[None]
        key_seg = seg
        row_tokens = tokens
    else:
        def bring(x):
            return x.reshape(tokens, -1)

        causal, block_f, block_b = "mask", block, block
        seg = segments
        key_seg = lax.all_gather(segments, "wide", axis=1, tiled=True)
        row_tokens = tok_count
    terms = (segment_terms(seg)[0], segment_terms(key_seg)[1])

    def by_row(x):
        return x.reshape(-1, row_tokens, x.shape[-1])

    def flat(x):
        return x.reshape(-1, x.shape[-1])

    def keys_of(x):
        return lax.all_gather(x, "wide", axis=1, tiled=True)

    def key_grads(x):
        return x if swapped else lax.psum_scatter(x, "wide", scatter_dimension=1, tiled=True)

    def project(x, w, bias, scaled, carried=None):
        outs = [(w.shape[1], BF)]
        if carried is not None:
            outs.append((carried.shape[-1], BF))
        out = run(
            token_call, functools.partial(project_kernel, scaled=scaled, carried=len(outs) == 2),
            block, (x,) if carried is None else (x, (carried, "other")), (w, bias), outs, scalars,
            us=3,
        )
        y = out[0][None] if swapped else by_row(out[0])
        return y if carried is None else (y, (carried, partner(out[1], "wide")))

    def attention(q, k, v, is_causal):
        return run(
            attend, q, k, v, terms, scalars, width, causal if is_causal else "no", block_f, swapped
        )

    def attention_back(q, k, v, g, o, extra, is_causal, first, count, held=()):
        return run(
            attend_back, q, k, v, by_row(g), o, extra, terms, scalars, first, count,
            causal if is_causal else "no", block_b, swapped, held,
        )

    def input_grad(grads, w, start=None):
        blocked = list(grads) + ([] if start is None else [start])
        outs = [("kept", 2, width, F32), ("sent", width, BF)] if swapped else [(width, F32)]
        kernel = functools.partial(
            input_grad_kernel, count=len(grads), start=0 if start is None else 1,
            kept_blocks=kept_blocks,
        )
        out = run(
            token_call, kernel, block, blocked, (w,), outs, scalars
        )
        return out[0], out[-1]

    def send_back(x):
        return partner(x, "wide") if swapped else None

    def give(out, got):
        if not swapped:
            return out.reshape(row_count, tok_count, width)
        return run(store_other, out, got, scalars)[0]

    def exchange(*reductions):
        if split:
            chain.pending += tuple(r.exchange() for r in reductions)

    zeros = jnp.zeros_like(self_q_b)
    qkv_bias = jnp.concatenate([self_q_b, zeros, self_v_b])
    ckv_bias = jnp.concatenate([zeros, cross_v_b])
    x_in = bring(target)
    if swapped:
        ckv = [project((encoded, None), cross_kv_w, ckv_bias, False)]
        qkv = [project((target, None), self_qkv_w, qkv_bias, True)]
        chain.pending += terms
        got, x_enc = project(x_in[1], self_qkv_w, qkv_bias, True, encoded)
        qkv.append(got)
        self_q, self_k, self_v = (qkv, 0), (qkv, width), (qkv, 2 * width)
    else:
        x_enc, upstream = bring(encoded), bring(out_grad)
        ckv = [keys_of(project(x_enc, cross_kv_w, ckv_bias, False))]
        qkv = [project(x_in, self_qkv_w, qkv_bias, True)]
        both = [keys_of(qkv[0][..., width:])]
        self_q, self_k, self_v = (qkv, 0), (both, 0), (both, width)
    self_o, self_x = attention(self_q, self_k, self_v, True)
    self_ob = flat(self_o)
    n1, i1, h1b, cq = run(
        token_call, after_self_kernel, block, (self_ob, x_in),
        (self_out_w, self_out_b, norm1_gain, norm1_bias, cross_q_w, cross_q_b),
        [(width, F32), (LANES, F32), (width, BF), (width, BF)], scalars,
    )
    if swapped:
        got, upstream = project(x_enc[1], cross_kv_w, ckv_bias, False, out_grad)
        ckv.append(got)
    cross_q, cross_k, cross_v = ([by_row(cq)], 0), (ckv, 0), (ckv, width)
    cross_o, cross_x = attention(cross_q, cross_k, cross_v, False)
    cross_ob = flat(cross_o)
    outs = [("kept", 2, width, BF), ("sent", width, BF)] if swapped else [(width, BF)]
    *h3, act, dbf, h2b, dpre, dr2, dbc, dco, mid_sums = run(
        token_call, functools.partial(middle_kernel, chunk=width, kept_blocks=kept_blocks),
        block, (cross_ob, n1, upstream),
        (
            norm1_gain, norm1_bias, cross_out_w, cross_out_b, norm2_gain, norm2_bias,
            ffn_in_w, ffn_in_b, ffn_out_w, ffn_out_b, norm3_gain, norm3_bias,
        ),
        outs
        + [
            (hidden, BF), (width, BF), (width, BF), (hidden, BF), (width, F32),
            (width, BF), (width, BF), ("whole", width, LANES, F32),
        ],
        scalars,
        scratch=[pltpu.VMEM((block, hidden), F32), pltpu.VMEM((LANES, width), F32)],
        vmem=56,
        us=45,
    )
    got_out = send_back(h3[-1])

    rb = Reduction(
        chain, run(
            weight_grads, [(h2b, dpre, 0, hidden, 0), (cross_ob, dbc, 0, width, parts)],
            [mid_sums], scalars, wide, core_side,
        ),
        Y_FIRST,
    )
    ra = Reduction(
        chain, run(tall_grad, act, dbf, scalars, core_wide), X_FIRST
    )
    exchange(ra)
    exchange(rb)
    cross_args = (cross_q, cross_k, cross_v, dco, cross_o, cross_x, False)
    dcq, dck, dcv = attention_back(*cross_args, 0, pairs)
    dcq, dck, dcv = flat(dcq), flat(key_grads(dck)), flat(key_grads(dcv))
    exchange(ra)
    exchange(rb)
    layer_out = give(h3[0], got_out)
    rc = Reduction(
        chain,
        run(
            weight_grads,
            [(h1b, dcq, 0, width, 0), (x_enc, dck, 0, width, None), (x_enc, dcv, 0, width, 1)],
            [], scalars, wide, core_side,
        ),
        Y_FIRST,
    )
    dr1, dba, dso, low_sums = run(
        token_call, before_self_kernel, block, (dcq, dr2, n1, i1),
        (cross_q_w, norm1_gain, self_out_w),
        [(width, F32), (width, BF), (width, BF), ("whole", width, LANES, F32)], scalars,
        scratch=[pltpu.VMEM((LANES, width), F32)],
    )
    exchange(rc)
    exchange(ra)
    exchange(rb)
    enc_kept, enc_sent = input_grad([dck, dcv], cross_kv_w)
    got_enc = send_back(enc_sent)
    exchange(ra)
    exchange(rb)
    cut = pairs // 2
    self_args = (self_q, self_k, self_v, dso, self_o, self_x, True)
    first = attention_back(*self_args, 0, cut if swapped else pairs)
    dsq, dsk, dsv = (flat(x) for x in first)
    exchange(rc)
    exchange(ra, rb)
    if swapped:
        one, two = cut * LANES, width - cut * LANES
        rd = Reduction(
                chain, run(
                weight_grads,
                [
                    (self_ob, dba, 0, width, 2),
                    (x_in, dsq, 0, one, 0), (x_in, dsk, 0, one, None), (x_in, dsv, 0, one, 1),
                ],
                [low_sums], scalars, wide, core_wide,
            ),
            X_FIRST,
        )
        exchange(rd)
        exchange(rc)
        second = attention_back(*self_args, cut, pairs - cut, first)
        dsq, dsk, dsv = (flat(x) for x in second)
        exchange(rd)
        exchange(ra, rb)
        re = Reduction(
                chain, run(
                weight_grads,
                [(x_in, dsq, one, two, 0), (x_in, dsk, one, two, None), (x_in, dsv, one, two, 1)],
                [], scalars, wide, core_wide,
            ),
            X_FIRST,
        )
        exchange(rc)
        exchange(re)
    else:
        encoded_grad = give(enc_kept, got_enc)
        dsk, dsv = (
            flat(key_grads(x.reshape(row_count, -1, width))) for x in (dsk, dsv)
        )
        rd = Reduction(
                chain, run(
                weight_grads, [(self_ob, dba, 0, width, 2)], [low_sums], scalars, wide, core_wide
            ),
            X_FIRST,
        )
        re = Reduction(
                chain, run(
                weight_grads,
                [(x_in, dsq, 0, width, 0), (x_in, dsk, 0, width, None), (x_in, dsv, 0, width, 1)],
                [], scalars, wide, core_wide,
            ),
            X_FIRST,
        )
    in_kept, in_sent = input_grad([dsq, dsk, dsv], self_qkv_w, dr1)
    got_in = send_back(in_sent)

    vectors_b = [(0, parts), (parts, 1)] + [(MID_ROWS + i, 1) for i in range(5)]
    vectors_c = [(0, 1), (1, 1)]
    vectors_d = [(0, 1), (1, 1), (2, 1), (LOW_ROWS, 1), (LOW_ROWS + 1, 1)]
    pieces_b = [[(0, 0, hidden)], [(0, hidden, width)]]
    pieces_c = [[(0, 0, width)], [(0, width, 2 * width)]]
    if split:
        exchange(rd)
        exchange(re)
        (ffn_out_w_grad,) = run(widen, [ra.pieces], [[(0, 0, width)]], [], scalars)
        exchange(rc)
        exchange(rd)
        exchange(re)
        out_b = run(widen, [rb.pieces], pieces_b, vectors_b, scalars)
        exchange(rd)
        exchange(re)
        encoded_grad = give(enc_kept, got_enc)
        exchange(rc)
        exchange(rd)
        out_c = run(widen, [rc.pieces], pieces_c, vectors_c, scalars)
        exchange(re)
        target_grad = give(in_kept, got_in)
        exchange(re)
        pieces_d = [[(0, 0, width)], []]
        for i in range(3):
            pieces_d[1] += [(0, width + i * one, one), (1, i * two, two)]
        out_d = run(widen, [rd.pieces, re.pieces], pieces_d, vectors_d, scalars)
    else:
        target_grad = give(in_kept, got_in)

        def columns_of(x, pieces, vectors):
            return [
                jnp.concatenate([x[:, start : start + size] for _, start, size in p], 1).astype(F32)
                for p in pieces
            ] + list(vectors_of(x[:, -LANES:], vectors))

        ffn_out_w_grad = ra.result().astype(F32)
        out_b = columns_of(rb.result(), pieces_b, vectors_b)
        out_c = columns_of(rc.result(), pieces_c, vectors_c)
        low = rd.result()
        high = re.result()
        both = jnp.concatenate(
            [low[:, :width], high[:, : 3 * width], low[:, -LANES:] + high[:, -LANES:]], 1
        )
        out_d = columns_of(both, [[(0, 0, width)], [(0, width, 3 * width)]], vectors_d)
    (
        ffn_in_w_grad, cross_out_w_grad, ffn_in_b_grad, cross_out_b_grad, norm3_gain_grad,
        norm3_bias_grad, ffn_out_b_grad, norm2_gain_grad, norm2_bias_grad,
    ) = out_b
    cross_q_w_grad, cross_kv_w_grad, cross_q_b_grad, cross_v_b_grad = out_c
    (
        self_out_w_grad, self_qkv_w_grad, self_q_b_grad, self_v_b_grad, self_out_b_grad,
        norm1_gain_grad, norm1_bias_grad,
    ) = out_d
    return (
        layer_out, target_grad, encoded_grad,
        self_qkv_w_grad, self_q_b_grad, self_v_b_grad,
        self_out_w_grad, self_out_b_grad, norm1_gain_grad, norm1_bias_grad,
        cross_q_w_grad, cross_q_b_grad, cross_kv_w_grad, cross_v_b_grad,
        cross_out_w_grad, cross_out_b_grad, norm2_gain_grad, norm2_bias_grad,
        ffn_in_w_grad, ffn_in_b_grad, ffn_out_w_grad, ffn_out_b_grad,
        norm3_gain_grad, norm3_bias_grad,
    )


def solution(mesh):
    wide, narrow = mesh.shape["wide"], mesh.shape["narrow"]
    core = 2 if narrow % 2 == 0 else 1
    side = 2 if narrow % (2 * core) == 0 else 1
    near = 2 if narrow % (2 * core * side) == 0 else 1
    devices = mesh.devices.reshape(wide, narrow // (near * side * core), near, side, core)
    split = Mesh(devices, ("wide",) + ROWS)
    token_spec = P(ROWS, "wide", None)
    in_specs = (token_spec, token_spec, P(ROWS, "wide"), token_spec) + (P(),) * 21
    matrix, vector = P("wide", None), P("wide")
    out_specs = (token_spec,) * 3 + (
        matrix, vector, vector, matrix, vector, vector, vector,
        matrix, vector, matrix, vector, matrix, vector, vector, vector,
        matrix, vector, matrix, vector, vector, vector,
    )
    return jax.shard_map(body, mesh=split, in_specs=in_specs, out_specs=out_specs, check_vma=False)
```

```python
import functools

import jax
import jax.numpy as jnp
from jax import lax
from jax.experimental import pallas as pl
from jax.experimental.pallas import tpu as pltpu
from jax.sharding import Mesh, PartitionSpec as P

HD = 64
LANES = 128
WIDE, CORE, SIDE, NEAR, SHIFT = range(5)
MB = 2**20
norm_epsilon = 1e-05
masked_score = -1e9
BF = jnp.bfloat16
F32 = jnp.float32

NN = (((1,), (0,)), ((), ()))
NT = (((1,), (1,)), ((), ()))
TN = (((0,), (0,)), ((), ()))


def dot(a, b, dims=NN):
    return lax.dot_general(a, b, dims, preferred_element_type=F32)


def segment_terms(seg):
    lane = jnp.arange(LANES) % HD
    same = seg[..., None] == lane
    query_terms = jnp.where((lane < 4) & ~same, masked_score, 0.0).astype(BF)
    key_terms = jnp.where(((lane < 4) & same) | ((lane >= 4) & (lane < 7)), 1.0, 0.0).astype(BF)
    return query_terms, key_terms


def head_lanes(shape, head):
    lane = lax.broadcasted_iota(jnp.int32, shape, 1)
    return (lane < HD) if head == 0 else (lane >= HD)


def causal_scores(scores, causal, first_query, block, query_axis):
    if causal == "block":
        queries = lax.broadcasted_iota(jnp.int32, (block, block), query_axis)
        keys = lax.broadcasted_iota(jnp.int32, (block, block), 1 - query_axis)
        count = scores.shape[1 - query_axis]
        before = lax.slice_in_dim(scores, 0, count - block, axis=1 - query_axis)
        corner = lax.slice_in_dim(scores, count - block, count, axis=1 - query_axis)
        corner = jnp.where(keys <= queries, corner, masked_score)
        if count == block:
            return corner
        return jnp.concatenate([before, corner], 1 - query_axis)
    if causal == "mask":
        queries = first_query + lax.broadcasted_iota(jnp.int32, scores.shape, query_axis)
        keys = lax.broadcasted_iota(jnp.int32, scores.shape, 1 - query_axis)
        return jnp.where(keys <= queries, scores, masked_score)
    return scores


def in_order(parts, shift, half, there):
    if len(parts) == 1:
        return parts[0][there, :]
    return jnp.where(shift == 0, parts[half][...], parts[1 - half][...])


def array_places(count, shift, swapped):
    if not swapped:
        return [(slice(0, count), slice(0, count))]
    half = count // 2
    return [
        (
            slice(part * half, (part + 1) * half),
            pl.ds(pl.multiple_of(lax.rem(part * half + shift, count), half), half),
        )
        for part in (0, 1)
    ]


def row_block(index, block, count, shift, swapped):
    if not swapped:
        return pl.ds(index * block, block)
    return pl.ds(pl.multiple_of(lax.rem(index * block + shift, count), block), block)


def split_parts(refs, counts):
    groups = []
    for count in counts:
        groups.append(refs[:count])
        refs = refs[count:]
    return groups, refs


def forward_kernel(*refs, counts, causal, block, swapped):
    scalars, refs = refs[0], refs[1:]
    (q_parts, k_parts, v_parts), refs = split_parts(refs, counts)
    qt_ref, kt_ref = refs[:2]
    o_ref, qx_ref, ka, va, qa = refs[2:]
    tq, ts = qa.shape[1], ka.shape[1]
    shift = scalars[SHIFT]
    for part, (here, there) in enumerate(array_places(ts, shift, swapped)):
        k = in_order(k_parts, shift, part, there)
        v = in_order(v_parts, shift, part, there)
        extra = kt_ref[there, :]
        for head in (0, 1):
            own = head_lanes(k.shape, head)
            ka[head, here, :] = jnp.where(own, k, extra)
            va[head, here, :] = jnp.where(own, v, extra)
    for part, (here, there) in enumerate(array_places(tq, shift, swapped)):
        q = in_order(q_parts, shift, part, there)
        extra = qt_ref[there, :]
        for head in (0, 1):
            qa[head, here, :] = jnp.where(head_lanes(q.shape, head), q, extra)
    lane = lax.broadcasted_iota(jnp.int32, (block, LANES), 1)
    for index in range(tq // block):
        count = (index + 1) * block if causal == "block" else ts
        there = row_block(index, block, tq, shift, swapped)
        outs, extra = [], qt_ref[there, :].astype(F32)
        rows = slice(index * block, (index + 1) * block)
        both = [dot(qa[head, rows, :], ka[head, :count, :], NT) for head in (0, 1)]
        for head in (0, 1):
            scores = causal_scores(both[head], causal, shift + index * block, block, 0)
            top = jnp.max(scores, 1, keepdims=True)
            weights = jnp.exp(scores - top).astype(BF)
            sums = dot(weights, va[head, :count, :])
            at = HD + 4 if head == 0 else 4
            total = sums[:, at + 2 : at + 3]
            outs.append(sums / total)
            for i, piece in enumerate(three_parts(-(top + jnp.log(total)))):
                extra = jnp.where(lane == at + i, piece, extra)
        o_ref[there, :] = jnp.where(lane < HD, outs[0], outs[1]).astype(BF)
        qx_ref[there, :] = extra.astype(BF)


def three_parts(x):
    parts = []
    for _ in range(3):
        part = x.astype(BF).astype(F32)
        parts.append(part)
        x = x - part
    return parts


def backward_kernel(*refs, counts, causal, block, swapped, scaling):
    scalars, refs = refs[0], refs[1:]
    (q_parts, k_parts, v_parts), refs = split_parts(refs, counts)
    g_ref, o_ref, qx_ref, kt_ref = refs[:4]
    (
        dq_ref, dk_ref, dv_ref, ka, va, qa, ga, k_turned, dk_sum, dv_sum, dq_turned,
    ) = refs[4:]
    tq, ts = qa.shape[1], ka.shape[1]
    shift = scalars[SHIFT]
    for part, (here, there) in enumerate(array_places(ts, shift, swapped)):
        k = in_order(k_parts, shift, part, there)
        v = in_order(v_parts, shift, part, there)
        extra = kt_ref[there, :]
        for head in (0, 1):
            own = head_lanes(k.shape, head)
            ka[head, here, :] = jnp.where(own, k, extra)
            va[head, here, :] = jnp.where(own, v, extra)
        k_turned[:, here] = k.astype(F32).T.astype(BF)
    source = lax.broadcasted_iota(jnp.int32, (LANES, LANES), 0)
    target = lax.broadcasted_iota(jnp.int32, (LANES, LANES), 1)
    rides = (target % HD >= 4) & (target % HD < 7) & ((source < HD) == (target >= HD))
    spread = jnp.where(rides, -1.0, 0.0).astype(BF)
    for part, (here, there) in enumerate(array_places(tq, shift, swapped)):
        q = in_order(q_parts, shift, part, there)
        g, extra = g_ref[there, :], qx_ref[there, :]
        products = g.astype(F32) * o_ref[there, :].astype(F32)
        rough = products.astype(BF)
        delta = dot(rough, spread) + dot((products - rough.astype(F32)).astype(BF), spread)
        lane = lax.broadcasted_iota(jnp.int32, q.shape, 1) % HD
        pieces = three_parts(delta)
        g_extra = jnp.where(lane == 4, pieces[0], jnp.where(lane == 5, pieces[1], pieces[2]))
        g_extra = g_extra.astype(BF)
        for head in (0, 1):
            own = head_lanes(q.shape, head)
            qa[head, here, :] = jnp.where(own, q, extra)
            ga[head, here, :] = jnp.where(own, g, g_extra)
    blocks = tq // block
    for index in reversed(range(blocks)):
        count = (index + 1) * block if causal == "block" else ts
        rows = slice(index * block, (index + 1) * block)
        for head in (0, 1):
            q, g = qa[head, rows, :], ga[head, rows, :]
            scores = dot(ka[head, :count, :], q, NT)
            scores = causal_scores(scores, causal, shift + index * block, block, 1)
            probs = jnp.exp(scores)
            grads = (probs * dot(va[head, :count, :], g, NT)).astype(BF)
            dv, dk = dot(probs.astype(BF), g), dot(grads, q)
            if index == blocks - 1:
                dv_sum[head, :count, :] = dv
                dk_sum[head, :count, :] = dk
            else:
                dv_sum[head, :count, :] += dv
                dk_sum[head, :count, :] += dk
            own_rows = slice(HD * head, HD * (head + 1))
            dq_turned[own_rows, rows] = dot(k_turned[own_rows, :count], grads)
        there = row_block(index, block, tq, shift, swapped)
        dq_ref[there, :] = dq_turned[:, rows].T.astype(BF) * jnp.asarray(scaling, BF)
    for here, there in array_places(ts, shift, swapped):
        own = head_lanes((here.stop - here.start, LANES), 0)
        dk_ref[there, :] = jnp.where(own, dk_sum[0, here, :], dk_sum[1, here, :]).astype(BF)
        dv_ref[there, :] = jnp.where(own, dv_sum[0, here, :], dv_sum[1, here, :]).astype(BF)


ANYWHERE = pl.BlockSpec(memory_space=pl.ANY)


def stay(*arrays):
    return [pltpu.with_memory_space_constraint(x, pltpu.HBM) for x in arrays]


def head_spec(count, start):
    return pl.BlockSpec((pl.Squeezed(), count, LANES), lambda row, pair, _: (row, 0, start + pair))


def shared_spec(count):
    return pl.BlockSpec((pl.Squeezed(), count, LANES), lambda row, pair, _: (row, 0, 0))


def part_specs(q, k, v, first):
    specs, arrays = [], []
    for parts, column in (q, k, v):
        for x in parts:
            specs.append(head_spec(x.shape[1], column // LANES + first))
            arrays.append(x)
    return specs, arrays


class Chain:
    def __init__(self):
        self.last = ()

    def launch(
        self, kernel, scalars, grid, in_specs, arrays, out_specs, out_shape, scratch=(), vmem=48,
        us=5, held=(), free=0,
    ):
        ins = len(arrays)
        arrays = [*stay(*arrays[: ins - free]), *arrays[ins - free :]]
        extra = stay(*held, *self.last)

        outs = len(out_shape)

        def run(scalar_ref, *refs):
            rest = refs[ins + len(extra) :]
            kernel(scalar_ref, *refs[:ins], *rest[:outs], *rest[outs + 1 :])
            rest[outs][...] = jnp.zeros((8, LANES), F32)

        mark = pl.BlockSpec((8, LANES), lambda *_: (0, 0))

        results = pl.pallas_call(
            run,
            grid_spec=pltpu.PrefetchScalarGridSpec(
                num_scalar_prefetch=1,
                grid=grid,
                in_specs=list(in_specs) + [ANYWHERE] * len(extra),
                out_specs=[*out_specs, mark],
                scratch_shapes=list(scratch),
            ),
            out_shape=[pltpu.HBM(x.shape, x.dtype) for x in out_shape]
            + [pltpu.HBM((8, LANES), F32)],
            input_output_aliases={1 + ins + i: i for i in range(len(held))},
            compiler_params=pltpu.CompilerParams(vmem_limit_bytes=vmem * MB),
            cost_estimate=pl.CostEstimate(
                flops=0, bytes_accessed=us * 72000, transcendentals=0
            ),
        )(scalars, *arrays, *extra)
        self.last = (results[-1],)
        return results[:-1]

    def after_last(self, *arrays):
        *arrays, last = lax.optimization_barrier((*arrays, *self.last))
        self.last = (last,)
        return arrays


def attend(chain, q, k, v, terms, scalars, width, causal, block, swapped):
    specs, arrays = part_specs(q, k, v, 0)
    rows = arrays[0].shape[0]
    tq, ts = (sum(x.shape[1] for x in one[0]) for one in (q, k))
    return chain.launch(
        functools.partial(
            forward_kernel, counts=[len(x[0]) for x in (q, k, v)], causal=causal, block=block,
            swapped=swapped,
        ),
        scalars,
        (rows, width // LANES),
        specs + [shared_spec(tq), shared_spec(ts)],
        [*arrays, *terms],
        [head_spec(tq, 0), head_spec(tq, 0)],
        [jax.ShapeDtypeStruct((rows, tq, width), BF)] * 2,
        scratch=[pltpu.VMEM((2, n, LANES), BF) for n in (ts, ts, tq)],
        us=21,
    )


def attend_back(
    chain, q, k, v, g, o, extra, terms, scalars, first, pairs, causal, block, swapped, held=()
):
    specs, arrays = part_specs(q, k, v, first)
    rows, _, width = o.shape
    tq, ts = (sum(x.shape[1] for x in one[0]) for one in (q, k))
    return chain.launch(
        functools.partial(
            backward_kernel, counts=[len(x[0]) for x in (q, k, v)], causal=causal, block=block,
            swapped=swapped, scaling=HD**-0.5,
        ),
        scalars,
        (rows, pairs),
        specs + [head_spec(tq, first)] * 3 + [shared_spec(ts)],
        [*arrays, g, o, extra, terms[1]],
        [head_spec(tq, first), head_spec(ts, first), head_spec(ts, first)],
        [jax.ShapeDtypeStruct((rows, n, width), BF) for n in (tq, ts, ts)],
        scratch=[pltpu.VMEM((2, n, LANES), BF) for n in (ts, ts, tq, tq)]
        + [
            pltpu.VMEM((LANES, ts), BF),
            pltpu.VMEM((2, ts, LANES), F32),
            pltpu.VMEM((2, ts, LANES), F32),
            pltpu.VMEM((LANES, tq), F32),
        ],
        us=6 * pairs,
        held=held,
    )


def norm(resid):
    center = resid - jnp.mean(resid, -1, keepdims=True)
    inverse = lax.rsqrt(jnp.mean(center * center, -1, keepdims=True) + norm_epsilon)
    return center * inverse, inverse


def norm_back(upstream, normed, inverse, gain_vec):
    w = upstream * gain_vec
    return (
        w - jnp.mean(w, -1, keepdims=True) - normed * jnp.mean(w * normed, -1, keepdims=True)
    ) * inverse


def gelu_parts(pre):
    bell = jnp.exp(pre * pre * -0.5)
    t = 1.0 / (1.0 + jnp.abs(pre) * (0.3275911 * 0.5**0.5))
    poly = 0.5 * 1.061405429
    for c in (-1.453152027, 1.421413741, -0.284496736, 0.254829592):
        poly = poly * t + 0.5 * c
    tail = poly * t * bell
    phi_sum = jnp.where(pre >= 0, 1.0 - tail, tail)
    return pre * phi_sum, phi_sum + pre * (bell * 0.3989422804014327)


def add_rows(sums_ref, first, rows):
    for index, value in enumerate(rows):
        here = slice(first + index, first + index + 1)
        sums_ref[here, :] += jnp.sum(value.astype(F32), 0, keepdims=True)


def finish_rows(sums_ref, out_ref):
    @pl.when(pl.program_id(0) == pl.num_programs(0) - 1)
    def _():
        out_ref[...] = sums_ref[...].T


def clear(ref):
    @pl.when(pl.program_id(0) == 0)
    def _():
        ref[...] = jnp.zeros_like(ref)


def row(ref):
    return ref[...][None, :]


def project_kernel(x_ref, *refs, scaled, carried):
    if carried:
        refs[-1][...] = refs[0][...]
        refs = refs[1:-1]
    w_ref, b_ref, out_ref = refs
    width = b_ref.shape[0] // 3
    y = dot(x_ref[...], w_ref[...]) + row(b_ref)
    if scaled:
        out_ref[:, :width] = (y[:, :width] * HD**-0.5).astype(BF)
        out_ref[:, width:] = y[:, width:].astype(BF)
    else:
        out_ref[...] = y.astype(BF)


def after_self_kernel(
    o_ref, x_ref, w_ref, b_ref, gain_ref, bias_ref, qw_ref, qb_ref, n1_ref, i1_ref, h1b_ref, cq_ref,
):
    resid = x_ref[...].astype(F32) + (dot(o_ref[...], w_ref[...]) + row(b_ref))
    n1, i1 = norm(resid)
    h1b = (n1 * row(gain_ref) + row(bias_ref)).astype(BF)
    n1_ref[...] = n1
    i1_ref[...] = jnp.broadcast_to(i1, i1_ref.shape)
    h1b_ref[...] = h1b
    cq_ref[...] = ((dot(h1b, qw_ref[...]) + row(qb_ref)) * HD**-0.5).astype(BF)


def middle_kernel(
    o_ref, n1_ref, up_ref, g1_ref, s1_ref, ow_ref, ob_ref, g2_ref, s2_ref,
    w1_ref, b1_ref, w2_ref, b2_ref, g3_ref, s3_ref,
    *refs, chunk, kept_blocks,
):
    *outs, act_ref, dbf_ref, h2b_ref, dpre_ref, dr2_ref, dbc_ref, dco_ref, sums_ref, slope, sums = refs
    clear(sums)
    h1 = n1_ref[...] * row(g1_ref) + row(s1_ref)
    n2, i2 = norm(h1 + (dot(o_ref[...], ow_ref[...]) + row(ob_ref)))
    h2 = n2 * row(g2_ref) + row(s2_ref)
    h2b = h2.astype(BF)
    h2b_ref[...] = h2b
    hidden = w1_ref.shape[1]
    cols = [slice(c, c + chunk) for c in range(0, hidden, chunk)]
    bias1 = row(b1_ref)
    branch = row(b2_ref)
    for c in cols:
        pre = dot(h2b, w1_ref[:, c]) + bias1[:, c]
        value, slope_c = gelu_parts(pre)
        slope[:, c] = slope_c
        act_c = value.astype(BF)
        act_ref[:, c] = act_c
        branch = branch + dot(act_c, w2_ref[c, :])
    n3, i3 = norm(h2 + branch)
    out = (n3 * row(g3_ref) + row(s3_ref)).astype(BF)
    store_halves(outs, out, kept_blocks)
    up = up_ref[...].astype(F32)
    dr3 = norm_back(up, n3, i3, row(g3_ref))
    dbf = dr3.astype(BF)
    dbf_ref[...] = dbf
    dh2 = dr3
    for c in cols:
        dpre_c = (dot(dbf, w2_ref[c, :], NT) * slope[:, c]).astype(BF)
        dpre_ref[:, c] = dpre_c
        dh2 = dh2 + dot(dpre_c, w1_ref[:, c], NT)
    dr2 = norm_back(dh2, n2, i2, row(g2_ref))
    dbc = dr2.astype(BF)
    dr2_ref[...] = dr2
    dbc_ref[...] = dbc
    dco_ref[...] = dot(dbc, ow_ref[...], NT).astype(BF)
    add_rows(sums, MID_ROWS, (up * n3, up, dbf, dh2 * n2, dh2))
    finish_rows(sums, sums_ref)


def before_self_kernel(
    dcq_ref, dr2_ref, n1_ref, i1_ref, qw_ref, g1_ref, ow_ref, dr1_ref, dba_ref, dso_ref, sums_ref,
    sums,
):
    clear(sums)
    n1 = n1_ref[...]
    dh1 = dr2_ref[...] + dot(dcq_ref[...], qw_ref[...], NT)
    dr1 = norm_back(dh1, n1, i1_ref[:, 0:1], row(g1_ref))
    dba = dr1.astype(BF)
    dr1_ref[...] = dr1
    dba_ref[...] = dba
    dso_ref[...] = dot(dba, ow_ref[...], NT).astype(BF)
    add_rows(sums, LOW_ROWS, (dh1 * n1, dh1))
    finish_rows(sums, sums_ref)


def input_grad_kernel(*refs, count, start, kept_blocks):
    grads, w_ref, outs = refs[:count], refs[count + start], refs[count + start + 1 :]
    total = refs[count][...] if start else None
    width = grads[0].shape[-1]
    for index, ref in enumerate(grads):
        part = dot(ref[...], w_ref[:, index * width : (index + 1) * width], NT)
        total = part if total is None else total + part
    store_halves(outs, total, kept_blocks)


def store_halves(outs, value, kept_blocks):
    if kept_blocks is None:
        outs[0][...] = value.astype(outs[0].dtype)
        return
    step = pl.program_id(0)

    @pl.when(step < kept_blocks)
    def _():
        outs[0][...] = value.astype(outs[0].dtype)

    @pl.when(step >= kept_blocks)
    def _():
        outs[1][...] = value.astype(outs[1].dtype)


class Joined:
    def __init__(self, kept, got, use_kept):
        self.kept, self.got, self.use_kept = kept, got, use_kept

    def __getitem__(self, index):
        return jnp.where(self.use_kept, self.kept[index], self.got[index])


def token_call(
    chain, kernel, block, blocked, whole, outs, scalars, scratch=(), vmem=24, us=5, free=True
):
    def length(x):
        if not isinstance(x, tuple):
            return x.shape[0]
        return x[0].shape[1] * (1 if x[1] is None or isinstance(x[1], str) else 2)

    tokens = length(blocked[0])
    half = tokens // block // 2
    count = tokens // block
    in_specs, arrays, kinds = [], [], []
    for x in blocked:
        if not isinstance(x, tuple):
            in_specs.append(pl.BlockSpec((block, x.shape[1]), lambda i, _: (i, 0)))
            arrays.append(x)
            kinds.append(1)
            continue
        stack, got = x
        shape = (pl.Squeezed(), block, stack.shape[2])
        if got is None or isinstance(got, str):
            row = (lambda p: 1 - p[0]) if got else (lambda p: p[0])
            in_specs.append(pl.BlockSpec(shape, lambda i, p, row=row: (row(p), i, 0)))
            arrays.append(stack)
            kinds.append(1)
        else:
            in_specs.append(pl.BlockSpec(shape, lambda i, p: (p[0], jnp.minimum(i, half - 1), 0)))
            in_specs.append(
                pl.BlockSpec(shape[1:], lambda i, p: (jnp.maximum(i - half, 0), 0))
            )
            arrays += [stack, got]
            kinds.append(2)
    for x in whole:
        zeros = (0,) * x.ndim
        in_specs.append(
            pl.BlockSpec(x.shape, lambda i, _, z=zeros: z, pipeline_mode=pl.Buffered(1))
        )
    out_specs, out_shape = [], []
    for out in outs:
        if out[0] == "whole":
            out_specs.append(pl.BlockSpec(out[1:3], lambda i, _: (0, 0)))
            shape = out[1:3]
        elif out[0] == "kept":
            shape = (out[1], tokens // 2, out[2])
            out_specs.append(
                pl.BlockSpec(
                    (pl.Squeezed(), block, out[2]),
                    lambda i, p: (p[0], jnp.minimum(i, half - 1), 0),
                )
            )
        elif out[0] == "sent":
            shape = (tokens // 2, out[1])
            out_specs.append(
                pl.BlockSpec((block, out[1]), lambda i, _: (jnp.maximum(i - half, 0), 0))
            )
        else:
            shape = (count * block, out[0])
            out_specs.append(pl.BlockSpec((block, out[0]), lambda i, _: (i, 0)))
        out_shape.append(jax.ShapeDtypeStruct(shape, out[-1]))

    def run(_, *refs):
        used = []
        for kind in kinds:
            if kind == 1:
                used.append(refs[0])
            else:
                used.append(Joined(refs[0], refs[1], pl.program_id(0) < half))
            refs = refs[kind:]
        kernel(*used, *refs)

    return chain.launch(
        run, scalars, (count,), in_specs, [*arrays, *whole], out_specs, out_shape, scratch, vmem, us,
        free=len(whole) if free else 0,
    )


def store_kernel(_, got_ref, out_ref):
    out_ref[...] = got_ref[...].astype(out_ref.dtype)


def store_other(chain, held, got, scalars):
    n, c = got.shape
    return chain.launch(
        store_kernel,
        scalars,
        (2,),
        [pl.BlockSpec((n // 2, c), lambda i, _: (i, 0))],
        [got],
        [pl.BlockSpec((pl.Squeezed(), n // 2, c), lambda i, p: (1 - p[0], i, 0))],
        [jax.ShapeDtypeStruct(held.shape, held.dtype)],
        vmem=16,
        us=3,
        held=(held,),
    )


MID_ROWS, LOW_ROWS = 8, 16


def weight_grads(chain, items, extras, scalars, wide, order):
    first_left = items[0][0]
    m = (first_left[0] if isinstance(first_left, tuple) else first_left).shape[-1]
    block = min(item[3] for item in items)
    block = min(block, m)
    specs, arrays, steps = [], [], []
    known = {}
    for left, right, start, columns, sum_row in items:
        key = id(left)
        if key not in known:
            known[key] = (len(arrays), isinstance(left, tuple))
            if isinstance(left, tuple):
                stack, got = left
                specs.append(
                    pl.BlockSpec(
                        (pl.Squeezed(),) + stack.shape[1:], lambda j, p: (p[0], 0, 0),
                        pipeline_mode=pl.Buffered(1),
                    )
                )
                arrays.append(stack)
                left = got
            specs.append(
                pl.BlockSpec(left.shape, lambda j, p: (0, 0), pipeline_mode=pl.Buffered(1))
            )
            arrays.append(left)
        begin, blocks = len(steps), columns // block
        where = len(arrays)
        specs.append(
            pl.BlockSpec(
                (right.shape[0], block),
                lambda j, p, b=begin, n=blocks, f=start // block: (0, f + jnp.clip(j - b, 0, n - 1)),
            )
        )
        arrays.append(right)
        for index in range(blocks):
            steps.append((known[key], where, sum_row, start + index * block, right.shape[1]))
    for extra in extras:
        specs.append(
            pl.BlockSpec(extra.shape, lambda j, p: (0, 0), pipeline_mode=pl.Buffered(1))
        )
    slab = m // len(order)
    size = m // wide
    apart = len(order) > 1
    slabs = len(order) // 2

    def kernel(scalar_ref, *refs):
        ins, rest = refs[: len(arrays)], refs[len(arrays) :]
        extra_refs, (*outs, sums) = rest[: len(extras)], rest[len(extras) :]
        clear(sums)
        step = pl.program_id(0)

        def store(value):
            if not apart:
                outs[0][...] = value.astype(BF)
                return
            core = scalar_ref[CORE]
            for to in range(slabs):
                halves = [
                    value[order[at] * slab : (order[at] + 1) * slab].astype(BF)
                    for at in (to, slabs + to)
                ]
                here = slice(to * slab, (to + 1) * slab)
                outs[0][here, :] = jnp.where(core == 0, halves[1], halves[0])
                outs[1][here, :] = jnp.where(core == 0, halves[0], halves[1])

        for index, ((left, split), right, sum_row, column, columns) in enumerate(steps):

            @pl.when(step == index)
            def _():
                grad = ins[right][...]
                if split:
                    half = ins[left].shape[0]
                    value = dot(ins[left][...], grad[:half], TN)
                    value = value + dot(ins[left + 1][...], grad[half:], TN)
                else:
                    value = dot(ins[left][...], grad, TN)
                store(value)
                if sum_row is None:
                    return
                total = jnp.sum(grad.astype(F32), 0, keepdims=True)
                if columns == m:
                    sums[sum_row : sum_row + 1, column : column + block] = total
                    return
                for piece in range(block // size):
                    w, k = divmod(column // size + piece, columns // m)
                    sums[sum_row + k : sum_row + k + 1, w * size : (w + 1) * size] = total[
                        :, piece * size : (piece + 1) * size
                    ]

        @pl.when(step == len(steps))
        def _():
            value = sums[...].T
            for ref in extra_refs:
                value = value + ref[...]
            store(jnp.concatenate([value, jnp.zeros((m, block - LANES), F32)], 1))

    n = block * len(steps) + LANES
    rows = m // 2 if apart else m
    return chain.launch(
        kernel,
        scalars,
        (len(steps) + 1,),
        specs,
        [*arrays, *extras],
        [pl.BlockSpec((rows, block), lambda j, _: (0, j))] * (m // rows),
        [jax.ShapeDtypeStruct((rows, n), BF)] * (m // rows),
        scratch=[pltpu.VMEM((LANES, m), F32)],
        us=max(4, n // 400),
    )


def tall_grad(chain, left, right, scalars, order):
    tokens, rows = left.shape
    width = right.shape[1]
    apart = len(order) > 1
    blocks = len(order) if apart else 4
    size = rows // blocks
    half = blocks // 2

    def source(j, s):
        if not apart:
            return j
        to = jnp.where(s[CORE] == 0, (j + half) % blocks, j)
        block = 0
        for at, slab in enumerate(order):
            block = jnp.where(to == at, slab, block)
        return block

    def kernel(_, left_ref, right_ref, *refs):
        value = dot(left_ref[...], right_ref[...], TN).astype(BF)
        if not apart:
            refs[-1][...] = value
            return
        other, own = refs[-2:]

        @pl.when(pl.program_id(0) < half)
        def _():
            other[...] = value

        @pl.when(pl.program_id(0) >= half)
        def _():
            own[...] = value

    if apart:
        out_specs = [
            pl.BlockSpec((size, width), lambda j, _: (jnp.minimum(j, half - 1), 0)),
            pl.BlockSpec((size, width), lambda j, _: (jnp.maximum(j - half, 0), 0)),
        ]
        out_shape = [jax.ShapeDtypeStruct((rows // 2, width), BF)] * 2
    else:
        out_specs = [pl.BlockSpec((size, width), lambda j, _: (j, 0))]
        out_shape = [jax.ShapeDtypeStruct((rows, width), BF)]
    return chain.launch(
        kernel,
        scalars,
        (blocks,),
        [
            pl.BlockSpec((tokens, size), lambda j, s: (0, source(j, s))),
            pl.BlockSpec(right.shape, lambda j, _: (0, 0), pipeline_mode=pl.Buffered(1)),
        ],
        [left, right],
        out_specs,
        out_shape,
        us=9,
    )


def vector_rows(x, columns, outs):
    turned = x.astype(F32).T
    for (start, count), out in zip(columns, outs):
        rows = [turned[start + i] for i in range(count)]
        out[...] = rows[0] if count == 1 else jnp.concatenate(rows)


def widen(chain, groups, pieces, columns, scalars):
    pairs = len(groups[0]) == 2
    arrays = [x for group in groups for x in group]
    rows = groups[0][0].shape[0] * len(groups[0])
    size = rows // 8
    specs = [
        pl.BlockSpec(x.shape, lambda i, _: (0, 0), pipeline_mode=pl.Buffered(1)) for x in arrays
    ]

    def convert(ins, outs, index):
        step = pl.program_id(0)
        for out, parts in zip(outs, pieces):
            at = 0
            for group, start, count in parts:
                cols = slice(start, start + count)
                if pairs:
                    here = pl.ds(pl.multiple_of(step % 4 * size, size), size)
                    piece = ins[2 * group + index][here, cols]
                else:
                    piece = ins[8 * group + index][:, cols]
                out[:, at : at + count] = piece.astype(F32)
                at += count

    def extra_of(ins, s):
        count = len(groups[0])
        places = []
        for position in range(count):
            total = 0.0
            for index in range(count):
                flips = position ^ index
                if pairs:
                    same = s[CORE] == flips
                else:
                    same = (
                        (s[CORE] == flips // 4)
                        & (s[SIDE] == flips // 2 % 2)
                        & (s[NEAR] == flips % 2)
                    )
                value = sum(
                    ins[count * group + index][:, x[0].shape[1] - LANES :].astype(F32)
                    for group, x in enumerate(groups)
                )
                total = total + jnp.where(same, value, 0.0)
            places.append(total)
        return jnp.concatenate(places, 0)

    def kernel(s, *refs):
        ins, outs = refs[: len(arrays)], refs[len(arrays) :]
        matrices, vectors = outs[: len(pieces)], outs[len(pieces) :]
        step = pl.program_id(0)
        which = (step // 4 != s[CORE]).astype(jnp.int32)
        if not pairs:
            which = (
                4 * which
                + 2 * (step // 2 % 2 != s[SIDE]).astype(jnp.int32)
                + (step % 2 != s[NEAR]).astype(jnp.int32)
            )
        for index in range(len(groups[0])):

            @pl.when(which == index)
            def _():
                convert(ins, matrices, index)

        if columns:

            @pl.when(step == 7)
            def _():
                vector_rows(extra_of(ins, s), columns, vectors)

    widths = [sum(p[2] for p in parts) for parts in pieces]
    lengths = [count * rows for _, count in columns]
    return chain.launch(
        kernel,
        scalars,
        (8,),
        specs,
        arrays,
        [pl.BlockSpec((size, w), lambda i, _: (i, 0)) for w in widths]
        + [pl.BlockSpec((n,), lambda i, _: (0,)) for n in lengths],
        [jax.ShapeDtypeStruct((rows, w), F32) for w in widths]
        + [jax.ShapeDtypeStruct((n,), F32) for n in lengths],
        vmem=24,
        us=4,
        free=len(arrays),
    )


def vectors_kernel(x_ref, *outs, columns):
    vector_rows(x_ref[...], columns, outs)


def vectors_of(x, columns):
    return pl.pallas_call(
        functools.partial(vectors_kernel, columns=columns),
        out_shape=[jax.ShapeDtypeStruct((count * x.shape[0],), F32) for _, count in columns],
    )(x)


def partner(x, axis, bit=1):
    count = lax.axis_size(axis)
    return lax.ppermute(x, axis, [(i, i ^ bit) for i in range(count)])


def partner_both(x):
    return lax.ppermute(x, ("near", "side"), [(i, 3 - i) for i in range(4)])


ROWS = ("far", "near", "side", "core")


class Reduction:
    def __init__(self, arrays, order):
        self.arrays = arrays
        self.steps = ["core", *order] if len(arrays) == 2 else []
        self.step, self.flying, self.terms = None, [], []

    def total(self, turned=None):
        value = 0.0
        for x, path in self.terms:
            index, parts = 0, 1
            for axis in path:
                index, parts = 2 * index + lax.axis_index(axis), 2 * parts
            if turned:
                index, parts = 2 * index + 1 - lax.axis_index(turned), 2 * parts
            rows = x.shape[0] // parts
            value = value + lax.dynamic_slice_in_dim(x, index * rows, rows, 0).astype(F32)
        return value.astype(BF)

    def land(self, got):
        if not got:
            return
        if self.step == "core":
            self.terms = [(self.arrays[1], ()), (got[0], ())]
        elif self.step in ("wide", "side", "near", "far"):
            self.terms += [(x, ()) for x in got]
        elif self.step == "spread":
            self.pieces = [self.sent, *got]
        elif self.step in JOINS:
            self.terms = [(self.sent, ()), (got[0], ())]
        self.flying = []

    def joined(self):
        (mine, _), (got, _) = self.terms
        first = lax.axis_index(self.step[5:]) == 0
        return jnp.concatenate([jnp.where(first, mine, got), jnp.where(first, got, mine)], 0)

    def prepare(self):
        last, self.step = self.step, self.steps.pop(0)
        if self.step == "core":
            return [self.arrays[0]]
        if last in JOINS:
            self.step, step = last, self.step
            sent = self.joined()
            self.step = step
            return [sent]
        if self.step in JOINS:
            return [self.total()]
        if self.step == "join":
            return self.pieces
        if self.step in ("far", "spread"):
            return [self.total()]
        sent = self.total(self.step)
        self.terms = [(x, path + (self.step,)) for x, path in self.terms]
        return [sent]

    def start(self, sent):
        if self.step in JOINS:
            self.sent = sent[0]
            self.flying = [partner(sent[0], self.step[5:])]
            self.pieces = [sent[0], *self.flying]
        elif self.step == "spread":
            self.sent = sent[0]
            self.flying = [
                partner(sent[0], "near"), partner(sent[0], "side"), partner_both(sent[0])
            ]
        elif self.step == "join":
            self.pieces = [*sent, *(partner(x, "core") for x in sent)]
        elif self.step != "far" or lax.axis_size("far") == 2:
            self.flying = [partner(sent[0], self.step)]

    def result(self):
        x = lax.psum_scatter(self.arrays[0], "wide", scatter_dimension=0, tiled=True)
        return lax.psum(x, ROWS)


CORE_WIDE = (0, 2, 1, 3)
CORE_SIDE = (0, 4, 1, 5, 2, 6, 3, 7)
X_FIRST = ("wide", "side", "near", "far", "spread", "join")
JOINS = ("join_near", "join_side", "join_core")
X_THEN_Y = ("wide", "side", "near", "far") + JOINS
Y_THEN_X = ("side", "wide", "near", "far") + JOINS


def body(
    target, encoded, segments, out_grad,
    self_qkv_w, self_q_b, self_v_b, self_out_w, self_out_b, norm1_gain, norm1_bias,
    cross_q_w, cross_q_b, cross_kv_w, cross_v_b, cross_out_w, cross_out_b, norm2_gain, norm2_bias,
    ffn_in_w, ffn_in_b, ffn_out_w, ffn_out_b, norm3_gain, norm3_bias,
):
    row_count, tok_count, width = target.shape
    hidden = ffn_in_w.shape[1]
    parts = hidden // width
    pairs = width // LANES
    wide = lax.axis_size("wide")
    index = lax.axis_index("wide").astype(jnp.int32)
    scalars = jnp.stack(
        [index]
        + [lax.axis_index(a).astype(jnp.int32) for a in ("core", "side", "near")]
        + [index * tok_count]
    )
    swapped = wide == 2 and row_count == 2
    split = swapped and all(lax.axis_size(a) == 2 for a in ("side", "near", "core"))
    core_wide = CORE_WIDE if split else (0,)
    core_side = CORE_SIDE if split else (0,)
    tokens = row_count * tok_count
    block = min(256, tok_count)
    kept_blocks = tok_count // block if swapped else None

    chain = Chain()

    def run(call, *args, **kwargs):
        return call(chain, *args, **kwargs)

    if swapped:
        def bring(x):
            return x, partner(lax.dynamic_index_in_dim(x, 1 - index, 0, keepdims=False), "wide")

        causal, block_f, block_b = "block", 2 * block, block
        seg_kept, seg_got = bring(segments)
        seg = jnp.concatenate(
            [lax.dynamic_index_in_dim(seg_kept, index, 0, keepdims=False), seg_got]
        )[None]
        key_seg = seg
        row_tokens = tokens
    else:
        def bring(x):
            return x.reshape(tokens, -1)

        causal, block_f, block_b = "mask", block, block
        seg = segments
        key_seg = lax.all_gather(segments, "wide", axis=1, tiled=True)
        row_tokens = tok_count
    terms = (segment_terms(seg)[0], segment_terms(key_seg)[1])

    def by_row(x):
        return x.reshape(-1, row_tokens, x.shape[-1])

    def flat(x):
        return x.reshape(-1, x.shape[-1])

    def keys_of(x):
        return lax.all_gather(x, "wide", axis=1, tiled=True)

    def key_grads(x):
        return x if swapped else lax.psum_scatter(x, "wide", scatter_dimension=1, tiled=True)

    def project(x, w, bias, scaled, carried=None):
        outs = [(w.shape[1], BF)]
        if carried is not None:
            outs.append((carried.shape[-1], BF))
        out = run(
            token_call, functools.partial(project_kernel, scaled=scaled, carried=len(outs) == 2),
            block, (x,) if carried is None else (x, (carried, "other")), (w, bias), outs, scalars,
            us=3,
        )
        y = out[0][None] if swapped else by_row(out[0])
        return y if carried is None else (y, (carried, partner(out[1], "wide")))

    def attention(q, k, v, is_causal):
        return run(
            attend, q, k, v, terms, scalars, width, causal if is_causal else "no", block_f, swapped
        )

    def attention_back(q, k, v, g, o, extra, is_causal, first, count, held=()):
        return run(
            attend_back, q, k, v, by_row(g), o, extra, terms, scalars, first, count,
            causal if is_causal else "no", block_b, swapped, held,
        )

    def input_grad(grads, w, start=None):
        blocked = list(grads) + ([] if start is None else [start])
        outs = [("kept", 2, width, F32), ("sent", width, BF)] if swapped else [(width, F32)]
        kernel = functools.partial(
            input_grad_kernel, count=len(grads), start=0 if start is None else 1,
            kept_blocks=kept_blocks,
        )
        out = run(
            token_call, kernel, block, blocked, (w,), outs, scalars
        )
        return out[0], out[-1]

    def send_back(x):
        return partner(x, "wide") if swapped else None

    def give(out, got):
        if not swapped:
            return out.reshape(row_count, tok_count, width)
        return run(store_other, out, got, scalars)[0]

    def arrive(*reductions, others=()):
        landed = chain.after_last(*others, *(x for r in reductions for x in r.flying))
        others, landed = landed[: len(others)], landed[len(others) :]
        for r in reductions:
            count = len(r.flying)
            r.land(landed[:count])
            landed = landed[count:]
        return others

    def exchange(*reductions, also=(), landing=()):
        if not split:
            return [send_back(x) for x in also] + list(landing)
        flying = [x for r in reductions for x in r.flying]
        landed = chain.after_last(*landing, *flying)
        landing, landed = landed[: len(landing)], landed[len(landing) :]
        for r in reductions:
            count = len(r.flying)
            r.land(landed[:count])
            landed = landed[count:]
        sent = [r.prepare() for r in reductions]
        flat_sent = chain.after_last(*(x for one in sent for x in one), *also)
        for r, one in zip(reductions, sent):
            r.start(flat_sent[: len(one)])
            flat_sent = flat_sent[len(one) :]
        return [send_back(x) for x in flat_sent] + list(landing)

    zeros = jnp.zeros_like(self_q_b)
    qkv_bias = jnp.concatenate([self_q_b, zeros, self_v_b])
    ckv_bias = jnp.concatenate([zeros, cross_v_b])
    x_in = bring(target)
    if swapped:
        ckv = [project((encoded, None), cross_kv_w, ckv_bias, False)]
        qkv = [project((target, None), self_qkv_w, qkv_bias, True)]
        terms = tuple(chain.after_last(*terms))
        got, x_enc = project(x_in[1], self_qkv_w, qkv_bias, True, encoded)
        qkv.append(got)
        self_q, self_k, self_v = (qkv, 0), (qkv, width), (qkv, 2 * width)
    else:
        x_enc, upstream = bring(encoded), bring(out_grad)
        ckv = [keys_of(project(x_enc, cross_kv_w, ckv_bias, False))]
        qkv = [project(x_in, self_qkv_w, qkv_bias, True)]
        both = [keys_of(qkv[0][..., width:])]
        self_q, self_k, self_v = (qkv, 0), (both, 0), (both, width)
    self_o, self_x = attention(self_q, self_k, self_v, True)
    self_ob = flat(self_o)
    n1, i1, h1b, cq = run(
        token_call, after_self_kernel, block, (self_ob, x_in),
        (self_out_w, self_out_b, norm1_gain, norm1_bias, cross_q_w, cross_q_b),
        [(width, F32), (LANES, F32), (width, BF), (width, BF)], scalars,
    )
    if swapped:
        got, upstream = project(x_enc[1], cross_kv_w, ckv_bias, False, out_grad)
        ckv.append(got)
    cross_q, cross_k, cross_v = ([by_row(cq)], 0), (ckv, 0), (ckv, width)
    cross_o, cross_x = attention(cross_q, cross_k, cross_v, False)
    cross_ob = flat(cross_o)
    outs = [("kept", 2, width, BF), ("sent", width, BF)] if swapped else [(width, BF)]
    *h3, act, dbf, h2b, dpre, dr2, dbc, dco, mid_sums = run(
        token_call, functools.partial(middle_kernel, chunk=width, kept_blocks=kept_blocks),
        block, (cross_ob, n1, upstream),
        (
            norm1_gain, norm1_bias, cross_out_w, cross_out_b, norm2_gain, norm2_bias,
            ffn_in_w, ffn_in_b, ffn_out_w, ffn_out_b, norm3_gain, norm3_bias,
        ),
        outs
        + [
            (hidden, BF), (width, BF), (width, BF), (hidden, BF), (width, F32),
            (width, BF), (width, BF), ("whole", width, LANES, F32),
        ],
        scalars,
        scratch=[pltpu.VMEM((block, hidden), F32), pltpu.VMEM((LANES, width), F32)],
        vmem=56,
        us=45,
    )

    rb = Reduction(
        run(
            weight_grads, [(h2b, dpre, 0, hidden, 0), (cross_ob, dbc, 0, width, parts)],
            [mid_sums], scalars, wide, core_side,
        ),
        Y_THEN_X,
    )
    exchange(rb)
    ra = Reduction(run(tall_grad, act, dbf, scalars, core_wide), X_THEN_Y)
    exchange(ra)
    exchange(ra, rb)
    dcq, dck, dcv = attention_back(
        cross_q, cross_k, cross_v, dco, cross_o, cross_x, False, 0, pairs
    )
    dcq, dck, dcv = flat(dcq), flat(key_grads(dck)), flat(key_grads(dcv))
    exchange(ra, rb)
    dr1, dba, dso, low_sums = run(
        token_call, before_self_kernel, block, (dcq, dr2, n1, i1),
        (cross_q_w, norm1_gain, self_out_w),
        [(width, F32), (width, BF), (width, BF), ("whole", width, LANES, F32)], scalars,
        scratch=[pltpu.VMEM((LANES, width), F32)],
        free=False,
    )
    rc = Reduction(
        run(
            weight_grads,
            [
                (h1b, dcq, 0, width, 0), (x_enc, dck, 0, width, None), (x_enc, dcv, 0, width, 1),
                (self_ob, dba, 0, width, 2),
            ],
            [low_sums], scalars, wide, core_side,
        ),
        Y_THEN_X,
    )
    (got_out,) = exchange(ra, rb, rc, also=(h3[-1],))
    self_args = (self_q, self_k, self_v, dso, self_o, self_x, True)
    if swapped:
        cut = pairs // 3
        held = attention_back(*self_args, 0, cut)
        exchange(ra, rb, rc)
        dsq, dsk, dsv = attention_back(*self_args, cut, pairs - cut, held)
    else:
        dsq, dsk, dsv = attention_back(*self_args, 0, pairs)
    dsq, dsk, dsv = flat(dsq), flat(key_grads(dsk)), flat(key_grads(dsv))
    rd = Reduction(
        run(
            weight_grads,
            [(x_in, dsq, 0, width, 0), (x_in, dsk, 0, width, None), (x_in, dsv, 0, width, 1)],
            [], scalars, wide, core_wide,
        ),
        X_FIRST,
    )
    (got_out,) = exchange(rd, ra, rb, rc, landing=(got_out,))
    in_kept, in_sent = input_grad([dsq, dsk, dsv], self_qkv_w, dr1)

    vectors_b = [(0, parts), (parts, 1)] + [(MID_ROWS + i, 1) for i in range(5)]
    vectors_c = [(0, 1), (1, 1), (2, 1), (LOW_ROWS, 1), (LOW_ROWS + 1, 1)]
    vectors_d = [(0, 1), (1, 1)]
    pieces_b = [[(0, 0, hidden)], [(0, hidden, width)]]
    pieces_c = [[(0, 0, width)], [(0, width, 2 * width)], [(0, 3 * width, width)]]
    if split:
        arrive(rd, ra, rb, rc)
        exchange(rd)
        exchange(ra, rc)
        enc_kept, enc_sent = input_grad([dck, dcv], cross_kv_w)
        layer_out = give(h3[0], got_out)
        arrive(rd, ra, rc)
        exchange(rd)
        (got_in,) = exchange(rc, rb, ra, also=(in_sent,))
        (ffn_out_w_grad,) = run(widen, [ra.pieces], [[(0, 0, width)]], [], scalars)
        exchange(rd)
        (got_enc,) = exchange(rc, also=(enc_sent,))
        (got_in,) = arrive(rd, others=(got_in,))
        exchange(rd)
        exchange(rc, rb)
        out_b = run(widen, [rb.pieces], pieces_b, vectors_b, scalars)
        (got_enc,) = arrive(rd, others=(got_enc,))
        exchange(rd)
        exchange(rc)
        target_grad = give(in_kept, got_in)
        encoded_grad = give(enc_kept, got_enc)
        exchange(rd)
        out_c = run(widen, [rc.pieces], pieces_c, vectors_c, scalars)
        pieces_d = [[(0, 0, 3 * width)]]
        out_d = run(widen, [rd.pieces], pieces_d, vectors_d, scalars)
    else:
        enc_kept, _ = input_grad([dck, dcv], cross_kv_w)
        layer_out, target_grad, encoded_grad = (
            give(x, None) for x in (h3[0], in_kept, enc_kept)
        )

        def columns_of(x, pieces, vectors):
            return [
                jnp.concatenate([x[:, start : start + size] for _, start, size in p], 1).astype(F32)
                for p in pieces
            ] + list(vectors_of(x[:, -LANES:], vectors))

        ffn_out_w_grad = ra.result().astype(F32)
        out_b = columns_of(rb.result(), pieces_b, vectors_b)
        out_c = columns_of(rc.result(), pieces_c, vectors_c)
        out_d = columns_of(rd.result(), [[(0, 0, 3 * width)]], vectors_d)
    (
        ffn_in_w_grad, cross_out_w_grad, ffn_in_b_grad, cross_out_b_grad, norm3_gain_grad,
        norm3_bias_grad, ffn_out_b_grad, norm2_gain_grad, norm2_bias_grad,
    ) = out_b
    (
        cross_q_w_grad, cross_kv_w_grad, self_out_w_grad, cross_q_b_grad, cross_v_b_grad,
        self_out_b_grad, norm1_gain_grad, norm1_bias_grad,
    ) = out_c
    self_qkv_w_grad, self_q_b_grad, self_v_b_grad = out_d
    return (
        layer_out, target_grad, encoded_grad,
        self_qkv_w_grad, self_q_b_grad, self_v_b_grad,
        self_out_w_grad, self_out_b_grad, norm1_gain_grad, norm1_bias_grad,
        cross_q_w_grad, cross_q_b_grad, cross_kv_w_grad, cross_v_b_grad,
        cross_out_w_grad, cross_out_b_grad, norm2_gain_grad, norm2_bias_grad,
        ffn_in_w_grad, ffn_in_b_grad, ffn_out_w_grad, ffn_out_b_grad,
        norm3_gain_grad, norm3_bias_grad,
    )


def solution(mesh):
    wide, narrow = mesh.shape["wide"], mesh.shape["narrow"]
    core = 2 if narrow % 2 == 0 else 1
    side = 2 if narrow % (2 * core) == 0 else 1
    near = 2 if narrow % (2 * core * side) == 0 else 1
    devices = mesh.devices.reshape(wide, narrow // (near * side * core), near, side, core)
    split = Mesh(devices, ("wide",) + ROWS)
    token_spec = P(ROWS, "wide", None)
    in_specs = (token_spec, token_spec, P(ROWS, "wide"), token_spec) + (P(),) * 21
    matrix, vector = P("wide", None), P("wide")
    out_specs = (token_spec,) * 3 + (
        matrix, vector, vector, matrix, vector, vector, vector,
        matrix, vector, matrix, vector, matrix, vector, vector, vector,
        matrix, vector, matrix, vector, vector, vector,
    )
    return jax.shard_map(body, mesh=split, in_specs=in_specs, out_specs=out_specs, check_vma=False)
```

```python
import functools

import jax
import jax.numpy as jnp
from jax import lax
from jax.experimental import pallas as pl
from jax.experimental.pallas import tpu as pltpu
from jax.sharding import Mesh, PartitionSpec as P

HD = 64
LANES = 128
WIDE, CORE, SIDE, NEAR, SHIFT = range(5)
MB = 2**20
norm_epsilon = 1e-05
masked_score = -1e9
BF = jnp.bfloat16
F32 = jnp.float32

NN = (((1,), (0,)), ((), ()))
NT = (((1,), (1,)), ((), ()))
TN = (((0,), (0,)), ((), ()))


def dot(a, b, dims=NN):
    return lax.dot_general(a, b, dims, preferred_element_type=F32)


def segment_terms(seg):
    lane = jnp.arange(LANES) % HD
    same = seg[..., None] == lane
    query_terms = jnp.where((lane < 4) & ~same, masked_score, 0.0).astype(BF)
    key_terms = jnp.where(((lane < 4) & same) | ((lane >= 4) & (lane < 7)), 1.0, 0.0).astype(BF)
    return query_terms, key_terms


def head_lanes(shape, head):
    lane = lax.broadcasted_iota(jnp.int32, shape, 1)
    return (lane < HD) if head == 0 else (lane >= HD)


def causal_scores(scores, causal, first_query, block, query_axis):
    if causal == "block":
        queries = lax.broadcasted_iota(jnp.int32, (block, block), query_axis)
        keys = lax.broadcasted_iota(jnp.int32, (block, block), 1 - query_axis)
        count = scores.shape[1 - query_axis]
        before = lax.slice_in_dim(scores, 0, count - block, axis=1 - query_axis)
        corner = lax.slice_in_dim(scores, count - block, count, axis=1 - query_axis)
        corner = jnp.where(keys <= queries, corner, masked_score)
        if count == block:
            return corner
        return jnp.concatenate([before, corner], 1 - query_axis)
    if causal == "mask":
        queries = first_query + lax.broadcasted_iota(jnp.int32, scores.shape, query_axis)
        keys = lax.broadcasted_iota(jnp.int32, scores.shape, 1 - query_axis)
        return jnp.where(keys <= queries, scores, masked_score)
    return scores


def in_order(parts, shift, half, there):
    if len(parts) == 1:
        return parts[0][there, :]
    return jnp.where(shift == 0, parts[half][...], parts[1 - half][...])


def array_places(count, shift, swapped):
    if not swapped:
        return [(slice(0, count), slice(0, count))]
    half = count // 2
    return [
        (
            slice(part * half, (part + 1) * half),
            pl.ds(pl.multiple_of(lax.rem(part * half + shift, count), half), half),
        )
        for part in (0, 1)
    ]


def row_block(index, block, count, shift, swapped):
    if not swapped:
        return pl.ds(index * block, block)
    return pl.ds(pl.multiple_of(lax.rem(index * block + shift, count), block), block)


def split_parts(refs, counts):
    groups = []
    for count in counts:
        groups.append(refs[:count])
        refs = refs[count:]
    return groups, refs


def forward_kernel(*refs, counts, causal, block, swapped):
    scalars, refs = refs[0], refs[1:]
    (q_parts, k_parts, v_parts), refs = split_parts(refs, counts)
    qt_ref, kt_ref = refs[:2]
    o_ref, qx_ref, ka, va, qa = refs[2:]
    tq, ts = qa.shape[1], ka.shape[1]
    shift = scalars[SHIFT]
    for part, (here, there) in enumerate(array_places(ts, shift, swapped)):
        k = in_order(k_parts, shift, part, there)
        v = in_order(v_parts, shift, part, there)
        extra = kt_ref[there, :]
        for head in (0, 1):
            own = head_lanes(k.shape, head)
            ka[head, here, :] = jnp.where(own, k, extra)
            va[head, here, :] = jnp.where(own, v, extra)
    for part, (here, there) in enumerate(array_places(tq, shift, swapped)):
        q = in_order(q_parts, shift, part, there)
        extra = qt_ref[there, :]
        for head in (0, 1):
            qa[head, here, :] = jnp.where(head_lanes(q.shape, head), q, extra)
    lane = lax.broadcasted_iota(jnp.int32, (block, LANES), 1)
    for index in range(tq // block):
        count = (index + 1) * block if causal == "block" else ts
        there = row_block(index, block, tq, shift, swapped)
        outs, extra = [], qt_ref[there, :].astype(F32)
        rows = slice(index * block, (index + 1) * block)
        both = [dot(qa[head, rows, :], ka[head, :count, :], NT) for head in (0, 1)]
        for head in (0, 1):
            scores = causal_scores(both[head], causal, shift + index * block, block, 0)
            top = jnp.max(scores, 1, keepdims=True)
            weights = jnp.exp(scores - top).astype(BF)
            sums = dot(weights, va[head, :count, :])
            at = HD + 4 if head == 0 else 4
            total = sums[:, at + 2 : at + 3]
            outs.append(sums / total)
            for i, piece in enumerate(three_parts(-(top + jnp.log(total)))):
                extra = jnp.where(lane == at + i, piece, extra)
        o_ref[there, :] = jnp.where(lane < HD, outs[0], outs[1]).astype(BF)
        qx_ref[there, :] = extra.astype(BF)


def three_parts(x):
    parts = []
    for _ in range(3):
        part = x.astype(BF).astype(F32)
        parts.append(part)
        x = x - part
    return parts


def backward_kernel(*refs, counts, causal, block, swapped, scaling):
    scalars, refs = refs[0], refs[1:]
    (q_parts, k_parts, v_parts), refs = split_parts(refs, counts)
    g_ref, o_ref, qx_ref, kt_ref = refs[:4]
    (
        dq_ref, dk_ref, dv_ref, ka, va, qa, ga, k_turned, dk_sum, dv_sum, dq_turned,
    ) = refs[4:]
    tq, ts = qa.shape[1], ka.shape[1]
    shift = scalars[SHIFT]
    for part, (here, there) in enumerate(array_places(ts, shift, swapped)):
        k = in_order(k_parts, shift, part, there)
        v = in_order(v_parts, shift, part, there)
        extra = kt_ref[there, :]
        for head in (0, 1):
            own = head_lanes(k.shape, head)
            ka[head, here, :] = jnp.where(own, k, extra)
            va[head, here, :] = jnp.where(own, v, extra)
        k_turned[:, here] = k.astype(F32).T.astype(BF)
    source = lax.broadcasted_iota(jnp.int32, (LANES, LANES), 0)
    target = lax.broadcasted_iota(jnp.int32, (LANES, LANES), 1)
    rides = (target % HD >= 4) & (target % HD < 7) & ((source < HD) == (target >= HD))
    spread = jnp.where(rides, -1.0, 0.0).astype(BF)
    for part, (here, there) in enumerate(array_places(tq, shift, swapped)):
        q = in_order(q_parts, shift, part, there)
        g, extra = g_ref[there, :], qx_ref[there, :]
        products = g.astype(F32) * o_ref[there, :].astype(F32)
        rough = products.astype(BF)
        delta = dot(rough, spread) + dot((products - rough.astype(F32)).astype(BF), spread)
        lane = lax.broadcasted_iota(jnp.int32, q.shape, 1) % HD
        pieces = three_parts(delta)
        g_extra = jnp.where(lane == 4, pieces[0], jnp.where(lane == 5, pieces[1], pieces[2]))
        g_extra = g_extra.astype(BF)
        for head in (0, 1):
            own = head_lanes(q.shape, head)
            qa[head, here, :] = jnp.where(own, q, extra)
            ga[head, here, :] = jnp.where(own, g, g_extra)
    blocks = tq // block
    for index in reversed(range(blocks)):
        count = (index + 1) * block if causal == "block" else ts
        rows = slice(index * block, (index + 1) * block)
        for head in (0, 1):
            q, g = qa[head, rows, :], ga[head, rows, :]
            scores = dot(ka[head, :count, :], q, NT)
            scores = causal_scores(scores, causal, shift + index * block, block, 1)
            probs = jnp.exp(scores)
            grads = (probs * dot(va[head, :count, :], g, NT)).astype(BF)
            dv, dk = dot(probs.astype(BF), g), dot(grads, q)
            if index == blocks - 1:
                dv_sum[head, :count, :] = dv
                dk_sum[head, :count, :] = dk
            else:
                dv_sum[head, :count, :] += dv
                dk_sum[head, :count, :] += dk
            own_rows = slice(HD * head, HD * (head + 1))
            dq_turned[own_rows, rows] = dot(k_turned[own_rows, :count], grads)
        there = row_block(index, block, tq, shift, swapped)
        dq_ref[there, :] = dq_turned[:, rows].T.astype(BF) * jnp.asarray(scaling, BF)
    for here, there in array_places(ts, shift, swapped):
        own = head_lanes((here.stop - here.start, LANES), 0)
        dk_ref[there, :] = jnp.where(own, dk_sum[0, here, :], dk_sum[1, here, :]).astype(BF)
        dv_ref[there, :] = jnp.where(own, dv_sum[0, here, :], dv_sum[1, here, :]).astype(BF)


ANYWHERE = pl.BlockSpec(memory_space=pl.ANY)


def stay(*arrays):
    return [pltpu.with_memory_space_constraint(x, pltpu.HBM) for x in arrays]


def head_spec(count, start):
    return pl.BlockSpec((pl.Squeezed(), count, LANES), lambda row, pair, _: (row, 0, start + pair))


def shared_spec(count):
    return pl.BlockSpec((pl.Squeezed(), count, LANES), lambda row, pair, _: (row, 0, 0))


def part_specs(q, k, v, first):
    specs, arrays = [], []
    for parts, column in (q, k, v):
        for x in parts:
            specs.append(head_spec(x.shape[1], column // LANES + first))
            arrays.append(x)
    return specs, arrays


class Chain:
    def __init__(self):
        self.last = ()

    def launch(
        self, kernel, scalars, grid, in_specs, arrays, out_specs, out_shape, scratch=(), vmem=48,
        us=5, held=(), free=0,
    ):
        ins = len(arrays)
        arrays = [*stay(*arrays[: ins - free]), *arrays[ins - free :]]
        extra = stay(*held, *self.last)

        outs = len(out_shape)

        def run(scalar_ref, *refs):
            rest = refs[ins + len(extra) :]
            kernel(scalar_ref, *refs[:ins], *rest[:outs], *rest[outs + 1 :])
            rest[outs][...] = jnp.zeros((8, LANES), F32)

        mark = pl.BlockSpec((8, LANES), lambda *_: (0, 0))

        results = pl.pallas_call(
            run,
            grid_spec=pltpu.PrefetchScalarGridSpec(
                num_scalar_prefetch=1,
                grid=grid,
                in_specs=list(in_specs) + [ANYWHERE] * len(extra),
                out_specs=[*out_specs, mark],
                scratch_shapes=list(scratch),
            ),
            out_shape=[pltpu.HBM(x.shape, x.dtype) for x in out_shape]
            + [pltpu.HBM((8, LANES), F32)],
            input_output_aliases={1 + ins + i: i for i in range(len(held))},
            compiler_params=pltpu.CompilerParams(vmem_limit_bytes=vmem * MB),
            cost_estimate=pl.CostEstimate(
                flops=0, bytes_accessed=us * 72000, transcendentals=0
            ),
        )(scalars, *arrays, *extra)
        self.last = (results[-1],)
        return results[:-1]

    def after_last(self, *arrays):
        *arrays, last = lax.optimization_barrier((*arrays, *self.last))
        self.last = (last,)
        return arrays


def attend(chain, q, k, v, terms, scalars, width, causal, block, swapped):
    specs, arrays = part_specs(q, k, v, 0)
    rows = arrays[0].shape[0]
    tq, ts = (sum(x.shape[1] for x in one[0]) for one in (q, k))
    return chain.launch(
        functools.partial(
            forward_kernel, counts=[len(x[0]) for x in (q, k, v)], causal=causal, block=block,
            swapped=swapped,
        ),
        scalars,
        (rows, width // LANES),
        specs + [shared_spec(tq), shared_spec(ts)],
        [*arrays, *terms],
        [head_spec(tq, 0), head_spec(tq, 0)],
        [jax.ShapeDtypeStruct((rows, tq, width), BF)] * 2,
        scratch=[pltpu.VMEM((2, n, LANES), BF) for n in (ts, ts, tq)],
        us=21,
    )


def attend_back(
    chain, q, k, v, g, o, extra, terms, scalars, first, pairs, causal, block, swapped, held=()
):
    specs, arrays = part_specs(q, k, v, first)
    rows, _, width = o.shape
    tq, ts = (sum(x.shape[1] for x in one[0]) for one in (q, k))
    return chain.launch(
        functools.partial(
            backward_kernel, counts=[len(x[0]) for x in (q, k, v)], causal=causal, block=block,
            swapped=swapped, scaling=HD**-0.5,
        ),
        scalars,
        (rows, pairs),
        specs + [head_spec(tq, first)] * 3 + [shared_spec(ts)],
        [*arrays, g, o, extra, terms[1]],
        [head_spec(tq, first), head_spec(ts, first), head_spec(ts, first)],
        [jax.ShapeDtypeStruct((rows, n, width), BF) for n in (tq, ts, ts)],
        scratch=[pltpu.VMEM((2, n, LANES), BF) for n in (ts, ts, tq, tq)]
        + [
            pltpu.VMEM((LANES, ts), BF),
            pltpu.VMEM((2, ts, LANES), F32),
            pltpu.VMEM((2, ts, LANES), F32),
            pltpu.VMEM((LANES, tq), F32),
        ],
        us=6 * pairs,
        held=held,
    )


def norm(resid):
    center = resid - jnp.mean(resid, -1, keepdims=True)
    inverse = lax.rsqrt(jnp.mean(center * center, -1, keepdims=True) + norm_epsilon)
    return center * inverse, inverse


def norm_back(upstream, normed, inverse, gain_vec):
    w = upstream * gain_vec
    return (
        w - jnp.mean(w, -1, keepdims=True) - normed * jnp.mean(w * normed, -1, keepdims=True)
    ) * inverse


def gelu_parts(pre):
    bell = jnp.exp(pre * pre * -0.5)
    t = 1.0 / (1.0 + jnp.abs(pre) * (0.3275911 * 0.5**0.5))
    poly = 0.5 * 1.061405429
    for c in (-1.453152027, 1.421413741, -0.284496736, 0.254829592):
        poly = poly * t + 0.5 * c
    tail = poly * t * bell
    phi_sum = jnp.where(pre >= 0, 1.0 - tail, tail)
    return pre * phi_sum, phi_sum + pre * (bell * 0.3989422804014327)


def add_rows(sums_ref, first, rows):
    for index, value in enumerate(rows):
        here = slice(first + index, first + index + 1)
        sums_ref[here, :] += jnp.sum(value.astype(F32), 0, keepdims=True)


def finish_rows(sums_ref, out_ref):
    @pl.when(pl.program_id(0) == pl.num_programs(0) - 1)
    def _():
        out_ref[...] = sums_ref[...].T


def clear(ref):
    @pl.when(pl.program_id(0) == 0)
    def _():
        ref[...] = jnp.zeros_like(ref)


def row(ref):
    return ref[...][None, :]


def project_kernel(x_ref, *refs, scaled, carried):
    if carried:
        refs[-1][...] = refs[0][...]
        refs = refs[1:-1]
    w_ref, b_ref, out_ref = refs
    width = b_ref.shape[0] // 3
    y = dot(x_ref[...], w_ref[...]) + row(b_ref)
    if scaled:
        out_ref[:, :width] = (y[:, :width] * HD**-0.5).astype(BF)
        out_ref[:, width:] = y[:, width:].astype(BF)
    else:
        out_ref[...] = y.astype(BF)


def after_self_kernel(
    o_ref, x_ref, w_ref, b_ref, gain_ref, bias_ref, qw_ref, qb_ref, n1_ref, i1_ref, h1b_ref, cq_ref,
):
    resid = x_ref[...].astype(F32) + (dot(o_ref[...], w_ref[...]) + row(b_ref))
    n1, i1 = norm(resid)
    h1b = (n1 * row(gain_ref) + row(bias_ref)).astype(BF)
    n1_ref[...] = n1
    i1_ref[...] = jnp.broadcast_to(i1, i1_ref.shape)
    h1b_ref[...] = h1b
    cq_ref[...] = ((dot(h1b, qw_ref[...]) + row(qb_ref)) * HD**-0.5).astype(BF)


def middle_kernel(
    o_ref, n1_ref, up_ref, g1_ref, s1_ref, ow_ref, ob_ref, g2_ref, s2_ref,
    w1_ref, b1_ref, w2_ref, b2_ref, g3_ref, s3_ref,
    *refs, chunk, kept_blocks,
):
    *outs, act_ref, dbf_ref, h2b_ref, dpre_ref, dr2_ref, dbc_ref, dco_ref, sums_ref, slope, sums = refs
    clear(sums)
    h1 = n1_ref[...] * row(g1_ref) + row(s1_ref)
    n2, i2 = norm(h1 + (dot(o_ref[...], ow_ref[...]) + row(ob_ref)))
    h2 = n2 * row(g2_ref) + row(s2_ref)
    h2b = h2.astype(BF)
    h2b_ref[...] = h2b
    hidden = w1_ref.shape[1]
    cols = [slice(c, c + chunk) for c in range(0, hidden, chunk)]
    bias1 = row(b1_ref)
    branch = row(b2_ref)
    for c in cols:
        pre = dot(h2b, w1_ref[:, c]) + bias1[:, c]
        value, slope_c = gelu_parts(pre)
        slope[:, c] = slope_c
        act_c = value.astype(BF)
        act_ref[:, c] = act_c
        branch = branch + dot(act_c, w2_ref[c, :])
    n3, i3 = norm(h2 + branch)
    out = (n3 * row(g3_ref) + row(s3_ref)).astype(BF)
    store_halves(outs, out, kept_blocks)
    up = up_ref[...].astype(F32)
    dr3 = norm_back(up, n3, i3, row(g3_ref))
    dbf = dr3.astype(BF)
    dbf_ref[...] = dbf
    dh2 = dr3
    for c in cols:
        dpre_c = (dot(dbf, w2_ref[c, :], NT) * slope[:, c]).astype(BF)
        dpre_ref[:, c] = dpre_c
        dh2 = dh2 + dot(dpre_c, w1_ref[:, c], NT)
    dr2 = norm_back(dh2, n2, i2, row(g2_ref))
    dbc = dr2.astype(BF)
    dr2_ref[...] = dr2
    dbc_ref[...] = dbc
    dco_ref[...] = dot(dbc, ow_ref[...], NT).astype(BF)
    add_rows(sums, MID_ROWS, (up * n3, up, dbf, dh2 * n2, dh2))
    finish_rows(sums, sums_ref)


def before_self_kernel(
    dcq_ref, dr2_ref, n1_ref, i1_ref, qw_ref, g1_ref, ow_ref, dr1_ref, dba_ref, dso_ref, sums_ref,
    sums,
):
    clear(sums)
    n1 = n1_ref[...]
    dh1 = dr2_ref[...] + dot(dcq_ref[...], qw_ref[...], NT)
    dr1 = norm_back(dh1, n1, i1_ref[:, 0:1], row(g1_ref))
    dba = dr1.astype(BF)
    dr1_ref[...] = dr1
    dba_ref[...] = dba
    dso_ref[...] = dot(dba, ow_ref[...], NT).astype(BF)
    add_rows(sums, LOW_ROWS, (dh1 * n1, dh1))
    finish_rows(sums, sums_ref)


def input_grad_kernel(*refs, count, start, kept_blocks):
    grads, w_ref, outs = refs[:count], refs[count + start], refs[count + start + 1 :]
    total = refs[count][...] if start else None
    width = grads[0].shape[-1]
    for index, ref in enumerate(grads):
        part = dot(ref[...], w_ref[:, index * width : (index + 1) * width], NT)
        total = part if total is None else total + part
    store_halves(outs, total, kept_blocks)


def store_halves(outs, value, kept_blocks):
    if kept_blocks is None:
        outs[0][...] = value.astype(outs[0].dtype)
        return
    step = pl.program_id(0)

    @pl.when(step < kept_blocks)
    def _():
        outs[0][...] = value.astype(outs[0].dtype)

    @pl.when(step >= kept_blocks)
    def _():
        outs[1][...] = value.astype(outs[1].dtype)


class Joined:
    def __init__(self, kept, got, use_kept):
        self.kept, self.got, self.use_kept = kept, got, use_kept

    def __getitem__(self, index):
        return jnp.where(self.use_kept, self.kept[index], self.got[index])


def token_call(
    chain, kernel, block, blocked, whole, outs, scalars, scratch=(), vmem=24, us=5, free=True
):
    def length(x):
        if not isinstance(x, tuple):
            return x.shape[0]
        return x[0].shape[1] * (1 if x[1] is None or isinstance(x[1], str) else 2)

    tokens = length(blocked[0])
    half = tokens // block // 2
    count = tokens // block
    in_specs, arrays, kinds = [], [], []
    for x in blocked:
        if not isinstance(x, tuple):
            in_specs.append(pl.BlockSpec((block, x.shape[1]), lambda i, _: (i, 0)))
            arrays.append(x)
            kinds.append(1)
            continue
        stack, got = x
        shape = (pl.Squeezed(), block, stack.shape[2])
        if got is None or isinstance(got, str):
            row = (lambda p: 1 - p[0]) if got else (lambda p: p[0])
            in_specs.append(pl.BlockSpec(shape, lambda i, p, row=row: (row(p), i, 0)))
            arrays.append(stack)
            kinds.append(1)
        else:
            in_specs.append(pl.BlockSpec(shape, lambda i, p: (p[0], jnp.minimum(i, half - 1), 0)))
            in_specs.append(
                pl.BlockSpec(shape[1:], lambda i, p: (jnp.maximum(i - half, 0), 0))
            )
            arrays += [stack, got]
            kinds.append(2)
    for x in whole:
        zeros = (0,) * x.ndim
        in_specs.append(
            pl.BlockSpec(x.shape, lambda i, _, z=zeros: z, pipeline_mode=pl.Buffered(1))
        )
    out_specs, out_shape = [], []
    for out in outs:
        if out[0] == "whole":
            out_specs.append(pl.BlockSpec(out[1:3], lambda i, _: (0, 0)))
            shape = out[1:3]
        elif out[0] == "kept":
            shape = (out[1], tokens // 2, out[2])
            out_specs.append(
                pl.BlockSpec(
                    (pl.Squeezed(), block, out[2]),
                    lambda i, p: (p[0], jnp.minimum(i, half - 1), 0),
                )
            )
        elif out[0] == "sent":
            shape = (tokens // 2, out[1])
            out_specs.append(
                pl.BlockSpec((block, out[1]), lambda i, _: (jnp.maximum(i - half, 0), 0))
            )
        else:
            shape = (count * block, out[0])
            out_specs.append(pl.BlockSpec((block, out[0]), lambda i, _: (i, 0)))
        out_shape.append(jax.ShapeDtypeStruct(shape, out[-1]))

    def run(_, *refs):
        used = []
        for kind in kinds:
            if kind == 1:
                used.append(refs[0])
            else:
                used.append(Joined(refs[0], refs[1], pl.program_id(0) < half))
            refs = refs[kind:]
        kernel(*used, *refs)

    return chain.launch(
        run, scalars, (count,), in_specs, [*arrays, *whole], out_specs, out_shape, scratch, vmem, us,
        free=len(whole) if free else 0,
    )


def store_kernel(_, got_ref, out_ref):
    out_ref[...] = got_ref[...].astype(out_ref.dtype)


def store_other(chain, held, got, scalars):
    n, c = got.shape
    return chain.launch(
        store_kernel,
        scalars,
        (2,),
        [pl.BlockSpec((n // 2, c), lambda i, _: (i, 0))],
        [got],
        [pl.BlockSpec((pl.Squeezed(), n // 2, c), lambda i, p: (1 - p[0], i, 0))],
        [jax.ShapeDtypeStruct(held.shape, held.dtype)],
        vmem=16,
        us=3,
        held=(held,),
    )


MID_ROWS, LOW_ROWS = 8, 16


def weight_grads(chain, items, extras, scalars, wide, order):
    first_left = items[0][0]
    m = (first_left[0] if isinstance(first_left, tuple) else first_left).shape[-1]
    block = min(item[3] for item in items)
    block = min(block, m)
    specs, arrays, steps = [], [], []
    known = {}
    for left, right, start, columns, sum_row in items:
        key = id(left)
        if key not in known:
            known[key] = (len(arrays), isinstance(left, tuple))
            if isinstance(left, tuple):
                stack, got = left
                specs.append(
                    pl.BlockSpec(
                        (pl.Squeezed(),) + stack.shape[1:], lambda j, p: (p[0], 0, 0),
                        pipeline_mode=pl.Buffered(1),
                    )
                )
                arrays.append(stack)
                left = got
            specs.append(
                pl.BlockSpec(left.shape, lambda j, p: (0, 0), pipeline_mode=pl.Buffered(1))
            )
            arrays.append(left)
        begin, blocks = len(steps), columns // block
        where = len(arrays)
        specs.append(
            pl.BlockSpec(
                (right.shape[0], block),
                lambda j, p, b=begin, n=blocks, f=start // block: (0, f + jnp.clip(j - b, 0, n - 1)),
            )
        )
        arrays.append(right)
        for index in range(blocks):
            steps.append((known[key], where, sum_row, start + index * block, right.shape[1]))
    for extra in extras:
        specs.append(
            pl.BlockSpec(extra.shape, lambda j, p: (0, 0), pipeline_mode=pl.Buffered(1))
        )
    slab = m // len(order)
    size = m // wide
    apart = len(order) > 1
    slabs = len(order) // 2

    def kernel(scalar_ref, *refs):
        ins, rest = refs[: len(arrays)], refs[len(arrays) :]
        extra_refs, (*outs, sums) = rest[: len(extras)], rest[len(extras) :]
        clear(sums)
        step = pl.program_id(0)

        def store(value):
            if not apart:
                outs[0][...] = value.astype(BF)
                return
            core = scalar_ref[CORE]
            for to in range(slabs):
                halves = [
                    value[order[at] * slab : (order[at] + 1) * slab].astype(BF)
                    for at in (to, slabs + to)
                ]
                here = slice(to * slab, (to + 1) * slab)
                outs[0][here, :] = jnp.where(core == 0, halves[1], halves[0])
                outs[1][here, :] = jnp.where(core == 0, halves[0], halves[1])

        for index, ((left, split), right, sum_row, column, columns) in enumerate(steps):

            @pl.when(step == index)
            def _():
                grad = ins[right][...]
                if split:
                    half = ins[left].shape[0]
                    value = dot(ins[left][...], grad[:half], TN)
                    value = value + dot(ins[left + 1][...], grad[half:], TN)
                else:
                    value = dot(ins[left][...], grad, TN)
                store(value)
                if sum_row is None:
                    return
                total = jnp.sum(grad.astype(F32), 0, keepdims=True)
                if columns == m:
                    sums[sum_row : sum_row + 1, column : column + block] = total
                    return
                for piece in range(block // size):
                    w, k = divmod(column // size + piece, columns // m)
                    sums[sum_row + k : sum_row + k + 1, w * size : (w + 1) * size] = total[
                        :, piece * size : (piece + 1) * size
                    ]

        @pl.when(step == len(steps))
        def _():
            value = sums[...].T
            for ref in extra_refs:
                value = value + ref[...]
            store(jnp.concatenate([value, jnp.zeros((m, block - LANES), F32)], 1))

    n = block * len(steps) + LANES
    rows = m // 2 if apart else m
    return chain.launch(
        kernel,
        scalars,
        (len(steps) + 1,),
        specs,
        [*arrays, *extras],
        [pl.BlockSpec((rows, block), lambda j, _: (0, j))] * (m // rows),
        [jax.ShapeDtypeStruct((rows, n), BF)] * (m // rows),
        scratch=[pltpu.VMEM((LANES, m), F32)],
        us=max(4, n // 400),
    )


def tall_grad(chain, left, right, scalars, order):
    tokens, rows = left.shape
    width = right.shape[1]
    apart = len(order) > 1
    blocks = len(order) if apart else 4
    size = rows // blocks
    half = blocks // 2

    def source(j, s):
        if not apart:
            return j
        to = jnp.where(s[CORE] == 0, (j + half) % blocks, j)
        block = 0
        for at, slab in enumerate(order):
            block = jnp.where(to == at, slab, block)
        return block

    def kernel(_, left_ref, right_ref, *refs):
        value = dot(left_ref[...], right_ref[...], TN).astype(BF)
        if not apart:
            refs[-1][...] = value
            return
        other, own = refs[-2:]

        @pl.when(pl.program_id(0) < half)
        def _():
            other[...] = value

        @pl.when(pl.program_id(0) >= half)
        def _():
            own[...] = value

    if apart:
        out_specs = [
            pl.BlockSpec((size, width), lambda j, _: (jnp.minimum(j, half - 1), 0)),
            pl.BlockSpec((size, width), lambda j, _: (jnp.maximum(j - half, 0), 0)),
        ]
        out_shape = [jax.ShapeDtypeStruct((rows // 2, width), BF)] * 2
    else:
        out_specs = [pl.BlockSpec((size, width), lambda j, _: (j, 0))]
        out_shape = [jax.ShapeDtypeStruct((rows, width), BF)]
    return chain.launch(
        kernel,
        scalars,
        (blocks,),
        [
            pl.BlockSpec((tokens, size), lambda j, s: (0, source(j, s))),
            pl.BlockSpec(right.shape, lambda j, _: (0, 0), pipeline_mode=pl.Buffered(1)),
        ],
        [left, right],
        out_specs,
        out_shape,
        us=9,
    )


def vector_rows(x, columns, outs):
    turned = x.astype(F32).T
    for (start, count), out in zip(columns, outs):
        rows = [turned[start + i] for i in range(count)]
        out[...] = rows[0] if count == 1 else jnp.concatenate(rows)


def widen(chain, groups, pieces, columns, scalars):
    pairs = len(groups[0]) == 2
    arrays = [x for group in groups for x in group]
    rows = groups[0][0].shape[0] * len(groups[0])
    size = rows // 8
    specs = [
        pl.BlockSpec(x.shape, lambda i, _: (0, 0), pipeline_mode=pl.Buffered(1)) for x in arrays
    ]

    def convert(ins, outs, index):
        step = pl.program_id(0)
        for out, parts in zip(outs, pieces):
            at = 0
            for group, start, count in parts:
                cols = slice(start, start + count)
                if pairs:
                    here = pl.ds(pl.multiple_of(step % 4 * size, size), size)
                    piece = ins[2 * group + index][here, cols]
                else:
                    piece = ins[8 * group + index][:, cols]
                out[:, at : at + count] = piece.astype(F32)
                at += count

    def extra_of(ins, s):
        count = len(groups[0])
        places = []
        for position in range(count):
            total = 0.0
            for index in range(count):
                flips = position ^ index
                if pairs:
                    same = s[CORE] == flips
                else:
                    same = (
                        (s[CORE] == flips // 4)
                        & (s[SIDE] == flips // 2 % 2)
                        & (s[NEAR] == flips % 2)
                    )
                value = sum(
                    ins[count * group + index][:, x[0].shape[1] - LANES :].astype(F32)
                    for group, x in enumerate(groups)
                )
                total = total + jnp.where(same, value, 0.0)
            places.append(total)
        return jnp.concatenate(places, 0)

    def kernel(s, *refs):
        ins, outs = refs[: len(arrays)], refs[len(arrays) :]
        matrices, vectors = outs[: len(pieces)], outs[len(pieces) :]
        step = pl.program_id(0)
        which = (step // 4 != s[CORE]).astype(jnp.int32)
        if not pairs:
            which = (
                4 * which
                + 2 * (step // 2 % 2 != s[SIDE]).astype(jnp.int32)
                + (step % 2 != s[NEAR]).astype(jnp.int32)
            )
        for index in range(len(groups[0])):

            @pl.when(which == index)
            def _():
                convert(ins, matrices, index)

        if columns:

            @pl.when(step == 7)
            def _():
                vector_rows(extra_of(ins, s), columns, vectors)

    widths = [sum(p[2] for p in parts) for parts in pieces]
    lengths = [count * rows for _, count in columns]
    return chain.launch(
        kernel,
        scalars,
        (8,),
        specs,
        arrays,
        [pl.BlockSpec((size, w), lambda i, _: (i, 0)) for w in widths]
        + [pl.BlockSpec((n,), lambda i, _: (0,)) for n in lengths],
        [jax.ShapeDtypeStruct((rows, w), F32) for w in widths]
        + [jax.ShapeDtypeStruct((n,), F32) for n in lengths],
        vmem=24,
        us=4,
        free=len(arrays),
    )


def vectors_kernel(x_ref, *outs, columns):
    vector_rows(x_ref[...], columns, outs)


def vectors_of(x, columns):
    return pl.pallas_call(
        functools.partial(vectors_kernel, columns=columns),
        out_shape=[jax.ShapeDtypeStruct((count * x.shape[0],), F32) for _, count in columns],
    )(x)


def partner(x, axis, bit=1):
    count = lax.axis_size(axis)
    return lax.ppermute(x, axis, [(i, i ^ bit) for i in range(count)])


def partner_both(x):
    return lax.ppermute(x, ("near", "side"), [(i, 3 - i) for i in range(4)])


ROWS = ("far", "near", "side", "core")


class Reduction:
    def __init__(self, arrays, order):
        self.arrays = arrays
        self.steps = ["core", *order] if len(arrays) == 2 else []
        self.step, self.flying, self.terms = None, [], []

    def total(self, turned=None):
        value = 0.0
        for x, path in self.terms:
            index, parts = 0, 1
            for axis in path:
                index, parts = 2 * index + lax.axis_index(axis), 2 * parts
            if turned:
                index, parts = 2 * index + 1 - lax.axis_index(turned), 2 * parts
            rows = x.shape[0] // parts
            value = value + lax.dynamic_slice_in_dim(x, index * rows, rows, 0).astype(F32)
        return value.astype(BF)

    def land(self, got):
        if not got:
            return
        if self.step == "core":
            self.terms = [(self.arrays[1], ()), (got[0], ())]
        elif self.step in ("wide", "side", "near", "far"):
            self.terms += [(x, ()) for x in got]
        elif self.step == "spread":
            self.pieces = [self.sent, *got]
        elif self.step in JOINS:
            self.terms = [(self.sent, ()), (got[0], ())]
        self.flying = []

    def joined(self):
        (mine, _), (got, _) = self.terms
        first = lax.axis_index(self.step[5:]) == 0
        return jnp.concatenate([jnp.where(first, mine, got), jnp.where(first, got, mine)], 0)

    def prepare(self):
        last, self.step = self.step, self.steps.pop(0)
        if self.step == "core":
            return [self.arrays[0]]
        if last in JOINS:
            self.step, step = last, self.step
            sent = self.joined()
            self.step = step
            return [sent]
        if self.step in JOINS:
            return [self.total()]
        if self.step == "join":
            return self.pieces
        if self.step in ("far", "spread"):
            return [self.total()]
        sent = self.total(self.step)
        self.terms = [(x, path + (self.step,)) for x, path in self.terms]
        return [sent]

    def start(self, sent):
        if self.step in JOINS:
            self.sent = sent[0]
            self.flying = [partner(sent[0], self.step[5:])]
            self.pieces = [sent[0], *self.flying]
        elif self.step == "spread":
            self.sent = sent[0]
            self.flying = [
                partner(sent[0], "near"), partner(sent[0], "side"), partner_both(sent[0])
            ]
        elif self.step == "join":
            self.pieces = [*sent, *(partner(x, "core") for x in sent)]
        elif self.step != "far" or lax.axis_size("far") == 2:
            self.flying = [partner(sent[0], self.step)]

    def result(self):
        x = lax.psum_scatter(self.arrays[0], "wide", scatter_dimension=0, tiled=True)
        return lax.psum(x, ROWS)


CORE_WIDE = (0, 2, 1, 3)
CORE_SIDE = (0, 4, 1, 5, 2, 6, 3, 7)
X_FIRST = ("wide", "side", "near", "far", "spread", "join")
JOINS = ("join_near", "join_side", "join_core")
X_THEN_Y = ("wide", "side", "near", "far") + JOINS
Y_THEN_X = ("side", "wide", "near", "far") + JOINS


def body(
    target, encoded, segments, out_grad,
    self_qkv_w, self_q_b, self_v_b, self_out_w, self_out_b, norm1_gain, norm1_bias,
    cross_q_w, cross_q_b, cross_kv_w, cross_v_b, cross_out_w, cross_out_b, norm2_gain, norm2_bias,
    ffn_in_w, ffn_in_b, ffn_out_w, ffn_out_b, norm3_gain, norm3_bias,
):
    row_count, tok_count, width = target.shape
    hidden = ffn_in_w.shape[1]
    parts = hidden // width
    pairs = width // LANES
    wide = lax.axis_size("wide")
    index = lax.axis_index("wide").astype(jnp.int32)
    scalars = jnp.stack(
        [index]
        + [lax.axis_index(a).astype(jnp.int32) for a in ("core", "side", "near")]
        + [index * tok_count]
    )
    swapped = wide == 2 and row_count == 2
    split = swapped and all(lax.axis_size(a) == 2 for a in ("side", "near", "core"))
    core_wide = CORE_WIDE if split else (0,)
    core_side = CORE_SIDE if split else (0,)
    tokens = row_count * tok_count
    block = min(256, tok_count)
    kept_blocks = tok_count // block if swapped else None

    chain = Chain()

    def run(call, *args, **kwargs):
        return call(chain, *args, **kwargs)

    if swapped:
        def bring(x):
            return x, partner(lax.dynamic_index_in_dim(x, 1 - index, 0, keepdims=False), "wide")

        causal, block_f, block_b = "block", 2 * block, block
        seg_kept, seg_got = bring(segments)
        seg = jnp.concatenate(
            [lax.dynamic_index_in_dim(seg_kept, index, 0, keepdims=False), seg_got]
        )[None]
        key_seg = seg
        row_tokens = tokens
    else:
        def bring(x):
            return x.reshape(tokens, -1)

        causal, block_f, block_b = "mask", block, block
        seg = segments
        key_seg = lax.all_gather(segments, "wide", axis=1, tiled=True)
        row_tokens = tok_count
    terms = (segment_terms(seg)[0], segment_terms(key_seg)[1])

    def by_row(x):
        return x.reshape(-1, row_tokens, x.shape[-1])

    def flat(x):
        return x.reshape(-1, x.shape[-1])

    def keys_of(x):
        return lax.all_gather(x, "wide", axis=1, tiled=True)

    def key_grads(x):
        return x if swapped else lax.psum_scatter(x, "wide", scatter_dimension=1, tiled=True)

    def project(x, w, bias, scaled, carried=None):
        outs = [(w.shape[1], BF)]
        if carried is not None:
            outs.append((carried.shape[-1], BF))
        out = run(
            token_call, functools.partial(project_kernel, scaled=scaled, carried=len(outs) == 2),
            block, (x,) if carried is None else (x, (carried, "other")), (w, bias), outs, scalars,
            us=3,
        )
        y = out[0][None] if swapped else by_row(out[0])
        return y if carried is None else (y, (carried, partner(out[1], "wide")))

    def attention(q, k, v, is_causal):
        return run(
            attend, q, k, v, terms, scalars, width, causal if is_causal else "no", block_f, swapped
        )

    def attention_back(q, k, v, g, o, extra, is_causal, first, count, held=()):
        return run(
            attend_back, q, k, v, by_row(g), o, extra, terms, scalars, first, count,
            causal if is_causal else "no", block_b, swapped, held,
        )

    def input_grad(grads, w, start=None):
        blocked = list(grads) + ([] if start is None else [start])
        outs = [("kept", 2, width, F32), ("sent", width, BF)] if swapped else [(width, F32)]
        kernel = functools.partial(
            input_grad_kernel, count=len(grads), start=0 if start is None else 1,
            kept_blocks=kept_blocks,
        )
        out = run(
            token_call, kernel, block, blocked, (w,), outs, scalars
        )
        return out[0], out[-1]

    def send_back(x):
        return partner(x, "wide") if swapped else None

    def give(out, got):
        if not swapped:
            return out.reshape(row_count, tok_count, width)
        return run(store_other, out, got, scalars)[0]

    def arrive(*reductions, others=()):
        landed = chain.after_last(*others, *(x for r in reductions for x in r.flying))
        others, landed = landed[: len(others)], landed[len(others) :]
        for r in reductions:
            count = len(r.flying)
            r.land(landed[:count])
            landed = landed[count:]
        return others

    def exchange(*reductions, also=(), landing=()):
        if not split:
            return [send_back(x) for x in also] + list(landing)
        flying = [x for r in reductions for x in r.flying]
        landed = chain.after_last(*landing, *flying)
        landing, landed = landed[: len(landing)], landed[len(landing) :]
        for r in reductions:
            count = len(r.flying)
            r.land(landed[:count])
            landed = landed[count:]
        sent = [r.prepare() for r in reductions]
        flat_sent = chain.after_last(*(x for one in sent for x in one), *also)
        for r, one in zip(reductions, sent):
            r.start(flat_sent[: len(one)])
            flat_sent = flat_sent[len(one) :]
        return [send_back(x) for x in flat_sent] + list(landing)

    zeros = jnp.zeros_like(self_q_b)
    qkv_bias = jnp.concatenate([self_q_b, zeros, self_v_b])
    ckv_bias = jnp.concatenate([zeros, cross_v_b])
    x_in = bring(target)
    if swapped:
        ckv = [project((encoded, None), cross_kv_w, ckv_bias, False)]
        qkv = [project((target, None), self_qkv_w, qkv_bias, True)]
        terms = tuple(chain.after_last(*terms))
        got, x_enc = project(x_in[1], self_qkv_w, qkv_bias, True, encoded)
        qkv.append(got)
        self_q, self_k, self_v = (qkv, 0), (qkv, width), (qkv, 2 * width)
    else:
        x_enc, upstream = bring(encoded), bring(out_grad)
        ckv = [keys_of(project(x_enc, cross_kv_w, ckv_bias, False))]
        qkv = [project(x_in, self_qkv_w, qkv_bias, True)]
        both = [keys_of(qkv[0][..., width:])]
        self_q, self_k, self_v = (qkv, 0), (both, 0), (both, width)
    self_o, self_x = attention(self_q, self_k, self_v, True)
    self_ob = flat(self_o)
    n1, i1, h1b, cq = run(
        token_call, after_self_kernel, block, (self_ob, x_in),
        (self_out_w, self_out_b, norm1_gain, norm1_bias, cross_q_w, cross_q_b),
        [(width, F32), (LANES, F32), (width, BF), (width, BF)], scalars,
    )
    if swapped:
        got, upstream = project(x_enc[1], cross_kv_w, ckv_bias, False, out_grad)
        ckv.append(got)
    cross_q, cross_k, cross_v = ([by_row(cq)], 0), (ckv, 0), (ckv, width)
    cross_o, cross_x = attention(cross_q, cross_k, cross_v, False)
    cross_ob = flat(cross_o)
    outs = [("kept", 2, width, BF), ("sent", width, BF)] if swapped else [(width, BF)]
    *h3, act, dbf, h2b, dpre, dr2, dbc, dco, mid_sums = run(
        token_call, functools.partial(middle_kernel, chunk=width, kept_blocks=kept_blocks),
        block, (cross_ob, n1, upstream),
        (
            norm1_gain, norm1_bias, cross_out_w, cross_out_b, norm2_gain, norm2_bias,
            ffn_in_w, ffn_in_b, ffn_out_w, ffn_out_b, norm3_gain, norm3_bias,
        ),
        outs
        + [
            (hidden, BF), (width, BF), (width, BF), (hidden, BF), (width, F32),
            (width, BF), (width, BF), ("whole", width, LANES, F32),
        ],
        scalars,
        scratch=[pltpu.VMEM((block, hidden), F32), pltpu.VMEM((LANES, width), F32)],
        vmem=56,
        us=45,
    )

    rb = Reduction(
        run(
            weight_grads, [(h2b, dpre, 0, hidden, 0), (cross_ob, dbc, 0, width, parts)],
            [mid_sums], scalars, wide, core_side,
        ),
        Y_THEN_X,
    )
    exchange(rb)
    ra = Reduction(run(tall_grad, act, dbf, scalars, core_wide), X_THEN_Y)
    exchange(ra)
    exchange(ra, rb)
    dcq, dck, dcv = attention_back(
        cross_q, cross_k, cross_v, dco, cross_o, cross_x, False, 0, pairs
    )
    dcq, dck, dcv = flat(dcq), flat(key_grads(dck)), flat(key_grads(dcv))
    exchange(ra, rb)
    dr1, dba, dso, low_sums = run(
        token_call, before_self_kernel, block, (dcq, dr2, n1, i1),
        (cross_q_w, norm1_gain, self_out_w),
        [(width, F32), (width, BF), (width, BF), ("whole", width, LANES, F32)], scalars,
        scratch=[pltpu.VMEM((LANES, width), F32)],
        free=False,
    )
    rc = Reduction(
        run(
            weight_grads,
            [
                (h1b, dcq, 0, width, 0), (x_enc, dck, 0, width, None), (x_enc, dcv, 0, width, 1),
                (self_ob, dba, 0, width, 2),
            ],
            [low_sums], scalars, wide, core_side,
        ),
        Y_THEN_X,
    )
    (got_out,) = exchange(ra, rb, rc, also=(h3[-1],))
    self_args = (self_q, self_k, self_v, dso, self_o, self_x, True)
    if swapped:
        cut = pairs // 3
        held = attention_back(*self_args, 0, cut)
        exchange(ra, rb, rc)
        dsq, dsk, dsv = attention_back(*self_args, cut, pairs - cut, held)
    else:
        dsq, dsk, dsv = attention_back(*self_args, 0, pairs)
    dsq, dsk, dsv = flat(dsq), flat(key_grads(dsk)), flat(key_grads(dsv))
    rd = Reduction(
        run(
            weight_grads,
            [(x_in, dsq, 0, width, 0), (x_in, dsk, 0, width, None), (x_in, dsv, 0, width, 1)],
            [], scalars, wide, core_wide,
        ),
        X_FIRST,
    )
    if split:
        arrive(rb)
    (got_out,) = exchange(rd, ra, rc, landing=(got_out,))
    in_kept, in_sent = input_grad([dsq, dsk, dsv], self_qkv_w, dr1)

    vectors_b = [(0, parts), (parts, 1)] + [(MID_ROWS + i, 1) for i in range(5)]
    vectors_c = [(0, 1), (1, 1), (2, 1), (LOW_ROWS, 1), (LOW_ROWS + 1, 1)]
    vectors_d = [(0, 1), (1, 1)]
    pieces_b = [[(0, 0, hidden)], [(0, hidden, width)]]
    pieces_c = [[(0, 0, width)], [(0, width, 2 * width)], [(0, 3 * width, width)]]
    if split:
        arrive(rd, ra, rc)
        exchange(rd)
        (got_in,) = exchange(ra, rb, rc, also=(in_sent,))
        enc_kept, enc_sent = input_grad([dck, dcv], cross_kv_w)
        arrive(rd, ra, rb, rc)
        exchange(rd)
        (got_enc,) = exchange(rc, rb, also=(enc_sent,))
        layer_out = give(h3[0], got_out)
        (got_in,) = arrive(rd, others=(got_in,))
        exchange(rd)
        exchange(rc, ra)
        (ffn_out_w_grad,) = run(widen, [ra.pieces], [[(0, 0, width)]], [], scalars)
        exchange(rd)
        exchange(rc)
        target_grad = give(in_kept, got_in)
        (got_enc,) = arrive(rd, others=(got_enc,))
        exchange(rd)
        exchange(rc, rb)
        out_b = run(widen, [rb.pieces], pieces_b, vectors_b, scalars)
        out_c = run(widen, [rc.pieces], pieces_c, vectors_c, scalars)
        exchange(rd)
        encoded_grad = give(enc_kept, got_enc)
        pieces_d = [[(0, 0, 3 * width)]]
        out_d = run(widen, [rd.pieces], pieces_d, vectors_d, scalars)
    else:
        enc_kept, _ = input_grad([dck, dcv], cross_kv_w)
        layer_out, target_grad, encoded_grad = (
            give(x, None) for x in (h3[0], in_kept, enc_kept)
        )

        def columns_of(x, pieces, vectors):
            return [
                jnp.concatenate([x[:, start : start + size] for _, start, size in p], 1).astype(F32)
                for p in pieces
            ] + list(vectors_of(x[:, -LANES:], vectors))

        ffn_out_w_grad = ra.result().astype(F32)
        out_b = columns_of(rb.result(), pieces_b, vectors_b)
        out_c = columns_of(rc.result(), pieces_c, vectors_c)
        out_d = columns_of(rd.result(), [[(0, 0, 3 * width)]], vectors_d)
    (
        ffn_in_w_grad, cross_out_w_grad, ffn_in_b_grad, cross_out_b_grad, norm3_gain_grad,
        norm3_bias_grad, ffn_out_b_grad, norm2_gain_grad, norm2_bias_grad,
    ) = out_b
    (
        cross_q_w_grad, cross_kv_w_grad, self_out_w_grad, cross_q_b_grad, cross_v_b_grad,
        self_out_b_grad, norm1_gain_grad, norm1_bias_grad,
    ) = out_c
    self_qkv_w_grad, self_q_b_grad, self_v_b_grad = out_d
    return (
        layer_out, target_grad, encoded_grad,
        self_qkv_w_grad, self_q_b_grad, self_v_b_grad,
        self_out_w_grad, self_out_b_grad, norm1_gain_grad, norm1_bias_grad,
        cross_q_w_grad, cross_q_b_grad, cross_kv_w_grad, cross_v_b_grad,
        cross_out_w_grad, cross_out_b_grad, norm2_gain_grad, norm2_bias_grad,
        ffn_in_w_grad, ffn_in_b_grad, ffn_out_w_grad, ffn_out_b_grad,
        norm3_gain_grad, norm3_bias_grad,
    )


def solution(mesh):
    wide, narrow = mesh.shape["wide"], mesh.shape["narrow"]
    core = 2 if narrow % 2 == 0 else 1
    side = 2 if narrow % (2 * core) == 0 else 1
    near = 2 if narrow % (2 * core * side) == 0 else 1
    devices = mesh.devices.reshape(wide, narrow // (near * side * core), near, side, core)
    split = Mesh(devices, ("wide",) + ROWS)
    token_spec = P(ROWS, "wide", None)
    in_specs = (token_spec, token_spec, P(ROWS, "wide"), token_spec) + (P(),) * 21
    matrix, vector = P("wide", None), P("wide")
    out_specs = (token_spec,) * 3 + (
        matrix, vector, vector, matrix, vector, vector, vector,
        matrix, vector, matrix, vector, matrix, vector, vector, vector,
        matrix, vector, matrix, vector, vector, vector,
    )
    return jax.shard_map(body, mesh=split, in_specs=in_specs, out_specs=out_specs, check_vma=False)
```

```python
import functools

import jax
import jax.numpy as jnp
from jax import lax
from jax.experimental import pallas as pl
from jax.experimental.pallas import tpu as pltpu
from jax.sharding import Mesh, PartitionSpec as P

HD = 64
LANES = 128
WIDE, CORE, SIDE, NEAR, SHIFT = range(5)
MB = 2**20
norm_epsilon = 1e-05
masked_score = -1e9
BF = jnp.bfloat16
F32 = jnp.float32

NN = (((1,), (0,)), ((), ()))
NT = (((1,), (1,)), ((), ()))
TN = (((0,), (0,)), ((), ()))


def dot(a, b, dims=NN):
    return lax.dot_general(a, b, dims, preferred_element_type=F32)


def segment_terms(seg):
    lane = jnp.arange(LANES) % HD
    same = seg[..., None] == lane
    query_terms = jnp.where((lane < 4) & ~same, masked_score, 0.0).astype(BF)
    key_terms = jnp.where(((lane < 4) & same) | ((lane >= 4) & (lane < 7)), 1.0, 0.0).astype(BF)
    return query_terms, key_terms


def head_lanes(shape, head):
    lane = lax.broadcasted_iota(jnp.int32, shape, 1)
    return (lane < HD) if head == 0 else (lane >= HD)


def causal_scores(scores, causal, first_query, block, query_axis):
    if causal == "block":
        queries = lax.broadcasted_iota(jnp.int32, (block, block), query_axis)
        keys = lax.broadcasted_iota(jnp.int32, (block, block), 1 - query_axis)
        count = scores.shape[1 - query_axis]
        before = lax.slice_in_dim(scores, 0, count - block, axis=1 - query_axis)
        corner = lax.slice_in_dim(scores, count - block, count, axis=1 - query_axis)
        corner = jnp.where(keys <= queries, corner, masked_score)
        if count == block:
            return corner
        return jnp.concatenate([before, corner], 1 - query_axis)
    if causal == "mask":
        queries = first_query + lax.broadcasted_iota(jnp.int32, scores.shape, query_axis)
        keys = lax.broadcasted_iota(jnp.int32, scores.shape, 1 - query_axis)
        return jnp.where(keys <= queries, scores, masked_score)
    return scores


def in_order(parts, shift, half, there):
    if len(parts) == 1:
        return parts[0][there, :]
    return jnp.where(shift == 0, parts[half][...], parts[1 - half][...])


def array_places(count, shift, swapped):
    if not swapped:
        return [(slice(0, count), slice(0, count))]
    half = count // 2
    return [
        (
            slice(part * half, (part + 1) * half),
            pl.ds(pl.multiple_of(lax.rem(part * half + shift, count), half), half),
        )
        for part in (0, 1)
    ]


def row_block(index, block, count, shift, swapped):
    if not swapped:
        return pl.ds(index * block, block)
    return pl.ds(pl.multiple_of(lax.rem(index * block + shift, count), block), block)


def split_parts(refs, counts):
    groups = []
    for count in counts:
        groups.append(refs[:count])
        refs = refs[count:]
    return groups, refs


def forward_kernel(*refs, counts, causal, block, swapped):
    scalars, refs = refs[0], refs[1:]
    (q_parts, k_parts, v_parts), refs = split_parts(refs, counts)
    qt_ref, kt_ref = refs[:2]
    o_ref, qx_ref, ka, va, qa = refs[2:]
    tq, ts = qa.shape[1], ka.shape[1]
    shift = scalars[SHIFT]
    for part, (here, there) in enumerate(array_places(ts, shift, swapped)):
        k = in_order(k_parts, shift, part, there)
        v = in_order(v_parts, shift, part, there)
        extra = kt_ref[there, :]
        for head in (0, 1):
            own = head_lanes(k.shape, head)
            ka[head, here, :] = jnp.where(own, k, extra)
            va[head, here, :] = jnp.where(own, v, extra)
    for part, (here, there) in enumerate(array_places(tq, shift, swapped)):
        q = in_order(q_parts, shift, part, there)
        extra = qt_ref[there, :]
        for head in (0, 1):
            qa[head, here, :] = jnp.where(head_lanes(q.shape, head), q, extra)
    lane = lax.broadcasted_iota(jnp.int32, (block, LANES), 1)
    for index in range(tq // block):
        count = (index + 1) * block if causal == "block" else ts
        there = row_block(index, block, tq, shift, swapped)
        outs, extra = [], qt_ref[there, :].astype(F32)
        rows = slice(index * block, (index + 1) * block)
        both = [dot(qa[head, rows, :], ka[head, :count, :], NT) for head in (0, 1)]
        for head in (0, 1):
            scores = causal_scores(both[head], causal, shift + index * block, block, 0)
            top = jnp.max(scores, 1, keepdims=True)
            weights = jnp.exp(scores - top).astype(BF)
            sums = dot(weights, va[head, :count, :])
            at = HD + 4 if head == 0 else 4
            total = sums[:, at + 2 : at + 3]
            outs.append(sums / total)
            for i, piece in enumerate(three_parts(-(top + jnp.log(total)))):
                extra = jnp.where(lane == at + i, piece, extra)
        o_ref[there, :] = jnp.where(lane < HD, outs[0], outs[1]).astype(BF)
        qx_ref[there, :] = extra.astype(BF)


def three_parts(x):
    parts = []
    for _ in range(3):
        part = x.astype(BF).astype(F32)
        parts.append(part)
        x = x - part
    return parts


def backward_kernel(*refs, counts, causal, block, swapped, scaling):
    scalars, refs = refs[0], refs[1:]
    (q_parts, k_parts, v_parts), refs = split_parts(refs, counts)
    g_ref, o_ref, qx_ref, kt_ref = refs[:4]
    (
        dq_ref, dk_ref, dv_ref, ka, va, qa, ga, k_turned, dk_sum, dv_sum, dq_turned,
    ) = refs[4:]
    tq, ts = qa.shape[1], ka.shape[1]
    shift = scalars[SHIFT]
    for part, (here, there) in enumerate(array_places(ts, shift, swapped)):
        k = in_order(k_parts, shift, part, there)
        v = in_order(v_parts, shift, part, there)
        extra = kt_ref[there, :]
        for head in (0, 1):
            own = head_lanes(k.shape, head)
            ka[head, here, :] = jnp.where(own, k, extra)
            va[head, here, :] = jnp.where(own, v, extra)
        k_turned[:, here] = k.astype(F32).T.astype(BF)
    source = lax.broadcasted_iota(jnp.int32, (LANES, LANES), 0)
    target = lax.broadcasted_iota(jnp.int32, (LANES, LANES), 1)
    rides = (target % HD >= 4) & (target % HD < 7) & ((source < HD) == (target >= HD))
    spread = jnp.where(rides, -1.0, 0.0).astype(BF)
    for part, (here, there) in enumerate(array_places(tq, shift, swapped)):
        q = in_order(q_parts, shift, part, there)
        g, extra = g_ref[there, :], qx_ref[there, :]
        products = g.astype(F32) * o_ref[there, :].astype(F32)
        rough = products.astype(BF)
        delta = dot(rough, spread) + dot((products - rough.astype(F32)).astype(BF), spread)
        lane = lax.broadcasted_iota(jnp.int32, q.shape, 1) % HD
        pieces = three_parts(delta)
        g_extra = jnp.where(lane == 4, pieces[0], jnp.where(lane == 5, pieces[1], pieces[2]))
        g_extra = g_extra.astype(BF)
        for head in (0, 1):
            own = head_lanes(q.shape, head)
            qa[head, here, :] = jnp.where(own, q, extra)
            ga[head, here, :] = jnp.where(own, g, g_extra)
    blocks = tq // block
    for index in reversed(range(blocks)):
        count = (index + 1) * block if causal == "block" else ts
        rows = slice(index * block, (index + 1) * block)
        for head in (0, 1):
            q, g = qa[head, rows, :], ga[head, rows, :]
            scores = dot(ka[head, :count, :], q, NT)
            scores = causal_scores(scores, causal, shift + index * block, block, 1)
            probs = jnp.exp(scores)
            grads = (probs * dot(va[head, :count, :], g, NT)).astype(BF)
            dv, dk = dot(probs.astype(BF), g), dot(grads, q)
            if index == blocks - 1:
                dv_sum[head, :count, :] = dv
                dk_sum[head, :count, :] = dk
            else:
                dv_sum[head, :count, :] += dv
                dk_sum[head, :count, :] += dk
            own_rows = slice(HD * head, HD * (head + 1))
            dq_turned[own_rows, rows] = dot(k_turned[own_rows, :count], grads)
        there = row_block(index, block, tq, shift, swapped)
        dq_ref[there, :] = dq_turned[:, rows].T.astype(BF) * jnp.asarray(scaling, BF)
    for here, there in array_places(ts, shift, swapped):
        own = head_lanes((here.stop - here.start, LANES), 0)
        dk_ref[there, :] = jnp.where(own, dk_sum[0, here, :], dk_sum[1, here, :]).astype(BF)
        dv_ref[there, :] = jnp.where(own, dv_sum[0, here, :], dv_sum[1, here, :]).astype(BF)


ANYWHERE = pl.BlockSpec(memory_space=pl.ANY)


def stay(*arrays):
    return [pltpu.with_memory_space_constraint(x, pltpu.HBM) for x in arrays]


def head_spec(count, start):
    return pl.BlockSpec((pl.Squeezed(), count, LANES), lambda row, pair, _: (row, 0, start + pair))


def shared_spec(count):
    return pl.BlockSpec((pl.Squeezed(), count, LANES), lambda row, pair, _: (row, 0, 0))


def part_specs(q, k, v, first):
    specs, arrays = [], []
    for parts, column in (q, k, v):
        for x in parts:
            specs.append(head_spec(x.shape[1], column // LANES + first))
            arrays.append(x)
    return specs, arrays


class Chain:
    def __init__(self):
        self.last = ()

    def launch(
        self, kernel, scalars, grid, in_specs, arrays, out_specs, out_shape, scratch=(), vmem=48,
        us=5, held=(), free=0,
    ):
        ins = len(arrays)
        arrays = [*stay(*arrays[: ins - free]), *arrays[ins - free :]]
        extra = stay(*held, *self.last)

        outs = len(out_shape)

        def run(scalar_ref, *refs):
            rest = refs[ins + len(extra) :]
            kernel(scalar_ref, *refs[:ins], *rest[:outs], *rest[outs + 1 :])
            rest[outs][...] = jnp.zeros((8, LANES), F32)

        mark = pl.BlockSpec((8, LANES), lambda *_: (0, 0))

        results = pl.pallas_call(
            run,
            grid_spec=pltpu.PrefetchScalarGridSpec(
                num_scalar_prefetch=1,
                grid=grid,
                in_specs=list(in_specs) + [ANYWHERE] * len(extra),
                out_specs=[*out_specs, mark],
                scratch_shapes=list(scratch),
            ),
            out_shape=[pltpu.HBM(x.shape, x.dtype) for x in out_shape]
            + [pltpu.HBM((8, LANES), F32)],
            input_output_aliases={1 + ins + i: i for i in range(len(held))},
            compiler_params=pltpu.CompilerParams(vmem_limit_bytes=vmem * MB),
            cost_estimate=pl.CostEstimate(
                flops=0, bytes_accessed=us * 72000, transcendentals=0
            ),
        )(scalars, *arrays, *extra)
        self.last = (results[-1],)
        return results[:-1]

    def after_last(self, *arrays):
        *arrays, last = lax.optimization_barrier((*arrays, *self.last))
        self.last = (last,)
        return arrays


def attend(chain, q, k, v, terms, scalars, width, causal, block, swapped):
    specs, arrays = part_specs(q, k, v, 0)
    rows = arrays[0].shape[0]
    tq, ts = (sum(x.shape[1] for x in one[0]) for one in (q, k))
    return chain.launch(
        functools.partial(
            forward_kernel, counts=[len(x[0]) for x in (q, k, v)], causal=causal, block=block,
            swapped=swapped,
        ),
        scalars,
        (rows, width // LANES),
        specs + [shared_spec(tq), shared_spec(ts)],
        [*arrays, *terms],
        [head_spec(tq, 0), head_spec(tq, 0)],
        [jax.ShapeDtypeStruct((rows, tq, width), BF)] * 2,
        scratch=[pltpu.VMEM((2, n, LANES), BF) for n in (ts, ts, tq)],
        us=21,
    )


def attend_back(
    chain, q, k, v, g, o, extra, terms, scalars, first, pairs, causal, block, swapped, held=()
):
    specs, arrays = part_specs(q, k, v, first)
    rows, _, width = o.shape
    tq, ts = (sum(x.shape[1] for x in one[0]) for one in (q, k))
    return chain.launch(
        functools.partial(
            backward_kernel, counts=[len(x[0]) for x in (q, k, v)], causal=causal, block=block,
            swapped=swapped, scaling=HD**-0.5,
        ),
        scalars,
        (rows, pairs),
        specs + [head_spec(tq, first)] * 3 + [shared_spec(ts)],
        [*arrays, g, o, extra, terms[1]],
        [head_spec(tq, first), head_spec(ts, first), head_spec(ts, first)],
        [jax.ShapeDtypeStruct((rows, n, width), BF) for n in (tq, ts, ts)],
        scratch=[pltpu.VMEM((2, n, LANES), BF) for n in (ts, ts, tq, tq)]
        + [
            pltpu.VMEM((LANES, ts), BF),
            pltpu.VMEM((2, ts, LANES), F32),
            pltpu.VMEM((2, ts, LANES), F32),
            pltpu.VMEM((LANES, tq), F32),
        ],
        us=6 * pairs,
        held=held,
    )


def norm(resid):
    center = resid - jnp.mean(resid, -1, keepdims=True)
    inverse = lax.rsqrt(jnp.mean(center * center, -1, keepdims=True) + norm_epsilon)
    return center * inverse, inverse


def norm_back(upstream, normed, inverse, gain_vec):
    w = upstream * gain_vec
    return (
        w - jnp.mean(w, -1, keepdims=True) - normed * jnp.mean(w * normed, -1, keepdims=True)
    ) * inverse


def gelu_parts(pre):
    bell = jnp.exp(pre * pre * -0.5)
    t = 1.0 / (1.0 + jnp.abs(pre) * (0.3275911 * 0.5**0.5))
    poly = 0.5 * 1.061405429
    for c in (-1.453152027, 1.421413741, -0.284496736, 0.254829592):
        poly = poly * t + 0.5 * c
    tail = poly * t * bell
    phi_sum = jnp.where(pre >= 0, 1.0 - tail, tail)
    return pre * phi_sum, phi_sum + pre * (bell * 0.3989422804014327)


def add_rows(sums_ref, first, rows):
    for index, value in enumerate(rows):
        here = slice(first + index, first + index + 1)
        sums_ref[here, :] += jnp.sum(value.astype(F32), 0, keepdims=True)


def finish_rows(sums_ref, out_ref):
    @pl.when(pl.program_id(0) == pl.num_programs(0) - 1)
    def _():
        out_ref[...] = sums_ref[...].T


def clear(ref):
    @pl.when(pl.program_id(0) == 0)
    def _():
        ref[...] = jnp.zeros_like(ref)


def row(ref):
    return ref[...][None, :]


def project_kernel(x_ref, *refs, scaled, carried):
    if carried:
        refs[-1][...] = refs[0][...]
        refs = refs[1:-1]
    w_ref, b_ref, out_ref = refs
    width = b_ref.shape[0] // 3
    y = dot(x_ref[...], w_ref[...]) + row(b_ref)
    if scaled:
        out_ref[:, :width] = (y[:, :width] * HD**-0.5).astype(BF)
        out_ref[:, width:] = y[:, width:].astype(BF)
    else:
        out_ref[...] = y.astype(BF)


def after_self_kernel(
    o_ref, x_ref, w_ref, b_ref, gain_ref, bias_ref, qw_ref, qb_ref, n1_ref, i1_ref, h1b_ref, cq_ref,
):
    resid = x_ref[...].astype(F32) + (dot(o_ref[...], w_ref[...]) + row(b_ref))
    n1, i1 = norm(resid)
    h1b = (n1 * row(gain_ref) + row(bias_ref)).astype(BF)
    n1_ref[...] = n1
    i1_ref[...] = jnp.broadcast_to(i1, i1_ref.shape)
    h1b_ref[...] = h1b
    cq_ref[...] = ((dot(h1b, qw_ref[...]) + row(qb_ref)) * HD**-0.5).astype(BF)


def middle_kernel(
    o_ref, n1_ref, up_ref, g1_ref, s1_ref, ow_ref, ob_ref, g2_ref, s2_ref,
    w1_ref, b1_ref, w2_ref, b2_ref, g3_ref, s3_ref,
    *refs, chunk, kept_blocks,
):
    *outs, act_ref, dbf_ref, h2b_ref, dpre_ref, dr2_ref, dbc_ref, dco_ref, sums_ref, slope, sums = refs
    clear(sums)
    h1 = n1_ref[...] * row(g1_ref) + row(s1_ref)
    n2, i2 = norm(h1 + (dot(o_ref[...], ow_ref[...]) + row(ob_ref)))
    h2 = n2 * row(g2_ref) + row(s2_ref)
    h2b = h2.astype(BF)
    h2b_ref[...] = h2b
    hidden = w1_ref.shape[1]
    cols = [slice(c, c + chunk) for c in range(0, hidden, chunk)]
    bias1 = row(b1_ref)
    branch = row(b2_ref)
    for c in cols:
        pre = dot(h2b, w1_ref[:, c]) + bias1[:, c]
        value, slope_c = gelu_parts(pre)
        slope[:, c] = slope_c
        act_c = value.astype(BF)
        act_ref[:, c] = act_c
        branch = branch + dot(act_c, w2_ref[c, :])
    n3, i3 = norm(h2 + branch)
    out = (n3 * row(g3_ref) + row(s3_ref)).astype(BF)
    store_halves(outs, out, kept_blocks)
    up = up_ref[...].astype(F32)
    dr3 = norm_back(up, n3, i3, row(g3_ref))
    dbf = dr3.astype(BF)
    dbf_ref[...] = dbf
    dh2 = dr3
    for c in cols:
        dpre_c = (dot(dbf, w2_ref[c, :], NT) * slope[:, c]).astype(BF)
        dpre_ref[:, c] = dpre_c
        dh2 = dh2 + dot(dpre_c, w1_ref[:, c], NT)
    dr2 = norm_back(dh2, n2, i2, row(g2_ref))
    dbc = dr2.astype(BF)
    dr2_ref[...] = dr2
    dbc_ref[...] = dbc
    dco_ref[...] = dot(dbc, ow_ref[...], NT).astype(BF)
    add_rows(sums, MID_ROWS, (up * n3, up, dbf, dh2 * n2, dh2))
    finish_rows(sums, sums_ref)


def before_self_kernel(
    dcq_ref, dr2_ref, n1_ref, i1_ref, qw_ref, g1_ref, ow_ref, dr1_ref, dba_ref, dso_ref, sums_ref,
    sums,
):
    clear(sums)
    n1 = n1_ref[...]
    dh1 = dr2_ref[...] + dot(dcq_ref[...], qw_ref[...], NT)
    dr1 = norm_back(dh1, n1, i1_ref[:, 0:1], row(g1_ref))
    dba = dr1.astype(BF)
    dr1_ref[...] = dr1
    dba_ref[...] = dba
    dso_ref[...] = dot(dba, ow_ref[...], NT).astype(BF)
    add_rows(sums, LOW_ROWS, (dh1 * n1, dh1))
    finish_rows(sums, sums_ref)


def input_grad_kernel(*refs, count, start, kept_blocks):
    grads, w_ref, outs = refs[:count], refs[count + start], refs[count + start + 1 :]
    total = refs[count][...] if start else None
    width = grads[0].shape[-1]
    for index, ref in enumerate(grads):
        part = dot(ref[...], w_ref[:, index * width : (index + 1) * width], NT)
        total = part if total is None else total + part
    store_halves(outs, total, kept_blocks)


def store_halves(outs, value, kept_blocks):
    if kept_blocks is None:
        outs[0][...] = value.astype(outs[0].dtype)
        return
    step = pl.program_id(0)

    @pl.when(step < kept_blocks)
    def _():
        outs[0][...] = value.astype(outs[0].dtype)

    @pl.when(step >= kept_blocks)
    def _():
        outs[1][...] = value.astype(outs[1].dtype)


class Joined:
    def __init__(self, kept, got, use_kept):
        self.kept, self.got, self.use_kept = kept, got, use_kept

    def __getitem__(self, index):
        return jnp.where(self.use_kept, self.kept[index], self.got[index])


def token_call(
    chain, kernel, block, blocked, whole, outs, scalars, scratch=(), vmem=24, us=5, free=True
):
    def length(x):
        if not isinstance(x, tuple):
            return x.shape[0]
        return x[0].shape[1] * (1 if x[1] is None or isinstance(x[1], str) else 2)

    tokens = length(blocked[0])
    half = tokens // block // 2
    count = tokens // block
    in_specs, arrays, kinds = [], [], []
    for x in blocked:
        if not isinstance(x, tuple):
            in_specs.append(pl.BlockSpec((block, x.shape[1]), lambda i, _: (i, 0)))
            arrays.append(x)
            kinds.append(1)
            continue
        stack, got = x
        shape = (pl.Squeezed(), block, stack.shape[2])
        if got is None or isinstance(got, str):
            row = (lambda p: 1 - p[0]) if got else (lambda p: p[0])
            in_specs.append(pl.BlockSpec(shape, lambda i, p, row=row: (row(p), i, 0)))
            arrays.append(stack)
            kinds.append(1)
        else:
            in_specs.append(pl.BlockSpec(shape, lambda i, p: (p[0], jnp.minimum(i, half - 1), 0)))
            in_specs.append(
                pl.BlockSpec(shape[1:], lambda i, p: (jnp.maximum(i - half, 0), 0))
            )
            arrays += [stack, got]
            kinds.append(2)
    for x in whole:
        zeros = (0,) * x.ndim
        in_specs.append(
            pl.BlockSpec(x.shape, lambda i, _, z=zeros: z, pipeline_mode=pl.Buffered(1))
        )
    out_specs, out_shape = [], []
    for out in outs:
        if out[0] == "whole":
            out_specs.append(pl.BlockSpec(out[1:3], lambda i, _: (0, 0)))
            shape = out[1:3]
        elif out[0] == "kept":
            shape = (out[1], tokens // 2, out[2])
            out_specs.append(
                pl.BlockSpec(
                    (pl.Squeezed(), block, out[2]),
                    lambda i, p: (p[0], jnp.minimum(i, half - 1), 0),
                )
            )
        elif out[0] == "sent":
            shape = (tokens // 2, out[1])
            out_specs.append(
                pl.BlockSpec((block, out[1]), lambda i, _: (jnp.maximum(i - half, 0), 0))
            )
        else:
            shape = (count * block, out[0])
            out_specs.append(pl.BlockSpec((block, out[0]), lambda i, _: (i, 0)))
        out_shape.append(jax.ShapeDtypeStruct(shape, out[-1]))

    def run(_, *refs):
        used = []
        for kind in kinds:
            if kind == 1:
                used.append(refs[0])
            else:
                used.append(Joined(refs[0], refs[1], pl.program_id(0) < half))
            refs = refs[kind:]
        kernel(*used, *refs)

    return chain.launch(
        run, scalars, (count,), in_specs, [*arrays, *whole], out_specs, out_shape, scratch, vmem, us,
        free=len(whole) if free else 0,
    )


def store_kernel(_, got_ref, out_ref):
    out_ref[...] = got_ref[...].astype(out_ref.dtype)


def store_other(chain, held, got, scalars):
    n, c = got.shape
    return chain.launch(
        store_kernel,
        scalars,
        (2,),
        [pl.BlockSpec((n // 2, c), lambda i, _: (i, 0))],
        [got],
        [pl.BlockSpec((pl.Squeezed(), n // 2, c), lambda i, p: (1 - p[0], i, 0))],
        [jax.ShapeDtypeStruct(held.shape, held.dtype)],
        vmem=16,
        us=3,
        held=(held,),
    )


MID_ROWS, LOW_ROWS = 8, 16


def weight_grads(chain, items, extras, scalars, wide, order):
    first_left = items[0][0]
    m = (first_left[0] if isinstance(first_left, tuple) else first_left).shape[-1]
    block = min(item[3] for item in items)
    block = min(block, m)
    specs, arrays, steps = [], [], []
    known = {}
    for left, right, start, columns, sum_row in items:
        key = id(left)
        if key not in known:
            known[key] = (len(arrays), isinstance(left, tuple))
            if isinstance(left, tuple):
                stack, got = left
                specs.append(
                    pl.BlockSpec(
                        (pl.Squeezed(),) + stack.shape[1:], lambda j, p: (p[0], 0, 0),
                        pipeline_mode=pl.Buffered(1),
                    )
                )
                arrays.append(stack)
                left = got
            specs.append(
                pl.BlockSpec(left.shape, lambda j, p: (0, 0), pipeline_mode=pl.Buffered(1))
            )
            arrays.append(left)
        begin, blocks = len(steps), columns // block
        where = len(arrays)
        specs.append(
            pl.BlockSpec(
                (right.shape[0], block),
                lambda j, p, b=begin, n=blocks, f=start // block: (0, f + jnp.clip(j - b, 0, n - 1)),
            )
        )
        arrays.append(right)
        for index in range(blocks):
            steps.append((known[key], where, sum_row, start + index * block, right.shape[1]))
    for extra in extras:
        specs.append(
            pl.BlockSpec(extra.shape, lambda j, p: (0, 0), pipeline_mode=pl.Buffered(1))
        )
    slab = m // len(order)
    size = m // wide
    apart = len(order) > 1
    slabs = len(order) // 2

    def kernel(scalar_ref, *refs):
        ins, rest = refs[: len(arrays)], refs[len(arrays) :]
        extra_refs, (*outs, sums) = rest[: len(extras)], rest[len(extras) :]
        clear(sums)
        step = pl.program_id(0)

        def store(value):
            if not apart:
                outs[0][...] = value.astype(BF)
                return
            core = scalar_ref[CORE]
            for to in range(slabs):
                halves = [
                    value[order[at] * slab : (order[at] + 1) * slab].astype(BF)
                    for at in (to, slabs + to)
                ]
                here = slice(to * slab, (to + 1) * slab)
                outs[0][here, :] = jnp.where(core == 0, halves[1], halves[0])
                outs[1][here, :] = jnp.where(core == 0, halves[0], halves[1])

        for index, ((left, split), right, sum_row, column, columns) in enumerate(steps):

            @pl.when(step == index)
            def _():
                grad = ins[right][...]
                if split:
                    half = ins[left].shape[0]
                    value = dot(ins[left][...], grad[:half], TN)
                    value = value + dot(ins[left + 1][...], grad[half:], TN)
                else:
                    value = dot(ins[left][...], grad, TN)
                store(value)
                if sum_row is None:
                    return
                total = jnp.sum(grad.astype(F32), 0, keepdims=True)
                if columns == m:
                    sums[sum_row : sum_row + 1, column : column + block] = total
                    return
                for piece in range(block // size):
                    w, k = divmod(column // size + piece, columns // m)
                    sums[sum_row + k : sum_row + k + 1, w * size : (w + 1) * size] = total[
                        :, piece * size : (piece + 1) * size
                    ]

        @pl.when(step == len(steps))
        def _():
            value = sums[...].T
            for ref in extra_refs:
                value = value + ref[...]
            store(jnp.concatenate([value, jnp.zeros((m, block - LANES), F32)], 1))

    n = block * len(steps) + LANES
    rows = m // 2 if apart else m
    return chain.launch(
        kernel,
        scalars,
        (len(steps) + 1,),
        specs,
        [*arrays, *extras],
        [pl.BlockSpec((rows, block), lambda j, _: (0, j))] * (m // rows),
        [jax.ShapeDtypeStruct((rows, n), BF)] * (m // rows),
        scratch=[pltpu.VMEM((LANES, m), F32)],
        us=max(4, n // 400),
    )


def tall_grad(chain, left, right, scalars, order):
    tokens, rows = left.shape
    width = right.shape[1]
    apart = len(order) > 1
    blocks = len(order) if apart else 4
    size = rows // blocks
    half = blocks // 2

    def source(j, s):
        if not apart:
            return j
        to = jnp.where(s[CORE] == 0, (j + half) % blocks, j)
        block = 0
        for at, slab in enumerate(order):
            block = jnp.where(to == at, slab, block)
        return block

    def kernel(_, left_ref, right_ref, *refs):
        value = dot(left_ref[...], right_ref[...], TN).astype(BF)
        if not apart:
            refs[-1][...] = value
            return
        other, own = refs[-2:]

        @pl.when(pl.program_id(0) < half)
        def _():
            other[...] = value

        @pl.when(pl.program_id(0) >= half)
        def _():
            own[...] = value

    if apart:
        out_specs = [
            pl.BlockSpec((size, width), lambda j, _: (jnp.minimum(j, half - 1), 0)),
            pl.BlockSpec((size, width), lambda j, _: (jnp.maximum(j - half, 0), 0)),
        ]
        out_shape = [jax.ShapeDtypeStruct((rows // 2, width), BF)] * 2
    else:
        out_specs = [pl.BlockSpec((size, width), lambda j, _: (j, 0))]
        out_shape = [jax.ShapeDtypeStruct((rows, width), BF)]
    return chain.launch(
        kernel,
        scalars,
        (blocks,),
        [
            pl.BlockSpec((tokens, size), lambda j, s: (0, source(j, s))),
            pl.BlockSpec(right.shape, lambda j, _: (0, 0), pipeline_mode=pl.Buffered(1)),
        ],
        [left, right],
        out_specs,
        out_shape,
        us=9,
    )


def vector_rows(x, columns, outs):
    turned = x.astype(F32).T
    for (start, count), out in zip(columns, outs):
        rows = [turned[start + i] for i in range(count)]
        out[...] = rows[0] if count == 1 else jnp.concatenate(rows)


def widen(chain, groups, pieces, columns, scalars):
    pairs = len(groups[0]) == 2
    arrays = [x for group in groups for x in group]
    rows = groups[0][0].shape[0] * len(groups[0])
    size = rows // 8
    specs = [
        pl.BlockSpec(x.shape, lambda i, _: (0, 0), pipeline_mode=pl.Buffered(1)) for x in arrays
    ]

    def convert(ins, outs, index):
        step = pl.program_id(0)
        for out, parts in zip(outs, pieces):
            at = 0
            for group, start, count in parts:
                cols = slice(start, start + count)
                if pairs:
                    here = pl.ds(pl.multiple_of(step % 4 * size, size), size)
                    piece = ins[2 * group + index][here, cols]
                else:
                    piece = ins[8 * group + index][:, cols]
                out[:, at : at + count] = piece.astype(F32)
                at += count

    def extra_of(ins, s):
        count = len(groups[0])
        places = []
        for position in range(count):
            total = 0.0
            for index in range(count):
                flips = position ^ index
                if pairs:
                    same = s[CORE] == flips
                else:
                    same = (
                        (s[CORE] == flips // 4)
                        & (s[SIDE] == flips // 2 % 2)
                        & (s[NEAR] == flips % 2)
                    )
                value = sum(
                    ins[count * group + index][:, x[0].shape[1] - LANES :].astype(F32)
                    for group, x in enumerate(groups)
                )
                total = total + jnp.where(same, value, 0.0)
            places.append(total)
        return jnp.concatenate(places, 0)

    def kernel(s, *refs):
        ins, outs = refs[: len(arrays)], refs[len(arrays) :]
        matrices, vectors = outs[: len(pieces)], outs[len(pieces) :]
        step = pl.program_id(0)
        which = (step // 4 != s[CORE]).astype(jnp.int32)
        if not pairs:
            which = (
                4 * which
                + 2 * (step // 2 % 2 != s[SIDE]).astype(jnp.int32)
                + (step % 2 != s[NEAR]).astype(jnp.int32)
            )
        for index in range(len(groups[0])):

            @pl.when(which == index)
            def _():
                convert(ins, matrices, index)

        if columns:

            @pl.when(step == 7)
            def _():
                vector_rows(extra_of(ins, s), columns, vectors)

    widths = [sum(p[2] for p in parts) for parts in pieces]
    lengths = [count * rows for _, count in columns]
    return chain.launch(
        kernel,
        scalars,
        (8,),
        specs,
        arrays,
        [pl.BlockSpec((size, w), lambda i, _: (i, 0)) for w in widths]
        + [pl.BlockSpec((n,), lambda i, _: (0,)) for n in lengths],
        [jax.ShapeDtypeStruct((rows, w), F32) for w in widths]
        + [jax.ShapeDtypeStruct((n,), F32) for n in lengths],
        vmem=24,
        us=4,
        free=len(arrays),
    )


def vectors_kernel(x_ref, *outs, columns):
    vector_rows(x_ref[...], columns, outs)


def vectors_of(x, columns):
    return pl.pallas_call(
        functools.partial(vectors_kernel, columns=columns),
        out_shape=[jax.ShapeDtypeStruct((count * x.shape[0],), F32) for _, count in columns],
    )(x)


def partner(x, axis, bit=1):
    count = lax.axis_size(axis)
    return lax.ppermute(x, axis, [(i, i ^ bit) for i in range(count)])


def partner_both(x):
    return lax.ppermute(x, ("near", "side"), [(i, 3 - i) for i in range(4)])


ROWS = ("far", "near", "side", "core")


class Reduction:
    def __init__(self, arrays, order):
        self.arrays = arrays
        self.steps = ["core", *order] if len(arrays) == 2 else []
        self.step, self.flying, self.terms = None, [], []

    def total(self, turned=None):
        value = 0.0
        for x, path in self.terms:
            index, parts = 0, 1
            for axis in path:
                index, parts = 2 * index + lax.axis_index(axis), 2 * parts
            if turned:
                index, parts = 2 * index + 1 - lax.axis_index(turned), 2 * parts
            rows = x.shape[0] // parts
            value = value + lax.dynamic_slice_in_dim(x, index * rows, rows, 0).astype(F32)
        return value.astype(BF)

    def land(self, got):
        if not got:
            return
        if self.step == "core":
            self.terms = [(self.arrays[1], ()), (got[0], ())]
        elif self.step in ("wide", "side", "near", "far"):
            self.terms += [(x, ()) for x in got]
        elif self.step == "spread":
            self.pieces = [self.sent, *got]
        elif self.step in JOINS:
            self.terms = [(self.sent, ()), (got[0], ())]
        self.flying = []

    def joined(self):
        (mine, _), (got, _) = self.terms
        first = lax.axis_index(self.step[5:]) == 0
        return jnp.concatenate([jnp.where(first, mine, got), jnp.where(first, got, mine)], 0)

    def prepare(self):
        last, self.step = self.step, self.steps.pop(0)
        if self.step == "core":
            return [self.arrays[0]]
        if last in JOINS:
            self.step, step = last, self.step
            sent = self.joined()
            self.step = step
            return [sent]
        if self.step in JOINS:
            return [self.total()]
        if self.step == "join":
            return self.pieces
        if self.step in ("far", "spread"):
            return [self.total()]
        sent = self.total(self.step)
        self.terms = [(x, path + (self.step,)) for x, path in self.terms]
        return [sent]

    def start(self, sent):
        if self.step in JOINS:
            self.sent = sent[0]
            self.flying = [partner(sent[0], self.step[5:])]
            self.pieces = [sent[0], *self.flying]
        elif self.step == "spread":
            self.sent = sent[0]
            self.flying = [
                partner(sent[0], "near"), partner(sent[0], "side"), partner_both(sent[0])
            ]
        elif self.step == "join":
            self.pieces = [*sent, *(partner(x, "core") for x in sent)]
        elif self.step != "far" or lax.axis_size("far") == 2:
            self.flying = [partner(sent[0], self.step)]

    def result(self):
        x = lax.psum_scatter(self.arrays[0], "wide", scatter_dimension=0, tiled=True)
        return lax.psum(x, ROWS)


CORE_WIDE = (0, 2, 1, 3)
CORE_SIDE = (0, 4, 1, 5, 2, 6, 3, 7)
X_FIRST = ("wide", "side", "near", "far", "spread", "join")
JOINS = ("join_near", "join_side", "join_core")
X_THEN_Y = ("wide", "side", "near", "far") + JOINS
Y_THEN_X = ("side", "wide", "near", "far") + JOINS


def body(
    target, encoded, segments, out_grad,
    self_qkv_w, self_q_b, self_v_b, self_out_w, self_out_b, norm1_gain, norm1_bias,
    cross_q_w, cross_q_b, cross_kv_w, cross_v_b, cross_out_w, cross_out_b, norm2_gain, norm2_bias,
    ffn_in_w, ffn_in_b, ffn_out_w, ffn_out_b, norm3_gain, norm3_bias,
):
    row_count, tok_count, width = target.shape
    hidden = ffn_in_w.shape[1]
    parts = hidden // width
    pairs = width // LANES
    wide = lax.axis_size("wide")
    index = lax.axis_index("wide").astype(jnp.int32)
    scalars = jnp.stack(
        [index]
        + [lax.axis_index(a).astype(jnp.int32) for a in ("core", "side", "near")]
        + [index * tok_count]
    )
    swapped = wide == 2 and row_count == 2
    split = swapped and all(lax.axis_size(a) == 2 for a in ("side", "near", "core"))
    core_wide = CORE_WIDE if split else (0,)
    core_side = CORE_SIDE if split else (0,)
    tokens = row_count * tok_count
    block = min(256, tok_count)
    kept_blocks = tok_count // block if swapped else None

    chain = Chain()

    def run(call, *args, **kwargs):
        return call(chain, *args, **kwargs)

    if swapped:
        def bring(x):
            return x, partner(lax.dynamic_index_in_dim(x, 1 - index, 0, keepdims=False), "wide")

        causal, block_f, block_b = "block", 2 * block, block
        seg_kept, seg_got = bring(segments)
        seg = jnp.concatenate(
            [lax.dynamic_index_in_dim(seg_kept, index, 0, keepdims=False), seg_got]
        )[None]
        key_seg = seg
        row_tokens = tokens
    else:
        def bring(x):
            return x.reshape(tokens, -1)

        causal, block_f, block_b = "mask", block, block
        seg = segments
        key_seg = lax.all_gather(segments, "wide", axis=1, tiled=True)
        row_tokens = tok_count
    terms = (segment_terms(seg)[0], segment_terms(key_seg)[1])

    def by_row(x):
        return x.reshape(-1, row_tokens, x.shape[-1])

    def flat(x):
        return x.reshape(-1, x.shape[-1])

    def keys_of(x):
        return lax.all_gather(x, "wide", axis=1, tiled=True)

    def key_grads(x):
        return x if swapped else lax.psum_scatter(x, "wide", scatter_dimension=1, tiled=True)

    def project(x, w, bias, scaled, carried=None):
        outs = [(w.shape[1], BF)]
        if carried is not None:
            outs.append((carried.shape[-1], BF))
        out = run(
            token_call, functools.partial(project_kernel, scaled=scaled, carried=len(outs) == 2),
            block, (x,) if carried is None else (x, (carried, "other")), (w, bias), outs, scalars,
            us=3,
        )
        y = out[0][None] if swapped else by_row(out[0])
        return y if carried is None else (y, (carried, partner(out[1], "wide")))

    def attention(q, k, v, is_causal):
        return run(
            attend, q, k, v, terms, scalars, width, causal if is_causal else "no", block_f, swapped
        )

    def attention_back(q, k, v, g, o, extra, is_causal, first, count, held=()):
        return run(
            attend_back, q, k, v, by_row(g), o, extra, terms, scalars, first, count,
            causal if is_causal else "no", block_b, swapped, held,
        )

    def input_grad(grads, w, start=None):
        blocked = list(grads) + ([] if start is None else [start])
        outs = [("kept", 2, width, F32), ("sent", width, BF)] if swapped else [(width, F32)]
        kernel = functools.partial(
            input_grad_kernel, count=len(grads), start=0 if start is None else 1,
            kept_blocks=kept_blocks,
        )
        out = run(
            token_call, kernel, block, blocked, (w,), outs, scalars
        )
        return out[0], out[-1]

    def send_back(x):
        return partner(x, "wide") if swapped else None

    def give(out, got):
        if not swapped:
            return out.reshape(row_count, tok_count, width)
        return run(store_other, out, got, scalars)[0]

    def arrive(*reductions, others=()):
        landed = chain.after_last(*others, *(x for r in reductions for x in r.flying))
        others, landed = landed[: len(others)], landed[len(others) :]
        for r in reductions:
            count = len(r.flying)
            r.land(landed[:count])
            landed = landed[count:]
        return others

    def exchange(*reductions, also=(), landing=()):
        if not split:
            return [send_back(x) for x in also] + list(landing)
        flying = [x for r in reductions for x in r.flying]
        landed = chain.after_last(*landing, *flying)
        landing, landed = landed[: len(landing)], landed[len(landing) :]
        for r in reductions:
            count = len(r.flying)
            r.land(landed[:count])
            landed = landed[count:]
        sent = [r.prepare() for r in reductions]
        flat_sent = chain.after_last(*(x for one in sent for x in one), *also)
        for r, one in zip(reductions, sent):
            r.start(flat_sent[: len(one)])
            flat_sent = flat_sent[len(one) :]
        return [send_back(x) for x in flat_sent] + list(landing)

    zeros = jnp.zeros_like(self_q_b)
    qkv_bias = jnp.concatenate([self_q_b, zeros, self_v_b])
    ckv_bias = jnp.concatenate([zeros, cross_v_b])
    x_in = bring(target)
    if swapped:
        ckv = [project((encoded, None), cross_kv_w, ckv_bias, False)]
        qkv = [project((target, None), self_qkv_w, qkv_bias, True)]
        terms = tuple(chain.after_last(*terms))
        got, x_enc = project(x_in[1], self_qkv_w, qkv_bias, True, encoded)
        qkv.append(got)
        self_q, self_k, self_v = (qkv, 0), (qkv, width), (qkv, 2 * width)
    else:
        x_enc, upstream = bring(encoded), bring(out_grad)
        ckv = [keys_of(project(x_enc, cross_kv_w, ckv_bias, False))]
        qkv = [project(x_in, self_qkv_w, qkv_bias, True)]
        both = [keys_of(qkv[0][..., width:])]
        self_q, self_k, self_v = (qkv, 0), (both, 0), (both, width)
    self_o, self_x = attention(self_q, self_k, self_v, True)
    self_ob = flat(self_o)
    n1, i1, h1b, cq = run(
        token_call, after_self_kernel, 2 * block, (self_ob, x_in),
        (self_out_w, self_out_b, norm1_gain, norm1_bias, cross_q_w, cross_q_b),
        [(width, F32), (LANES, F32), (width, BF), (width, BF)], scalars,
    )
    if swapped:
        got, upstream = project(x_enc[1], cross_kv_w, ckv_bias, False, out_grad)
        ckv.append(got)
    cross_q, cross_k, cross_v = ([by_row(cq)], 0), (ckv, 0), (ckv, width)
    cross_o, cross_x = attention(cross_q, cross_k, cross_v, False)
    cross_ob = flat(cross_o)
    outs = [("kept", 2, width, BF), ("sent", width, BF)] if swapped else [(width, BF)]
    *h3, act, dbf, h2b, dpre, dr2, dbc, dco, mid_sums = run(
        token_call, functools.partial(middle_kernel, chunk=width, kept_blocks=kept_blocks),
        block, (cross_ob, n1, upstream),
        (
            norm1_gain, norm1_bias, cross_out_w, cross_out_b, norm2_gain, norm2_bias,
            ffn_in_w, ffn_in_b, ffn_out_w, ffn_out_b, norm3_gain, norm3_bias,
        ),
        outs
        + [
            (hidden, BF), (width, BF), (width, BF), (hidden, BF), (width, F32),
            (width, BF), (width, BF), ("whole", width, LANES, F32),
        ],
        scalars,
        scratch=[pltpu.VMEM((block, hidden), F32), pltpu.VMEM((LANES, width), F32)],
        vmem=56,
        us=45,
    )

    rb = Reduction(
        run(
            weight_grads, [(h2b, dpre, 0, hidden, 0), (cross_ob, dbc, 0, width, parts)],
            [mid_sums], scalars, wide, core_side,
        ),
        Y_THEN_X,
    )
    exchange(rb)
    ra = Reduction(run(tall_grad, act, dbf, scalars, core_wide), X_THEN_Y)
    exchange(ra)
    exchange(ra, rb)
    dcq, dck, dcv = attention_back(
        cross_q, cross_k, cross_v, dco, cross_o, cross_x, False, 0, pairs
    )
    dcq, dck, dcv = flat(dcq), flat(key_grads(dck)), flat(key_grads(dcv))
    exchange(ra, rb)
    dr1, dba, dso, low_sums = run(
        token_call, before_self_kernel, 2 * block, (dcq, dr2, n1, i1),
        (cross_q_w, norm1_gain, self_out_w),
        [(width, F32), (width, BF), (width, BF), ("whole", width, LANES, F32)], scalars,
        scratch=[pltpu.VMEM((LANES, width), F32)],
        free=False,
        vmem=40,
    )
    rc = Reduction(
        run(
            weight_grads,
            [
                (h1b, dcq, 0, width, 0), (x_enc, dck, 0, width, None), (x_enc, dcv, 0, width, 1),
                (self_ob, dba, 0, width, 2),
            ],
            [low_sums], scalars, wide, core_side,
        ),
        Y_THEN_X,
    )
    (got_out,) = exchange(ra, rb, rc, also=(h3[-1],))
    self_args = (self_q, self_k, self_v, dso, self_o, self_x, True)
    if swapped:
        cut = pairs // 2
        held = attention_back(*self_args, 0, cut)
        exchange(ra, rb, rc)
        dsq, dsk, dsv = attention_back(*self_args, cut, pairs - cut, held)
    else:
        dsq, dsk, dsv = attention_back(*self_args, 0, pairs)
    dsq, dsk, dsv = flat(dsq), flat(key_grads(dsk)), flat(key_grads(dsv))
    rd = Reduction(
        run(
            weight_grads,
            [(x_in, dsq, 0, width, 0), (x_in, dsk, 0, width, None), (x_in, dsv, 0, width, 1)],
            [], scalars, wide, core_wide,
        ),
        X_FIRST,
    )
    if split:
        arrive(rb)
    (got_out,) = exchange(rd, ra, rc, landing=(got_out,))
    in_kept, in_sent = input_grad([dsq, dsk, dsv], self_qkv_w, dr1)

    vectors_b = [(0, parts), (parts, 1)] + [(MID_ROWS + i, 1) for i in range(5)]
    vectors_c = [(0, 1), (1, 1), (2, 1), (LOW_ROWS, 1), (LOW_ROWS + 1, 1)]
    vectors_d = [(0, 1), (1, 1)]
    pieces_b = [[(0, 0, hidden)], [(0, hidden, width)]]
    pieces_c = [[(0, 0, width)], [(0, width, 2 * width)], [(0, 3 * width, width)]]
    if split:
        arrive(rd, ra, rc)
        exchange(rd)
        (got_in,) = exchange(ra, rb, rc, also=(in_sent,))
        enc_kept, enc_sent = input_grad([dck, dcv], cross_kv_w)
        arrive(rd, ra, rb, rc)
        exchange(rd)
        (got_enc,) = exchange(rc, rb, also=(enc_sent,))
        layer_out = give(h3[0], got_out)
        (got_in,) = arrive(rd, others=(got_in,))
        exchange(rd)
        exchange(rc, ra)
        (ffn_out_w_grad,) = run(widen, [ra.pieces], [[(0, 0, width)]], [], scalars)
        exchange(rd)
        exchange(rc)
        target_grad = give(in_kept, got_in)
        (got_enc,) = arrive(rd, others=(got_enc,))
        exchange(rd)
        exchange(rc, rb)
        out_b = run(widen, [rb.pieces], pieces_b, vectors_b, scalars)
        out_c = run(widen, [rc.pieces], pieces_c, vectors_c, scalars)
        exchange(rd)
        encoded_grad = give(enc_kept, got_enc)
        pieces_d = [[(0, 0, 3 * width)]]
        out_d = run(widen, [rd.pieces], pieces_d, vectors_d, scalars)
    else:
        enc_kept, _ = input_grad([dck, dcv], cross_kv_w)
        layer_out, target_grad, encoded_grad = (
            give(x, None) for x in (h3[0], in_kept, enc_kept)
        )

        def columns_of(x, pieces, vectors):
            return [
                jnp.concatenate([x[:, start : start + size] for _, start, size in p], 1).astype(F32)
                for p in pieces
            ] + list(vectors_of(x[:, -LANES:], vectors))

        ffn_out_w_grad = ra.result().astype(F32)
        out_b = columns_of(rb.result(), pieces_b, vectors_b)
        out_c = columns_of(rc.result(), pieces_c, vectors_c)
        out_d = columns_of(rd.result(), [[(0, 0, 3 * width)]], vectors_d)
    (
        ffn_in_w_grad, cross_out_w_grad, ffn_in_b_grad, cross_out_b_grad, norm3_gain_grad,
        norm3_bias_grad, ffn_out_b_grad, norm2_gain_grad, norm2_bias_grad,
    ) = out_b
    (
        cross_q_w_grad, cross_kv_w_grad, self_out_w_grad, cross_q_b_grad, cross_v_b_grad,
        self_out_b_grad, norm1_gain_grad, norm1_bias_grad,
    ) = out_c
    self_qkv_w_grad, self_q_b_grad, self_v_b_grad = out_d
    return (
        layer_out, target_grad, encoded_grad,
        self_qkv_w_grad, self_q_b_grad, self_v_b_grad,
        self_out_w_grad, self_out_b_grad, norm1_gain_grad, norm1_bias_grad,
        cross_q_w_grad, cross_q_b_grad, cross_kv_w_grad, cross_v_b_grad,
        cross_out_w_grad, cross_out_b_grad, norm2_gain_grad, norm2_bias_grad,
        ffn_in_w_grad, ffn_in_b_grad, ffn_out_w_grad, ffn_out_b_grad,
        norm3_gain_grad, norm3_bias_grad,
    )


def solution(mesh):
    wide, narrow = mesh.shape["wide"], mesh.shape["narrow"]
    core = 2 if narrow % 2 == 0 else 1
    side = 2 if narrow % (2 * core) == 0 else 1
    near = 2 if narrow % (2 * core * side) == 0 else 1
    devices = mesh.devices.reshape(wide, narrow // (near * side * core), near, side, core)
    split = Mesh(devices, ("wide",) + ROWS)
    token_spec = P(ROWS, "wide", None)
    in_specs = (token_spec, token_spec, P(ROWS, "wide"), token_spec) + (P(),) * 21
    matrix, vector = P("wide", None), P("wide")
    out_specs = (token_spec,) * 3 + (
        matrix, vector, vector, matrix, vector, vector, vector,
        matrix, vector, matrix, vector, matrix, vector, vector, vector,
        matrix, vector, matrix, vector, vector, vector,
    )
    return jax.shard_map(body, mesh=split, in_specs=in_specs, out_specs=out_specs, check_vma=False)
```
